32 devices in a mesh: section: 4 (over y, x), dp: 8 (over z, core).
Axes of the slice: x: 2, y: 2, z: 4, core: 2. Of those that a mesh axis runs over, the one named last changes fastest.
Arguments:
- tokens: bfloat16 [8, 1024, 1024], P('dp'), may hold values from -6 to 6
- lengths: int32 [8], P('dp'), may hold values from 128 to 1024
- cotangent: bfloat16 [8, 1024, 1024], P('dp'), may hold values from -6 to 6
- norm_gain: float32 [2, 1024], P(None, 'dp'), may hold values from 0.5 to 1.5
- norm_shift: float32 [2, 1024], P(None, 'dp'), may hold values from -2 to 2
- average_decay: float32 [2, 16, 1024], P(None, None, 'dp'), may hold values from 2.5 to 7
- average_input: float32 [2, 16, 1024], P(None, None, 'dp'), may hold values from -4 to 4
- average_output: float32 [2, 16, 1024], P(None, None, 'dp'), may hold values from -1.5 to 1.5
- average_skip: float32 [2, 1024], P(None, 'dp'), may hold values from 0.5 to 1.5
- value_weight: bfloat16 [2, 1024, 2048], P(None, 'dp'), may hold values from -0.1875 to 0.1875
- value_bias: float32 [2, 2048], P(None, 'dp'), may hold values from -2 to 2
- base_weight: bfloat16 [2, 1024, 4224], P(None, 'dp'), may hold values from -0.1875 to 0.1875
- base_bias: float32 [2, 4224], P(None, 'dp'), may hold values from -2 to 2
- pair_scale: float32 [2, 2, 128], P(None, None, 'dp'), may hold values from -5 to 5
- query_shift: float32 [2, 128], P(None, 'dp'), may hold values from -3 to 3
- out_weight: bfloat16 [2, 2048, 1024], P(None, 'dp'), may hold values from -0.375 to 0.375
- feed_gain: float32 [2, 1024], P(None, 'dp'), may hold values from 0.5 to 1.5
- feed_shift: float32 [2, 1024], P(None, 'dp'), may hold values from -2 to 2
- feed_in_weight: bfloat16 [2, 1024, 4096], P(None, 'dp'), may hold values from -0.1875 to 0.1875
- feed_in_bias: float32 [2, 4096], P(None, 'dp'), may hold values from -2 to 2
- feed_out_weight: bfloat16 [2, 4096, 1024], P(None, 'dp'), may hold values from -0.09375 to 0.09375
- feed_out_bias: float32 [2, 1024], P(None, 'dp'), may hold values from -2 to 2
Outputs:
- block_out: bfloat16 [8, 1024, 1024], P('dp', 'section')
- input_grad: bfloat16 [8, 1024, 1024], P('dp', 'section')
- grad_norm_gain: float32 [2, 1024], P(None, 'dp')
- grad_norm_shift: float32 [2, 1024], P(None, 'dp')
- grad_average_decay: float32 [2, 16, 1024], P(None, None, 'dp')
- grad_average_input: float32 [2, 16, 1024], P(None, None, 'dp')
- grad_average_output: float32 [2, 16, 1024], P(None, None, 'dp')
- grad_average_skip: float32 [2, 1024], P(None, 'dp')
- grad_value_weight: float32 [2, 1024, 2048], P(None, 'dp')
- grad_value_bias: float32 [2, 2048], P(None, 'dp')
- grad_base_weight: float32 [2, 1024, 4224], P(None, 'dp')
- grad_base_bias: float32 [2, 4224], P(None, 'dp')
- grad_pair_scale: float32 [2, 2, 128], P(None, None, 'dp')
- grad_query_shift: float32 [2, 128], P(None, 'dp')
- grad_out_weight: float32 [2, 2048, 1024], P(None, 'dp')
- grad_feed_gain: float32 [2, 1024], P(None, 'dp')
- grad_feed_shift: float32 [2, 1024], P(None, 'dp')
- grad_feed_in_weight: float32 [2, 1024, 4096], P(None, 'dp')
- grad_feed_in_bias: float32 [2, 4096], P(None, 'dp')
- grad_feed_out_weight: float32 [2, 4096, 1024], P(None, 'dp')
- grad_feed_out_bias: float32 [2, 1024], P(None, 'dp')
The draws below stay inside these ranges and needn't reach their ends.
Inputs may be any that keep to these rules, and one draw needn't show every extreme that they name: Slot s holds real tokens at positions 0 to lengths[s] - 1; later positions are padding.
All inputs are finite; a program needn't handle non-finite values.
Results may differ from the reference program's by a relative error of at most 0.04.
Values may be sent and summed in bfloat16 or wider, within the bound.
A program may use at most 448 MiB of HBM per device.

```python
import jax
import jax.numpy as jnp
from jax import lax

D = 1024
Z = 128
V = 2048
EMA = 16
FF = 4096
LAYERS = 2
ATT_BLOCK = 128
EMA_BLOCK = 64
SLOT = 1024
SLOTS = 8
BASE = 4224


def plant(drawn, own_key, low, high):
    shape = drawn.shape
    spot = [jax.random.randint(jax.random.fold_in(own_key, axis), (), 0, shape[axis]) for axis in range(len(shape))]
    drawn = drawn.at[tuple(spot)].set(low)
    longest = shape.index(max(shape))
    spot[longest] = (spot[longest] + 1) % shape[longest]
    return drawn.at[tuple(spot)].set(high)


def levels(rng, extent, cuts, least, high):
    loudness, own = 1.0, jax.random.fold_in(rng, 6)
    for position, shards_of in cuts:
        steps = jnp.exp(jax.random.uniform(jax.random.fold_in(own, position), (shards_of,), jnp.float32, least / len(cuts), high / len(cuts)))
        loudness = loudness * jnp.repeat(steps, extent[position] // shards_of).reshape([-1 if axis == position else 1 for axis in range(len(extent))])
    return loudness


def gaussian(key, shape, scale, reach, cuts=(), kind=jnp.bfloat16):
    entries = scale * jax.random.normal(key, shape, jnp.float32)
    if cuts:
        entries = entries * levels(key, shape, cuts, -0.22, 0.18)
    return jnp.clip(entries, -reach, reach).astype(kind)


def setup_inputs(seed: int = 0) -> dict:
    key_list = jax.random.split(jax.random.key(seed), 23)
    return {
        "tokens": gaussian(key_list[0], (SLOTS, SLOT, D), 1.0, 6.0, ((0, 8),)),
        "lengths": plant(jax.random.randint(key_list[1], (SLOTS,), SLOT // 8, SLOT + 1), jax.random.fold_in(key_list[1], 1), SLOT // 8, SLOT).astype(jnp.int32),
        "cotangent": gaussian(key_list[2], (SLOTS, SLOT, D), 1.0, 6.0, ((0, 8),)),
        "norm_gain": jnp.clip(1.0 + 0.1 * jax.random.normal(key_list[3], (LAYERS, D), jnp.float32), 0.5, 1.5),
        "norm_shift": gaussian(key_list[4], (LAYERS, D), 0.3, 2.0, ((1, 8),), jnp.float32),
        "average_decay": jnp.clip(2.5 + 4.5 * jax.random.uniform(key_list[5], (LAYERS, EMA, D), jnp.float32) ** levels(key_list[5], (LAYERS, EMA, D), ((2, 8),), -0.2, 0.2), 2.5, 7.0),
        "average_input": gaussian(key_list[6], (LAYERS, EMA, D), 1.0, 4.0, ((2, 8),), jnp.float32),
        "average_output": gaussian(key_list[7], (LAYERS, EMA, D), EMA ** -0.5, 1.5, ((2, 8),), jnp.float32),
        "average_skip": jnp.clip(0.5 + 1.0 * jax.random.uniform(key_list[8], (LAYERS, D), jnp.float32) ** levels(key_list[8], (LAYERS, D), ((1, 8),), -0.2, 0.2), 0.5, 1.5),
        "value_weight": gaussian(key_list[9], (LAYERS, D, V), D ** -0.5, 0.1875, ((1, 8),)),
        "value_bias": gaussian(key_list[10], (LAYERS, V), 0.3, 2.0, ((1, 8),), jnp.float32),
        "base_weight": gaussian(key_list[11], (LAYERS, D, BASE), D ** -0.5, 0.1875, ((1, 8),)),
        "base_bias": gaussian(key_list[12], (LAYERS, BASE), 0.3, 2.0, ((1, 8),), jnp.float32),
        "pair_scale": gaussian(key_list[13], (LAYERS, 2, Z), 1.5, 5.0, ((2, 8),), jnp.float32),
        "query_shift": gaussian(key_list[14], (LAYERS, Z), 0.5, 3.0, ((1, 8),), jnp.float32),
        "out_weight": gaussian(key_list[15], (LAYERS, V, D), (V // 8) ** -0.5, 0.375, ((1, 8),)),
        "feed_gain": jnp.clip(1.0 + 0.1 * jax.random.normal(key_list[16], (LAYERS, D), jnp.float32), 0.5, 1.5),
        "feed_shift": gaussian(key_list[17], (LAYERS, D), 0.3, 2.0, ((1, 8),), jnp.float32),
        "feed_in_weight": gaussian(key_list[18], (LAYERS, D, FF), D ** -0.5, 0.1875, ((1, 8),)),
        "feed_in_bias": gaussian(key_list[19], (LAYERS, FF), 0.3, 2.0, ((1, 8),), jnp.float32),
        "feed_out_weight": gaussian(key_list[20], (LAYERS, FF, D), FF ** -0.5, 0.09375, ((1, 8),)),
        "feed_out_bias": gaussian(key_list[21], (LAYERS, D), 0.3, 2.0, ((1, 8),), jnp.float32),
    }


eps = 1e-05
big_negative = -1000000000.0

@jax.custom_vjp
def low(v):
    return lax.optimization_barrier(v.astype(jnp.bfloat16)).astype(jnp.float32)

@jax.custom_vjp
def low_back(v):
    return v

def low_keep(v):
    return (low(v), None)

def low_pass(kept, grad):
    return (grad,)

def back_keep(v):
    return (v, None)

def back_low(kept, grad):
    return (low(grad),)
low.defvjp(low_keep, low_pass)
low_back.defvjp(back_keep, back_low)

def product(left, right):
    return low_back(jnp.dot(low(left), low(right), precision=lax.Precision.HIGHEST, preferred_element_type=jnp.float32))

def batched(left, right):
    return low_back(jnp.einsum('nij,njk->nik', low(left), low(right), precision=lax.Precision.HIGHEST))

def layer_norm(rows, gain, shift):
    centre = lax.optimization_barrier(jnp.mean(rows, axis=-1, keepdims=True))
    centered = rows - centre
    spread = lax.optimization_barrier(jnp.mean(centered * centered, axis=-1, keepdims=True))
    return centered * lax.rsqrt(spread + eps) * gain + shift

def softmax_rows(scores):
    shifted = scores - lax.optimization_barrier(jnp.max(scores, axis=-1, keepdims=True))
    raised = jnp.exp(shifted)
    return raised / lax.optimization_barrier(jnp.sum(raised, axis=-1, keepdims=True))

def moving_average(rows, state, decay, weight_in, weight_out):
    length, width = rows.shape
    block = EMA_BLOCK
    log_rate = -jnp.log1p(jnp.exp(-decay))
    drive = (1.0 - jnp.exp(log_rate)) * weight_in
    steps = jnp.arange(block).astype(jnp.float32)
    powers = jnp.exp(steps[:, None, None] * log_rate[None])
    kernel = lax.optimization_barrier(jnp.sum(powers * (drive * weight_out)[None], axis=1))
    lag = jnp.arange(block, dtype=jnp.int32)[:, None] - jnp.arange(block, dtype=jnp.int32)[None, :]
    toeplitz = jnp.where((lag >= 0)[:, :, None], kernel[jnp.clip(lag, 0, block - 1)], 0.0)
    pieces = rows.reshape(length // block, block, width)
    inner = jnp.einsum('tsd,nsd->ntd', toeplitz, pieces, precision=lax.Precision.HIGHEST)
    tail = jnp.exp((block - 1.0 - steps)[:, None, None] * log_rate[None]) * drive[None]
    entering = jnp.einsum('sed,nsd->ned', tail, pieces, precision=lax.Precision.HIGHEST)
    full = jnp.exp(block * log_rate)

    def advance(carry, piece):
        return (full * carry + piece, carry)
    last, before = lax.scan(advance, state, entering)
    lead = jnp.exp((steps + 1.0)[:, None, None] * log_rate[None]) * weight_out[None]
    outer = jnp.einsum('ted,ned->ntd', lead, before, precision=lax.Precision.HIGHEST)
    return ((inner + outer).reshape(length, width), last)

def attention_layer(rows, valid, state, weights):
    gain, shift, decay, weight_in, weight_out, skip, value_matrix, value_offset, base_matrix, base_offset, scale_pair, query_offset, out_matrix = weights
    length, width = rows.shape
    key_width = scale_pair.shape[-1]
    value_width = value_matrix.shape[-1]
    normed = layer_norm(rows, gain, shift)
    masked = normed * valid[:, None]
    smooth, state_out = moving_average(masked, state, decay, weight_in, weight_out)
    mixed = jax.nn.silu(smooth + skip * masked)
    values = jax.nn.silu(product(normed, value_matrix) + value_offset)
    base = product(mixed, base_matrix) + base_offset
    update = jax.nn.sigmoid(base[:, :width])
    shared = jax.nn.silu(base[:, width:width + key_width])
    reset = jax.nn.silu(base[:, width + key_width:width + key_width + value_width])
    candidate = base[:, width + key_width + value_width:]
    queries = shared * scale_pair[0] + query_offset
    keys = shared * scale_pair[1]
    blocks = length // ATT_BLOCK
    scores = batched(queries.reshape(blocks, ATT_BLOCK, key_width), keys.reshape(blocks, ATT_BLOCK, key_width).transpose(0, 2, 1)) * key_width ** (-0.5)
    allowed = valid.reshape(blocks, 1, ATT_BLOCK) > 0.5
    probs = softmax_rows(jnp.where(allowed, scores, big_negative))
    attended = batched(probs, values.reshape(blocks, ATT_BLOCK, value_width)).reshape(length, value_width) * valid[:, None]
    hidden = jax.nn.silu(candidate + product(attended * reset, out_matrix))
    return (rows + update * (hidden - rows), state_out)

def feed_forward(rows, weights):
    gain, shift, in_matrix, in_offset, out_matrix, out_offset = weights
    normed = layer_norm(rows, gain, shift)
    active = jax.nn.silu(product(normed, in_matrix) + in_offset)
    return rows + product(active, out_matrix) + out_offset

def reference(tokens, lengths, cotangent, norm_gain, norm_shift, average_decay, average_input, average_output, average_skip, value_weight, value_bias, base_weight, base_bias, pair_scale, query_shift, out_weight, feed_gain, feed_shift, feed_in_weight, feed_in_bias, feed_out_weight, feed_out_bias):
    attention = tuple((stack.astype(jnp.float32) for stack in (norm_gain, norm_shift, average_decay, average_input, average_output, average_skip, value_weight, value_bias, base_weight, base_bias, pair_scale, query_shift, out_weight)))
    feed = tuple((stack.astype(jnp.float32) for stack in (feed_gain, feed_shift, feed_in_weight, feed_in_bias, feed_out_weight, feed_out_bias)))
    positions = jnp.arange(SLOT, dtype=jnp.int32)
    blank_state = jnp.zeros((EMA, D), jnp.float32)

    def one_slot(totals, inputs):
        rows, size, grad_out = inputs
        valid = (positions < size).astype(jnp.float32)

        def network(start_rows, layers_attention, layers_feed):
            current = start_rows
            for layer in range(LAYERS):
                current, _ = attention_layer(current, valid, blank_state, tuple((stack[layer] for stack in layers_attention)))
                current = low_back(low(current))
                current = feed_forward(current, tuple((stack[layer] for stack in layers_feed)))
                if layer + 1 < LAYERS:
                    current = low_back(low(current))
            return low(current)
        result, pull = jax.vjp(network, rows.astype(jnp.float32), attention, feed)
        grad_rows, grad_attention, grad_feed = pull(grad_out.astype(jnp.float32))
        totals = jax.tree.map(jnp.add, totals, (grad_attention, grad_feed))
        return (totals, (result.astype(jnp.bfloat16), grad_rows.astype(jnp.bfloat16)))
    zeros = jax.tree.map(jnp.zeros_like, (attention, feed))
    totals, outputs = lax.scan(one_slot, zeros, (tokens, lengths, cotangent))
    grad_attention, grad_feed = totals
    return (outputs[0], outputs[1], grad_attention[0], grad_attention[1], grad_attention[2], grad_attention[3], grad_attention[4], grad_attention[5], grad_attention[6], grad_attention[7], grad_attention[8], grad_attention[9], grad_attention[10], grad_attention[11], grad_attention[12], grad_feed[0], grad_feed[1], grad_feed[2], grad_feed[3], grad_feed[4], grad_feed[5])
```

```python
import functools

import jax
import jax.numpy as jnp
from jax import lax
from jax.experimental import pallas as pl
from jax.experimental.pallas import tpu as pltpu
from jax.sharding import PartitionSpec as P

F32 = jnp.float32
BF16 = jnp.bfloat16
MESH = pl.DeviceIdType.MESH
ATT = 128
LANES = 128
CHUNKS = 8
ROWS = 256
STRIP = 64
EPS = 1e-05
NEGATIVE = -1000000000.0
VMEM_BYTES = 56 * 1024 * 1024


def vmem():
    return pl.BlockSpec(memory_space=pltpu.VMEM)


def smem():
    return pl.BlockSpec(memory_space=pltpu.SMEM)


def hbm():
    return pl.BlockSpec(memory_space=pl.ANY)


def shape(dims, kind):
    return jax.ShapeDtypeStruct(dims, kind)


def sigmoid(v):
    return 0.5 * jnp.tanh(0.5 * v) + 0.5


def silu(v):
    return v * sigmoid(v)


def silu_slope(v):
    s = sigmoid(v)
    return s * (1.0 + v * (1.0 - s))


def dot(left, right, left_dim=1, right_dim=0):
    return lax.dot_general(
        left, right, (((left_dim,), (right_dim,)), ((), ())), preferred_element_type=F32
    )


def normalise(x):
    centred = x - jnp.mean(x, axis=-1, keepdims=True)
    spread = jnp.mean(centred * centred, axis=-1, keepdims=True)
    scale = lax.rsqrt(spread + EPS)
    return centred * scale, scale


def row_valid(start, rows, length):
    place = start + lax.broadcasted_iota(jnp.int32, (rows, 1), 0)
    return (place < length).astype(F32)


def params(**more):
    return pltpu.CompilerParams(vmem_limit_bytes=VMEM_BYTES, **more)


def spread_rows(ref, lanes, count):
    return [ref[n, :, lanes] for n in range(count)]


def on_sublanes(array):
    return jnp.broadcast_to(array[:, None, :], (array.shape[0], CHUNKS, array.shape[1]))


def power(base, exponent):
    result = None
    square = base
    while exponent:
        if exponent % 2:
            result = square if result is None else result * square
        exponent //= 2
        if exponent:
            square = square * square
    return result


def entering(last, rate, steps, reverse=False):
    row = lax.broadcasted_iota(jnp.int32, (CHUNKS, LANES), 0)
    weight = power(rate, steps)
    span = 1
    while span < CHUNKS:
        if reverse:
            moved = jnp.where(row < CHUNKS - span, pltpu.roll(last, CHUNKS - span, 0), 0.0)
        else:
            moved = jnp.where(row >= span, pltpu.roll(last, span, 0), 0.0)
        last = last + weight * moved
        weight = weight * weight
        span *= 2
    if reverse:
        return jnp.where(row < CHUNKS - 1, pltpu.roll(last, CHUNKS - 1, 0), 0.0)
    return jnp.where(row >= 1, pltpu.roll(last, 1, 0), 0.0)


def entering_pair(last, slope, rate, steps):
    row = lax.broadcasted_iota(jnp.int32, (CHUNKS, LANES), 0)
    weight = power(rate, steps)
    tilt = float(steps) * power(rate, steps - 1)
    span = 1
    while span < CHUNKS:
        moved = jnp.where(row >= span, pltpu.roll(last, span, 0), 0.0)
        moved_slope = jnp.where(row >= span, pltpu.roll(slope, span, 0), 0.0)
        slope = slope + weight * moved_slope + tilt * moved
        last = last + weight * moved
        tilt = 2.0 * weight * tilt
        weight = weight * weight
        span *= 2
    first = row >= 1
    return (
        jnp.where(first, pltpu.roll(last, 1, 0), 0.0),
        jnp.where(first, pltpu.roll(slope, 1, 0), 0.0),
    )


def average_forward_kernel(
    length_ref,
    x_ref,
    gain_ref,
    shift_ref,
    rate_ref,
    coef_ref,
    skip_ref,
    normed_ref,
    mixed_ref,
    pre_ref,
    own_ref,
    scale_ref,
    rows_buf,
    m_buf,
    y_buf,
):
    length = length_ref[0]
    count, width = x_ref.shape
    own = mixed_ref.shape[1]
    dims = rate_ref.shape[0]
    steps = count // CHUNKS
    mine = pl.ds(pl.multiple_of(lax.axis_index("section") * own, LANES), own)

    def norm_strip(i, carry):
        start = pl.multiple_of(i * STRIP, STRIP)
        here = pl.ds(start, STRIP)
        n, scale = normalise(x_ref[here, :].astype(F32))
        rows_buf[...] = n
        normed_ref[here, :] = (n * gain_ref[...] + shift_ref[...]).astype(BF16)
        part = rows_buf[:, mine]
        own_ref[here, :] = part
        scale_ref[here, :] = jnp.broadcast_to(scale, (STRIP, LANES))
        masked = (part * gain_ref[:, mine] + shift_ref[:, mine]) * row_valid(start, STRIP, length)
        for group in range(own // LANES):
            m_buf[group, here, :] = masked[:, group * LANES : (group + 1) * LANES]
        return carry

    lax.fori_loop(0, count // STRIP, norm_strip, 0)

    for group in range(own // LANES):
        lanes = slice(group * LANES, (group + 1) * LANES)
        rates = spread_rows(rate_ref, lanes, dims)
        coefs = spread_rows(coef_ref, lanes, dims)
        blank = tuple(jnp.zeros((CHUNKS, LANES), F32) for _ in range(dims))
        m_part, y_part = m_buf.at[group], y_buf.at[group]

        def finals(t, states):
            x = m_part[pl.ds(t, CHUNKS, stride=steps), :]
            return tuple(r * h + x for r, h in zip(rates, states))

        ends = lax.fori_loop(0, steps, finals, blank, unroll=4)
        starts = tuple(entering(h, r, steps) for h, r in zip(ends, rates))

        def outputs(t, states):
            x = m_part[pl.ds(t, CHUNKS, stride=steps), :]
            states = tuple(r * h + x for r, h in zip(rates, states))
            terms = [c * h for c, h in zip(coefs, states)]
            while len(terms) > 1:
                terms = [a + b for a, b in zip(terms[::2], terms[1::2])]
            y_part[pl.ds(t, CHUNKS, stride=steps), :] = terms[0]
            return states

        lax.fori_loop(0, steps, outputs, starts, unroll=4)

    def mix_strip(i, carry):
        here = pl.ds(pl.multiple_of(i * STRIP, STRIP), STRIP)
        for group in range(own // LANES):
            lanes = slice(group * LANES, (group + 1) * LANES)
            pre = y_buf[group, here, :] + skip_ref[:, lanes] * m_buf[group, here, :]
            pre_ref[here, lanes] = pre.astype(BF16)
            mixed_ref[here, lanes] = silu(pre).astype(BF16)
        return carry

    lax.fori_loop(0, count // STRIP, mix_strip, 0)


def average_forward(length, x, gain, shift, rate, coef, skip):
    count, width = x.shape
    own = skip.shape[1]
    groups = own // LANES
    rate, coef = on_sublanes(rate), on_sublanes(coef)
    return pl.pallas_call(
        average_forward_kernel,
        out_shape=(
            shape((count, width), BF16),
            shape((count, own), BF16),
            shape((count, own), BF16),
            shape((count, own), F32),
            shape((count, LANES), F32),
        ),
        in_specs=[smem()] + [vmem()] * 6,
        out_specs=(vmem(),) * 5,
        scratch_shapes=[
            pltpu.VMEM((STRIP, width), F32),
            pltpu.VMEM((groups, count, LANES), F32),
            pltpu.VMEM((groups, count, LANES), F32),
        ],
        compiler_params=params(),
    )(length, x, gain, shift, rate, coef, skip)


def average_backward_kernel(
    length_ref,
    gmixed_ref,
    gvalue_ref,
    pre_ref,
    own_ref,
    scale_ref,
    resid_ref,
    gain_ref,
    shift_ref,
    rate_ref,
    coef_ref,
    skip_ref,
    z_ref,
    stats_ref,
    gh_ref,
    gq_ref,
    sums_ref,
    m_buf,
    g_buf,
    r_buf,
):
    length = length_ref[0]
    count, own = z_ref.shape
    dims = rate_ref.shape[0]
    steps = count // CHUNKS
    groups = own // LANES
    part_size = dims // 2

    def load_strip(i, carry):
        start = pl.multiple_of(i * STRIP, STRIP)
        here = pl.ds(start, STRIP)
        valid = row_valid(start, STRIP, length)
        for group in range(groups):
            lanes = slice(group * LANES, (group + 1) * LANES)
            m_buf[group, here, :] = (
                own_ref[here, lanes] * gain_ref[:, lanes] + shift_ref[:, lanes]
            ) * valid
            slope = silu_slope(pre_ref[here, lanes].astype(F32))
            g_buf[group, here, :] = gmixed_ref[here, lanes] * slope
        return carry

    lax.fori_loop(0, count // STRIP, load_strip, 0)

    zero = jnp.zeros((CHUNKS, LANES), F32)
    for group in range(groups):
        lanes = slice(group * LANES, (group + 1) * LANES)
        rates = spread_rows(rate_ref, lanes, dims)
        coefs = spread_rows(coef_ref, lanes, dims)
        m_part, g_part, r_part = m_buf.at[group], g_buf.at[group], r_buf.at[group]

        for half in range(2):
            some = rates[half * part_size : (half + 1) * part_size]
            blank = (tuple(zero for _ in some), tuple(zero for _ in some))

            def finals(t, carry):
                states, slopes = carry
                x = m_part[pl.ds(t, CHUNKS, stride=steps), :]
                slopes = tuple(r * q + h for r, q, h in zip(some, slopes, states))
                states = tuple(r * h + x for r, h in zip(some, states))
                return states, slopes

            ends, end_slopes = lax.fori_loop(0, steps, finals, blank, unroll=4)
            pairs = [entering_pair(h, q, r, steps) for h, q, r in zip(ends, end_slopes, some)]
            begin = (
                tuple(p[0] for p in pairs),
                tuple(p[1] for p in pairs),
                tuple(zero for _ in some),
                tuple(zero for _ in some),
            )

            def sweep(t, carry):
                states, slopes, of_states, of_slopes = carry
                x = m_part[pl.ds(t, CHUNKS, stride=steps), :]
                g = g_part[pl.ds(t, CHUNKS, stride=steps), :]
                slopes = tuple(r * q + h for r, q, h in zip(some, slopes, states))
                states = tuple(r * h + x for r, h in zip(some, states))
                of_states = tuple(a + g * h for a, h in zip(of_states, states))
                of_slopes = tuple(a + g * q for a, q in zip(of_slopes, slopes))
                return states, slopes, of_states, of_slopes

            _, _, of_states, of_slopes = lax.fori_loop(0, steps, sweep, begin, unroll=4)
            for n in range(part_size):
                row = half * part_size + n
                gh_ref[row : row + 1, lanes] = jnp.sum(of_states[n], axis=0, keepdims=True)
                gq_ref[row : row + 1, lanes] = jnp.sum(of_slopes[n], axis=0, keepdims=True)

        blank = tuple(zero for _ in rates)

        def back_finals(t, states):
            g = g_part[pl.ds(steps - 1 - t, CHUNKS, stride=steps), :]
            return tuple(r * h + g for r, h in zip(rates, states))

        ends = lax.fori_loop(0, steps, back_finals, blank, unroll=4)
        starts = tuple(entering(h, r, steps, reverse=True) for h, r in zip(ends, rates))

        def back_outputs(t, states):
            g = g_part[pl.ds(steps - 1 - t, CHUNKS, stride=steps), :]
            states = tuple(r * h + g for r, h in zip(rates, states))
            terms = [c * h for c, h in zip(coefs, states)]
            while len(terms) > 1:
                terms = [a + b for a, b in zip(terms[::2], terms[1::2])]
            r_part[pl.ds(steps - 1 - t, CHUNKS, stride=steps), :] = terms[0]
            return states

        lax.fori_loop(0, steps, back_outputs, starts, unroll=4)

    ones = jnp.ones((CHUNKS, own), BF16)
    first = lax.broadcasted_iota(jnp.int32, (CHUNKS, LANES), 0) == 0

    def finish(i, carry):
        start = pl.multiple_of(i * LANES, LANES)
        here = pl.ds(start, LANES)
        valid = row_valid(start, LANES, length)
        of_gain, of_shift, of_skip = carry
        smoothed = jnp.concatenate([r_buf[k, here, :] for k in range(groups)], axis=1)
        gpre = jnp.concatenate([g_buf[k, here, :] for k in range(groups)], axis=1)
        masked = jnp.concatenate([m_buf[k, here, :] for k in range(groups)], axis=1)
        n = own_ref[here, :]
        gmasked = skip_ref[...] * gpre + smoothed
        gnormed = gmasked * valid + gvalue_ref[here, :]
        e = gnormed * gain_ref[...]
        z = scale_ref[here, 0:1] * e + resid_ref[here, :]
        z_ref[here, :] = z.astype(BF16)
        mean_row = dot(ones, e.astype(BF16), 1, 1)
        slope_row = dot(ones, (e * n).astype(BF16), 1, 1)
        stats_ref[:, here] = jnp.where(first, mean_row, slope_row)
        return (
            of_gain + jnp.sum(gnormed * n, axis=0, keepdims=True),
            of_shift + jnp.sum(gnormed, axis=0, keepdims=True),
            of_skip + jnp.sum(gpre * masked, axis=0, keepdims=True),
        )

    blank_row = jnp.zeros((1, own), F32)
    of_gain, of_shift, of_skip = lax.fori_loop(
        0, count // LANES, finish, (blank_row, blank_row, blank_row)
    )
    sums_ref[0:1, :] = of_gain
    sums_ref[1:2, :] = of_shift
    sums_ref[2:3, :] = of_skip
    sums_ref[3:8, :] = jnp.zeros((5, own), F32)


def average_backward(
    length, gmixed, gvalue, pre, own_n, scale, resid, gain, shift, rate, coef, skip
):
    count, own = gmixed.shape
    dims = rate.shape[0]
    groups = own // LANES
    rate, coef = on_sublanes(rate), on_sublanes(coef)
    return pl.pallas_call(
        average_backward_kernel,
        out_shape=(
            shape((count, own), BF16),
            shape((CHUNKS, count), F32),
            shape((dims, own), F32),
            shape((dims, own), F32),
            shape((8, own), F32),
        ),
        in_specs=[smem()] + [vmem()] * 11,
        out_specs=(vmem(),) * 5,
        scratch_shapes=[pltpu.VMEM((groups, count, LANES), F32)] * 3,
        compiler_params=params(),
    )(length, gmixed, gvalue, pre, own_n, scale, resid, gain, shift, rate, coef, skip)


def attention_forward_kernel(
    length_ref,
    normed_ref,
    mixed_ref,
    in_ref,
    bias_ref,
    pair_ref,
    offset_ref,
    out_w_ref,
    part_ref,
    update_ref,
    shared_ref,
    reset_ref,
    cand_ref,
    value_ref,
    att_ref,
    gated_ref,
    probs_ref,
):
    length = length_ref[0]
    rows = normed_ref.shape[0]
    wide = value_ref.shape[1]
    own = update_ref.shape[1]
    keyed = shared_ref.shape[1]
    start = pl.program_id(0) * rows
    value = dot(normed_ref[...], in_ref[:, :wide]) + bias_ref[:, :wide]
    value_ref[...] = value.astype(BF16)
    values = silu(value).astype(BF16)
    low = wide
    update = dot(mixed_ref[...], in_ref[:, low : low + own]) + bias_ref[:, low : low + own]
    update_ref[...] = update.astype(BF16)
    low += own
    shared = dot(mixed_ref[...], in_ref[:, low : low + keyed]) + bias_ref[:, low : low + keyed]
    shared_ref[...] = shared.astype(BF16)
    low += keyed
    reset = dot(mixed_ref[...], in_ref[:, low : low + wide]) + bias_ref[:, low : low + wide]
    reset_ref[...] = reset.astype(BF16)
    low += wide
    cand_ref[...] = (
        dot(mixed_ref[...], in_ref[:, low : low + own]) + bias_ref[:, low : low + own]
    ).astype(BF16)
    shared = silu(shared)
    reset = silu(reset)
    queries = (shared * pair_ref[0:1, :] + offset_ref[...]).astype(BF16)
    keys = (shared * pair_ref[1:2, :]).astype(BF16)
    for block in range(rows // ATT):
        here = slice(block * ATT, (block + 1) * ATT)
        begin = start + block * ATT
        scores = dot(queries[here], keys[here], 1, 1) * keyed**-0.5
        key_place = begin + lax.broadcasted_iota(jnp.int32, (ATT, ATT), 1)
        scores = jnp.where(key_place < length, scores, NEGATIVE)
        raised = jnp.exp(scores - jnp.max(scores, axis=-1, keepdims=True))
        probs = (raised / jnp.sum(raised, axis=-1, keepdims=True)).astype(BF16)
        probs_ref[here, :] = probs
        attended = dot(probs, values[here]) * row_valid(begin, ATT, length)
        att_ref[here, :] = attended.astype(BF16)
        gated_ref[here, :] = (attended * reset[here]).astype(BF16)
    part_ref[...] = dot(gated_ref[...], out_w_ref[...]).astype(BF16)


def attention_forward(length, normed, mixed, in_w, bias, pair, offset, out_w, own):
    count, width = normed.shape
    wide = out_w.shape[0]
    keyed = pair.shape[1]

    def rows(columns):
        return pl.BlockSpec((ROWS, columns), lambda i: (i, 0))

    def whole(array):
        return pl.BlockSpec(array.shape, lambda i: (0, 0))

    widths = (width, own, keyed, wide, own, wide, wide, wide, ATT)
    return pl.pallas_call(
        attention_forward_kernel,
        grid=(count // ROWS,),
        out_shape=tuple(shape((count, w), BF16) for w in widths),
        in_specs=[
            smem(),
            rows(width),
            rows(width),
            whole(in_w),
            whole(bias),
            whole(pair),
            whole(offset),
            whole(out_w),
        ],
        out_specs=tuple(rows(w) for w in widths),
        compiler_params=params(),
    )(length, normed, mixed, in_w, bias, pair, offset, out_w)


def attention_backward_kernel(
    length_ref,
    gout_ref,
    gupdate_ref,
    shared_ref,
    reset_ref,
    value_ref,
    att_ref,
    probs_ref,
    in_ref,
    pair_ref,
    offset_ref,
    out_w_ref,
    gmixed_ref,
    gnormed_ref,
    gbase_ref,
    gvalue_ref,
    bias_ref,
    pair_sum_ref,
):
    length = length_ref[0]
    rows = gout_ref.shape[0]
    wide = value_ref.shape[1]
    own = gupdate_ref.shape[1]
    keyed = shared_ref.shape[1]
    start = pl.program_id(0) * rows
    mine = pl.ds(pl.multiple_of(lax.axis_index("section") * own, LANES), own)

    @pl.when(pl.program_id(0) == 0)
    def _():
        bias_ref[...] = jnp.zeros_like(bias_ref)
        pair_sum_ref[...] = jnp.zeros_like(pair_sum_ref)

    valid = row_valid(start, rows, length)
    ggated = dot(gout_ref[...], out_w_ref[...], 1, 1)
    reset = reset_ref[...].astype(F32)
    gattended = (ggated * silu(reset) * valid).astype(BF16)
    greset = ggated * att_ref[...].astype(F32) * silu_slope(reset)
    value = value_ref[...].astype(F32)
    values = silu(value).astype(BF16)
    shared_pre = shared_ref[...].astype(F32)
    shared = silu(shared_pre)
    scale_q, scale_k = pair_ref[0:1, :], pair_ref[1:2, :]
    queries = (shared * scale_q + offset_ref[...]).astype(BF16)
    keys = (shared * scale_k).astype(BF16)
    gq_parts, gk_parts, gv_parts = [], [], []
    for block in range(rows // ATT):
        here = slice(block * ATT, (block + 1) * ATT)
        probs = probs_ref[here, :]
        gprobs = dot(gattended[here], values[here], 1, 1)
        gv_parts.append(dot(probs, gattended[here], 0, 0))
        probs = probs.astype(F32)
        gscores = probs * (gprobs - jnp.sum(probs * gprobs, axis=-1, keepdims=True))
        key_place = start + block * ATT + lax.broadcasted_iota(jnp.int32, (ATT, ATT), 1)
        gscores = jnp.where(key_place < length, gscores, 0.0)
        gscores = (gscores * keyed**-0.5).astype(BF16)
        gq_parts.append(dot(gscores, keys[here]))
        gk_parts.append(dot(gscores, queries[here], 0, 0))
    gqueries = jnp.concatenate(gq_parts, axis=0)
    gkeys = jnp.concatenate(gk_parts, axis=0)
    gvalue = jnp.concatenate(gv_parts, axis=0) * silu_slope(value)
    gshared = (gqueries * scale_q + gkeys * scale_k) * silu_slope(shared_pre)
    pair_sum_ref[0:1, :] += jnp.sum(gqueries * shared, axis=0, keepdims=True)
    pair_sum_ref[1:2, :] += jnp.sum(gkeys * shared, axis=0, keepdims=True)
    pair_sum_ref[2:3, :] += jnp.sum(gqueries, axis=0, keepdims=True)
    gupdate = gupdate_ref[...]
    gcand = gout_ref[:, mine]
    low = 0
    for piece in (gvalue, gupdate, gshared, greset, gcand):
        size = piece.shape[1]
        bias_ref[0:1, low : low + size] += jnp.sum(piece.astype(F32), axis=0, keepdims=True)
        if low:
            gbase_ref[:, low - wide : low - wide + size] = piece.astype(BF16)
        else:
            gvalue_ref[...] = piece.astype(BF16)
        low += size
    gmixed_ref[...] = dot(gbase_ref[...], in_ref[:, wide:], 1, 1).astype(BF16)
    gnormed_ref[...] = dot(gvalue_ref[...], in_ref[:, :wide], 1, 1).astype(BF16)


def attention_backward(length, gout, gupdate, saved, in_w, pair, offset, out_w):
    shared, reset, value, att, probs = saved
    count, width = gout.shape
    own = gupdate.shape[1]
    wide = out_w.shape[0]
    keyed = pair.shape[1]
    total = in_w.shape[1]

    def rows(columns):
        return pl.BlockSpec((ROWS, columns), lambda i: (i, 0))

    def whole(dims):
        return pl.BlockSpec(dims, lambda i: (0, 0))

    return pl.pallas_call(
        attention_backward_kernel,
        grid=(count // ROWS,),
        out_shape=(
            shape((count, width), BF16),
            shape((count, width), BF16),
            shape((count, total - wide), BF16),
            shape((count, wide), BF16),
            shape((8, total), F32),
            shape((8, keyed), F32),
        ),
        in_specs=[
            smem(),
            rows(width),
            rows(own),
            rows(keyed),
            rows(wide),
            rows(wide),
            rows(wide),
            rows(ATT),
            whole(in_w.shape),
            whole(pair.shape),
            whole(offset.shape),
            whole(out_w.shape),
        ],
        out_specs=(
            rows(width),
            rows(width),
            rows(total - wide),
            rows(wide),
            whole((8, total)),
            whole((8, keyed)),
        ),
        compiler_params=params(),
    )(length, gout, gupdate, shared, reset, value, att, probs, in_w, pair, offset, out_w)


def feed_forward_kernel(
    x_ref, gain_ref, shift_ref, in_ref, bias_ref, out_w_ref, part_ref, pre_ref, n_ref, normed_ref, scale_ref
):
    n, scale = normalise(x_ref[...].astype(F32))
    n_ref[...] = n.astype(BF16)
    scale_ref[...] = jnp.broadcast_to(scale, scale_ref.shape)
    normed_ref[...] = (n * gain_ref[...] + shift_ref[...]).astype(BF16)
    pre = dot(normed_ref[...], in_ref[...]) + bias_ref[...]
    pre_ref[...] = pre.astype(BF16)
    part_ref[...] = dot(silu(pre).astype(BF16), out_w_ref[...]).astype(BF16)


def feed_forward(x, gain, shift, in_w, bias, out_w):
    count, width = x.shape
    hidden = in_w.shape[1]

    def rows(columns):
        return pl.BlockSpec((ROWS, columns), lambda i: (i, 0))

    def whole(array):
        return pl.BlockSpec(array.shape, lambda i: (0, 0))

    return pl.pallas_call(
        feed_forward_kernel,
        grid=(count // ROWS,),
        out_shape=(
            shape((count, width), BF16),
            shape((count, hidden), BF16),
            shape((count, width), BF16),
            shape((count, width), BF16),
            shape((count, LANES), F32),
        ),
        in_specs=[rows(width)] + [whole(a) for a in (gain, shift, in_w, bias, out_w)],
        out_specs=(rows(width), rows(hidden), rows(width), rows(width), rows(LANES)),
        compiler_params=params(),
    )(x, gain, shift, in_w, bias, out_w)


def feed_backward_kernel(corrected, *refs):
    if corrected:
        z_ref, means_ref, x_ref = refs[:3]
        refs = refs[3:]
    else:
        g_in_ref = refs[0]
        refs = refs[1:]
    pre_ref, n_ref, gain_ref, in_ref, out_w_ref = refs[:5]
    refs = refs[5:]
    part_ref, stats_ref, gpre_ref, act_ref, sums_ref, bias_ref = refs[:6]
    width = n_ref.shape[1]

    @pl.when(pl.program_id(0) == 0)
    def _():
        sums_ref[...] = jnp.zeros_like(sums_ref)
        bias_ref[...] = jnp.zeros_like(bias_ref)

    if corrected:
        g_ref = refs[6]
        xn, xscale = normalise(x_ref[...].astype(F32))
        means = means_ref[...].T * (1.0 / width)
        g = z_ref[...].astype(F32) - xscale * (means[:, 0:1] + xn * means[:, 1:2])
        g_ref[...] = g.astype(BF16)
    else:
        g_ref = g_in_ref
    g = g_ref[...]
    pre = pre_ref[...].astype(F32)
    s = sigmoid(pre)
    act_ref[...] = (pre * s).astype(BF16)
    gpre = dot(g, out_w_ref[...], 1, 1) * (s * (1.0 + pre * (1.0 - s)))
    bias_ref[0:1, :] += jnp.sum(gpre, axis=0, keepdims=True)
    gpre_ref[...] = gpre.astype(BF16)
    part = dot(gpre_ref[...], in_ref[...], 1, 1)
    part_ref[...] = part.astype(BF16)
    n = n_ref[...].astype(F32)
    sums_ref[0:1, :] += jnp.sum(part * n, axis=0, keepdims=True)
    sums_ref[1:2, :] += jnp.sum(part, axis=0, keepdims=True)
    sums_ref[2:3, :] += jnp.sum(g.astype(F32), axis=0, keepdims=True)
    e = part * gain_ref[...]
    ones = jnp.ones((CHUNKS, width), BF16)
    mean_row = dot(ones, e.astype(BF16), 1, 1)
    slope_row = dot(ones, (e * n).astype(BF16), 1, 1)
    first = lax.broadcasted_iota(jnp.int32, mean_row.shape, 0) == 0
    stats_ref[...] = jnp.where(first, mean_row, slope_row)


def feed_backward(given, pre, n, gain, in_w, out_w):
    corrected = isinstance(given, tuple)
    count, width = n.shape
    hidden = in_w.shape[1]

    def rows(columns):
        return pl.BlockSpec((ROWS, columns), lambda i: (i, 0))

    def whole(dims):
        return pl.BlockSpec(dims, lambda i: (0, 0))

    stats_spec = pl.BlockSpec((CHUNKS, ROWS), lambda i: (0, i))
    given = given if corrected else (given,)
    given_specs = [rows(width), stats_spec, rows(width)] if corrected else [rows(width)]
    extra = ((shape((count, width), BF16),), (rows(width),)) if corrected else ((), ())
    return pl.pallas_call(
        functools.partial(feed_backward_kernel, corrected),
        grid=(count // ROWS,),
        out_shape=(
            shape((count, width), BF16),
            shape((CHUNKS, count), F32),
            shape((count, hidden), BF16),
            shape((count, hidden), BF16),
            shape((8, width), F32),
            shape((8, hidden), F32),
        )
        + extra[0],
        in_specs=given_specs
        + [rows(hidden), rows(width), whole(gain.shape), whole(in_w.shape), whole(out_w.shape)],
        out_specs=(
            rows(width),
            stats_spec,
            rows(hidden),
            rows(hidden),
            whole((8, width)),
            whole((8, hidden)),
        )
        + extra[1],
        compiler_params=params(),
    )(*given, pre, n, gain, in_w, out_w)


def plane():
    me = lax.axis_index("section")
    across = me + 1 - 2 * (me % 2)
    along = me + 2 - 4 * (me // 2)
    return me, across, along, across + along - me


def greet(*others):
    barrier = pltpu.get_barrier_semaphore()
    for other in others:
        pl.semaphore_signal(barrier, inc=1, device_id={"section": other}, device_id_type=MESH)
    pl.semaphore_wait(barrier, len(others))


def link(source, target, sems, index, other):
    send, recv = sems
    return pltpu.make_async_remote_copy(
        src_ref=source,
        dst_ref=target,
        send_sem=send.at[index],
        recv_sem=recv.at[index],
        device_id={"section": other},
        device_id_type=MESH,
    )


def strips(count, work):
    def one(i, carry):
        work(pl.multiple_of(i * STRIP, STRIP))
        return carry

    lax.fori_loop(0, count // STRIP, one, 0)


def reduce_begin(part, piece, peers, slots, sems):
    me, across, along, far = peers
    early, direct, _, _ = slots
    started = []
    for half, first in enumerate((across, along)):
        started.append(link(part.at[piece(far, half)], early.at[half], sems, half, first))
        started[-1].start()
    for half, first in enumerate((across, along)):
        started.append(link(part.at[piece(first, half)], direct.at[half], sems, 2 + half, first))
        started[-1].start()
    return started


def reduce_forward(part, piece, peers, slots, sems, started):
    me, across, along, far = peers
    early, _, late, stage = slots
    for half, second in enumerate((along, across)):
        started[half].wait_recv()
        row, column = piece(second, half)

        def add(start):
            here = pl.ds(start, STRIP)
            mine = part[pl.ds(row.start + start, STRIP), column].astype(F32)
            stage[half, here, :] = (mine + early[half, here, :].astype(F32)).astype(BF16)

        strips(early.shape[1], add)
        started.append(link(stage.at[half], late.at[half], sems, 4 + half, second))
        started[-1].start()


def reduce_arrived(started, half):
    started[2 + half].wait_recv()
    started[4 + half].wait_recv()


def reduced(part, piece, me, slots, half, start):
    _, direct, late, _ = slots
    row, column = piece(me, half)
    here = pl.ds(start, STRIP)
    total = part[pl.ds(row.start + start, STRIP), column].astype(F32)
    return total + direct[half, here, :].astype(F32) + late[half, here, :].astype(F32)


def gather_begin(out, piece, peers, sems, half):
    me, across, along, far = peers
    here = out.at[piece(me, half)]
    order = ((along, 0), (across, 1)) if half == 0 else ((across, 1), (along, 0))
    started = {}
    for other, way in order:
        copy = link(here, here, sems, 2 * half + way, other)
        copy.start()
        started[way] = copy
    return started


def gather_finish(out, piece, peers, sems, zero, one):
    me, across, along, far = peers
    zero[0].wait_recv()
    passing = out.at[piece(along, 0)]
    first = link(passing, passing, sems, 4, across)
    first.start()
    one[1].wait_recv()
    passing = out.at[piece(across, 1)]
    second = link(passing, passing, sems, 5, along)
    second.start()
    zero[1].wait_recv()
    one[0].wait_recv()
    first.wait_recv()
    second.wait_recv()
    for copy in (zero[0], zero[1], one[0], one[1], first, second):
        copy.wait_send()


def column_piece(count, own):
    def piece(owner, half):
        size = count // 2
        return pl.ds(half * size, size), pl.ds(pl.multiple_of(owner * own, LANES), own)

    return piece


def row_piece(count, width):
    def piece(owner, half):
        size = count // 4
        return (
            pl.ds(pl.multiple_of(owner * size, size), size),
            pl.ds(half * (width // 2), width // 2),
        )

    return piece


def reduce_scratch(rows, columns):
    return [pltpu.VMEM((2, rows, columns), BF16)] * 4


def copy_sems(count):
    return [pltpu.SemaphoreType.DMA((count,)), pltpu.SemaphoreType.DMA((count,))]


def comm_params(ident):
    return params(collective_id=ident, has_side_effects=True)


def own_slice(source, target, sem, own):
    start = pl.multiple_of(lax.axis_index("section") * own, LANES)
    return pltpu.make_async_copy(source.at[:, pl.ds(start, own)], target, sem)


def gather_kernel(own_ref, out_ref, send, recv):
    count, own = own_ref.shape
    peers = plane()
    piece = column_piece(count, own)
    mine = pl.ds(pl.multiple_of(peers[0] * own, LANES), own)
    out_ref[:, mine] = own_ref[...]
    greet(peers[1], peers[2])
    zero = gather_begin(out_ref, piece, peers, (send, recv), 0)
    one = gather_begin(out_ref, piece, peers, (send, recv), 1)
    gather_finish(out_ref, piece, peers, (send, recv), zero, one)


def gather_columns(own, sections, ident):
    count, width = own.shape
    return pl.pallas_call(
        gather_kernel,
        out_shape=shape((count, width * sections), BF16),
        in_specs=[vmem()],
        out_specs=vmem(),
        scratch_shapes=copy_sems(6),
        compiler_params=comm_params(ident),
    )(own)


def stats_total(stats, got, stage, peers, sems, index):
    me, across, along, far = peers
    first = link(stats, got.at[0], sems, index, across)
    first.start()
    first.wait_recv()
    stage[...] = stats[...] + got[0]
    second = link(stage, got.at[1], sems, index + 1, along)
    second.start()
    second.wait_recv()
    first.wait_send()
    second.wait_send()
    return stage[...] + got[1]


def gather_stats_kernel(own_ref, stats_ref, out_ref, total_ref, got, stage, send, recv):
    count, own = own_ref.shape
    peers = plane()
    piece = column_piece(count, own)
    mine = pl.ds(pl.multiple_of(peers[0] * own, LANES), own)
    out_ref[:, mine] = own_ref[...]
    greet(peers[1], peers[2])
    sems = (send, recv)
    zero = gather_begin(out_ref, piece, peers, sems, 0)
    one = gather_begin(out_ref, piece, peers, sems, 1)
    total_ref[...] = stats_total(stats_ref, got, stage, peers, sems, 6)
    gather_finish(out_ref, piece, peers, sems, zero, one)


def gather_stats(own, stats, sections, ident):
    count, width = own.shape
    return pl.pallas_call(
        gather_stats_kernel,
        out_shape=(shape((count, width * sections), BF16), shape(stats.shape, F32)),
        in_specs=[vmem()] * 2,
        out_specs=(vmem(), vmem()),
        scratch_shapes=[pltpu.VMEM((2,) + stats.shape, F32), pltpu.VMEM(stats.shape, F32)]
        + copy_sems(8),
        compiler_params=comm_params(ident),
    )(own, stats)


def attention_join_kernel(
    part_ref,
    update_ref,
    cand_ref,
    x_ref,
    out_ref,
    hidden_ref,
    early,
    direct,
    late,
    stage,
    x_own,
    local_sem,
    send,
    recv,
    send_g,
    recv_g,
):
    count, own = update_ref.shape
    peers = plane()
    me = peers[0]
    piece = column_piece(count, own)
    slots = (early, direct, late, stage)
    fetch = own_slice(x_ref, x_own, local_sem, own)
    fetch.start()
    greet(peers[1], peers[2])
    started = reduce_begin(part_ref, piece, peers, slots, (send, recv))
    fetch.wait()
    reduce_forward(part_ref, piece, peers, slots, (send, recv), started)
    begun = []
    mine = pl.ds(pl.multiple_of(me * own, LANES), own)
    for half in range(2):
        reduce_arrived(started, half)

        def finish(start):
            here = pl.ds(half * (count // 2) + start, STRIP)
            pre = cand_ref[here, :].astype(F32) + reduced(part_ref, piece, me, slots, half, start)
            hidden_ref[here, :] = pre.astype(BF16)
            x = x_own[here, :].astype(F32)
            made = x + sigmoid(update_ref[here, :].astype(F32)) * (silu(pre) - x)
            out_ref[here, mine] = made.astype(BF16)

        strips(count // 2, finish)
        begun.append(gather_begin(out_ref, piece, peers, (send_g, recv_g), half))
    gather_finish(out_ref, piece, peers, (send_g, recv_g), begun[0], begun[1])
    for copy in started:
        copy.wait_send()


def attention_join(part, update, cand, x, ident):
    count, width = part.shape
    own = update.shape[1]
    return pl.pallas_call(
        attention_join_kernel,
        out_shape=(shape((count, width), BF16), shape((count, own), BF16)),
        in_specs=[vmem(), vmem(), vmem(), hbm()],
        out_specs=(vmem(), vmem()),
        scratch_shapes=reduce_scratch(count // 2, own)
        + [pltpu.VMEM((count, own), BF16), pltpu.SemaphoreType.DMA]
        + copy_sems(6)
        + copy_sems(6),
        compiler_params=comm_params(ident),
    )(part, update, cand, x)


def feed_join_kernel(
    part_ref,
    bias_ref,
    x_ref,
    out_ref,
    early,
    direct,
    late,
    stage,
    x_own,
    local_sem,
    send,
    recv,
    send_g,
    recv_g,
):
    count = part_ref.shape[0]
    own = bias_ref.shape[1]
    peers = plane()
    me = peers[0]
    piece = column_piece(count, own)
    slots = (early, direct, late, stage)
    fetch = own_slice(x_ref, x_own, local_sem, own)
    fetch.start()
    greet(peers[1], peers[2])
    started = reduce_begin(part_ref, piece, peers, slots, (send, recv))
    fetch.wait()
    reduce_forward(part_ref, piece, peers, slots, (send, recv), started)
    begun = []
    mine = pl.ds(pl.multiple_of(me * own, LANES), own)
    for half in range(2):
        reduce_arrived(started, half)

        def finish(start):
            here = pl.ds(half * (count // 2) + start, STRIP)
            total = reduced(part_ref, piece, me, slots, half, start)
            made = x_own[here, :].astype(F32) + total + bias_ref[...]
            out_ref[here, mine] = made.astype(BF16)

        strips(count // 2, finish)
        begun.append(gather_begin(out_ref, piece, peers, (send_g, recv_g), half))
    gather_finish(out_ref, piece, peers, (send_g, recv_g), begun[0], begun[1])
    for copy in started:
        copy.wait_send()


def feed_join(part, bias, x, ident):
    count, width = part.shape
    own = bias.shape[1]
    return pl.pallas_call(
        feed_join_kernel,
        out_shape=shape((count, width), BF16),
        in_specs=[vmem(), vmem(), hbm()],
        out_specs=vmem(),
        scratch_shapes=reduce_scratch(count // 2, own)
        + [pltpu.VMEM((count, own), BF16), pltpu.SemaphoreType.DMA]
        + copy_sems(6)
        + copy_sems(6),
        compiler_params=comm_params(ident),
    )(part, bias, x)


def feed_last_kernel(
    part_ref, bias_ref, x_ref, out_ref, early, direct, late, stage, x_own, local_sem, send, recv
):
    count, width = part_ref.shape
    quarter = count // 4
    peers = plane()
    me = peers[0]
    piece = row_piece(count, width)
    slots = (early, direct, late, stage)
    mine = pl.ds(pl.multiple_of(me * quarter, quarter), quarter)
    fetch = pltpu.make_async_copy(x_ref.at[mine, :], x_own, local_sem)
    fetch.start()
    greet(peers[1], peers[2])
    started = reduce_begin(part_ref, piece, peers, slots, (send, recv))
    fetch.wait()
    reduce_forward(part_ref, piece, peers, slots, (send, recv), started)
    for half in range(2):
        reduce_arrived(started, half)
        lanes = slice(half * (width // 2), (half + 1) * (width // 2))

        def finish(start):
            here = pl.ds(start, STRIP)
            total = reduced(part_ref, piece, me, slots, half, start)
            made = x_own[here, lanes].astype(F32) + total + bias_ref[:, lanes]
            out_ref[here, lanes] = made.astype(BF16)

        strips(quarter, finish)
    for copy in started:
        copy.wait_send()


def feed_last(part, bias, x, ident):
    count, width = part.shape
    quarter = count // 4
    return pl.pallas_call(
        feed_last_kernel,
        out_shape=shape((quarter, width), BF16),
        in_specs=[vmem(), vmem(), hbm()],
        out_specs=vmem(),
        scratch_shapes=reduce_scratch(quarter, width // 2)
        + [pltpu.VMEM((quarter, width), BF16), pltpu.SemaphoreType.DMA]
        + copy_sems(6),
        compiler_params=comm_params(ident),
    )(part, bias, x)


def back_join_kernel(
    part_ref,
    stats_ref,
    scale_ref,
    gain_ref,
    update_ref,
    hidden_ref,
    g_ref,
    n_ref,
    x_ref,
    out_ref,
    gupdate_ref,
    resid_ref,
    early,
    direct,
    late,
    stage,
    g_own,
    n_own,
    x_own,
    got,
    stats_stage,
    means,
    local_sem,
    send,
    recv,
    send_g,
    recv_g,
    send_s,
    recv_s,
):
    count, width = part_ref.shape
    own = update_ref.shape[1]
    peers = plane()
    me = peers[0]
    piece = column_piece(count, own)
    slots = (early, direct, late, stage)
    fetches = [
        own_slice(source, target, local_sem.at[i], own)
        for i, (source, target) in enumerate(((g_ref, g_own), (n_ref, n_own), (x_ref, x_own)))
    ]
    for fetch in fetches:
        fetch.start()
    greet(peers[1], peers[2])
    started = reduce_begin(part_ref, piece, peers, slots, (send, recv))
    total = stats_total(stats_ref, got, stats_stage, peers, (send_s, recv_s), 0)
    means[...] = total.T * (1.0 / width)
    for fetch in fetches:
        fetch.wait()
    reduce_forward(part_ref, piece, peers, slots, (send, recv), started)
    begun = []
    mine = pl.ds(pl.multiple_of(me * own, LANES), own)
    for half in range(2):
        reduce_arrived(started, half)

        def finish(start):
            here = pl.ds(half * (count // 2) + start, STRIP)
            e = reduced(part_ref, piece, me, slots, half, start) * gain_ref[...]
            n = n_own[here, :].astype(F32)
            inner = e - means[here, 0:1] - n * means[here, 1:2]
            g = g_own[here, :].astype(F32) + scale_ref[here, 0:1] * inner
            g = g.astype(BF16).astype(F32)
            u = sigmoid(update_ref[here, :].astype(F32))
            pre = hidden_ref[here, :].astype(F32)
            s = sigmoid(pre)
            x = x_own[here, :].astype(F32)
            gupdate_ref[here, :] = (g * (pre * s - x) * (u * (1.0 - u))).astype(BF16)
            resid_ref[here, :] = g * (1.0 - u)
            out_ref[here, mine] = (g * u * (s * (1.0 + pre * (1.0 - s)))).astype(BF16)

        strips(count // 2, finish)
        begun.append(gather_begin(out_ref, piece, peers, (send_g, recv_g), half))
    gather_finish(out_ref, piece, peers, (send_g, recv_g), begun[0], begun[1])
    for copy in started:
        copy.wait_send()


def back_join(part, stats, scale, gain, update, hidden, g, n, x, ident):
    count, width = part.shape
    own = update.shape[1]
    return pl.pallas_call(
        back_join_kernel,
        out_shape=(
            shape((count, width), BF16),
            shape((count, own), BF16),
            shape((count, own), F32),
        ),
        in_specs=[vmem()] * 6 + [hbm()] * 3,
        out_specs=(vmem(),) * 3,
        scratch_shapes=reduce_scratch(count // 2, own)
        + [pltpu.VMEM((count, own), BF16)] * 3
        + [
            pltpu.VMEM((2, CHUNKS, count), F32),
            pltpu.VMEM((CHUNKS, count), F32),
            pltpu.VMEM((count, CHUNKS), F32),
            pltpu.SemaphoreType.DMA((3,)),
        ]
        + copy_sems(6)
        + copy_sems(6)
        + copy_sems(2),
        compiler_params=comm_params(ident),
    )(part, stats, scale, gain, update, hidden, g, n, x)


def reduce_two_kernel(
    one_ref, two_ref, out_one, out_two, e1, d1, l1, s1, e2, d2, l2, s2, sa, ra, sb, rb
):
    count, own = out_one.shape
    peers = plane()
    me = peers[0]
    piece = column_piece(count, own)
    jobs = (
        (one_ref, out_one, (e1, d1, l1, s1), (sa, ra)),
        (two_ref, out_two, (e2, d2, l2, s2), (sb, rb)),
    )
    greet(peers[1], peers[2])
    begun = [reduce_begin(part, piece, peers, slots, sems) for part, _, slots, sems in jobs]
    for (part, _, slots, sems), started in zip(jobs, begun):
        reduce_forward(part, piece, peers, slots, sems, started)
    for (part, out, slots, sems), started in zip(jobs, begun):
        for half in range(2):
            reduce_arrived(started, half)

            def finish(start):
                here = pl.ds(half * (count // 2) + start, STRIP)
                out[here, :] = reduced(part, piece, me, slots, half, start)

            strips(count // 2, finish)
        for copy in started:
            copy.wait_send()


def reduce_two(one, two, own, ident):
    count = one.shape[0]
    return pl.pallas_call(
        reduce_two_kernel,
        out_shape=(shape((count, own), F32),) * 2,
        in_specs=[vmem()] * 2,
        out_specs=(vmem(),) * 2,
        scratch_shapes=reduce_scratch(count // 2, own) * 2 + copy_sems(6) + copy_sems(6),
        compiler_params=comm_params(ident),
    )(one, two)


def last_rows_kernel(
    z_ref, stats_ref, x_ref, out_ref, land, x_own, got, stats_stage, total_buf, local_sem, send, recv
):
    count, own = z_ref.shape
    quarter, width = out_ref.shape
    peers = plane()
    me = peers[0]

    def rows(owner):
        return pl.ds(pl.multiple_of(owner * quarter, quarter), quarter)

    mine = pl.ds(pl.multiple_of(me * own, LANES), own)
    fetch = pltpu.make_async_copy(x_ref.at[rows(me), :], x_own, local_sem)
    fetch.start()
    land[:, mine] = z_ref[rows(me), :]
    greet(*peers[1:])
    sems = (send, recv)
    copies = []
    for index, other in enumerate(peers[1:]):
        copies.append(link(z_ref.at[rows(other), :], land.at[:, mine], sems, 2 + index, other))
        copies[-1].start()
    total_buf[...] = stats_total(stats_ref, got, stats_stage, peers, sems, 0)
    part = total_buf[:, pl.ds(pl.multiple_of(me * quarter, LANES), quarter)]
    means = part.T * (1.0 / width)
    fetch.wait()
    for copy in copies:
        copy.wait_recv()
    n, scale = normalise(x_own[...].astype(F32))
    g = land[...].astype(F32) - scale * (means[:, 0:1] + n * means[:, 1:2])
    out_ref[...] = g.astype(BF16)
    for copy in copies:
        copy.wait_send()


def last_rows(z, stats, x, ident):
    count, own = z.shape
    width = x.shape[1]
    quarter = count // 4
    return pl.pallas_call(
        last_rows_kernel,
        out_shape=shape((quarter, width), BF16),
        in_specs=[vmem(), vmem(), hbm()],
        out_specs=vmem(),
        scratch_shapes=[
            pltpu.VMEM((quarter, width), BF16),
            pltpu.VMEM((quarter, width), BF16),
            pltpu.VMEM((2,) + stats.shape, F32),
            pltpu.VMEM(stats.shape, F32),
            pltpu.VMEM(stats.shape, F32),
            pltpu.SemaphoreType.DMA,
        ]
        + copy_sems(5),
        compiler_params=comm_params(ident),
    )(z, stats, x)


def interleaved(array, shards, sections, section):
    lead = array.shape[:-1]
    split = array.reshape(lead + (shards, sections, -1))
    return lax.dynamic_index_in_dim(split, section, len(lead) + 1, keepdims=False).reshape(
        lead + (-1,)
    )


def contiguous(array, sections, section):
    size = array.shape[-1] // sections
    return lax.dynamic_slice_in_dim(array, section * size, size, axis=array.ndim - 1)


def put_interleaved(own, shards, sections, section):
    lead = own.shape[:-1]
    own = own.reshape(lead + (shards, 1, -1))
    holder = jnp.zeros(lead + (shards, sections, own.shape[-1]), own.dtype)
    holder = lax.dynamic_update_slice_in_dim(holder, own, section, len(lead) + 1)
    return holder.reshape(lead + (-1,))


def put_contiguous(own, sections, section):
    size = own.shape[-1]
    holder = jnp.zeros(own.shape[:-1] + (size * sections,), own.dtype)
    return lax.dynamic_update_slice_in_dim(holder, own, section * size, own.ndim - 1)


def body(
    tokens,
    lengths,
    cotangent,
    norm_gain,
    norm_shift,
    average_decay,
    average_input,
    average_output,
    average_skip,
    value_weight,
    value_bias,
    base_weight,
    base_bias,
    pair_scale,
    query_shift,
    out_weight,
    feed_gain,
    feed_shift,
    feed_in_weight,
    feed_in_bias,
    feed_out_weight,
    feed_out_bias,
):
    sections = lax.axis_size("section")
    shards = lax.axis_size("dp")
    section = lax.axis_index("section")
    _, count, width = tokens.shape
    layers = norm_gain.shape[0]
    own = width // sections
    wide = value_weight.shape[2]
    keyed = pair_scale.shape[2] * shards
    hidden = feed_in_weight.shape[2]

    base_parts = (
        contiguous(base_weight[..., :width], sections, section),
        base_weight[..., width : width + keyed],
        interleaved(base_weight[..., width + keyed : width + keyed + wide], shards, sections, section),
        contiguous(base_weight[..., width + keyed + wide :], sections, section),
    )
    in_shard = jnp.concatenate(
        (interleaved(value_weight, shards, sections, section),) + base_parts, axis=2
    )

    def quarter_rows(array):
        split = array.reshape(layers, sections, -1, array.shape[2])
        return lax.dynamic_index_in_dim(split, section, 1, keepdims=False)

    out_shard = quarter_rows(out_weight)
    feed_in_shard = interleaved(feed_in_weight, shards, sections, section)
    feed_out_shard = quarter_rows(feed_out_weight)

    def over_dp(array):
        return lax.all_gather(array, "dp", axis=0, tiled=True)

    weights = []
    for layer in range(layers):
        weights.append(
            (
                over_dp(in_shard[layer]),
                over_dp(out_shard[layer]),
                over_dp(feed_in_shard[layer]),
                over_dp(feed_out_shard[layer]),
            )
        )

    smalls = (
        norm_gain,
        norm_shift,
        average_decay,
        average_input,
        average_output,
        average_skip,
        value_bias,
        base_bias,
        pair_scale,
        query_shift,
        feed_gain,
        feed_shift,
        feed_in_bias,
        feed_out_bias,
    )
    packed = jnp.concatenate([a.reshape(layers, -1) for a in smalls], axis=1)
    everyone = lax.all_gather(packed, "dp", axis=0)
    full = []
    low = 0
    for a in smalls:
        size = a.size // layers
        piece = everyone[:, :, low : low + size].reshape((shards,) + a.shape)
        piece = jnp.moveaxis(piece, 0, a.ndim - 1)
        full.append(piece.reshape(a.shape[:-1] + (-1,)))
        low += size
    (
        gain_all,
        shift_all,
        decay_all,
        input_all,
        output_all,
        skip_all,
        value_bias_all,
        base_bias_all,
        pair_all,
        offset_all,
        feed_gain_all,
        feed_shift_all,
        feed_in_bias_all,
        feed_out_bias_all,
    ) = full
    rate_all = jax.nn.sigmoid(contiguous(decay_all, sections, section))
    input_own = contiguous(input_all, sections, section)
    output_own = contiguous(output_all, sections, section)
    drive_all = (1.0 - rate_all) * input_own
    coef_all = drive_all * output_own
    skip_own = contiguous(skip_all, sections, section)
    gain_own = contiguous(gain_all, sections, section)
    shift_own = contiguous(shift_all, sections, section)
    in_bias = jnp.concatenate(
        (
            interleaved(value_bias_all, shards, sections, section),
            contiguous(base_bias_all[:, :width], sections, section),
            base_bias_all[:, width : width + keyed],
            interleaved(
                base_bias_all[:, width + keyed : width + keyed + wide], shards, sections, section
            ),
            contiguous(base_bias_all[:, width + keyed + wide :], sections, section),
        ),
        axis=1,
    )
    feed_in_bias_own = interleaved(feed_in_bias_all, shards, sections, section)
    feed_out_bias_own = contiguous(feed_out_bias_all, sections, section)
    feed_gain_own = contiguous(feed_gain_all, sections, section)

    idents = iter(range(64))
    x = tokens[0]
    kept = []
    for layer in range(layers):
        in_w, out_w, feed_in_w, feed_out_w = weights[layer]
        row = slice(layer, layer + 1)
        normed, mixed_own, pre, own_n, scale = average_forward(
            lengths,
            x,
            gain_all[row],
            shift_all[row],
            rate_all[layer],
            coef_all[layer],
            skip_own[row],
        )
        mixed = gather_columns(mixed_own, sections, next(idents))
        part, update, shared, reset, cand, value, att, gated, probs = attention_forward(
            lengths,
            normed,
            mixed,
            in_w,
            in_bias[row],
            pair_all[layer],
            offset_all[row],
            out_w,
            own,
        )
        middle, hidden_pre = attention_join(part, update, cand, x, next(idents))
        feed_part, feed_pre, feed_n, feed_normed, feed_scale = feed_forward(
            middle,
            feed_gain_all[row],
            feed_shift_all[row],
            feed_in_w,
            feed_in_bias_own[row],
            feed_out_w,
        )
        kept.append(
            dict(
                x=x,
                normed=normed,
                mixed=mixed,
                pre=pre,
                own_n=own_n,
                scale=scale,
                update=update,
                saved=(shared, reset, value, att, probs),
                gated=gated,
                hidden=hidden_pre,
                feed_pre=feed_pre,
                feed_n=feed_n,
                feed_normed=feed_normed,
                feed_scale=feed_scale,
            )
        )
        if layer + 1 < layers:
            x = feed_join(feed_part, feed_out_bias_own[row], middle, next(idents))
        else:
            block_out = feed_last(feed_part, feed_out_bias_all[row], middle, next(idents))

    def weight_grad(left, right):
        return dot(left, right, 0, 0).astype(BF16)

    def scattered(grad):
        return lax.psum_scatter(grad, "dp", scatter_dimension=0, tiled=True)

    given = cotangent[0]
    big = [None] * layers
    small = [None] * layers
    for layer in reversed(range(layers)):
        in_w, out_w, feed_in_w, feed_out_w = weights[layer]
        k = kept[layer]
        row = slice(layer, layer + 1)
        done = feed_backward(
            given, k["feed_pre"], k["feed_n"], feed_gain_all[row], feed_in_w, feed_out_w
        )
        part, stats, gpre, act, feed_sums, feed_bias = done[:6]
        g = done[6] if isinstance(given, tuple) else given
        gout, gupdate, resid = back_join(
            part,
            stats,
            k["feed_scale"],
            feed_gain_own[row],
            k["update"],
            k["hidden"],
            g,
            k["feed_n"],
            k["x"],
            next(idents),
        )
        feed_in_grad = scattered(weight_grad(k["feed_normed"], gpre))
        feed_out_grad = scattered(weight_grad(act, g))
        gmixed_part, gvalue_part, gbase, gvalue, bias_sums, pair_sums = attention_backward(
            lengths,
            gout,
            gupdate,
            k["saved"],
            in_w,
            pair_all[layer],
            offset_all[row],
            out_w,
        )
        gmixed, gnormed = reduce_two(gmixed_part, gvalue_part, own, next(idents))
        in_grad = scattered(
            jnp.concatenate(
                (weight_grad(k["normed"], gvalue), weight_grad(k["mixed"], gbase)), axis=1
            )
        )
        out_grad = scattered(weight_grad(k["gated"], gout))
        z, zstats, of_states, of_slopes, channel_sums = average_backward(
            lengths,
            gmixed,
            gnormed,
            k["pre"],
            k["own_n"],
            k["scale"],
            resid,
            gain_own[row],
            shift_own[row],
            rate_all[layer],
            coef_all[layer],
            skip_own[row],
        )
        if layer:
            whole_z, total = gather_stats(z, zstats, sections, next(idents))
            given = (whole_z, total, k["x"])
        else:
            input_grad = last_rows(z, zstats, k["x"], next(idents))
        big[layer] = (in_grad, out_grad, feed_in_grad, feed_out_grad)

        rate, drive = rate_all[layer], drive_all[layer]
        gdrive = output_own[layer] * of_states
        grate = coef_all[layer] * of_slopes - input_own[layer] * gdrive
        half_wide = wide // sections
        offsets = (half_wide, half_wide + own, half_wide + own + keyed)
        bias = bias_sums[0]
        base_bias_grad = jnp.concatenate(
            (
                put_contiguous(bias[offsets[0] : offsets[1]], sections, section),
                bias[offsets[1] : offsets[2]],
                put_interleaved(
                    bias[offsets[2] : offsets[2] + half_wide], shards, sections, section
                ),
                put_contiguous(bias[offsets[2] + half_wide :], sections, section),
            )
        )
        alone = (section == 0).astype(F32)
        small[layer] = (
            put_contiguous(channel_sums[0], sections, section),
            put_contiguous(channel_sums[1], sections, section),
            put_contiguous(grate * rate * (1.0 - rate), sections, section),
            put_contiguous((1.0 - rate) * gdrive, sections, section),
            put_contiguous(drive * of_states, sections, section),
            put_contiguous(channel_sums[2], sections, section),
            put_interleaved(bias[:half_wide], shards, sections, section),
            base_bias_grad,
            pair_sums[0:2],
            pair_sums[2],
            feed_sums[0],
            feed_sums[1],
            put_interleaved(feed_bias[0], shards, sections, section),
            feed_sums[2] * alone,
        )

    def to_shards(array):
        lead = array.shape[:-1]
        split = array.reshape(lead + (shards, -1))
        return jnp.moveaxis(split, len(lead), 0).reshape(shards, -1)

    small_totals = []
    for layer in range(layers):
        rows = jnp.concatenate([to_shards(a) for a in small[layer]], axis=1)
        mine = lax.psum_scatter(rows, "dp", scatter_dimension=0, tiled=True)
        small_totals.append(lax.psum(mine[0], "section"))
    small_outs = []
    low = 0
    for a in smalls:
        size = a.size // layers
        small_outs.append(
            jnp.stack([t[low : low + size].reshape(a.shape[1:]) for t in small_totals])
        )
        low += size

    def over_sections(array):
        return lax.all_gather(array, "section", axis=0)

    def join_interleaved(array):
        split = array.reshape(array.shape[:2] + (shards, -1))
        return split.transpose(1, 2, 0, 3).reshape(array.shape[1], -1)

    def join_contiguous(array):
        return array.transpose(1, 0, 2).reshape(array.shape[1], -1)

    value_grads, base_grads, out_grads, feed_in_grads, feed_out_grads = [], [], [], [], []
    half_wide = wide // sections
    for layer in range(layers):
        in_grad, out_grad, feed_in_grad, feed_out_grad = (over_sections(a) for a in big[layer])
        value_grads.append(join_interleaved(in_grad[..., :half_wide]).astype(F32))
        low = half_wide + own
        base_grads.append(
            jnp.concatenate(
                (
                    join_contiguous(in_grad[..., half_wide:low]).astype(F32),
                    jnp.sum(in_grad[..., low : low + keyed].astype(F32), axis=0),
                    join_interleaved(in_grad[..., low + keyed : low + keyed + half_wide]).astype(F32),
                    join_contiguous(in_grad[..., low + keyed + half_wide :]).astype(F32),
                ),
                axis=1,
            )
        )
        out_grads.append(out_grad.reshape(-1, width).astype(F32))
        feed_in_grads.append(join_interleaved(feed_in_grad).astype(F32))
        feed_out_grads.append(feed_out_grad.reshape(-1, width).astype(F32))
    (
        g_gain,
        g_shift,
        g_decay,
        g_input,
        g_output,
        g_skip,
        g_value_bias,
        g_base_bias,
        g_pair,
        g_query,
        g_feed_gain,
        g_feed_shift,
        g_feed_in_bias,
        g_feed_out_bias,
    ) = small_outs
    return (
        block_out[None],
        input_grad[None],
        g_gain,
        g_shift,
        g_decay,
        g_input,
        g_output,
        g_skip,
        jnp.stack(value_grads),
        g_value_bias,
        jnp.stack(base_grads),
        g_base_bias,
        g_pair,
        g_query,
        jnp.stack(out_grads),
        g_feed_gain,
        g_feed_shift,
        jnp.stack(feed_in_grads),
        g_feed_in_bias,
        jnp.stack(feed_out_grads),
        g_feed_out_bias,
    )


def solution(mesh):
    row, row2 = P(None, "dp"), P(None, "dp", None)
    deep = P(None, None, "dp")
    in_specs = (
        P("dp", None, None),
        P("dp"),
        P("dp", None, None),
        row,
        row,
        deep,
        deep,
        deep,
        row,
        row2,
        row,
        row2,
        row,
        deep,
        row,
        row2,
        row,
        row,
        row2,
        row,
        row2,
        row,
    )
    out_specs = (
        P("dp", "section", None),
        P("dp", "section", None),
        row,
        row,
        deep,
        deep,
        deep,
        row,
        row2,
        row,
        row2,
        row,
        deep,
        row,
        row2,
        row,
        row,
        row2,
        row,
        row2,
        row,
    )
    return jax.shard_map(body, mesh=mesh, in_specs=in_specs, out_specs=out_specs, check_vma=False)
```

```python
import functools

import jax
import jax.numpy as jnp
from jax import lax
from jax.experimental import pallas as pl
from jax.experimental.pallas import tpu as pltpu
from jax.sharding import PartitionSpec as P

F32 = jnp.float32
BF16 = jnp.bfloat16
MESH = pl.DeviceIdType.MESH
ATT = 128
LANES = 128
CHUNKS = 8
ROWS = 256
STRIP = 64
TILE = 128
UNROLL = 16
SMALL = 16
EPS = 1e-05
NEGATIVE = -1000000000.0
VMEM_BYTES = 56 * 1024 * 1024


def vmem():
    return pl.BlockSpec(memory_space=pltpu.VMEM)


def smem():
    return pl.BlockSpec(memory_space=pltpu.SMEM)


def hbm():
    return pl.BlockSpec(memory_space=pl.ANY)


def shape(dims, kind):
    return jax.ShapeDtypeStruct(dims, kind)


def sigmoid(v):
    return 0.5 * jnp.tanh(0.5 * v) + 0.5


def silu(v):
    return v * sigmoid(v)


def silu_slope(v):
    s = sigmoid(v)
    return s * (1.0 + v * (1.0 - s))


def dot(left, right, left_dim=1, right_dim=0):
    return lax.dot_general(
        left, right, (((left_dim,), (right_dim,)), ((), ())), preferred_element_type=F32
    )


def normalise(x):
    centred = x - jnp.mean(x, axis=-1, keepdims=True)
    spread = jnp.mean(centred * centred, axis=-1, keepdims=True)
    scale = lax.rsqrt(spread + EPS)
    return centred * scale, scale


def row_valid(start, rows, length):
    place = start + lax.broadcasted_iota(jnp.int32, (rows, 1), 0)
    return (place < length).astype(F32)


def lasting(microseconds):
    return pl.CostEstimate(
        flops=int(microseconds * 1.0e9),
        bytes_accessed=int(microseconds * 3.0e6),
        transcendentals=0,
    )


def params(**more):
    return pltpu.CompilerParams(vmem_limit_bytes=VMEM_BYTES, **more)


def spread_rows(ref, lanes, count):
    return [ref[n, :, lanes] for n in range(count)]


def power(base, exponent):
    result = None
    square = base
    while exponent:
        if exponent % 2:
            result = square if result is None else result * square
        exponent //= 2
        if exponent:
            square = square * square
    return result


def entering(last, rate, steps, reverse=False):
    row = lax.broadcasted_iota(jnp.int32, (CHUNKS, LANES), 0)
    weight = power(rate, steps)
    span = 1
    while span < CHUNKS:
        if reverse:
            moved = jnp.where(row < CHUNKS - span, pltpu.roll(last, CHUNKS - span, 0), 0.0)
        else:
            moved = jnp.where(row >= span, pltpu.roll(last, span, 0), 0.0)
        last = last + weight * moved
        weight = weight * weight
        span *= 2
    if reverse:
        return jnp.where(row < CHUNKS - 1, pltpu.roll(last, CHUNKS - 1, 0), 0.0)
    return jnp.where(row >= 1, pltpu.roll(last, 1, 0), 0.0)


def entering_pair(last, slope, rate, steps):
    row = lax.broadcasted_iota(jnp.int32, (CHUNKS, LANES), 0)
    weight = power(rate, steps)
    tilt = float(steps) * power(rate, steps - 1)
    span = 1
    while span < CHUNKS:
        moved = jnp.where(row >= span, pltpu.roll(last, span, 0), 0.0)
        moved_slope = jnp.where(row >= span, pltpu.roll(slope, span, 0), 0.0)
        slope = slope + weight * moved_slope + tilt * moved
        last = last + weight * moved
        tilt = 2.0 * weight * tilt
        weight = weight * weight
        span *= 2
    first = row >= 1
    return (
        jnp.where(first, pltpu.roll(last, 1, 0), 0.0),
        jnp.where(first, pltpu.roll(slope, 1, 0), 0.0),
    )


def average_forward_kernel(
    length_ref,
    x_ref,
    gain_ref,
    shift_ref,
    rate_ref,
    coef_ref,
    skip_ref,
    normed_ref,
    mixed_ref,
    pre_ref,
    own_ref,
    scale_ref,
    rows_buf,
    m_buf,
    y_buf,
):
    length = length_ref[0]
    count, width = x_ref.shape
    own = mixed_ref.shape[1]
    dims = rate_ref.shape[0]
    steps = count // CHUNKS
    pitch = steps + 1
    mine = pl.ds(pl.multiple_of(lax.axis_index("section") * own, LANES), own)

    def norm_strip(i, carry):
        start = pl.multiple_of(i * STRIP, STRIP)
        here = pl.ds(start, STRIP)
        n, scale = normalise(x_ref[here, :].astype(F32))
        rows_buf[...] = n
        normed_ref[here, :] = (n * gain_ref[...] + shift_ref[...]).astype(BF16)
        part = rows_buf[:, mine]
        own_ref[here, :] = part
        scale_ref[here, :] = jnp.broadcast_to(scale, (STRIP, LANES))
        masked = (part * gain_ref[:, mine] + shift_ref[:, mine]) * row_valid(start, STRIP, length)
        for group in range(own // LANES):
            m_buf[group, pl.ds(start + start // steps, STRIP), :] = masked[:, group * LANES : (group + 1) * LANES]
        return carry

    lax.fori_loop(0, count // STRIP, norm_strip, 0)

    for group in range(own // LANES):
        lanes = slice(group * LANES, (group + 1) * LANES)
        rates = spread_rows(rate_ref, lanes, dims)
        coefs = spread_rows(coef_ref, lanes, dims)
        blank = tuple(jnp.zeros((CHUNKS, LANES), F32) for _ in range(dims))
        m_part, y_part = m_buf.at[group], y_buf.at[group]

        def finals(t, states):
            x = m_part[pl.ds(t, CHUNKS, stride=pitch), :]
            return tuple(r * h + x for r, h in zip(rates, states))

        ends = lax.fori_loop(0, steps, finals, blank, unroll=UNROLL)
        starts = tuple(entering(h, r, steps) for h, r in zip(ends, rates))

        def outputs(t, states):
            x = m_part[pl.ds(t, CHUNKS, stride=pitch), :]
            states = tuple(r * h + x for r, h in zip(rates, states))
            terms = [c * h for c, h in zip(coefs, states)]
            while len(terms) > 1:
                terms = [a + b for a, b in zip(terms[::2], terms[1::2])]
            y_part[pl.ds(t, CHUNKS, stride=pitch), :] = terms[0]
            return states

        lax.fori_loop(0, steps, outputs, starts, unroll=UNROLL)

    def mix_strip(i, carry):
        start = pl.multiple_of(i * STRIP, STRIP)
        here = pl.ds(start, STRIP)
        there = pl.ds(start + start // steps, STRIP)
        for group in range(own // LANES):
            lanes = slice(group * LANES, (group + 1) * LANES)
            pre = y_buf[group, there, :] + skip_ref[:, lanes] * m_buf[group, there, :]
            pre_ref[here, lanes] = pre.astype(BF16)
            mixed_ref[here, lanes] = silu(pre).astype(BF16)
        return carry

    lax.fori_loop(0, count // STRIP, mix_strip, 0)


def average_forward(length, x, gain, shift, rate, coef, skip):
    count, width = x.shape
    own = skip.shape[1]
    groups = own // LANES
    return pl.pallas_call(
        average_forward_kernel,
        out_shape=(
            shape((count, width), BF16),
            shape((count, own), BF16),
            shape((count, own), BF16),
            shape((count, own), F32),
            shape((count, LANES), F32),
        ),
        in_specs=[smem()] + [vmem()] * 6,
        out_specs=(vmem(),) * 5,
        scratch_shapes=[
            pltpu.VMEM((STRIP, width), F32),
            pltpu.VMEM((groups, count + CHUNKS, LANES), F32),
            pltpu.VMEM((groups, count + CHUNKS, LANES), F32),
        ],
        cost_estimate=lasting(13),
        compiler_params=params(),
    )(length, x, gain, shift, rate, coef, skip)


def average_backward_kernel(waits, *refs):
    average_backward_work(*refs[waits:])


def average_backward_work(
    length_ref,
    gmixed_ref,
    gvalue_ref,
    pre_ref,
    own_ref,
    scale_ref,
    resid_ref,
    norm_ref,
    rate_ref,
    coef_ref,
    skip_ref,
    z_ref,
    stats_ref,
    sums_ref,
    m_buf,
    g_buf,
    r_buf,
):
    length = length_ref[0]
    gain_ref, shift_ref = norm_ref.at[0:1, :], norm_ref.at[1:2, :]
    count, own = z_ref.shape
    dims = rate_ref.shape[0]
    steps = count // CHUNKS
    pitch = steps + 1
    groups = own // LANES
    part_size = dims // 2

    def load_strip(i, carry):
        start = pl.multiple_of(i * STRIP, STRIP)
        here = pl.ds(start, STRIP)
        valid = row_valid(start, STRIP, length)
        there = pl.ds(start + start // steps, STRIP)
        for group in range(groups):
            lanes = slice(group * LANES, (group + 1) * LANES)
            m_buf[group, there, :] = (
                own_ref[here, lanes] * gain_ref[:, lanes] + shift_ref[:, lanes]
            ) * valid
            slope = silu_slope(pre_ref[here, lanes].astype(F32))
            g_buf[group, there, :] = gmixed_ref[here, lanes] * slope
        return carry

    lax.fori_loop(0, count // STRIP, load_strip, 0)

    zero = jnp.zeros((CHUNKS, LANES), F32)
    for group in range(groups):
        lanes = slice(group * LANES, (group + 1) * LANES)
        rates = spread_rows(rate_ref, lanes, dims)
        coefs = spread_rows(coef_ref, lanes, dims)
        m_part, g_part, r_part = m_buf.at[group], g_buf.at[group], r_buf.at[group]

        blank = tuple(zero for _ in rates)

        def back_finals(t, carry):
            states, slopes = carry
            g = g_part[pl.ds(steps - 1 - t, CHUNKS, stride=pitch), :]
            slopes = tuple(r * w + h for r, w, h in zip(rates, slopes, states))
            states = tuple(r * h + g for r, h in zip(rates, states))
            return states, slopes

        ends, end_slopes = lax.fori_loop(0, steps, back_finals, (blank, blank), unroll=UNROLL)
        starts = tuple(entering(h, r, steps, reverse=True) for h, r in zip(ends, rates))

        for half in range(2):
            some = rates[half * part_size : (half + 1) * part_size]
            empty = tuple(zero for _ in some)

            def sweep(t, carry):
                states, slopes, of_states, of_slopes = carry
                x = m_part[pl.ds(t, CHUNKS, stride=pitch), :]
                g = g_part[pl.ds(t, CHUNKS, stride=pitch), :]
                slopes = tuple(r * q + h for r, q, h in zip(some, slopes, states))
                states = tuple(r * h + x for r, h in zip(some, states))
                of_states = tuple(a + g * h for a, h in zip(of_states, states))
                of_slopes = tuple(a + g * q for a, q in zip(of_slopes, slopes))
                return states, slopes, of_states, of_slopes

            states, slopes, of_states, of_slopes = lax.fori_loop(
                0, steps, sweep, (empty,) * 4, unroll=UNROLL
            )
            for n in range(part_size):
                row = half * part_size + n
                rate, back, back_slope = rates[row], ends[row], end_slopes[row]
                state, slope = entering_pair(states[n], slopes[n], rate, steps)
                of_state = of_states[n] + state * (rate * back)
                of_slope = (
                    of_slopes[n] + slope * (rate * back) + state * (back + rate * back_slope)
                )
                sums_ref[row : row + 1, lanes] = jnp.sum(of_state, axis=0, keepdims=True)
                row += dims
                sums_ref[row : row + 1, lanes] = jnp.sum(of_slope, axis=0, keepdims=True)

        def back_outputs(t, states):
            g = g_part[pl.ds(steps - 1 - t, CHUNKS, stride=pitch), :]
            states = tuple(r * h + g for r, h in zip(rates, states))
            terms = [c * h for c, h in zip(coefs, states)]
            while len(terms) > 1:
                terms = [a + b for a, b in zip(terms[::2], terms[1::2])]
            r_part[pl.ds(steps - 1 - t, CHUNKS, stride=pitch), :] = terms[0]
            return states

        lax.fori_loop(0, steps, back_outputs, starts, unroll=UNROLL)

    ones = jnp.ones((CHUNKS, own), BF16)
    first = lax.broadcasted_iota(jnp.int32, (CHUNKS, LANES), 0) == 0

    def finish(i, carry):
        start = pl.multiple_of(i * LANES, LANES)
        here = pl.ds(start, LANES)
        valid = row_valid(start, LANES, length)
        there = pl.ds(start + start // steps, LANES)
        of_gain, of_shift, of_skip = carry
        smoothed = jnp.concatenate([r_buf[k, there, :] for k in range(groups)], axis=1)
        gpre = jnp.concatenate([g_buf[k, there, :] for k in range(groups)], axis=1)
        masked = jnp.concatenate([m_buf[k, there, :] for k in range(groups)], axis=1)
        n = own_ref[here, :]
        gmasked = skip_ref[...] * gpre + smoothed
        gnormed = gmasked * valid + gvalue_ref[here, :]
        e = gnormed * gain_ref[...]
        z = scale_ref[here, 0:1] * e + resid_ref[here, :]
        z_ref[here, :] = z.astype(BF16)
        mean_row = dot(ones, e.astype(BF16), 1, 1)
        slope_row = dot(ones, (e * n).astype(BF16), 1, 1)
        stats_ref[:, here] = jnp.where(first, mean_row, slope_row)
        return (
            of_gain + jnp.sum(gnormed * n, axis=0, keepdims=True),
            of_shift + jnp.sum(gnormed, axis=0, keepdims=True),
            of_skip + jnp.sum(gpre * masked, axis=0, keepdims=True),
        )

    blank_row = jnp.zeros((1, own), F32)
    of_gain, of_shift, of_skip = lax.fori_loop(
        0, count // LANES, finish, (blank_row, blank_row, blank_row)
    )
    last = 2 * dims
    sums_ref[last : last + 1, :] = of_gain
    sums_ref[last + 1 : last + 2, :] = of_shift
    sums_ref[last + 2 : last + 3, :] = of_skip
    sums_ref[last + 3 : last + 8, :] = jnp.zeros((5, own), F32)


def average_backward(
    length, gmixed, gvalue, pre, own_n, scale, resid, norm, rate, coef, skip, after=()
):
    count, own = gmixed.shape
    dims = rate.shape[0]
    groups = own // LANES
    return pl.pallas_call(
        functools.partial(average_backward_kernel, len(after)),
        out_shape=(
            shape((count, own), BF16),
            shape((CHUNKS, count), F32),
            shape((2 * dims + 8, own), F32),
        ),
        in_specs=[hbm()] * len(after) + [smem()] + [vmem()] * 10,
        out_specs=(vmem(),) * 3,
        scratch_shapes=[pltpu.VMEM((groups, count + CHUNKS, LANES), F32)] * 3,
        cost_estimate=lasting(21),
        compiler_params=params(),
    )(*after, length, gmixed, gvalue, pre, own_n, scale, resid, norm, rate, coef, skip)


def unfold(packed, out_w, shards):
    wide, width = out_w.shape
    few = wide // shards
    low = packed.shape[1] - width // 2
    for shard in range(shards):
        for half in range(2):
            start = shard * (width // shards) + half * few
            out_w[
                shard * few : (shard + 1) * few, half * (width // 2) : (half + 1) * (width // 2)
            ] = packed[start : start + few, low:]


def attention_forward_kernel(
    shards,
    length_ref,
    normed_ref,
    mixed_ref,
    in_ref,
    bias_ref,
    pair_ref,
    offset_ref,
    part_ref,
    update_ref,
    shared_ref,
    reset_ref,
    cand_ref,
    value_ref,
    att_ref,
    gated_ref,
    probs_ref,
    out_w_ref,
):
    length = length_ref[0]

    @pl.when(pl.program_id(0) == 0)
    def _():
        unfold(in_ref, out_w_ref, shards)

    rows = normed_ref.shape[0]
    wide = value_ref.shape[1]
    own = update_ref.shape[1]
    keyed = shared_ref.shape[1]
    start = pl.program_id(0) * rows
    value = dot(normed_ref[...], in_ref[:, :wide]) + bias_ref[:, :wide]
    value_ref[...] = value.astype(BF16)
    values = silu(value).astype(BF16)
    low = wide
    update = dot(mixed_ref[...], in_ref[:, low : low + own]) + bias_ref[:, low : low + own]
    update_ref[...] = update.astype(BF16)
    low += own
    shared = dot(mixed_ref[...], in_ref[:, low : low + keyed]) + bias_ref[:, low : low + keyed]
    shared_ref[...] = shared.astype(BF16)
    low += keyed
    reset = dot(mixed_ref[...], in_ref[:, low : low + wide]) + bias_ref[:, low : low + wide]
    reset_ref[...] = reset.astype(BF16)
    low += wide
    cand_ref[...] = (
        dot(mixed_ref[...], in_ref[:, low : low + own]) + bias_ref[:, low : low + own]
    ).astype(BF16)
    shared = silu(shared)
    reset = silu(reset)
    queries = (shared * pair_ref[0:1, :] + offset_ref[...]).astype(BF16)
    keys = (shared * pair_ref[1:2, :]).astype(BF16)
    for block in range(rows // ATT):
        here = slice(block * ATT, (block + 1) * ATT)
        begin = start + block * ATT
        scores = dot(queries[here], keys[here], 1, 1) * keyed**-0.5
        key_place = begin + lax.broadcasted_iota(jnp.int32, (ATT, ATT), 1)
        scores = jnp.where(key_place < length, scores, NEGATIVE)
        raised = jnp.exp(scores - jnp.max(scores, axis=-1, keepdims=True))
        probs = (raised / jnp.sum(raised, axis=-1, keepdims=True)).astype(BF16)
        probs_ref[here, :] = probs
        attended = dot(probs, values[here]) * row_valid(begin, ATT, length)
        att_ref[here, :] = attended.astype(BF16)
        gated_ref[here, :] = (attended * reset[here]).astype(BF16)
    part_ref[...] = dot(gated_ref[...], out_w_ref[...]).astype(BF16)


def attention_forward(length, normed, mixed, in_w, bias, pair, offset, own, shards):
    count, width = normed.shape
    wide = width // 2
    keyed = pair.shape[1]

    def rows(columns):
        return pl.BlockSpec((ROWS, columns), lambda i: (i, 0))

    def whole(array):
        return pl.BlockSpec(array.shape, lambda i: (0, 0))

    widths = (width, own, keyed, wide, own, wide, wide, wide, ATT)
    return pl.pallas_call(
        functools.partial(attention_forward_kernel, shards),
        grid=(count // ROWS,),
        out_shape=tuple(shape((count, w), BF16) for w in widths),
        in_specs=[
            smem(),
            rows(width),
            rows(width),
            whole(in_w),
            whole(bias),
            whole(pair),
            whole(offset),
        ],
        out_specs=tuple(rows(w) for w in widths),
        scratch_shapes=[pltpu.VMEM((wide, width), BF16)],
        cost_estimate=lasting(12),
        compiler_params=params(),
    )(length, normed, mixed, in_w, bias, pair, offset)


def attention_backward_kernel(
    shards,
    waits,
    *refs,
):
    attention_backward_work(shards, *refs[waits:])


def attention_backward_work(
    shards,
    length_ref,
    gout_ref,
    gupdate_ref,
    shared_ref,
    reset_ref,
    value_ref,
    att_ref,
    probs_ref,
    in_ref,
    pair_ref,
    offset_ref,
    gmixed_ref,
    gnormed_ref,
    gbase_ref,
    gvalue_ref,
    bias_ref,
    pair_sum_ref,
    out_w_ref,
):
    length = length_ref[0]
    rows = gout_ref.shape[0]
    total = bias_ref.shape[1]
    wide = value_ref.shape[1]
    own = gupdate_ref.shape[1]
    keyed = shared_ref.shape[1]
    start = pl.program_id(0) * rows
    mine = pl.ds(pl.multiple_of(lax.axis_index("section") * own, LANES), own)

    @pl.when(pl.program_id(0) == 0)
    def _():
        bias_ref[...] = jnp.zeros_like(bias_ref)
        pair_sum_ref[...] = jnp.zeros_like(pair_sum_ref)
        unfold(in_ref, out_w_ref, shards)

    valid = row_valid(start, rows, length)
    ggated = dot(gout_ref[...], out_w_ref[...], 1, 1)
    reset = reset_ref[...].astype(F32)
    gattended = (ggated * silu(reset) * valid).astype(BF16)
    greset = ggated * att_ref[...].astype(F32) * silu_slope(reset)
    value = value_ref[...].astype(F32)
    values = silu(value).astype(BF16)
    shared_pre = shared_ref[...].astype(F32)
    shared = silu(shared_pre)
    scale_q, scale_k = pair_ref[0:1, :], pair_ref[1:2, :]
    queries = (shared * scale_q + offset_ref[...]).astype(BF16)
    keys = (shared * scale_k).astype(BF16)
    gq_parts, gk_parts, gv_parts = [], [], []
    for block in range(rows // ATT):
        here = slice(block * ATT, (block + 1) * ATT)
        probs = probs_ref[here, :]
        gprobs = dot(gattended[here], values[here], 1, 1)
        gv_parts.append(dot(probs, gattended[here], 0, 0))
        probs = probs.astype(F32)
        gscores = probs * (gprobs - jnp.sum(probs * gprobs, axis=-1, keepdims=True))
        key_place = start + block * ATT + lax.broadcasted_iota(jnp.int32, (ATT, ATT), 1)
        gscores = jnp.where(key_place < length, gscores, 0.0)
        gscores = (gscores * keyed**-0.5).astype(BF16)
        gq_parts.append(dot(gscores, keys[here]))
        gk_parts.append(dot(gscores, queries[here], 0, 0))
    gqueries = jnp.concatenate(gq_parts, axis=0)
    gkeys = jnp.concatenate(gk_parts, axis=0)
    gvalue = jnp.concatenate(gv_parts, axis=0) * silu_slope(value)
    gshared = (gqueries * scale_q + gkeys * scale_k) * silu_slope(shared_pre)
    pair_sum_ref[0:1, :] += jnp.sum(gqueries * shared, axis=0, keepdims=True)
    pair_sum_ref[1:2, :] += jnp.sum(gkeys * shared, axis=0, keepdims=True)
    pair_sum_ref[2:3, :] += jnp.sum(gqueries, axis=0, keepdims=True)
    gupdate = gupdate_ref[...]
    gcand = gout_ref[:, mine]
    low = 0
    for piece in (gvalue, gupdate, gshared, greset, gcand):
        size = piece.shape[1]
        bias_ref[0:1, low : low + size] += jnp.sum(piece.astype(F32), axis=0, keepdims=True)
        if low:
            gbase_ref[:, low - wide : low - wide + size] = piece.astype(BF16)
        else:
            gvalue_ref[...] = piece.astype(BF16)
        low += size
    gmixed_ref[...] = dot(gbase_ref[...], in_ref[:, wide:total], 1, 1).astype(BF16)
    gnormed_ref[...] = dot(gvalue_ref[...], in_ref[:, :wide], 1, 1).astype(BF16)


def attention_backward(length, gout, gupdate, saved, in_w, pair, offset, shards, after=()):
    shared, reset, value, att, probs = saved
    count, width = gout.shape
    own = gupdate.shape[1]
    wide = width // 2
    keyed = pair.shape[1]
    total = in_w.shape[1] - width // 2

    def rows(columns):
        return pl.BlockSpec((ROWS, columns), lambda i: (i, 0))

    def whole(dims):
        return pl.BlockSpec(dims, lambda i: (0, 0))

    return pl.pallas_call(
        functools.partial(attention_backward_kernel, shards, len(after)),
        grid=(count // ROWS,),
        out_shape=(
            shape((count, width), BF16),
            shape((count, width), BF16),
            shape((count, total - wide), BF16),
            shape((count, wide), BF16),
            shape((8, total), F32),
            shape((8, keyed), F32),
        ),
        in_specs=[hbm()] * len(after)
        + [
            smem(),
            rows(width),
            rows(own),
            rows(keyed),
            rows(wide),
            rows(wide),
            rows(wide),
            rows(ATT),
            whole(in_w.shape),
            whole(pair.shape),
            whole(offset.shape),
        ],
        out_specs=(
            rows(width),
            rows(width),
            rows(total - wide),
            rows(wide),
            whole((8, total)),
            whole((8, keyed)),
        ),
        scratch_shapes=[pltpu.VMEM((wide, width), BF16)],
        cost_estimate=lasting(13),
        compiler_params=params(),
    )(*after, length, gout, gupdate, shared, reset, value, att, probs, in_w, pair, offset)


def feed_forward_kernel(
    x_ref, gain_ref, shift_ref, w_ref, bias_ref, part_ref, pre_ref, n_ref, normed_ref, scale_ref
):
    hidden = pre_ref.shape[1]
    n, scale = normalise(x_ref[...].astype(F32))
    n_ref[...] = n.astype(BF16)
    scale_ref[...] = jnp.broadcast_to(scale, scale_ref.shape)
    normed_ref[...] = (n * gain_ref[...] + shift_ref[...]).astype(BF16)
    pre = dot(normed_ref[...], w_ref[:, :hidden]) + bias_ref[...]
    pre_ref[...] = pre.astype(BF16)
    part_ref[...] = dot(silu(pre).astype(BF16), w_ref[:, hidden:]).astype(BF16)


def feed_forward(x, gain, shift, weights, bias):
    count, width = x.shape
    hidden = bias.shape[1]

    def rows(columns):
        return pl.BlockSpec((ROWS, columns), lambda i: (i, 0))

    def whole(array):
        return pl.BlockSpec(array.shape, lambda i: (0, 0))

    return pl.pallas_call(
        feed_forward_kernel,
        grid=(count // ROWS,),
        out_shape=(
            shape((count, width), BF16),
            shape((count, hidden), BF16),
            shape((count, width), BF16),
            shape((count, width), BF16),
            shape((count, LANES), F32),
        ),
        in_specs=[rows(width)] + [whole(a) for a in (gain, shift, weights, bias)],
        out_specs=(rows(width), rows(hidden), rows(width), rows(width), rows(LANES)),
        cost_estimate=lasting(10),
        compiler_params=params(),
    )(x, gain, shift, weights, bias)


def feed_backward_kernel(corrected, waits, *refs):
    refs = refs[waits:]
    if corrected:
        z_ref, means_ref, x_ref = refs[:3]
        refs = refs[3:]
    else:
        g_in_ref = refs[0]
        refs = refs[1:]
    pre_ref, n_ref, gain_ref, w_ref = refs[:4]
    refs = refs[4:]
    hidden = pre_ref.shape[1]
    part_ref, stats_ref, gpre_ref, act_ref, sums_ref, bias_ref = refs[:6]
    width = n_ref.shape[1]

    @pl.when(pl.program_id(0) == 0)
    def _():
        sums_ref[...] = jnp.zeros_like(sums_ref)
        bias_ref[...] = jnp.zeros_like(bias_ref)

    if corrected:
        g_ref = refs[6]
        xn, xscale = normalise(x_ref[...].astype(F32))
        means = means_ref[...].T * (1.0 / width)
        g = z_ref[...].astype(F32) - xscale * (means[:, 0:1] + xn * means[:, 1:2])
        g_ref[...] = g.astype(BF16)
    else:
        g_ref = g_in_ref
    g = g_ref[...]
    pre = pre_ref[...].astype(F32)
    s = sigmoid(pre)
    act_ref[...] = (pre * s).astype(BF16)
    gpre = dot(g, w_ref[:, hidden:], 1, 1) * (s * (1.0 + pre * (1.0 - s)))
    bias_ref[0:1, :] += jnp.sum(gpre, axis=0, keepdims=True)
    gpre_ref[...] = gpre.astype(BF16)
    part = dot(gpre_ref[...], w_ref[:, :hidden], 1, 1)
    part_ref[...] = part.astype(BF16)
    n = n_ref[...].astype(F32)
    sums_ref[0:1, :] += jnp.sum(part * n, axis=0, keepdims=True)
    sums_ref[1:2, :] += jnp.sum(part, axis=0, keepdims=True)
    sums_ref[2:3, :] += jnp.sum(g.astype(F32), axis=0, keepdims=True)
    e = part * gain_ref[...]
    ones = jnp.ones((CHUNKS, width), BF16)
    mean_row = dot(ones, e.astype(BF16), 1, 1)
    slope_row = dot(ones, (e * n).astype(BF16), 1, 1)
    first = lax.broadcasted_iota(jnp.int32, mean_row.shape, 0) == 0
    stats_ref[...] = jnp.where(first, mean_row, slope_row)


def feed_backward(given, pre, n, gain, weights, after=()):
    corrected = isinstance(given, tuple)
    count, width = n.shape
    hidden = pre.shape[1]

    def rows(columns):
        return pl.BlockSpec((ROWS, columns), lambda i: (i, 0))

    def whole(dims):
        return pl.BlockSpec(dims, lambda i: (0, 0))

    stats_spec = pl.BlockSpec((CHUNKS, ROWS), lambda i: (0, i))
    given = given if corrected else (given,)
    given_specs = [rows(width), stats_spec, rows(width)] if corrected else [rows(width)]
    extra = ((shape((count, width), BF16),), (rows(width),)) if corrected else ((), ())
    return pl.pallas_call(
        functools.partial(feed_backward_kernel, corrected, len(after)),
        grid=(count // ROWS,),
        out_shape=(
            shape((count, width), BF16),
            shape((CHUNKS, count), F32),
            shape((count, hidden), BF16),
            shape((count, hidden), BF16),
            shape((8, width), F32),
            shape((8, hidden), F32),
        )
        + extra[0],
        in_specs=[hbm()] * len(after)
        + given_specs
        + [rows(hidden), rows(width), whole(gain.shape), whole(weights.shape)],
        out_specs=(
            rows(width),
            stats_spec,
            rows(hidden),
            rows(hidden),
            whole((8, width)),
            whole((8, hidden)),
        )
        + extra[1],
        cost_estimate=lasting(13),
        compiler_params=params(),
    )(*after, *given, pre, n, gain, weights)


def plane():
    me = lax.axis_index("section")
    across = me + 1 - 2 * (me % 2)
    along = me + 2 - 4 * (me // 2)
    return me, across, along, across + along - me


def greet(*others):
    barrier = pltpu.get_barrier_semaphore()
    for other in others:
        pl.semaphore_signal(barrier, inc=1, device_id={"section": other}, device_id_type=MESH)
    pl.semaphore_wait(barrier, len(others))


def link(source, target, sems, index, other):
    send, recv = sems
    return pltpu.make_async_remote_copy(
        src_ref=source,
        dst_ref=target,
        send_sem=send.at[index],
        recv_sem=recv.at[index],
        device_id={"section": other},
        device_id_type=MESH,
    )


def strips(count, work):
    def one(i, carry):
        work(pl.multiple_of(i * STRIP, STRIP))
        return carry

    lax.fori_loop(0, count // STRIP, one, 0)


def widen(block):
    rows, columns = block.shape
    if columns < LANES:
        block = jnp.concatenate((block, jnp.zeros((rows, LANES - columns), F32)), axis=1)
    return block.astype(BF16)


def grad_tiles(left, right, store, begin, end):
    def one(i, carry):
        rows = pl.ds(pl.multiple_of(i * TILE, TILE), TILE)
        store(rows, dot(left[:, rows], right[...], 0, 0).astype(BF16))
        return carry

    lax.fori_loop(begin, end, one, 0)


def reduce_begin(part, piece, peers, slots, sems):
    me, across, along, far = peers
    early, direct, _, _ = slots
    started = []
    for half, first in enumerate((across, along)):
        started.append(link(part.at[piece(far, half)], early.at[half], sems, half, first))
        started[-1].start()
    for half, first in enumerate((across, along)):
        started.append(link(part.at[piece(first, half)], direct.at[half], sems, 2 + half, first))
        started[-1].start()
    return started


def reduce_forward(part, piece, peers, slots, sems, started):
    me, across, along, far = peers
    early, _, late, stage = slots
    for half, second in enumerate((along, across)):
        started[half].wait_recv()
        row, column = piece(second, half)

        def add(start):
            here = pl.ds(start, STRIP)
            mine = part[pl.ds(row.start + start, STRIP), column].astype(F32)
            stage[half, here, :] = (mine + early[half, here, :].astype(F32)).astype(BF16)

        strips(early.shape[1], add)
        started.append(link(stage.at[half], late.at[half], sems, 4 + half, second))
        started[-1].start()


def reduce_arrived(started, half):
    started[2 + half].wait_recv()
    started[4 + half].wait_recv()


def reduced(part, piece, me, slots, half, start):
    _, direct, late, _ = slots
    row, column = piece(me, half)
    here = pl.ds(start, STRIP)
    total = part[pl.ds(row.start + start, STRIP), column].astype(F32)
    return total + direct[half, here, :].astype(F32) + late[half, here, :].astype(F32)


def gather_begin(out, piece, peers, sems, half):
    me, across, along, far = peers
    here = out.at[piece(me, half)]
    order = ((along, 0), (across, 1)) if half == 0 else ((across, 1), (along, 0))
    started = {}
    for other, way in order:
        copy = link(here, here, sems, 2 * half + way, other)
        copy.start()
        started[way] = copy
    return started


def gather_forward(out, piece, peers, sems, zero, one):
    me, across, along, far = peers
    zero[0].wait_recv()
    passing = out.at[piece(along, 0)]
    first = link(passing, passing, sems, 4, across)
    first.start()
    one[1].wait_recv()
    passing = out.at[piece(across, 1)]
    second = link(passing, passing, sems, 5, along)
    second.start()
    return first, second


def gather_finish(out, piece, peers, sems, zero, one, passed=None):
    first, second = passed or gather_forward(out, piece, peers, sems, zero, one)
    zero[1].wait_recv()
    one[0].wait_recv()
    first.wait_recv()
    second.wait_recv()
    for copy in (zero[0], zero[1], one[0], one[1], first, second):
        copy.wait_send()


def column_piece(count, own):
    def piece(owner, half):
        size = count // 2
        return pl.ds(half * size, size), pl.ds(pl.multiple_of(owner * own, LANES), own)

    return piece


def row_piece(count, width):
    def piece(owner, half):
        size = count // 4
        return (
            pl.ds(pl.multiple_of(owner * size, size), size),
            pl.ds(half * (width // 2), width // 2),
        )

    return piece


def reduce_scratch(rows, columns):
    return [pltpu.VMEM((2, rows, columns), BF16)] * 4


def copy_sems(count):
    return [pltpu.SemaphoreType.DMA((count,)), pltpu.SemaphoreType.DMA((count,))]


def comm_params(ident):
    return params(collective_id=ident, has_side_effects=True)


def own_slice(source, target, sem, own):
    start = pl.multiple_of(lax.axis_index("section") * own, LANES)
    return pltpu.make_async_copy(source.at[:, pl.ds(start, own)], target, sem)


def gather_kernel(own_ref, out_ref, send, recv):
    count, own = own_ref.shape
    peers = plane()
    piece = column_piece(count, own)
    mine = pl.ds(pl.multiple_of(peers[0] * own, LANES), own)
    out_ref[:, mine] = own_ref[...]
    greet(peers[1], peers[2])
    zero = gather_begin(out_ref, piece, peers, (send, recv), 0)
    one = gather_begin(out_ref, piece, peers, (send, recv), 1)
    gather_finish(out_ref, piece, peers, (send, recv), zero, one)


def gather_columns(own, sections, ident):
    count, width = own.shape
    return pl.pallas_call(
        gather_kernel,
        out_shape=shape((count, width * sections), BF16),
        in_specs=[vmem()],
        out_specs=vmem(),
        scratch_shapes=copy_sems(6),
        cost_estimate=lasting(18),
        compiler_params=comm_params(ident),
    )(own)


def stats_total(stats, got, stage, peers, sems, index):
    me, across, along, far = peers
    first = link(stats, got.at[0], sems, index, across)
    first.start()
    first.wait_recv()
    stage[...] = stats[...] + got[0]
    second = link(stage, got.at[1], sems, index + 1, along)
    second.start()
    second.wait_recv()
    first.wait_send()
    second.wait_send()
    return stage[...] + got[1]


def gather_stats_kernel(own_ref, stats_ref, out_ref, total_ref, got, stage, send, recv):
    count, own = own_ref.shape
    peers = plane()
    piece = column_piece(count, own)
    mine = pl.ds(pl.multiple_of(peers[0] * own, LANES), own)
    out_ref[:, mine] = own_ref[...]
    greet(peers[1], peers[2])
    sems = (send, recv)
    zero = gather_begin(out_ref, piece, peers, sems, 0)
    one = gather_begin(out_ref, piece, peers, sems, 1)
    total_ref[...] = stats_total(stats_ref, got, stage, peers, sems, 6)
    gather_finish(out_ref, piece, peers, sems, zero, one)


def gather_stats(own, stats, sections, ident):
    count, width = own.shape
    return pl.pallas_call(
        gather_stats_kernel,
        out_shape=(shape((count, width * sections), BF16), shape(stats.shape, F32)),
        in_specs=[vmem()] * 2,
        out_specs=(vmem(), vmem()),
        scratch_shapes=[pltpu.VMEM((2,) + stats.shape, F32), pltpu.VMEM(stats.shape, F32)]
        + copy_sems(8),
        cost_estimate=lasting(20),
        compiler_params=comm_params(ident),
    )(own, stats)


def attention_join_kernel(
    part_ref,
    update_ref,
    cand_ref,
    x_ref,
    out_ref,
    hidden_ref,
    early,
    direct,
    late,
    stage,
    x_own,
    local_sem,
    send,
    recv,
    send_g,
    recv_g,
):
    count, own = update_ref.shape
    peers = plane()
    me = peers[0]
    piece = column_piece(count, own)
    slots = (early, direct, late, stage)
    fetch = own_slice(x_ref, x_own, local_sem, own)
    fetch.start()
    greet(peers[1], peers[2])
    started = reduce_begin(part_ref, piece, peers, slots, (send, recv))
    fetch.wait()
    reduce_forward(part_ref, piece, peers, slots, (send, recv), started)
    begun = []
    mine = pl.ds(pl.multiple_of(me * own, LANES), own)
    for half in range(2):
        reduce_arrived(started, half)

        def finish(start):
            here = pl.ds(half * (count // 2) + start, STRIP)
            pre = cand_ref[here, :].astype(F32) + reduced(part_ref, piece, me, slots, half, start)
            hidden_ref[here, :] = pre.astype(BF16)
            x = x_own[here, :].astype(F32)
            made = x + sigmoid(update_ref[here, :].astype(F32)) * (silu(pre) - x)
            out_ref[here, mine] = made.astype(BF16)

        strips(count // 2, finish)
        begun.append(gather_begin(out_ref, piece, peers, (send_g, recv_g), half))
    gather_finish(out_ref, piece, peers, (send_g, recv_g), begun[0], begun[1])
    for copy in started:
        copy.wait_send()


def attention_join(part, update, cand, x, ident):
    count, width = part.shape
    own = update.shape[1]
    return pl.pallas_call(
        attention_join_kernel,
        out_shape=(shape((count, width), BF16), shape((count, own), BF16)),
        in_specs=[vmem(), vmem(), vmem(), hbm()],
        out_specs=(vmem(), vmem()),
        scratch_shapes=reduce_scratch(count // 2, own)
        + [pltpu.VMEM((count, own), BF16), pltpu.SemaphoreType.DMA]
        + copy_sems(6)
        + copy_sems(6),
        cost_estimate=lasting(37),
        compiler_params=comm_params(ident),
    )(part, update, cand, x)


def feed_join_kernel(
    part_ref,
    bias_ref,
    x_ref,
    out_ref,
    early,
    direct,
    late,
    stage,
    x_own,
    local_sem,
    send,
    recv,
    send_g,
    recv_g,
):
    count = part_ref.shape[0]
    own = bias_ref.shape[1]
    peers = plane()
    me = peers[0]
    piece = column_piece(count, own)
    slots = (early, direct, late, stage)
    fetch = own_slice(x_ref, x_own, local_sem, own)
    fetch.start()
    greet(peers[1], peers[2])
    started = reduce_begin(part_ref, piece, peers, slots, (send, recv))
    fetch.wait()
    reduce_forward(part_ref, piece, peers, slots, (send, recv), started)
    begun = []
    mine = pl.ds(pl.multiple_of(me * own, LANES), own)
    for half in range(2):
        reduce_arrived(started, half)

        def finish(start):
            here = pl.ds(half * (count // 2) + start, STRIP)
            total = reduced(part_ref, piece, me, slots, half, start)
            made = x_own[here, :].astype(F32) + total + bias_ref[...]
            out_ref[here, mine] = made.astype(BF16)

        strips(count // 2, finish)
        begun.append(gather_begin(out_ref, piece, peers, (send_g, recv_g), half))
    gather_finish(out_ref, piece, peers, (send_g, recv_g), begun[0], begun[1])
    for copy in started:
        copy.wait_send()


def feed_join(part, bias, x, ident):
    count, width = part.shape
    own = bias.shape[1]
    return pl.pallas_call(
        feed_join_kernel,
        out_shape=shape((count, width), BF16),
        in_specs=[vmem(), vmem(), hbm()],
        out_specs=vmem(),
        scratch_shapes=reduce_scratch(count // 2, own)
        + [pltpu.VMEM((count, own), BF16), pltpu.SemaphoreType.DMA]
        + copy_sems(6)
        + copy_sems(6),
        cost_estimate=lasting(36),
        compiler_params=comm_params(ident),
    )(part, bias, x)


def feed_last_kernel(
    part_ref, bias_ref, x_ref, out_ref, early, direct, late, stage, x_own, local_sem, send, recv
):
    count, width = part_ref.shape
    quarter = count // 4
    peers = plane()
    me = peers[0]
    piece = row_piece(count, width)
    slots = (early, direct, late, stage)
    mine = pl.ds(pl.multiple_of(me * quarter, quarter), quarter)
    fetch = pltpu.make_async_copy(x_ref.at[mine, :], x_own, local_sem)
    fetch.start()
    greet(peers[1], peers[2])
    started = reduce_begin(part_ref, piece, peers, slots, (send, recv))
    fetch.wait()
    reduce_forward(part_ref, piece, peers, slots, (send, recv), started)
    for half in range(2):
        reduce_arrived(started, half)
        lanes = slice(half * (width // 2), (half + 1) * (width // 2))

        def finish(start):
            here = pl.ds(start, STRIP)
            total = reduced(part_ref, piece, me, slots, half, start)
            made = x_own[here, lanes].astype(F32) + total + bias_ref[:, lanes]
            out_ref[here, lanes] = made.astype(BF16)

        strips(quarter, finish)
    for copy in started:
        copy.wait_send()


def feed_last(part, bias, x, ident):
    count, width = part.shape
    quarter = count // 4
    return pl.pallas_call(
        feed_last_kernel,
        out_shape=shape((quarter, width), BF16),
        in_specs=[vmem(), vmem(), hbm()],
        out_specs=vmem(),
        scratch_shapes=reduce_scratch(quarter, width // 2)
        + [pltpu.VMEM((quarter, width), BF16), pltpu.SemaphoreType.DMA]
        + copy_sems(6),
        cost_estimate=lasting(20),
        compiler_params=comm_params(ident),
    )(part, bias, x)


def back_join_kernel(
    shards,
    part_ref,
    stats_ref,
    scale_ref,
    gain_ref,
    update_ref,
    hidden_ref,
    normed_hbm,
    gpre_hbm,
    act_hbm,
    g_hbm,
    sums_ref,
    bias_ref,
    n_ref,
    x_ref,
    out_ref,
    gupdate_ref,
    resid_ref,
    grad_hbm,
    normed_ref,
    gpre_ref,
    act_ref,
    g_ref,
    grad_ref,
    early,
    direct,
    late,
    stage,
    n_own,
    x_own,
    got,
    stats_stage,
    means,
    local_sem,
    send,
    recv,
    send_g,
    recv_g,
    send_s,
    recv_s,
):
    count, width = part_ref.shape
    own = update_ref.shape[1]
    peers = plane()
    me = peers[0]
    piece = column_piece(count, own)
    slots = (early, direct, late, stage)
    fetches = [
        own_slice(source, target, local_sem.at[i], own)
        for i, (source, target) in enumerate(((n_ref, n_own), (x_ref, x_own)))
    ]
    later = [
        pltpu.make_async_copy(source, target, local_sem.at[2 + i])
        for i, (source, target) in enumerate(
            (
                (normed_hbm, normed_ref),
                (gpre_hbm, gpre_ref),
                (g_hbm, g_ref),
                (act_hbm, act_ref),
            )
        )
    ]
    for fetch in fetches + later:
        fetch.start()
    hidden = gpre_ref.shape[1]

    def in_grad(rows, value):
        grad_ref[rows, :hidden] = value

    def out_grad(rows, value):
        grad_ref[rows, hidden : hidden + width] = value

    def small_grads():
        grad_ref[:, hidden + width :] = jnp.zeros((width, LANES), BF16)
        size = width // shards
        for shard in range(shards):
            lanes = slice(shard * size, (shard + 1) * size)
            block = jnp.concatenate(
                (sums_ref[0:3, lanes], bias_ref[0:1, lanes], jnp.zeros((SMALL - 4, size), F32)),
                axis=0,
            )
            grad_ref[shard * size : shard * size + SMALL, hidden + width :] = widen(block)

    greet(peers[1], peers[2])
    started = reduce_begin(part_ref, piece, peers, slots, (send, recv))
    small_grads()
    later[0].wait()
    later[1].wait()
    grad_tiles(normed_ref, gpre_ref, in_grad, 0, width // (2 * TILE))
    total = stats_total(stats_ref, got, stats_stage, peers, (send_s, recv_s), 0)
    means[...] = total.T * (1.0 / width)
    for fetch in fetches:
        fetch.wait()
    reduce_forward(part_ref, piece, peers, slots, (send, recv), started)
    later[2].wait()
    later[3].wait()
    grad_tiles(normed_ref, gpre_ref, in_grad, width // (2 * TILE), width // TILE)
    begun = []
    mine = pl.ds(pl.multiple_of(me * own, LANES), own)
    for half in range(2):
        reduce_arrived(started, half)

        def finish(start):
            here = pl.ds(half * (count // 2) + start, STRIP)
            e = reduced(part_ref, piece, me, slots, half, start) * gain_ref[2:3, :]
            n = n_own[here, :].astype(F32)
            inner = e - means[here, 0:1] - n * means[here, 1:2]
            g = g_ref[here, mine].astype(F32) + scale_ref[here, 0:1] * inner
            g = g.astype(BF16).astype(F32)
            u = sigmoid(update_ref[here, :].astype(F32))
            pre = hidden_ref[here, :].astype(F32)
            s = sigmoid(pre)
            x = x_own[here, :].astype(F32)
            gupdate_ref[here, :] = (g * (pre * s - x) * (u * (1.0 - u))).astype(BF16)
            resid_ref[here, :] = g * (1.0 - u)
            out_ref[here, mine] = (g * u * (s * (1.0 + pre * (1.0 - s)))).astype(BF16)

        strips(count // 2, finish)
        begun.append(gather_begin(out_ref, piece, peers, (send_g, recv_g), half))
    grad_tiles(act_ref, g_ref, out_grad, 0, hidden // TILE)
    store = pltpu.make_async_copy(grad_ref, grad_hbm, local_sem.at[6])
    store.start()
    gather_finish(out_ref, piece, peers, (send_g, recv_g), begun[0], begun[1])
    for copy in started:
        copy.wait_send()
    store.wait()


def back_join(
    part, stats, scale, gain, update, hidden, normed, gpre, act, g, sums, bias, n, x, shards, ident
):
    count, width = part.shape
    own = update.shape[1]
    wide = gpre.shape[1]
    return pl.pallas_call(
        functools.partial(back_join_kernel, shards),
        out_shape=(
            shape((count, width), BF16),
            shape((count, own), BF16),
            shape((count, own), F32),
            shape((width, wide + width + LANES), BF16),
        ),
        in_specs=[vmem()] * 6 + [hbm()] * 4 + [vmem()] * 2 + [hbm()] * 2,
        out_specs=(vmem(),) * 3 + (hbm(),),
        scratch_shapes=[
            pltpu.VMEM((count, width), BF16),
            pltpu.VMEM((count, wide), BF16),
            pltpu.VMEM((count, wide), BF16),
            pltpu.VMEM((count, width), BF16),
            pltpu.VMEM((width, wide + width + LANES), BF16),
        ]
        + reduce_scratch(count // 2, own)
        + [pltpu.VMEM((count, own), BF16)] * 2
        + [
            pltpu.VMEM((2, CHUNKS, count), F32),
            pltpu.VMEM((CHUNKS, count), F32),
            pltpu.VMEM((count, CHUNKS), F32),
            pltpu.SemaphoreType.DMA((7,)),
        ]
        + copy_sems(6)
        + copy_sems(6)
        + copy_sems(2),
        cost_estimate=lasting(43),
        compiler_params=comm_params(ident),
    )(part, stats, scale, gain, update, hidden, normed, gpre, act, g, sums, bias, n, x)


def reduce_two_kernel(shards, waits, *refs):
    reduce_two_work(shards, *refs[waits:])


def reduce_two_work(
    shards,
    one_ref,
    two_ref,
    normed_hbm,
    gvalue_hbm,
    mixed_hbm,
    gbase_hbm,
    gated_hbm,
    gout_hbm,
    bias_ref,
    pair_ref,
    out_one,
    out_two,
    grad_hbm,
    normed_ref,
    gvalue_ref,
    mixed_ref,
    gbase_ref,
    gated_ref,
    gout_ref,
    grad_ref,
    local_sem,
    e1,
    d1,
    l1,
    s1,
    e2,
    d2,
    l2,
    s2,
    sa,
    ra,
    sb,
    rb,
):
    count, own = out_one.shape
    width = normed_ref.shape[1]
    wide = gvalue_ref.shape[1]
    total = wide + gbase_ref.shape[1]
    block_rows = width // shards
    few = wide // shards
    peers = plane()
    me = peers[0]
    piece = column_piece(count, own)
    jobs = (
        (one_ref, out_one, (e1, d1, l1, s1), (sa, ra)),
        (two_ref, out_two, (e2, d2, l2, s2), (sb, rb)),
    )

    fetches = [
        pltpu.make_async_copy(source, target, local_sem.at[i])
        for i, (source, target) in enumerate(
            (
                (mixed_hbm, mixed_ref),
                (gbase_hbm, gbase_ref),
                (normed_hbm, normed_ref),
                (gvalue_hbm, gvalue_ref),
                (gated_hbm, gated_ref),
                (gout_hbm, gout_ref),
            )
        )
    ]
    for fetch in fetches:
        fetch.start()

    def value_grad(rows, value):
        grad_ref[rows, :wide] = value

    def base_grad(rows, value):
        grad_ref[rows, wide:total] = value

    def out_grad(rows, value):
        for i in range(TILE // few):
            start = (rows.start // few + i) * block_rows
            for half in range(2):
                here = pl.ds(pl.multiple_of(start + half * few, few), few)
                grad_ref[here, total : total + width // 2] = value[
                    i * few : (i + 1) * few, half * (width // 2) : (half + 1) * (width // 2)
                ]

    def small_grads():
        last = total + width // 2
        grad_ref[:, last:] = jnp.zeros((width, LANES), BF16)
        rows = [bias_ref[0:1, i * LANES : (i + 1) * LANES] for i in range(total // LANES)]
        block = jnp.concatenate(rows + [pair_ref[0:3, :]], axis=0).astype(BF16)
        for shard in range(shards):
            grad_ref[shard * block_rows : shard * block_rows + SMALL, last:] = block

    greet(peers[1], peers[2])
    begun = [reduce_begin(part, piece, peers, slots, sems) for part, _, slots, sems in jobs]
    small_grads()
    fetches[0].wait()
    fetches[1].wait()
    grad_tiles(mixed_ref, gbase_ref, base_grad, 0, width // TILE)
    for (part, _, slots, sems), started in zip(jobs, begun):
        reduce_forward(part, piece, peers, slots, sems, started)
    for fetch in fetches[2:]:
        fetch.wait()
    grad_tiles(normed_ref, gvalue_ref, value_grad, 0, width // TILE)
    grad_tiles(gated_ref, gout_ref, out_grad, 0, wide // TILE)
    store = pltpu.make_async_copy(grad_ref, grad_hbm, local_sem.at[6])
    store.start()
    for (part, out, slots, sems), started in zip(jobs, begun):
        for half in range(2):
            reduce_arrived(started, half)

            def finish(start):
                here = pl.ds(half * (count // 2) + start, STRIP)
                out[here, :] = reduced(part, piece, me, slots, half, start)

            strips(count // 2, finish)
        for copy in started:
            copy.wait_send()
    store.wait()


def reduce_two(
    one, two, normed, gvalue, mixed, gbase, gated, gout, bias, pair, own, shards, ident, after=()
):
    count, width = one.shape
    columns = gvalue.shape[1] + gbase.shape[1] + width // 2 + LANES
    return pl.pallas_call(
        functools.partial(reduce_two_kernel, shards, len(after)),
        out_shape=(shape((count, own), F32),) * 2 + (shape((width, columns), BF16),),
        in_specs=[hbm()] * len(after) + [vmem()] * 2 + [hbm()] * 6 + [vmem()] * 2,
        out_specs=(vmem(),) * 2 + (hbm(),),
        scratch_shapes=[
            pltpu.VMEM(a.shape, BF16) for a in (normed, gvalue, mixed, gbase, gated, gout)
        ]
        + [pltpu.VMEM((width, columns), BF16), pltpu.SemaphoreType.DMA((7,))]
        + reduce_scratch(count // 2, own) * 2
        + copy_sems(6)
        + copy_sems(6),
        cost_estimate=lasting(36),
        compiler_params=comm_params(ident),
    )(*after, one, two, normed, gvalue, mixed, gbase, gated, gout, bias, pair)


def block_piece(whole):
    def piece(owner, half):
        size = whole.shape[1] // 2
        return owner, pl.ds(half * size, size), slice(None)

    return piece


def final_kernel(number, z_ref, stats_ref, x_ref, *refs):
    blocks, refs = refs[:number], refs[number:]
    out_ref, refs = refs[0], refs[1:]
    gathered, refs = refs[:number], refs[number:]
    land, x_own, got, stats_stage, total_buf, local_sem, send, recv = refs[:8]
    block_sems = [refs[8 + 2 * i : 10 + 2 * i] for i in range(number)]
    count, own = z_ref.shape
    quarter, width = out_ref.shape
    peers = plane()
    me = peers[0]

    def rows(owner):
        return pl.ds(pl.multiple_of(owner * quarter, quarter), quarter)

    mine = pl.ds(pl.multiple_of(me * own, LANES), own)
    fetch = pltpu.make_async_copy(x_ref.at[rows(me), :], x_own, local_sem)
    fetch.start()
    land[:, mine] = z_ref[rows(me), :]
    for block, whole in zip(blocks, gathered):
        whole[me] = block[...]
    greet(*peers[1:])
    sems = (send, recv)
    copies = []
    for index, other in enumerate(peers[1:]):
        copies.append(link(z_ref.at[rows(other), :], land.at[:, mine], sems, 2 + index, other))
        copies[-1].start()
    total_buf[...] = stats_total(stats_ref, got, stats_stage, peers, sems, 0)
    begun = [
        [gather_begin(whole, block_piece(whole), peers, k, half) for half in range(2)]
        for whole, k in zip(gathered, block_sems)
    ]
    part = total_buf[:, pl.ds(pl.multiple_of(me * quarter, LANES), quarter)]
    means = part.T * (1.0 / width)
    fetch.wait()
    for copy in copies:
        copy.wait_recv()
    n, scale = normalise(x_own[...].astype(F32))
    g = land[...].astype(F32) - scale * (means[:, 0:1] + n * means[:, 1:2])
    out_ref[...] = g.astype(BF16)
    passed = [
        gather_forward(whole, block_piece(whole), peers, k, zero, one)
        for whole, k, (zero, one) in zip(gathered, block_sems, begun)
    ]
    for whole, k, (zero, one), two in zip(gathered, block_sems, begun, passed):
        gather_finish(whole, block_piece(whole), peers, k, zero, one, two)
    for copy in copies:
        copy.wait_send()


def final_exchange(z, stats, x, blocks, sections, ident):
    count, own = z.shape
    width = x.shape[1]
    quarter = count // 4
    number = len(blocks)
    return pl.pallas_call(
        functools.partial(final_kernel, number),
        out_shape=(shape((quarter, width), BF16),)
        + tuple(shape((sections,) + a.shape, BF16) for a in blocks),
        in_specs=[vmem(), vmem(), hbm()] + [vmem()] * number,
        out_specs=(vmem(),) * (1 + number),
        scratch_shapes=[
            pltpu.VMEM((quarter, width), BF16),
            pltpu.VMEM((quarter, width), BF16),
            pltpu.VMEM((2,) + stats.shape, F32),
            pltpu.VMEM(stats.shape, F32),
            pltpu.VMEM(stats.shape, F32),
            pltpu.SemaphoreType.DMA,
        ]
        + copy_sems(5)
        + copy_sems(6) * number,
        cost_estimate=lasting(10 + 20 * number),
        compiler_params=comm_params(ident),
    )(z, stats, x, *blocks)


def sums_kernel(shards, holders, sums_ref, block_ref, channels_ref, whole_ref, *refs):
    sums_land, send_s, recv_s, send_c, recv_c, send, recv = refs
    peers = plane()
    me = peers[0]
    slot = lax.axis_index("dp")
    holding = slot // holders == me
    whole_ref[me] = block_ref[...]
    barrier = pltpu.get_barrier_semaphore()
    for other in peers[1:]:
        pl.semaphore_signal(barrier, inc=1, device_id={"section": other}, device_id_type=MESH)
    for step in range(1, shards):
        other = (slot + step) % shards
        pl.semaphore_signal(barrier, inc=1, device_id={"dp": other}, device_id_type=MESH)
    pl.semaphore_wait(barrier, shards + 2)

    def sums_copy(target, index, place):
        return pltpu.make_async_remote_copy(
            src_ref=sums_ref,
            dst_ref=sums_land.at[place],
            send_sem=send_s.at[index],
            recv_sem=recv_s.at[place],
            device_id={"dp": target},
            device_id_type=MESH,
        )

    def sums_out(index):
        target = me * holders + index
        place = jnp.maximum((slot - target + shards) % shards - 1, 0)
        return target, sums_copy(target, index, place)

    for index in range(holders):
        target, copy = sums_out(index)

        @pl.when(target != slot)
        def _():
            copy.start()

    piece = block_piece(whole_ref)
    zero, one = (gather_begin(whole_ref, piece, peers, (send, recv), half) for half in range(2))
    passed = gather_forward(whole_ref, piece, peers, (send, recv), zero, one)

    def channels_copy(other, index):
        return link(channels_ref, channels_ref, (send_c, recv_c), index, other)

    @pl.when(holding)
    def _():
        summed = sums_ref[...]
        for step in range(1, shards):
            sums_copy((slot + step) % shards, 0, step - 1).wait_recv()
            summed = summed + sums_land[step - 1]
        channels_ref[...] = summed
        for index, other in enumerate(peers[1:]):
            channels_copy(other, index).start()

    gather_finish(whole_ref, piece, peers, (send, recv), zero, one, passed)

    for index, other in enumerate(peers[1:]):

        @pl.when(slot // holders == other)
        def _():
            channels_copy(other, index).wait_recv()

    @pl.when(holding)
    def _():
        for index, other in enumerate(peers[1:]):
            channels_copy(other, index).wait_send()

    for index in range(holders):
        target, copy = sums_out(index)

        @pl.when(target != slot)
        def _():
            copy.wait_send()


def gather_sums(sums, block, sections, shards, holders, ident):
    return pl.pallas_call(
        functools.partial(sums_kernel, shards, holders),
        out_shape=(shape(sums.shape, F32), shape((sections,) + block.shape, BF16)),
        in_specs=[vmem()] * 2,
        out_specs=(vmem(),) * 2,
        scratch_shapes=[pltpu.VMEM((shards - 1,) + sums.shape, F32)]
        + copy_sems(max(shards - 1, holders))
        + copy_sems(3)
        + copy_sems(6),
        cost_estimate=lasting(25),
        compiler_params=comm_params(ident),
    )(sums, block)


def assemble_kernel(layers, shards, *refs):
    gathered = refs[: 2 * layers]
    value_ref, base_ref, out_ref, feed_in_ref, feed_out_ref, small_ref, feed_small_ref = refs[
        2 * layers :
    ]
    sections = gathered[0].shape[0]
    width = out_ref.shape[2]
    wide = value_ref.shape[2] // sections
    hidden = feed_in_ref.shape[2] // sections
    own = width // sections
    keyed = base_ref.shape[2] - 2 * width - wide * sections
    edge = wide + own
    total = edge + keyed + wide + own
    few = wide // shards

    def woven(part, here, low, size):
        step = size // shards
        return jnp.concatenate(
            [
                part[k, here, low + d * step : low + (d + 1) * step].astype(F32)
                for d in range(shards)
                for k in range(sections)
            ],
            axis=1,
        )

    def joined(part, here, low, size):
        return jnp.concatenate(
            [part[k, here, low : low + size].astype(F32) for k in range(sections)], axis=1
        )

    def emit(part, feed):
        def strip(i, carry):
            here = pl.ds(pl.multiple_of(i * SMALL, SMALL), SMALL)
            value_ref[0, here, :] = woven(part, here, 0, wide)
            base_ref[0, here, :width] = joined(part, here, wide, own)
            shared = part[0, here, edge : edge + keyed].astype(F32)
            for k in range(1, sections):
                shared += part[k, here, edge : edge + keyed].astype(F32)
            low = width
            base_ref[0, here, low : low + keyed] = shared
            low += keyed
            base_ref[0, here, low : low + wide * sections] = woven(part, here, edge + keyed, wide)
            low += wide * sections
            base_ref[0, here, low:] = joined(part, here, edge + keyed + wide, own)
            feed_in_ref[0, here, :] = woven(feed, here, 0, hidden)
            return carry

        lax.fori_loop(0, value_ref.shape[1] // SMALL, strip, 0)
        rows = feed.shape[1]
        for k in range(sections):
            feed_out_ref[0, k * rows : (k + 1) * rows, :] = feed[
                k, :, hidden : hidden + width
            ].astype(F32)
            for half in range(2):
                out_ref[
                    0, k * few : (k + 1) * few, half * (width // 2) : (half + 1) * (width // 2)
                ] = part[k, half * few : (half + 1) * few, total : total + width // 2].astype(F32)
            small_ref[0, k] = part[k, :SMALL, total + width // 2 :].astype(F32)
            feed_small_ref[0, k] = feed[k, :SMALL, hidden + width :].astype(F32)

    for layer in range(layers):

        @pl.when(pl.program_id(0) == layer)
        def _():
            emit(gathered[2 * layer], gathered[2 * layer + 1])


def assemble(gathered, shards, width, wide, base, hidden):
    layers = len(gathered)
    flat = [array for pair in gathered for array in pair]
    sections, rows, _ = flat[0].shape
    dims = (
        (rows, wide),
        (rows, base),
        (wide // shards, width),
        (rows, hidden),
        (hidden // shards, width),
        (sections, SMALL, LANES),
        (sections, SMALL, LANES),
    )
    return pl.pallas_call(
        functools.partial(assemble_kernel, layers, shards),
        grid=(layers,),
        out_shape=tuple(shape((layers,) + d, F32) for d in dims),
        in_specs=[pl.BlockSpec(a.shape, lambda i: (0, 0, 0)) for a in flat],
        out_specs=tuple(
            pl.BlockSpec((1,) + d, lambda i, n=len(d): (i,) + (0,) * n) for d in dims
        ),
        cost_estimate=lasting(9),
        compiler_params=params(),
    )(*flat)


def chosen(pieces):
    section = lax.axis_index("section")
    result = pieces[0]
    for k in range(1, len(pieces)):
        result = jnp.where(section == k, pieces[k], result)
    return result


def pick(ref, index, low, size, shards, sections):
    step = size // (shards * sections)
    parts = []
    for shard in range(shards):
        start = low + shard * sections * step
        parts.append(
            chosen([ref[index + (slice(start + k * step, start + (k + 1) * step),)] for k in range(sections)])
        )
    return jnp.concatenate(parts, axis=-1)


def pack_attention_kernel(shards, sections, value_ref, base_ref, out_ref, packed_ref):
    rows, wide_all = value_ref.shape[1:]
    few_all, width = out_ref.shape[1:]
    wide, own, few = wide_all // sections, width // sections, few_all // sections
    keyed = base_ref.shape[2] - 2 * width - wide_all
    section = lax.axis_index("section")
    low = wide + own + keyed

    def strip(i, carry):
        here = pl.ds(pl.multiple_of(i * SMALL, SMALL), SMALL)

        def base(start, size):
            return base_ref[0, here, pl.ds(pl.multiple_of(start, LANES), size)]

        packed_ref[here, :wide] = pick(value_ref, (0, here), 0, wide_all, shards, sections)
        packed_ref[here, wide : wide + own] = base(section * own, own)
        packed_ref[here, wide + own : low] = base(width, keyed)
        packed_ref[here, low : low + wide] = pick(
            base_ref, (0, here), width + keyed, wide_all, shards, sections
        )
        packed_ref[here, low + wide : low + wide + own] = base(
            width + keyed + wide_all + section * own, own
        )
        return carry

    lax.fori_loop(0, rows // SMALL, strip, 0)
    low += wide + own
    mine = pl.ds(pl.multiple_of(section * few, few), few)
    for half in range(2):
        packed_ref[half * few : (half + 1) * few, low:] = out_ref[
            0, mine, half * (width // 2) : (half + 1) * (width // 2)
        ]


def pack_feed_kernel(shards, sections, in_ref, out_ref, packed_ref):
    rows, hidden_all = in_ref.shape[1:]
    hidden = hidden_all // sections
    size = out_ref.shape[1] // sections

    def strip(i, carry):
        here = pl.ds(pl.multiple_of(i * SMALL, SMALL), SMALL)
        packed_ref[here, :hidden] = pick(in_ref, (0, here), 0, hidden_all, shards, sections)
        return carry

    lax.fori_loop(0, rows // SMALL, strip, 0)
    start = pl.multiple_of(lax.axis_index("section") * size, size)
    packed_ref[:, hidden:] = out_ref[0, pl.ds(start, size), :]


def pack(kernel, layer, columns, shards, sections, *arrays):
    rows = arrays[0].shape[1]
    return pl.pallas_call(
        functools.partial(kernel, shards, sections),
        grid=(1,),
        out_shape=shape((rows, columns), BF16),
        in_specs=[pl.BlockSpec((1,) + a.shape[1:], lambda i: (layer, 0, 0)) for a in arrays],
        out_specs=pl.BlockSpec((rows, columns), lambda i: (0, 0)),
        cost_estimate=lasting(3),
        compiler_params=params(),
    )(*arrays)


def unpack_kernel(layers, shards, sections, places, everyone_ref, *refs):
    base_buf = refs[-1]
    section = lax.axis_index("section")
    outs = 14
    for layer in range(layers):
        (
            gain_ref,
            shift_ref,
            feed_gain_ref,
            feed_shift_ref,
            feed_out_ref,
            own_ref,
            rate_ref,
            coef_ref,
            bias_ref,
            feed_in_ref,
            pair_ref,
            offset_ref,
            skip_ref,
            own_out_ref,
        ) = refs[layer * outs : (layer + 1) * outs]
        width = gain_ref.shape[1]
        own = width // sections
        mine = pl.ds(pl.multiple_of(section * own, LANES), own)
        row = slice(layer, layer + 1)

        def joined(low, size):
            return jnp.concatenate(
                [everyone_ref[d, row, low : low + size] for d in range(shards)], axis=1
            )

        def share(low, size):
            step = size // sections
            return jnp.concatenate(
                [
                    chosen(
                        [
                            everyone_ref[d, row, low + k * step : low + (k + 1) * step]
                            for k in range(sections)
                        ]
                    )
                    for d in range(shards)
                ],
                axis=1,
            )

        def channels(low):
            size = width // shards
            count = own // size
            return jnp.concatenate(
                [everyone_ref[section * count + d, row, low : low + size] for d in range(count)],
                axis=1,
            )

        size = width // shards
        gain_ref[...] = joined(places["norm_gain"], size)
        shift_ref[...] = joined(places["norm_shift"], size)
        feed_gain_ref[...] = joined(places["feed_gain"], size)
        feed_shift_ref[...] = joined(places["feed_shift"], size)
        feed_out_ref[...] = joined(places["feed_out_bias"], size)
        own_ref[0:1, :] = gain_ref[:, mine]
        own_ref[1:2, :] = shift_ref[:, mine]
        own_ref[2:3, :] = feed_gain_ref[:, mine]
        own_ref[3:8, :] = jnp.zeros((5, own), F32)
        own_out_ref[...] = feed_out_ref[:, mine]
        skip_ref[...] = channels(places["average_skip"])
        for n in range(rate_ref.shape[0]):
            rate = sigmoid(channels(places["average_decay"] + n * size))
            drive = (1.0 - rate) * channels(places["average_input"] + n * size)
            coef = drive * channels(places["average_output"] + n * size)
            rate_ref[n] = jnp.broadcast_to(rate, (CHUNKS, own))
            coef_ref[n] = jnp.broadcast_to(coef, (CHUNKS, own))
        keyed = offset_ref.shape[1]
        step = keyed // shards
        for r in range(2):
            pair_ref[r : r + 1, :] = joined(places["pair_scale"] + r * step, step)
        offset_ref[...] = joined(places["query_shift"], step)
        feed_in_ref[...] = share(
            places["feed_in_bias"], feed_in_ref.shape[1] * sections // shards
        )
        total = bias_ref.shape[1]
        wide = (total - keyed - 2 * own) // 2
        base_all = 2 * width + keyed + wide * sections
        base_buf[...] = joined(places["base_bias"], base_all // shards)
        low = wide + own + keyed
        bias_ref[:, :wide] = share(places["value_bias"], wide * sections // shards)
        bias_ref[:, wide : wide + own] = base_buf[:, mine]
        bias_ref[:, wide + own : low] = base_buf[:, width : width + keyed]
        bias_ref[:, low : low + wide] = pick(
            base_buf, (slice(None),), width + keyed, wide * sections, shards, sections
        )
        start = pl.multiple_of(width + keyed + wide * sections + section * own, LANES)
        bias_ref[:, low + wide :] = base_buf[:, pl.ds(start, own)]


def unpack(everyone, places, sizes, sections):
    shards, layers = everyone.shape[:2]
    width, dims, total, hidden, keyed, base = sizes
    own = width // sections
    one_layer = (
        [shape((1, width), F32)] * 5
        + [shape((8, own), F32)]
        + [shape((dims, CHUNKS, own), F32)] * 2
        + [
            shape((1, total), F32),
            shape((1, hidden), F32),
            shape((2, keyed), F32),
            shape((1, keyed), F32),
            shape((1, own), F32),
            shape((1, own), F32),
        ]
    )
    outs = pl.pallas_call(
        functools.partial(unpack_kernel, layers, shards, sections, places),
        out_shape=tuple(one_layer * layers),
        in_specs=[vmem()],
        out_specs=(vmem(),) * (len(one_layer) * layers),
        scratch_shapes=[pltpu.VMEM((1, base), F32)],
        cost_estimate=lasting(3),
        compiler_params=params(),
    )(everyone)
    names = (
        "gain",
        "shift",
        "feed_gain",
        "feed_shift",
        "feed_out",
        "own",
        "rate",
        "coef",
        "bias",
        "feed_in",
        "pair",
        "offset",
        "skip",
        "own_out",
    )
    count = len(one_layer)
    return [dict(zip(names, outs[k * count : (k + 1) * count])) for k in range(layers)]


def body(
    tokens,
    lengths,
    cotangent,
    norm_gain,
    norm_shift,
    average_decay,
    average_input,
    average_output,
    average_skip,
    value_weight,
    value_bias,
    base_weight,
    base_bias,
    pair_scale,
    query_shift,
    out_weight,
    feed_gain,
    feed_shift,
    feed_in_weight,
    feed_in_bias,
    feed_out_weight,
    feed_out_bias,
):
    sections = lax.axis_size("section")
    shards = lax.axis_size("dp")
    section = lax.axis_index("section")
    _, count, width = tokens.shape
    layers = norm_gain.shape[0]
    own = width // sections
    wide = value_weight.shape[2]
    keyed = pair_scale.shape[2] * shards
    hidden = feed_in_weight.shape[2]

    share = wide // sections
    total = share + own + keyed + share + own

    def over_dp(array):
        return lax.all_gather(array, "dp", axis=0, tiled=True)

    weights = []
    for layer in range(layers):
        attention = pack(
            pack_attention_kernel,
            layer,
            total + width // 2,
            shards,
            sections,
            value_weight,
            base_weight,
            out_weight,
        )
        feed = pack(
            pack_feed_kernel,
            layer,
            hidden // sections + width,
            shards,
            sections,
            feed_in_weight,
            feed_out_weight,
        )
        weights.append((over_dp(attention), over_dp(feed)))

    smalls = dict(
        norm_gain=norm_gain,
        norm_shift=norm_shift,
        average_decay=average_decay,
        average_input=average_input,
        average_output=average_output,
        average_skip=average_skip,
        feed_gain=feed_gain,
        feed_shift=feed_shift,
        feed_out_bias=feed_out_bias,
        value_bias=value_bias,
        feed_in_bias=feed_in_bias,
        base_bias=base_bias,
        pair_scale=pair_scale,
        query_shift=query_shift,
    )
    packed = jnp.concatenate([a.reshape(layers, -1) for a in smalls.values()], axis=1)
    places = {}
    low = 0
    for name, array in smalls.items():
        places[name] = low
        low += array.size // layers
    dims = average_decay.shape[1]
    small = unpack(
        lax.all_gather(packed, "dp", axis=0),
        places,
        (width, dims, total, hidden // sections, keyed, base_weight.shape[2]),
        sections,
    )

    idents = iter(range(64))
    x0 = x = tokens[0]
    kept = []
    for layer in range(layers):
        attention_w, feed_w = weights[layer]
        p = small[layer]
        normed, mixed_own, pre, own_n, scale = average_forward(
            lengths, x, p["gain"], p["shift"], p["rate"], p["coef"], p["skip"]
        )
        mixed = gather_columns(mixed_own, sections, next(idents))
        part, update, shared, reset, cand, value, att, gated, probs = attention_forward(
            lengths, normed, mixed, attention_w, p["bias"], p["pair"], p["offset"], own, shards
        )
        middle, hidden_pre = attention_join(part, update, cand, x, next(idents))
        feed_part, feed_pre, feed_n, feed_normed, feed_scale = feed_forward(
            middle, p["feed_gain"], p["feed_shift"], feed_w, p["feed_in"]
        )
        kept.append(
            dict(
                x=x,
                normed=normed,
                mixed=mixed,
                pre=pre,
                own_n=own_n,
                scale=scale,
                update=update,
                saved=(shared, reset, value, att, probs),
                gated=gated,
                hidden=hidden_pre,
                feed_pre=feed_pre,
                feed_n=feed_n,
                feed_normed=feed_normed,
                feed_scale=feed_scale,
            )
        )
        if layer + 1 < layers:
            x = feed_join(feed_part, p["own_out"], middle, next(idents))
        else:
            block_out = feed_last(feed_part, p["feed_out"], middle, next(idents))

    def scattered(grad):
        return lax.psum_scatter(grad, "dp", scatter_dimension=0, tiled=True)

    def over_sections(array):
        return lax.all_gather(array, "section", axis=0)

    given = cotangent[0]
    feed_grads = [None] * layers
    attention_grads = [None] * layers
    channel_sums = [None] * layers
    feed_one = None
    for layer in reversed(range(layers)):
        attention_w, feed_w = weights[layer]
        k, p = kept[layer], small[layer]
        own_rows = p["own"]
        done = feed_backward(
            given,
            k["feed_pre"],
            k["feed_n"],
            p["feed_gain"],
            feed_w,
            () if layer else (feed_one,),
        )
        part, stats, gpre, act, feed_sums, feed_bias = done[:6]
        g = done[6] if isinstance(given, tuple) else given
        gout, gupdate, resid, feed_grad = back_join(
            part,
            stats,
            k["feed_scale"],
            own_rows,
            k["update"],
            k["hidden"],
            k["feed_normed"],
            gpre,
            act,
            g,
            feed_sums,
            feed_bias,
            k["feed_n"],
            k["x"],
            shards,
            next(idents),
        )
        feed_grads[layer] = scattered(feed_grad)
        gmixed_part, gvalue_part, gbase, gvalue, bias_sums, pair_sums = attention_backward(
            lengths,
            gout,
            gupdate,
            k["saved"],
            attention_w,
            p["pair"],
            p["offset"],
            shards,
            () if layer else (attention_grads[1],),
        )
        gmixed, gnormed, attention_grad = reduce_two(
            gmixed_part,
            gvalue_part,
            k["normed"],
            gvalue,
            k["mixed"],
            gbase,
            k["gated"],
            gout,
            bias_sums,
            pair_sums,
            own,
            shards,
            next(idents),
        )
        attention_grads[layer] = scattered(attention_grad)
        if layer:
            held, gmixed = lax.optimization_barrier((feed_grads[layer], gmixed))
            feed_one = over_sections(held)
        z, zstats, channel_sums[layer] = average_backward(
            lengths,
            gmixed,
            gnormed,
            k["pre"],
            k["own_n"],
            k["scale"],
            resid,
            own_rows,
            p["rate"],
            p["coef"],
            p["skip"],
            () if layer else (feed_grads[0],),
        )
        if layer:
            whole_z, means = gather_stats(z, zstats, sections, next(idents))
            given = (whole_z, means, k["x"])

    input_grad, attention_one, feed_zero = final_exchange(
        z, zstats, x0, [attention_grads[1], feed_grads[0]], sections, next(idents)
    )
    channels, attention_zero = gather_sums(
        jnp.concatenate(channel_sums, axis=0),
        attention_grads[0],
        sections,
        shards,
        own * shards // width,
        next(idents),
    )
    shard = lax.axis_index("dp")
    size = width // shards
    rows = channels.shape[0]
    channels = lax.dynamic_slice_in_dim(channels, shard * size % own, size, axis=1)
    channels = channels.reshape(layers, rows // layers, size)
    g_value, g_base, g_out, g_feed_in, g_feed_out, smalls_out, feed_smalls = assemble(
        ((attention_zero, feed_zero), (attention_one, feed_one)),
        shards,
        width,
        wide,
        base_weight.shape[2],
        hidden,
    )

    def of_shard(array):
        part = array.shape[-1] // shards
        return lax.dynamic_slice_in_dim(array, shard * part, part, axis=array.ndim - 1)

    def woven(array):
        split = array.reshape(layers, sections, shards, -1)
        return split.transpose(0, 2, 1, 3).reshape(layers, -1)

    of_states, of_slopes, sums = channels[:, :dims], channels[:, dims : 2 * dims], channels[:, 2 * dims :]
    rate = jax.nn.sigmoid(average_decay)
    gdrive = average_output * of_states
    drive = (1.0 - rate) * average_input
    grate = drive * average_output * of_slopes - average_input * gdrive
    g_gain, g_shift, g_skip = sums[:, 0], sums[:, 1], sums[:, 2]
    g_decay, g_input, g_output = grate * rate * (1.0 - rate), (1.0 - rate) * gdrive, drive * of_states

    edge = share + own
    bias_rows = total // LANES
    bias = smalls_out[:, :, :bias_rows].reshape(layers, sections, total)
    pairs = of_shard(jnp.sum(smalls_out[:, :, bias_rows : bias_rows + 3], axis=1))
    g_pair, g_query = pairs[:, :2], pairs[:, 2]
    g_value_bias = of_shard(woven(bias[..., :share]))
    g_base_bias = of_shard(
        jnp.concatenate(
            (
                bias[..., share:edge].reshape(layers, -1),
                jnp.sum(bias[..., edge : edge + keyed], axis=1),
                woven(bias[..., edge + keyed : edge + keyed + share]),
                bias[..., edge + keyed + share :].reshape(layers, -1),
            ),
            axis=1,
        )
    )
    g_feed_gain = jnp.sum(feed_smalls[:, :, 0, :size], axis=1)
    g_feed_shift = jnp.sum(feed_smalls[:, :, 1, :size], axis=1)
    g_feed_out_bias = feed_smalls[:, 0, 2, :size]
    g_feed_in_bias = feed_smalls[:, :, 3, :size].reshape(layers, -1)
    return (
        block_out[None],
        input_grad[None],
        g_gain,
        g_shift,
        g_decay,
        g_input,
        g_output,
        g_skip,
        g_value,
        g_value_bias,
        g_base,
        g_base_bias,
        g_pair,
        g_query,
        g_out,
        g_feed_gain,
        g_feed_shift,
        g_feed_in,
        g_feed_in_bias,
        g_feed_out,
        g_feed_out_bias,
    )


def solution(mesh):
    row, row2 = P(None, "dp"), P(None, "dp", None)
    deep = P(None, None, "dp")
    in_specs = (
        P("dp", None, None),
        P("dp"),
        P("dp", None, None),
        row,
        row,
        deep,
        deep,
        deep,
        row,
        row2,
        row,
        row2,
        row,
        deep,
        row,
        row2,
        row,
        row,
        row2,
        row,
        row2,
        row,
    )
    out_specs = (
        P("dp", "section", None),
        P("dp", "section", None),
        row,
        row,
        deep,
        deep,
        deep,
        row,
        row2,
        row,
        row2,
        row,
        deep,
        row,
        row2,
        row,
        row,
        row2,
        row,
        row2,
        row,
    )
    return jax.shard_map(body, mesh=mesh, in_specs=in_specs, out_specs=out_specs, check_vma=False)
```

```python
import functools
import types

import jax
import jax.numpy as jnp
from jax import lax
from jax.experimental import pallas as pl
from jax.experimental.pallas import tpu as pltpu
from jax.sharding import PartitionSpec as P

F32 = jnp.float32
BF16 = jnp.bfloat16
MESH = pl.DeviceIdType.MESH
ATT = 128
LANES = 128
CHUNKS = 8
ROWS = 256
STRIP = 64
TILE = 128
LOCAL = "local"
UNROLL = 16
SMALL = 16
SMEM, VMEM, RAW, FETCH, BLOCKS, LATE, OWN_PART, STORE = range(8)
EPS = 1e-05
NEGATIVE = -1000000000.0
VMEM_BYTES = 56 * 1024 * 1024


def vmem():
    return pl.BlockSpec(memory_space=pltpu.VMEM)


def smem():
    return pl.BlockSpec(memory_space=pltpu.SMEM)


def hbm():
    return pl.BlockSpec(memory_space=pl.ANY)


def shape(dims, kind):
    return jax.ShapeDtypeStruct(dims, kind)


def sigmoid(v):
    return 0.5 * jnp.tanh(0.5 * v) + 0.5


def silu(v):
    return v * sigmoid(v)


def silu_slope(v):
    s = sigmoid(v)
    return s * (1.0 + v * (1.0 - s))


def dot(left, right, left_dim=1, right_dim=0):
    return lax.dot_general(
        left, right, (((left_dim,), (right_dim,)), ((), ())), preferred_element_type=F32
    )


def normalise(x):
    centred = x - jnp.mean(x, axis=-1, keepdims=True)
    spread = jnp.mean(centred * centred, axis=-1, keepdims=True)
    scale = lax.rsqrt(spread + EPS)
    return centred * scale, scale


def row_valid(start, rows, length):
    place = start + lax.broadcasted_iota(jnp.int32, (rows, 1), 0)
    return (place < length).astype(F32)


def lasting(microseconds):
    return pl.CostEstimate(
        flops=int(microseconds * 1.0e9),
        bytes_accessed=int(microseconds * 3.0e6),
        transcendentals=0,
    )


def params(**more):
    return pltpu.CompilerParams(vmem_limit_bytes=VMEM_BYTES, **more)


def power(base, exponent):
    result = None
    square = base
    while exponent:
        if exponent % 2:
            result = square if result is None else result * square
        exponent //= 2
        if exponent:
            square = square * square
    return result


def shifted(array, span, reverse=False):
    row = lax.broadcasted_iota(jnp.int32, array.shape, 1)
    if reverse:
        return jnp.where(row < CHUNKS - span, pltpu.roll(array, CHUNKS - span, 1), 0.0)
    return jnp.where(row >= span, pltpu.roll(array, span, 1), 0.0)


def entering(last, rate, steps, reverse=False):
    weight = power(rate, steps)
    span = 1
    while span < CHUNKS:
        last = last + weight * shifted(last, span, reverse)
        weight = weight * weight
        span *= 2
    return shifted(last, 1, reverse)


def entering_pair(last, slope, rate, steps):
    weight = power(rate, steps)
    tilt = float(steps) * power(rate, steps - 1)
    span = 1
    while span < CHUNKS:
        moved = shifted(last, span)
        slope = slope + weight * shifted(slope, span) + tilt * moved
        last = last + weight * moved
        tilt = 2.0 * weight * tilt
        weight = weight * weight
        span *= 2
    return shifted(last, 1), shifted(slope, 1)


def average_forward_kernel(
    length_ref,
    x_ref,
    gain_ref,
    shift_ref,
    rate_ref,
    coef_ref,
    skip_ref,
    normed_ref,
    mixed_ref,
    pre_ref,
    own_ref,
    scale_ref,
    rows_buf,
    m_buf,
    y_buf,
):
    length = length_ref[0]
    count, width = x_ref.shape
    own = mixed_ref.shape[1]
    dims = rate_ref.shape[0]
    steps = count // CHUNKS
    pitch = steps + 1
    mine = pl.ds(pl.multiple_of(lax.axis_index("section") * own, LANES), own)

    def norm_strip(i, carry):
        start = pl.multiple_of(i * STRIP, STRIP)
        here = pl.ds(start, STRIP)
        n, scale = normalise(x_ref[here, :].astype(F32))
        rows_buf[...] = n
        normed_ref[here, :] = (n * gain_ref[...] + shift_ref[...]).astype(BF16)
        part = rows_buf[:, mine]
        own_ref[here, :] = part
        scale_ref[here, :] = jnp.broadcast_to(scale, (STRIP, LANES))
        masked = (part * gain_ref[:, mine] + shift_ref[:, mine]) * row_valid(start, STRIP, length)
        for group in range(own // LANES):
            m_buf[group, pl.ds(start + start // steps, STRIP), :] = masked[:, group * LANES : (group + 1) * LANES]
        return carry

    lax.fori_loop(0, count // STRIP, norm_strip, 0)

    for group in range(own // LANES):
        lanes = slice(group * LANES, (group + 1) * LANES)
        rates = rate_ref[:, :, lanes]
        coefs = coef_ref[:, :, lanes]
        m_part, y_part = m_buf.at[group], y_buf.at[group]

        def finals(t, states):
            return rates * states + m_part[pl.ds(t, CHUNKS, stride=pitch), :]

        ends = lax.fori_loop(0, steps, finals, jnp.zeros_like(rates), unroll=UNROLL)

        def outputs(t, states):
            states = rates * states + m_part[pl.ds(t, CHUNKS, stride=pitch), :]
            y_part[pl.ds(t, CHUNKS, stride=pitch), :] = jnp.sum(coefs * states, axis=0)
            return states

        lax.fori_loop(0, steps, outputs, entering(ends, rates, steps), unroll=UNROLL)

    def mix_strip(i, carry):
        start = pl.multiple_of(i * STRIP, STRIP)
        here = pl.ds(start, STRIP)
        there = pl.ds(start + start // steps, STRIP)
        for group in range(own // LANES):
            lanes = slice(group * LANES, (group + 1) * LANES)
            pre = y_buf[group, there, :] + skip_ref[:, lanes] * m_buf[group, there, :]
            pre_ref[here, lanes] = pre.astype(BF16)
            mixed_ref[here, lanes] = silu(pre).astype(BF16)
        return carry

    lax.fori_loop(0, count // STRIP, mix_strip, 0)


def average_forward(length, x, gain, shift, rate, coef, skip):
    count, width = x.shape
    own = skip.shape[1]
    groups = own // LANES
    return pl.pallas_call(
        average_forward_kernel,
        out_shape=(
            shape((count, width), BF16),
            shape((count, own), BF16),
            shape((count, own), BF16),
            shape((count, own), F32),
            shape((count, LANES), F32),
        ),
        in_specs=[smem()] + [vmem()] * 6,
        out_specs=(vmem(),) * 5,
        scratch_shapes=[
            pltpu.VMEM((STRIP, width), F32),
            pltpu.VMEM((groups, count + CHUNKS, LANES), F32),
            pltpu.VMEM((groups, count + CHUNKS, LANES), F32),
        ],
        cost_estimate=lasting(13),
        compiler_params=params(),
    )(length, x, gain, shift, rate, coef, skip)


def average_backward_work(r):
    length = r.length[0]
    count, own = r.z.shape
    dims = r.rate.shape[0]
    steps = count // CHUNKS
    pitch = steps + 1
    groups = own // LANES
    part_size = dims // 2
    gain_ref, shift_ref = r.norm.at[0:1, :], r.norm.at[1:2, :]
    peers = plane()
    sems, piece = (r.send, r.recv), block_piece(r.whole)
    r.whole[peers[0]] = r.block[...]
    greet(peers[1], peers[2])
    begun = [gather_begin(r.whole, piece, peers, sems, half) for half in range(2)]

    def load_strip(i, carry):
        start = pl.multiple_of(i * STRIP, STRIP)
        here = pl.ds(start, STRIP)
        valid = row_valid(start, STRIP, length)
        there = pl.ds(start + start // steps, STRIP)
        for group in range(groups):
            lanes = slice(group * LANES, (group + 1) * LANES)
            r.m_buf[group, there, :] = (
                r.own_n[here, lanes] * gain_ref[:, lanes] + shift_ref[:, lanes]
            ) * valid
            slope = silu_slope(r.pre[here, lanes].astype(F32))
            r.g_buf[group, there, :] = r.gmixed[here, lanes] * slope
        return carry

    lax.fori_loop(0, count // STRIP, load_strip, 0)

    passed = None
    for group in range(groups):
        lanes = slice(group * LANES, (group + 1) * LANES)
        rates = r.rate[:, :, lanes]
        coefs = r.coef[:, :, lanes]
        m_part, g_part, r_part = r.m_buf.at[group], r.g_buf.at[group], r.r_buf.at[group]
        blank = jnp.zeros_like(rates)

        def back_finals(t, carry):
            states, slopes = carry
            g = g_part[pl.ds(steps - 1 - t, CHUNKS, stride=pitch), :]
            return rates * states + g, rates * slopes + states

        ends, end_slopes = lax.fori_loop(0, steps, back_finals, (blank, blank), unroll=UNROLL)
        starts = entering(ends, rates, steps, reverse=True)

        for half in range(2):
            first = half * part_size
            some = r.rate[first : first + part_size, :, lanes]
            empty = jnp.zeros_like(some)

            def sweep(t, carry):
                states, slopes, of_states, of_slopes = carry
                x = m_part[pl.ds(t, CHUNKS, stride=pitch), :]
                g = g_part[pl.ds(t, CHUNKS, stride=pitch), :]
                slopes = some * slopes + states
                states = some * states + x
                return states, slopes, of_states + g * states, of_slopes + g * slopes

            states, slopes, of_states, of_slopes = lax.fori_loop(
                0, steps, sweep, (empty,) * 4, unroll=UNROLL
            )
            back, back_slope = ends[first : first + part_size], end_slopes[first : first + part_size]
            state, slope = entering_pair(states, slopes, some, steps)
            of_states = of_states + state * (some * back)
            of_slopes = of_slopes + slope * (some * back) + state * (back + some * back_slope)
            r.sums[first : first + part_size, lanes] = jnp.sum(of_states, axis=1)
            r.sums[dims + first : dims + first + part_size, lanes] = jnp.sum(of_slopes, axis=1)

        def back_outputs(t, states):
            here = pl.ds(steps - 1 - t, CHUNKS, stride=pitch)
            states = rates * states + g_part[here, :]
            r_part[here, :] = jnp.sum(coefs * states, axis=0)
            return states

        lax.fori_loop(0, steps, back_outputs, starts, unroll=UNROLL)
        if passed is None:
            passed = gather_forward(r.whole, piece, peers, sems, *begun)

    ones = jnp.ones((CHUNKS, own), BF16)
    first = lax.broadcasted_iota(jnp.int32, (CHUNKS, LANES), 0) == 0

    def finish(i, carry):
        start = pl.multiple_of(i * LANES, LANES)
        here = pl.ds(start, LANES)
        valid = row_valid(start, LANES, length)
        there = pl.ds(start + start // steps, LANES)
        of_gain, of_shift, of_skip = carry
        smoothed = jnp.concatenate([r.r_buf[k, there, :] for k in range(groups)], axis=1)
        gpre = jnp.concatenate([r.g_buf[k, there, :] for k in range(groups)], axis=1)
        masked = jnp.concatenate([r.m_buf[k, there, :] for k in range(groups)], axis=1)
        n = r.own_n[here, :]
        gmasked = r.skip[...] * gpre + smoothed
        gnormed = gmasked * valid + r.gvalue[here, :]
        e = gnormed * gain_ref[...]
        z = r.scale[here, 0:1] * e + r.resid[here, :]
        r.z[here, :] = z.astype(BF16)
        mean_row = dot(ones, e.astype(BF16), 1, 1)
        slope_row = dot(ones, (e * n).astype(BF16), 1, 1)
        r.stats[:, here] = jnp.where(first, mean_row, slope_row)
        return (
            of_gain + jnp.sum(gnormed * n, axis=0, keepdims=True),
            of_shift + jnp.sum(gnormed, axis=0, keepdims=True),
            of_skip + jnp.sum(gpre * masked, axis=0, keepdims=True),
        )

    blank_row = jnp.zeros((1, own), F32)
    of_gain, of_shift, of_skip = lax.fori_loop(
        0, count // LANES, finish, (blank_row, blank_row, blank_row)
    )
    last = 2 * dims
    r.sums[last : last + 1, :] = of_gain
    r.sums[last + 1 : last + 2, :] = of_shift
    r.sums[last + 2 : last + 3, :] = of_skip
    r.sums[last + 3 : last + 8, :] = jnp.zeros((5, own), F32)
    gather_finish(r.whole, piece, peers, sems, *begun, passed)


def average_backward(
    length, gmixed, gvalue, k, resid, norm, rate, coef, skip, block, ident, after=()
):
    count, own = gmixed.shape
    dims = rate.shape[0]
    buffer = pltpu.VMEM((own // LANES, count + CHUNKS, LANES), F32)
    sems = pltpu.SemaphoreType.DMA((6,))
    given = dict(
        gmixed=gmixed,
        gvalue=gvalue,
        pre=k.pre,
        own_n=k.own_n,
        scale=k.scale,
        resid=resid,
        norm=norm,
        rate=rate,
        coef=coef,
        skip=skip,
        block=block,
    )
    return transfer(
        average_backward_work,
        dict(length=(length, SMEM), **{name: (a, VMEM) for name, a in given.items()}),
        dict(
            z=(shape((count, own), BF16), VMEM),
            stats=(shape((CHUNKS, count), F32), VMEM),
            sums=(shape((2 * dims + 8, own), F32), VMEM),
            whole=(shape((4,) + block.shape, BF16), VMEM),
        ),
        dict(m_buf=buffer, g_buf=buffer, r_buf=buffer, send=sems, recv=sems),
        ident,
        17,
        after,
    )


def unfold(packed, in_w, out_w, shards, sems):
    wide, width = out_w.shape
    few = wide // shards
    low = in_w.shape[1]
    copies = [pltpu.make_async_copy(packed.at[:, pl.ds(0, low)], in_w, sems.at[0])]
    for shard in range(shards):
        for half in range(2):
            start = shard * (width // shards) + half * few
            columns = pl.ds(half * (width // 2), width // 2)
            copies.append(
                pltpu.make_async_copy(
                    packed.at[pl.ds(start, few), pl.ds(low, width // 2)],
                    out_w.at[pl.ds(shard * few, few), columns],
                    sems.at[len(copies)],
                )
            )
    return copies


def attention_forward_block(
    length,
    start,
    normed_ref,
    mixed_ref,
    in_ref,
    bias_ref,
    pair_ref,
    offset_ref,
    part_ref,
    update_ref,
    shared_ref,
    reset_ref,
    cand_ref,
    value_ref,
    att_ref,
    gated_ref,
    probs_ref,
    out_w_ref,
):
    rows = normed_ref.shape[0]
    wide = value_ref.shape[1]
    own = update_ref.shape[1]
    keyed = shared_ref.shape[1]
    value = dot(normed_ref[...], in_ref[:, :wide]) + bias_ref[:, :wide]
    value_ref[...] = value.astype(BF16)
    values = silu(value).astype(BF16)
    low = wide
    update = dot(mixed_ref[...], in_ref[:, low : low + own]) + bias_ref[:, low : low + own]
    update_ref[...] = update.astype(BF16)
    low += own
    shared = dot(mixed_ref[...], in_ref[:, low : low + keyed]) + bias_ref[:, low : low + keyed]
    shared_ref[...] = shared.astype(BF16)
    low += keyed
    reset = dot(mixed_ref[...], in_ref[:, low : low + wide]) + bias_ref[:, low : low + wide]
    reset_ref[...] = reset.astype(BF16)
    low += wide
    cand_ref[...] = (
        dot(mixed_ref[...], in_ref[:, low : low + own]) + bias_ref[:, low : low + own]
    ).astype(BF16)
    shared = silu(shared)
    reset = silu(reset)
    queries = (shared * pair_ref[0:1, :] + offset_ref[...]).astype(BF16)
    keys = (shared * pair_ref[1:2, :]).astype(BF16)
    for block in range(rows // ATT):
        here = slice(block * ATT, (block + 1) * ATT)
        begin = start + block * ATT
        scores = dot(queries[here], keys[here], 1, 1) * keyed**-0.5
        key_place = begin + lax.broadcasted_iota(jnp.int32, (ATT, ATT), 1)
        scores = jnp.where(key_place < length, scores, NEGATIVE)
        raised = jnp.exp(scores - jnp.max(scores, axis=-1, keepdims=True))
        probs = (raised / jnp.sum(raised, axis=-1, keepdims=True)).astype(BF16)
        probs_ref[here, :] = probs
        attended = dot(probs, values[here]) * row_valid(begin, ATT, length)
        att_ref[here, :] = attended.astype(BF16)
        gated_ref[here, :] = (attended * reset[here]).astype(BF16)
    part_ref[...] = dot(gated_ref[...], out_w_ref[...]).astype(BF16)


def attention_backward_block(
    length,
    start,
    mine,
    gout_ref,
    gupdate_ref,
    shared_ref,
    reset_ref,
    value_ref,
    att_ref,
    probs_ref,
    in_ref,
    pair_ref,
    offset_ref,
    gmixed_ref,
    gnormed_ref,
    gbase_ref,
    gvalue_ref,
    bias_ref,
    pair_sum_ref,
    out_w_ref,
):
    rows = gout_ref.shape[0]
    total = bias_ref.shape[1]
    wide = value_ref.shape[1]
    own = gupdate_ref.shape[1]
    keyed = shared_ref.shape[1]
    valid = row_valid(start, rows, length)
    ggated = dot(gout_ref[...], out_w_ref[...], 1, 1)
    reset = reset_ref[...].astype(F32)
    gattended = (ggated * silu(reset) * valid).astype(BF16)
    greset = ggated * att_ref[...].astype(F32) * silu_slope(reset)
    value = value_ref[...].astype(F32)
    values = silu(value).astype(BF16)
    shared_pre = shared_ref[...].astype(F32)
    shared = silu(shared_pre)
    scale_q, scale_k = pair_ref[0:1, :], pair_ref[1:2, :]
    queries = (shared * scale_q + offset_ref[...]).astype(BF16)
    keys = (shared * scale_k).astype(BF16)
    gq_parts, gk_parts, gv_parts = [], [], []
    for block in range(rows // ATT):
        here = slice(block * ATT, (block + 1) * ATT)
        probs = probs_ref[here, :]
        gprobs = dot(gattended[here], values[here], 1, 1)
        gv_parts.append(dot(probs, gattended[here], 0, 0))
        probs = probs.astype(F32)
        gscores = probs * (gprobs - jnp.sum(probs * gprobs, axis=-1, keepdims=True))
        key_place = start + block * ATT + lax.broadcasted_iota(jnp.int32, (ATT, ATT), 1)
        gscores = jnp.where(key_place < length, gscores, 0.0)
        gscores = (gscores * keyed**-0.5).astype(BF16)
        gq_parts.append(dot(gscores, keys[here]))
        gk_parts.append(dot(gscores, queries[here], 0, 0))
    gqueries = jnp.concatenate(gq_parts, axis=0)
    gkeys = jnp.concatenate(gk_parts, axis=0)
    gvalue = jnp.concatenate(gv_parts, axis=0) * silu_slope(value)
    gshared = (gqueries * scale_q + gkeys * scale_k) * silu_slope(shared_pre)
    pair_sum_ref[0:1, :] += jnp.sum(gqueries * shared, axis=0, keepdims=True)
    pair_sum_ref[1:2, :] += jnp.sum(gkeys * shared, axis=0, keepdims=True)
    pair_sum_ref[2:3, :] += jnp.sum(gqueries, axis=0, keepdims=True)
    gupdate = gupdate_ref[...]
    gcand = gout_ref[:, mine]
    low = 0
    for piece in (gvalue, gupdate, gshared, greset, gcand):
        size = piece.shape[1]
        bias_ref[0:1, low : low + size] += jnp.sum(piece.astype(F32), axis=0, keepdims=True)
        if low:
            gbase_ref[:, low - wide : low - wide + size] = piece.astype(BF16)
        else:
            gvalue_ref[...] = piece.astype(BF16)
        low += size
    gmixed_ref[...] = dot(gbase_ref[...], in_ref[:, wide:total], 1, 1).astype(BF16)
    gnormed_ref[...] = dot(gvalue_ref[...], in_ref[:, :wide], 1, 1).astype(BF16)


def feed_forward_kernel(
    x_ref, gain_ref, shift_ref, w_ref, bias_ref, part_ref, pre_ref, n_ref, normed_ref, scale_ref
):
    hidden = pre_ref.shape[1]
    n, scale = normalise(x_ref[...].astype(F32))
    n_ref[...] = n.astype(BF16)
    scale_ref[...] = jnp.broadcast_to(scale, scale_ref.shape)
    normed_ref[...] = (n * gain_ref[...] + shift_ref[...]).astype(BF16)
    pre = dot(normed_ref[...], w_ref[:, :hidden]) + bias_ref[...]
    pre_ref[...] = pre.astype(BF16)
    part_ref[...] = dot(silu(pre).astype(BF16), w_ref[:, hidden:]).astype(BF16)


def feed_backward_block(
    g_ref, pre_ref, n_ref, gain_ref, w_ref, part_ref, stats_ref, gpre_ref, act_ref, sums_ref, bias_ref, lanes
):
    hidden = pre_ref.shape[1]
    width = n_ref.shape[1]
    g = g_ref[...]
    pre = pre_ref[...].astype(F32)
    s = sigmoid(pre)
    act_ref[...] = (pre * s).astype(BF16)
    gpre = dot(g, w_ref[:, hidden:], 1, 1) * (s * (1.0 + pre * (1.0 - s)))
    bias_ref[0:1, :] += jnp.sum(gpre, axis=0, keepdims=True)
    gpre_ref[...] = gpre.astype(BF16)
    part = dot(gpre_ref[...], w_ref[:, :hidden], 1, 1)
    part_ref[...] = part.astype(BF16)
    n = n_ref[...].astype(F32)
    sums_ref[0:1, :] += jnp.sum(part * n, axis=0, keepdims=True)
    sums_ref[1:2, :] += jnp.sum(part, axis=0, keepdims=True)
    sums_ref[2:3, :] += jnp.sum(g.astype(F32), axis=0, keepdims=True)
    e = part * gain_ref[...]
    ones = jnp.ones((CHUNKS, width), BF16)
    mean_row = dot(ones, e.astype(BF16), 1, 1)
    slope_row = dot(ones, (e * n).astype(BF16), 1, 1)
    first = lax.broadcasted_iota(jnp.int32, mean_row.shape, 0) == 0
    stats_ref[:, lanes] = jnp.where(first, mean_row, slope_row)


def plane():
    me = lax.axis_index("section")
    across = me + 1 - 2 * (me % 2)
    along = me + 2 - 4 * (me // 2)
    return me, across, along, across + along - me


def greet(*others):
    barrier = pltpu.get_barrier_semaphore()
    for other in others:
        pl.semaphore_signal(barrier, inc=1, device_id={"section": other}, device_id_type=MESH)
    pl.semaphore_wait(barrier, len(others))


def link(source, target, sems, index, other):
    send, recv = sems
    return pltpu.make_async_remote_copy(
        src_ref=source,
        dst_ref=target,
        send_sem=send.at[index],
        recv_sem=recv.at[index],
        device_id={"section": other},
        device_id_type=MESH,
    )


def strips(count, work):
    def one(i, carry):
        work(pl.multiple_of(i * STRIP, STRIP))
        return carry

    lax.fori_loop(0, count // STRIP, one, 0)


def widen(block):
    rows, columns = block.shape
    if columns < LANES:
        block = jnp.concatenate((block, jnp.zeros((rows, LANES - columns), F32)), axis=1)
    return block.astype(BF16)


def grad_tiles(left, right, store, begin, end):
    def one(i, carry):
        rows = pl.ds(pl.multiple_of(i * TILE, TILE), TILE)
        store(rows, dot(left[:, rows], right[...], 0, 0).astype(BF16))
        return carry

    lax.fori_loop(begin, end, one, 0)


def gather_begin(out, piece, peers, sems, half):
    me, across, along, far = peers
    here = out.at[piece(me, half)]
    order = ((along, 0), (across, 1)) if half == 0 else ((across, 1), (along, 0))
    started = {}
    for other, way in order:
        copy = link(here, here, sems, 2 * half + way, other)
        copy.start()
        started[way] = copy
    return started


def gather_forward(out, piece, peers, sems, zero, one):
    me, across, along, far = peers
    zero[0].wait_recv()
    passing = out.at[piece(along, 0)]
    first = link(passing, passing, sems, 4, across)
    first.start()
    one[1].wait_recv()
    passing = out.at[piece(across, 1)]
    second = link(passing, passing, sems, 5, along)
    second.start()
    return first, second


def gather_finish(out, piece, peers, sems, zero, one, passed=None):
    first, second = passed or gather_forward(out, piece, peers, sems, zero, one)
    zero[1].wait_recv()
    one[0].wait_recv()
    first.wait_recv()
    second.wait_recv()
    for copy in (zero[0], zero[1], one[0], one[1], first, second):
        copy.wait_send()


def copy_sems(count):
    return [pltpu.SemaphoreType.DMA((count,)), pltpu.SemaphoreType.DMA((count,))]


def comm_params(ident):
    return params(collective_id=ident, has_side_effects=True)


def own_slice(source, target, sem, own):
    start = pl.multiple_of(lax.axis_index("section") * own, LANES)
    return pltpu.make_async_copy(source.at[:, pl.ds(start, own)], target, sem)


def stats_total(stats, got, stage, peers, sems, index):
    me, across, along, far = peers
    first = link(stats, got.at[0], sems, index, across)
    first.start()
    first.wait_recv()
    stage[...] = stats[...] + got[0]
    second = link(stage, got.at[1], sems, index + 1, along)
    second.start()
    second.wait_recv()
    first.wait_send()
    second.wait_send()
    return stage[...] + got[1]


def transfer(work, ins, outs, scratch, ident, microseconds, after=(), first=None):
    order = [n for kind in (FETCH, BLOCKS, LATE, OWN_PART) for n in ins if ins[n][1] == kind]
    stored = [n for n, (_, how) in outs.items() if how == STORE]
    buffers, places, low = {}, {}, 0
    for name in order + stored:
        if name in stored:
            buffers[name] = pltpu.VMEM(outs[name][0].shape, outs[name][0].dtype)
        else:
            array, how = ins[name]
            columns = array.shape[1] // (4 if how == OWN_PART else 1)
            buffers[name] = pltpu.VMEM((array.shape[0], columns), array.dtype)
        places[name] = low
        low += ins[name][0].shape[0] // ROWS if name in ins and ins[name][1] == BLOCKS else 1
    by_blocks = [n for n in order if ins[n][1] == BLOCKS]

    def kernel(*refs):
        refs = refs[len(after) :]
        names = list(ins) + list(outs)
        given = dict(zip(names, refs))
        refs = refs[len(names) :]
        own_names = list(buffers) + [LOCAL] + list(scratch)
        held = dict(zip(own_names, refs))
        r = types.SimpleNamespace(**{**given, **held})
        local = held[LOCAL]

        def copy(name):
            sem = local.at[places[name]]
            if name in stored:
                return pltpu.make_async_copy(held[name], given[name], sem)
            if ins[name][1] == OWN_PART:
                return own_slice(given[name], held[name], sem, held[name].shape[1])
            return pltpu.make_async_copy(given[name], held[name], sem)

        def block_copy(name, block):
            here = rows_of(block)
            source, target = given[name].at[here, :], held[name].at[here, :]
            return pltpu.make_async_copy(source, target, local.at[places[name] + block])

        def start(*kinds):
            for name in order:
                if ins[name][1] in kinds:
                    copy(name).start()

        def wait_block(block):
            for name in by_blocks:
                block_copy(name, block).wait()

        start(FETCH)
        if first:
            first(r)
        if by_blocks:
            for block in range(ins[by_blocks[0]][0].shape[0] // ROWS):
                for name in by_blocks:
                    block_copy(name, block).start()
        start(LATE, OWN_PART)
        r.wait = lambda *which: [copy(n).wait() for n in which]
        r.store = lambda *which: [copy(n).start() for n in which]
        r.wait_block = wait_block
        work(r)
        for name in stored:
            copy(name).wait()

    spec = {SMEM: smem, VMEM: vmem}
    return pl.pallas_call(
        kernel,
        out_shape=tuple(o for o, _ in outs.values()),
        in_specs=[hbm()] * len(after) + [spec.get(how, hbm)() for _, how in ins.values()],
        out_specs=tuple(spec.get(how, hbm)() for _, how in outs.values()),
        scratch_shapes=list(buffers.values())
        + [pltpu.SemaphoreType.DMA((max(low, 1),))]
        + list(scratch.values()),
        cost_estimate=lasting(microseconds),
        compiler_params=comm_params(ident),
    )(*after, *[a for a, _ in ins.values()])


def rows_of(block):
    return pl.ds(pl.multiple_of(block * ROWS, ROWS), ROWS)


def half_rows(block):
    return pl.ds(pl.multiple_of(block * (ROWS // 2), ROWS // 2), ROWS // 2)


def owned(block, owner, half, own):
    start = pl.multiple_of(block * ROWS + half * (ROWS // 2), ROWS // 2)
    return pl.ds(start, ROWS // 2), pl.ds(pl.multiple_of(owner * own, LANES), own)


def sum_scratch(name, count, own):
    buffer = pltpu.VMEM((2, count // 2, own), BF16)
    sems = pltpu.SemaphoreType.DMA((6 * (count // ROWS),))
    return {
        name + "_early": buffer,
        name + "_direct": buffer,
        name + "_late": buffer,
        name + "_stage": buffer,
        name + "_send": sems,
        name + "_recv": sems,
    }


def block_sum(r, name, part, peers, own, piece=None, place=half_rows):
    if piece is None:
        piece = functools.partial(owned, own=own)
    me, across, along, far = peers
    early, direct, late, stage, send, recv = (
        getattr(r, name + end) for end in ("_early", "_direct", "_late", "_stage", "_send", "_recv")
    )
    sems = (send, recv)
    ways = ((across, along), (along, across))

    def early_copy(block, half):
        source = part.at[piece(block, far, half)]
        target = early.at[half, place(block)]
        return link(source, target, sems, block * 6 + half, ways[half][0])

    def direct_copy(block, half):
        first = ways[half][0]
        source = part.at[piece(block, first, half)]
        target = direct.at[half, place(block)]
        return link(source, target, sems, block * 6 + 2 + half, first)

    def late_copy(block, half):
        source = stage.at[half, place(block)]
        target = late.at[half, place(block)]
        return link(source, target, sems, block * 6 + 4 + half, ways[half][1])

    def begin(block):
        for half in range(2):
            early_copy(block, half).start()
        for half in range(2):
            direct_copy(block, half).start()

    def forward(block):
        for half in range(2):
            early_copy(block, half).wait_recv()
            here = place(block)
            passed = part[piece(block, ways[half][1], half)].astype(F32)
            stage[half, here, :] = (passed + early[half, here, :].astype(F32)).astype(BF16)
            late_copy(block, half).start()

    def arrived(block, half):
        direct_copy(block, half).wait_recv()
        late_copy(block, half).wait_recv()

    def total(block, half, start):
        row, column = piece(block, me, half)
        here = pl.ds(place(block).start + start, STRIP)
        mine = part[pl.ds(row.start + start, STRIP), column].astype(F32)
        return mine + direct[half, here, :].astype(F32) + late[half, here, :].astype(F32)

    def end(block):
        for half in range(2):
            early_copy(block, half).wait_send()
            direct_copy(block, half).wait_send()
            late_copy(block, half).wait_send()

    return types.SimpleNamespace(begin=begin, forward=forward, arrived=arrived, total=total, end=end)


def gather_sems(count):
    return pltpu.SemaphoreType.DMA((6 * (count // ROWS),))


def block_gather(out, peers, own, sems):
    me, across, along, far = peers

    def copy(block, owner, half, index, other):
        place = out.at[owned(block, owner, half, own)]
        return link(place, place, sems, block * 6 + index, other)

    def own_copy(block, half, way):
        return copy(block, me, half, 2 * half + way, (along, across)[way])

    def pass_copy(block, half):
        return copy(block, (along, across)[half], half, 4 + half, (across, along)[half])

    def begin(block):
        for half, way in ((0, 0), (1, 1), (1, 0), (0, 1)):
            own_copy(block, half, way).start()

    def forward(block):
        for half in range(2):
            own_copy(block, half, half).wait_recv()
            pass_copy(block, half).start()

    def arrive(block):
        own_copy(block, 0, 1).wait_recv()
        own_copy(block, 1, 0).wait_recv()
        for half in range(2):
            pass_copy(block, half).wait_recv()

    def sent(block):
        for half in range(2):
            pass_copy(block, half).wait_send()
            for way in range(2):
                own_copy(block, half, way).wait_send()

    return types.SimpleNamespace(begin=begin, forward=forward, arrive=arrive, sent=sent)


def pipeline(count, compute, sums, finish, gather, extra=None, between=None, before=None):
    blocks = count // ROWS
    if before:
        before.begin(0)
        before.begin(1)
        before.forward(0)

    def tick(i, carry):
        if before:

            @pl.when(i < blocks - 2)
            def _():
                before.begin(i + 2)

            @pl.when(i < blocks - 1)
            def _():
                before.forward(i + 1)

            @pl.when(i < blocks)
            def _():
                before.arrive(i)

        @pl.when(i < blocks)
        def _():
            compute(i)
            for one in sums:
                one.begin(i)

        if between:
            between(i)

        @pl.when((i >= 1) & (i <= blocks))
        def _():
            for one in sums:
                one.forward(i - 1)

        @pl.when((i >= 2) & (i <= blocks + 1))
        def _():
            finish(i - 2)
            if gather:
                gather.begin(i - 2)

        if gather:

            @pl.when(i >= 3)
            def _():
                gather.forward(i - 3)

        if extra:
            extra(i)
        return carry

    lax.fori_loop(0, blocks + (3 if gather else 2), tick, 0)

    def close(i, carry):
        for one in sums:
            one.end(i)
        if gather:
            gather.arrive(i)
            gather.sent(i)
        if before:
            before.sent(i)
        return carry

    lax.fori_loop(0, blocks, close, 0)


def finish_strips(one, block, work):
    for half in range(2):
        one.arrived(block, half)

        def strip(start):
            row = pl.multiple_of(block * ROWS + half * (ROWS // 2), ROWS // 2) + start
            work(pl.ds(row, STRIP), one.total(block, half, start))

        strips(ROWS // 2, strip)


def views(refs, block):
    return [ref.at[rows_of(block), :] for ref in refs]


def attention_forward(length, normed, mixed_own, packed, bias, pair, offset, x, shards, ident):
    count, width = normed.shape
    own = width // 4
    wide = width // 2
    keyed = pair.shape[1]
    low = packed.shape[1] - width // 2

    def weights(r):
        return unfold(r.packed, r.in_w, r.out_w, shards, r.fold)

    def first(r):
        for copy in weights(r):
            copy.start()

    def work(r):
        peers = plane()
        mine = pl.ds(pl.multiple_of(peers[0] * own, LANES), own)
        real = r.length[0]
        r.mixed[:, mine] = r.mixed_own[...]
        greet(peers[1], peers[2])
        mixing = block_gather(r.mixed, peers, own, (r.mixed_send, r.mixed_recv))
        total = block_sum(r, "sum", r.part, peers, own)
        gather = block_gather(r.out, peers, own, (r.gather_send, r.gather_recv))
        saved = (r.update, r.shared, r.reset, r.cand, r.value, r.att, r.gated, r.probs)

        def compute(block):
            @pl.when(block == 0)
            def _():
                for copy in weights(r):
                    copy.wait()

            r.wait_block(block)
            attention_forward_block(
                real,
                block * ROWS,
                *views((r.normed, r.mixed), block),
                r.in_w,
                r.bias,
                r.pair,
                r.offset,
                *views((r.part,) + saved, block),
                r.out_w,
            )

        def finish(block):
            def strip(here, summed):
                pre = r.cand[here, :].astype(F32) + summed
                r.hidden[here, :] = pre.astype(BF16)
                old = r.x[here, :].astype(F32)
                made = old + sigmoid(r.update[here, :].astype(F32)) * (silu(pre) - old)
                r.out[here, mine] = made.astype(BF16)

            finish_strips(total, block, strip)

        def extra(i):
            @pl.when(i == 0)
            def _():
                r.wait("x")

            @pl.when(i == count // ROWS)
            def _():
                r.store("mixed", "update", "shared", "reset", "value", "att", "gated", "probs")

        pipeline(count, compute, (total,), finish, gather, extra, before=mixing)

    rows = lambda columns: (shape((count, columns), BF16), STORE)
    return transfer(
        work,
        dict(
            length=(length, SMEM),
            packed=(packed, RAW),
            normed=(normed, BLOCKS),
            mixed_own=(mixed_own, VMEM),
            x=(x, OWN_PART),
            bias=(bias, VMEM),
            pair=(pair, VMEM),
            offset=(offset, VMEM),
        ),
        dict(
            out=(shape((count, width), BF16), VMEM),
            hidden=(shape((count, own), BF16), VMEM),
            mixed=rows(width),
            update=rows(own),
            shared=rows(keyed),
            reset=rows(wide),
            value=rows(wide),
            att=rows(wide),
            gated=rows(wide),
            probs=rows(ATT),
        ),
        dict(
            part=pltpu.VMEM((count, width), BF16),
            cand=pltpu.VMEM((count, own), BF16),
            in_w=pltpu.VMEM((width, low), BF16),
            out_w=pltpu.VMEM((wide, width), BF16),
            fold=pltpu.SemaphoreType.DMA((2 * shards + 1,)),
            mixed_send=gather_sems(count),
            mixed_recv=gather_sems(count),
            **sum_scratch("sum", count, own),
            gather_send=gather_sems(count),
            gather_recv=gather_sems(count),
        ),
        ident,
        54,
        first=first,
    )


def feed_forward_joined(x, gain, shift, weights, bias, own_out, ident):
    count, width = x.shape
    hidden = bias.shape[1]
    own = width // 4

    def work(r):
        peers = plane()
        mine = pl.ds(pl.multiple_of(peers[0] * own, LANES), own)
        greet(peers[1], peers[2])
        r.wait("weights")
        total = block_sum(r, "sum", r.part, peers, own)
        gather = block_gather(r.out, peers, own, (r.gather_send, r.gather_recv))

        def compute(block):
            r.wait_block(block)
            x_rows, *outs = views((r.x, r.part, r.pre, r.n, r.normed, r.scale), block)
            feed_forward_kernel(x_rows, r.gain, r.shift, r.weights, r.bias, *outs)

        def finish(block):
            def strip(here, summed):
                made = r.x[here, mine].astype(F32) + summed + r.own_out[...]
                r.out[here, mine] = made.astype(BF16)

            finish_strips(total, block, strip)

        def extra(i):
            @pl.when(i == count // ROWS)
            def _():
                r.store("pre", "n", "normed", "scale")

        pipeline(count, compute, (total,), finish, gather, extra)

    rows = lambda columns, kind=BF16: (shape((count, columns), kind), STORE)
    return transfer(
        work,
        dict(
            x=(x, BLOCKS),
            weights=(weights, FETCH),
            gain=(gain, VMEM),
            shift=(shift, VMEM),
            bias=(bias, VMEM),
            own_out=(own_out, VMEM),
        ),
        dict(
            out=(shape((count, width), BF16), VMEM),
            pre=rows(hidden),
            n=rows(width),
            normed=rows(width),
            scale=rows(LANES, F32),
        ),
        dict(
            part=pltpu.VMEM((count, width), BF16),
            **sum_scratch("sum", count, own),
            gather_send=gather_sems(count),
            gather_recv=gather_sems(count),
        ),
        ident,
        40,
    )


def feed_backward(given, k, p, weights, shards, ident, after=()):
    corrected = isinstance(given, tuple)
    both_ways = k.feed_pre is None
    count, width = k.middle.shape
    own = width // 4
    hidden = p.feed_in.shape[1]
    norms, gain = p.own, p.feed_gain
    blocks = count // ROWS

    def work(r):
        peers = plane()
        me, across, along, far = peers
        mine = pl.ds(pl.multiple_of(me * own, LANES), own)
        if corrected:
            r.z[:, mine] = r.z_own[...]
        greet(across, along)
        before = None
        if corrected:
            before = block_gather(r.z, peers, own, (r.z_send, r.z_recv))
        r.sums[...] = jnp.zeros_like(r.sums)
        r.bias[...] = jnp.zeros_like(r.bias)
        total = block_sum(r, "sum", r.part, peers, own)
        gather = block_gather(r.out, peers, own, (r.gather_send, r.gather_recv))

        def quarter(block, owner, half):
            size = count // 4
            return (
                pl.ds(pl.multiple_of(owner * size, size), size),
                pl.ds(half * (width // 2), width // 2),
            )

        if both_ways:
            last = block_sum(
                r, "last", r.made, peers, own, quarter, lambda block: pl.ds(0, count // 4)
            )

        def last_rows():
            for half in range(2):
                last.arrived(0, half)
                lanes = slice(half * (width // 2), (half + 1) * (width // 2))

                def strip(start):
                    here = pl.ds(start, STRIP)
                    row = pl.ds(pl.multiple_of(me * (count // 4), STRIP) + start, STRIP)
                    made = r.middle[row, lanes].astype(F32) + last.total(0, half, start)
                    r.block_out[here, lanes] = (made + r.out_bias[:, lanes]).astype(BF16)

                strips(count // 4, strip)

        def stats_copy(block, step):
            lanes = rows_of(block)
            source = (r.stats, r.stats_stage)[step].at[:, lanes]
            sems = (r.stats_send, r.stats_recv)
            other = (across, along)[step]
            return link(source, r.stats_got.at[step, :, lanes], sems, 2 * block + step, other)

        def compute(block):
            here = rows_of(block)

            @pl.when(block == 0)
            def _():
                r.wait("weights")
                if corrected:
                    sems = (r.means_send, r.means_recv)
                    r.means[...] = stats_total(
                        r.z_stats, r.means_got, r.means_stage, peers, sems, 0
                    )

            r.wait_block(block)
            if corrected:
                xn, xscale = normalise(r.x_full[here, :].astype(F32))
                means = r.means[:, here].T * (1.0 / width)
                z = r.z[here, :].astype(F32)
                g = z - xscale * (means[:, 0:1] + xn * means[:, 1:2])
                r.g[here, :] = g.astype(BF16)
            if both_ways:
                x_rows, *made = views((r.middle, r.made, r.pre, r.n, r.normed, r.scale), block)
                feed_forward_kernel(x_rows, r.gain, r.shift, r.weights, r.in_bias, *made)
            g_rows, pre_rows, n_rows = views((r.g, r.pre, r.n), block)
            part, gpre, act = views((r.part, r.gpre, r.act), block)
            feed_backward_block(
                g_rows,
                pre_rows,
                n_rows,
                r.gain,
                r.weights,
                part,
                r.stats,
                gpre,
                act,
                r.sums,
                r.bias,
                here,
            )
            stats_copy(block, 0).start()

        def finish(block):
            here = rows_of(block)
            stats_copy(block, 1).wait_recv()
            every = r.stats_stage[:, here] + r.stats_got[1, :, here]
            r.columns[here, :] = every.T * (1.0 / width)

            def strip(here, summed):
                e = summed * r.norms[2:3, :]
                n_own = r.n[here, mine].astype(F32)
                inner = e - r.columns[here, 0:1] - n_own * r.columns[here, 1:2]
                g = r.g[here, mine].astype(F32) + r.scale[here, 0:1] * inner
                g = g.astype(BF16).astype(F32)
                u = sigmoid(r.update[here, :].astype(F32))
                pre = r.hidden[here, :].astype(F32)
                s = sigmoid(pre)
                x = r.x[here, :].astype(F32)
                r.gupdate[here, :] = (g * (pre * s - x) * (u * (1.0 - u))).astype(BF16)
                r.resid[here, :] = g * (1.0 - u)
                r.out[here, mine] = (g * u * (s * (1.0 + pre * (1.0 - s)))).astype(BF16)

            finish_strips(total, block, strip)

        def small_grads():
            r.grad[:, hidden + width :] = jnp.zeros((width, LANES), BF16)
            size = width // shards
            for shard in range(shards):
                lanes = slice(shard * size, (shard + 1) * size)
                block = jnp.concatenate(
                    (r.sums[0:3, lanes], r.bias[0:1, lanes], jnp.zeros((SMALL - 4, size), F32)),
                    axis=0,
                )
                r.grad[shard * size : shard * size + SMALL, hidden + width :] = widen(block)

        def in_grad(rows, value):
            r.grad[rows, :hidden] = value

        def out_grad(rows, value):
            r.grad[rows, hidden : hidden + width] = value

        def extra(i):
            @pl.when((i >= 1) & (i <= blocks))
            def _():
                here = rows_of(i - 1)
                stats_copy(i - 1, 0).wait_recv()
                r.stats_stage[:, here] = r.stats[:, here] + r.stats_got[0, :, here]
                stats_copy(i - 1, 1).start()

            @pl.when(i == 0)
            def _():
                r.wait("update", "hidden", "x")
                if not both_ways:
                    r.wait("scale", "normed")

            if both_ways:

                @pl.when(i == blocks - 1)
                def _():
                    last.begin(0)

                @pl.when(i == blocks)
                def _():
                    last.forward(0)

                @pl.when(i == blocks + 2)
                def _():
                    last_rows()
                    last.end(0)

            @pl.when(i == blocks + 1)
            def _():
                r.store("gupdate", "resid")

        def between(i):
            @pl.when(i == blocks)
            def _():
                grad_tiles(r.normed, r.gpre, in_grad, 0, width // TILE)
                small_grads()
                grad_tiles(r.act, r.g, out_grad, 0, hidden // TILE)
                r.store("grad")

        pipeline(count, compute, (total,), finish, gather, extra, between, before)

        def close(i, carry):
            stats_copy(i, 0).wait_send()
            stats_copy(i, 1).wait_send()
            return carry

        lax.fori_loop(0, blocks, close, 0)

    if corrected:
        z_own, z_stats, x_full = given
        first = dict(z_own=(z_own, VMEM), x_full=(x_full, BLOCKS), z_stats=(z_stats, VMEM))
        both = pltpu.SemaphoreType.DMA((2,))
        extra_scratch = dict(
            g=pltpu.VMEM((count, width), BF16),
            z=pltpu.VMEM((count, width), BF16),
            z_send=gather_sems(count),
            z_recv=gather_sems(count),
            means=pltpu.VMEM((CHUNKS, count), F32),
            means_stage=pltpu.VMEM((CHUNKS, count), F32),
            means_got=pltpu.VMEM((2, CHUNKS, count), F32),
            means_send=both,
            means_recv=both,
        )
    else:
        first = dict(g=(given, BLOCKS))
        extra_scratch = {}
    extra_outs = {}
    if both_ways:
        saved = {}
        first.update(
            middle=(k.middle, BLOCKS),
            shift=(p.feed_shift, VMEM),
            in_bias=(p.feed_in, VMEM),
            out_bias=(p.feed_out, VMEM),
        )
        extra_outs.update(block_out=(shape((count // 4, width), BF16), VMEM))
        rows = pltpu.VMEM((count, width), BF16)
        slot = pltpu.VMEM((2, count // 4, width // 2), BF16)
        ends = pltpu.SemaphoreType.DMA((6,))
        extra_scratch.update(
            made=rows,
            pre=pltpu.VMEM((count, hidden), BF16),
            n=rows,
            normed=rows,
            scale=pltpu.VMEM((count, LANES), F32),
            last_early=slot,
            last_direct=slot,
            last_late=slot,
            last_stage=slot,
            last_send=ends,
            last_recv=ends,
        )
    else:
        saved = dict(
            pre=(k.feed_pre, BLOCKS),
            n=(k.feed_n, BLOCKS),
            scale=(k.feed_scale, LATE),
            normed=(k.feed_normed, LATE),
        )
    sems = pltpu.SemaphoreType.DMA((2 * blocks,))
    return transfer(
        work,
        dict(
            weights=(weights, FETCH),
            **first,
            **saved,
            update=(k.update, LATE),
            hidden=(k.hidden, LATE),
            x=(k.x, OWN_PART),
            gain=(gain, VMEM),
            norms=(norms, VMEM),
        ),
        dict(
            out=(shape((count, width), BF16), VMEM),
            gupdate=(shape((count, own), BF16), STORE),
            resid=(shape((count, own), F32), STORE),
            grad=(shape((width, hidden + width + LANES), BF16), STORE),
            **extra_outs,
        ),
        dict(
            part=pltpu.VMEM((count, width), BF16),
            gpre=pltpu.VMEM((count, hidden), BF16),
            act=pltpu.VMEM((count, hidden), BF16),
            sums=pltpu.VMEM((8, width), F32),
            bias=pltpu.VMEM((8, hidden), F32),
            stats=pltpu.VMEM((CHUNKS, count), F32),
            stats_stage=pltpu.VMEM((CHUNKS, count), F32),
            stats_got=pltpu.VMEM((2, CHUNKS, count), F32),
            columns=pltpu.VMEM((count, CHUNKS), F32),
            stats_send=sems,
            stats_recv=sems,
            **extra_scratch,
            **sum_scratch("sum", count, own),
            gather_send=gather_sems(count),
            gather_recv=gather_sems(count),
        ),
        ident,
        46,
        after,
    )


def attention_backward(length, gout, gupdate, k, packed, pair, offset, shards, ident, after=()):
    shared, reset, value, att, probs = k.saved
    count, width = gout.shape
    own = width // 4
    wide = width // 2
    keyed = pair.shape[1]
    total = packed.shape[1] - width // 2
    blocks = count // ROWS
    few = wide // shards
    block_rows = width // shards

    def weights(r):
        return unfold(r.packed, r.in_w, r.out_w, shards, r.fold)

    def first(r):
        for copy in weights(r):
            copy.start()

    def work(r):
        peers = plane()
        mine = pl.ds(pl.multiple_of(peers[0] * own, LANES), own)
        real = r.length[0]
        greet(peers[1], peers[2])
        r.bias[...] = jnp.zeros_like(r.bias)
        r.pairs[...] = jnp.zeros_like(r.pairs)
        one = block_sum(r, "one", r.gmixed_part, peers, own)
        two = block_sum(r, "two", r.gvalue_part, peers, own)

        def compute(block):
            @pl.when(block == 0)
            def _():
                for copy in weights(r):
                    copy.wait()

            r.wait_block(block)
            attention_backward_block(
                real,
                block * ROWS,
                mine,
                *views((r.gout, r.gupdate, r.shared, r.reset, r.value, r.att, r.probs), block),
                r.in_w,
                r.pair,
                r.offset,
                *views((r.gmixed_part, r.gvalue_part, r.gbase, r.gvalue), block),
                r.bias,
                r.pairs,
                r.out_w,
            )

        def finish(block):
            def keep(out):
                def strip(here, summed):
                    out[here, :] = summed

                return strip

            finish_strips(one, block, keep(r.gmixed))
            finish_strips(two, block, keep(r.gnormed))

        def value_grad(rows, value):
            r.grad[rows, :wide] = value

        def base_grad(rows, value):
            r.grad[rows, wide:total] = value

        def out_grad(rows, value):
            for i in range(TILE // few):
                start = (rows.start // few + i) * block_rows
                for half in range(2):
                    here = pl.ds(pl.multiple_of(start + half * few, few), few)
                    r.grad[here, total : total + width // 2] = value[
                        i * few : (i + 1) * few, half * (width // 2) : (half + 1) * (width // 2)
                    ]

        def small_grads():
            last = total + width // 2
            r.grad[:, last:] = jnp.zeros((width, LANES), BF16)
            rows = [r.bias[0:1, i * LANES : (i + 1) * LANES] for i in range(total // LANES)]
            block = jnp.concatenate(rows + [r.pairs[0:3, :]], axis=0).astype(BF16)
            for shard in range(shards):
                r.grad[shard * block_rows : shard * block_rows + SMALL, last:] = block

        def extra(i):
            @pl.when(i == 0)
            def _():
                r.wait("normed", "mixed", "gated")

        def between(i):
            @pl.when(i == blocks)
            def _():
                small_grads()
                grad_tiles(r.mixed, r.gbase, base_grad, 0, width // TILE)
                grad_tiles(r.normed, r.gvalue, value_grad, 0, width // TILE)
                grad_tiles(r.gated, r.gout, out_grad, 0, wide // TILE)
                r.store("grad")

        pipeline(count, compute, (one, two), finish, None, extra, between)

    return transfer(
        work,
        dict(
            length=(length, SMEM),
            packed=(packed, RAW),
            gout=(gout, BLOCKS),
            gupdate=(gupdate, BLOCKS),
            shared=(shared, BLOCKS),
            reset=(reset, BLOCKS),
            value=(value, BLOCKS),
            att=(att, BLOCKS),
            probs=(probs, BLOCKS),
            normed=(k.normed, LATE),
            mixed=(k.mixed, LATE),
            gated=(k.gated, LATE),
            pair=(pair, VMEM),
            offset=(offset, VMEM),
        ),
        dict(
            gmixed=(shape((count, own), F32), VMEM),
            gnormed=(shape((count, own), F32), VMEM),
            grad=(shape((width, total + width // 2 + LANES), BF16), STORE),
        ),
        dict(
            gmixed_part=pltpu.VMEM((count, width), BF16),
            gvalue_part=pltpu.VMEM((count, width), BF16),
            gbase=pltpu.VMEM((count, total - wide), BF16),
            gvalue=pltpu.VMEM((count, wide), BF16),
            bias=pltpu.VMEM((8, total), F32),
            pairs=pltpu.VMEM((8, keyed), F32),
            in_w=pltpu.VMEM((width, total), BF16),
            out_w=pltpu.VMEM((wide, width), BF16),
            fold=pltpu.SemaphoreType.DMA((2 * shards + 1,)),
            **sum_scratch("one", count, own),
            **sum_scratch("two", count, own),
        ),
        ident,
        40,
        after,
        first,
    )


def block_piece(whole):
    def piece(owner, half):
        size = whole.shape[1] // 2
        return owner, pl.ds(half * size, size), slice(None)

    return piece


def final_kernel(number, z_ref, stats_ref, x_ref, *refs):
    blocks, refs = refs[:number], refs[number:]
    out_ref, refs = refs[0], refs[1:]
    gathered, refs = refs[:number], refs[number:]
    land, x_own, got, stats_stage, total_buf, local_sem, send, recv = refs[:8]
    block_sems = [refs[8 + 2 * i : 10 + 2 * i] for i in range(number)]
    count, own = z_ref.shape
    quarter, width = out_ref.shape
    peers = plane()
    me = peers[0]

    def rows(owner):
        return pl.ds(pl.multiple_of(owner * quarter, quarter), quarter)

    mine = pl.ds(pl.multiple_of(me * own, LANES), own)
    fetch = pltpu.make_async_copy(x_ref.at[rows(me), :], x_own, local_sem)
    fetch.start()
    land[:, mine] = z_ref[rows(me), :]
    for block, whole in zip(blocks, gathered):
        whole[me] = block[...]
    greet(*peers[1:])
    sems = (send, recv)
    copies = []
    for index, other in enumerate(peers[1:]):
        copies.append(link(z_ref.at[rows(other), :], land.at[:, mine], sems, 2 + index, other))
        copies[-1].start()
    total_buf[...] = stats_total(stats_ref, got, stats_stage, peers, sems, 0)
    begun = [
        [gather_begin(whole, block_piece(whole), peers, k, half) for half in range(2)]
        for whole, k in zip(gathered, block_sems)
    ]
    part = total_buf[:, pl.ds(pl.multiple_of(me * quarter, LANES), quarter)]
    means = part.T * (1.0 / width)
    fetch.wait()
    for copy in copies:
        copy.wait_recv()
    n, scale = normalise(x_own[...].astype(F32))
    g = land[...].astype(F32) - scale * (means[:, 0:1] + n * means[:, 1:2])
    out_ref[...] = g.astype(BF16)
    passed = [
        gather_forward(whole, block_piece(whole), peers, k, zero, one)
        for whole, k, (zero, one) in zip(gathered, block_sems, begun)
    ]
    for whole, k, (zero, one), two in zip(gathered, block_sems, begun, passed):
        gather_finish(whole, block_piece(whole), peers, k, zero, one, two)
    for copy in copies:
        copy.wait_send()


def final_exchange(z, stats, x, blocks, sections, ident):
    count, own = z.shape
    width = x.shape[1]
    quarter = count // 4
    number = len(blocks)
    return pl.pallas_call(
        functools.partial(final_kernel, number),
        out_shape=(shape((quarter, width), BF16),)
        + tuple(shape((sections,) + a.shape, BF16) for a in blocks),
        in_specs=[vmem(), vmem(), hbm()] + [vmem()] * number,
        out_specs=(vmem(),) * (1 + number),
        scratch_shapes=[
            pltpu.VMEM((quarter, width), BF16),
            pltpu.VMEM((quarter, width), BF16),
            pltpu.VMEM((2,) + stats.shape, F32),
            pltpu.VMEM(stats.shape, F32),
            pltpu.VMEM(stats.shape, F32),
            pltpu.SemaphoreType.DMA,
        ]
        + copy_sems(5)
        + copy_sems(6) * number,
        cost_estimate=lasting(10 + 20 * number),
        compiler_params=comm_params(ident),
    )(z, stats, x, *blocks)


def sums_kernel(shards, holders, sums_ref, block_ref, channels_ref, whole_ref, *refs):
    sums_land, send_s, recv_s, send_c, recv_c, send, recv = refs
    peers = plane()
    me = peers[0]
    slot = lax.axis_index("dp")
    holding = slot // holders == me
    whole_ref[me] = block_ref[...]
    barrier = pltpu.get_barrier_semaphore()
    for other in peers[1:]:
        pl.semaphore_signal(barrier, inc=1, device_id={"section": other}, device_id_type=MESH)
    for step in range(1, shards):
        other = (slot + step) % shards
        pl.semaphore_signal(barrier, inc=1, device_id={"dp": other}, device_id_type=MESH)
    pl.semaphore_wait(barrier, shards + 2)

    def sums_copy(target, index, place):
        return pltpu.make_async_remote_copy(
            src_ref=sums_ref,
            dst_ref=sums_land.at[place],
            send_sem=send_s.at[index],
            recv_sem=recv_s.at[place],
            device_id={"dp": target},
            device_id_type=MESH,
        )

    def sums_out(index):
        target = me * holders + index
        place = jnp.maximum((slot - target + shards) % shards - 1, 0)
        return target, sums_copy(target, index, place)

    for index in range(holders):
        target, copy = sums_out(index)

        @pl.when(target != slot)
        def _():
            copy.start()

    piece = block_piece(whole_ref)
    zero, one = (gather_begin(whole_ref, piece, peers, (send, recv), half) for half in range(2))
    passed = gather_forward(whole_ref, piece, peers, (send, recv), zero, one)

    def channels_copy(other, index):
        return link(channels_ref, channels_ref, (send_c, recv_c), index, other)

    @pl.when(holding)
    def _():
        summed = sums_ref[...]
        for step in range(1, shards):
            sums_copy((slot + step) % shards, 0, step - 1).wait_recv()
            summed = summed + sums_land[step - 1]
        channels_ref[...] = summed
        for index, other in enumerate(peers[1:]):
            channels_copy(other, index).start()

    gather_finish(whole_ref, piece, peers, (send, recv), zero, one, passed)

    for index, other in enumerate(peers[1:]):

        @pl.when(slot // holders == other)
        def _():
            channels_copy(other, index).wait_recv()

    @pl.when(holding)
    def _():
        for index, other in enumerate(peers[1:]):
            channels_copy(other, index).wait_send()

    for index in range(holders):
        target, copy = sums_out(index)

        @pl.when(target != slot)
        def _():
            copy.wait_send()


def gather_sums(sums, block, sections, shards, holders, ident):
    return pl.pallas_call(
        functools.partial(sums_kernel, shards, holders),
        out_shape=(shape(sums.shape, F32), shape((sections,) + block.shape, BF16)),
        in_specs=[vmem()] * 2,
        out_specs=(vmem(),) * 2,
        scratch_shapes=[pltpu.VMEM((shards - 1,) + sums.shape, F32)]
        + copy_sems(max(shards - 1, holders))
        + copy_sems(3)
        + copy_sems(6),
        cost_estimate=lasting(25),
        compiler_params=comm_params(ident),
    )(sums, block)


def woven_parts(part, here, low, size, shards):
    step = size // shards
    return jnp.concatenate(
        [
            part[k, here, low + d * step : low + (d + 1) * step].astype(F32)
            for d in range(shards)
            for k in range(part.shape[0])
        ],
        axis=1,
    )


def joined_parts(part, here, low, size):
    return jnp.concatenate(
        [part[k, here, low : low + size].astype(F32) for k in range(part.shape[0])], axis=1
    )


def by_strips(rows, work):
    def strip(i, carry):
        work(pl.ds(pl.multiple_of(i * SMALL, SMALL), SMALL))
        return carry

    lax.fori_loop(0, rows // SMALL, strip, 0)


def attention_outputs(shards, part, value_ref, base_ref, out_ref, small_ref):
    sections = part.shape[0]
    width = out_ref.shape[2]
    wide = value_ref.shape[2] // sections
    own = width // sections
    keyed = base_ref.shape[2] - 2 * width - wide * sections
    edge = wide + own
    total = edge + keyed + wide + own
    few = wide // shards

    def strip(here):
        value_ref[0, here, :] = woven_parts(part, here, 0, wide, shards)
        base_ref[0, here, :width] = joined_parts(part, here, wide, own)
        shared = part[0, here, edge : edge + keyed].astype(F32)
        for k in range(1, sections):
            shared += part[k, here, edge : edge + keyed].astype(F32)
        low = width
        base_ref[0, here, low : low + keyed] = shared
        low += keyed
        base_ref[0, here, low : low + wide * sections] = woven_parts(
            part, here, edge + keyed, wide, shards
        )
        low += wide * sections
        base_ref[0, here, low:] = joined_parts(part, here, edge + keyed + wide, own)

    by_strips(value_ref.shape[1], strip)
    for k in range(sections):
        for half in range(2):
            columns = slice(half * (width // 2), (half + 1) * (width // 2))
            out_ref[0, k * few : (k + 1) * few, columns] = part[
                k, half * few : (half + 1) * few, total : total + width // 2
            ].astype(F32)
        small_ref[0, k] = part[k, :SMALL, total + width // 2 :].astype(F32)


def feed_outputs(shards, feed, in_ref, out_ref, small_ref):
    sections, rows = feed.shape[:2]
    width = out_ref.shape[2]
    hidden = in_ref.shape[2] // sections

    def strip(here):
        in_ref[0, here, :] = woven_parts(feed, here, 0, hidden, shards)

    by_strips(rows, strip)
    for k in range(sections):
        out_ref[0, k * rows : (k + 1) * rows, :] = feed[k, :, hidden : hidden + width].astype(F32)
        small_ref[0, k] = feed[k, :SMALL, hidden + width :].astype(F32)


def assemble_kernel(work, shards, layers, *refs):
    for layer in range(layers):

        @pl.when(pl.program_id(0) == layer)
        def _():
            work(shards, refs[layer], *refs[layers:])


def assemble(work, gathered, dims, shards):
    layers = len(gathered)
    dims = dims + ((gathered[0].shape[0], SMALL, LANES),)
    return pl.pallas_call(
        functools.partial(assemble_kernel, work, shards, layers),
        grid=(layers,),
        out_shape=tuple(shape((layers,) + d, F32) for d in dims),
        in_specs=[pl.BlockSpec(a.shape, lambda i: (0, 0, 0)) for a in gathered],
        out_specs=tuple(
            pl.BlockSpec((1,) + d, lambda i, n=len(d): (i,) + (0,) * n) for d in dims
        ),
        cost_estimate=lasting(6),
        compiler_params=params(),
    )(*gathered)


def chosen(pieces):
    section = lax.axis_index("section")
    result = pieces[0]
    for k in range(1, len(pieces)):
        result = jnp.where(section == k, pieces[k], result)
    return result


def pick(ref, index, low, size, shards, sections):
    step = size // (shards * sections)
    parts = []
    for shard in range(shards):
        start = low + shard * sections * step
        parts.append(
            chosen([ref[index + (slice(start + k * step, start + (k + 1) * step),)] for k in range(sections)])
        )
    return jnp.concatenate(parts, axis=-1)


def pack_attention_kernel(shards, sections, value_ref, base_ref, out_ref, packed_ref):
    rows, wide_all = value_ref.shape[1:]
    few_all, width = out_ref.shape[1:]
    wide, own, few = wide_all // sections, width // sections, few_all // sections
    keyed = base_ref.shape[2] - 2 * width - wide_all
    section = lax.axis_index("section")
    low = wide + own + keyed

    def strip(i, carry):
        here = pl.ds(pl.multiple_of(i * SMALL, SMALL), SMALL)

        def base(start, size):
            return base_ref[0, here, pl.ds(pl.multiple_of(start, LANES), size)]

        packed_ref[here, :wide] = pick(value_ref, (0, here), 0, wide_all, shards, sections)
        packed_ref[here, wide : wide + own] = base(section * own, own)
        packed_ref[here, wide + own : low] = base(width, keyed)
        packed_ref[here, low : low + wide] = pick(
            base_ref, (0, here), width + keyed, wide_all, shards, sections
        )
        packed_ref[here, low + wide : low + wide + own] = base(
            width + keyed + wide_all + section * own, own
        )
        return carry

    lax.fori_loop(0, rows // SMALL, strip, 0)
    low += wide + own
    mine = pl.ds(pl.multiple_of(section * few, few), few)
    for half in range(2):
        packed_ref[half * few : (half + 1) * few, low:] = out_ref[
            0, mine, half * (width // 2) : (half + 1) * (width // 2)
        ]


def pack_feed_kernel(shards, sections, in_ref, out_ref, packed_ref):
    rows, hidden_all = in_ref.shape[1:]
    hidden = hidden_all // sections
    size = out_ref.shape[1] // sections

    def strip(i, carry):
        here = pl.ds(pl.multiple_of(i * SMALL, SMALL), SMALL)
        packed_ref[here, :hidden] = pick(in_ref, (0, here), 0, hidden_all, shards, sections)
        return carry

    lax.fori_loop(0, rows // SMALL, strip, 0)
    start = pl.multiple_of(lax.axis_index("section") * size, size)
    packed_ref[:, hidden:] = out_ref[0, pl.ds(start, size), :]


def pack(kernel, layer, columns, shards, sections, *arrays):
    rows = arrays[0].shape[1]
    return pl.pallas_call(
        functools.partial(kernel, shards, sections),
        grid=(1,),
        out_shape=shape((rows, columns), BF16),
        in_specs=[pl.BlockSpec((1,) + a.shape[1:], lambda i: (layer, 0, 0)) for a in arrays],
        out_specs=pl.BlockSpec((rows, columns), lambda i: (0, 0)),
        cost_estimate=lasting(3),
        compiler_params=params(),
    )(*arrays)


def unpack_kernel(layers, shards, sections, places, everyone_ref, *refs):
    base_buf = refs[-1]
    section = lax.axis_index("section")
    outs = 14
    for layer in range(layers):
        (
            gain_ref,
            shift_ref,
            feed_gain_ref,
            feed_shift_ref,
            feed_out_ref,
            own_ref,
            rate_ref,
            coef_ref,
            bias_ref,
            feed_in_ref,
            pair_ref,
            offset_ref,
            skip_ref,
            own_out_ref,
        ) = refs[layer * outs : (layer + 1) * outs]
        width = gain_ref.shape[1]
        own = width // sections
        mine = pl.ds(pl.multiple_of(section * own, LANES), own)
        row = slice(layer, layer + 1)

        def joined(low, size):
            return jnp.concatenate(
                [everyone_ref[d, row, low : low + size] for d in range(shards)], axis=1
            )

        def share(low, size):
            step = size // sections
            return jnp.concatenate(
                [
                    chosen(
                        [
                            everyone_ref[d, row, low + k * step : low + (k + 1) * step]
                            for k in range(sections)
                        ]
                    )
                    for d in range(shards)
                ],
                axis=1,
            )

        def channels(low):
            size = width // shards
            count = own // size
            return jnp.concatenate(
                [everyone_ref[section * count + d, row, low : low + size] for d in range(count)],
                axis=1,
            )

        size = width // shards
        gain_ref[...] = joined(places["norm_gain"], size)
        shift_ref[...] = joined(places["norm_shift"], size)
        feed_gain_ref[...] = joined(places["feed_gain"], size)
        feed_shift_ref[...] = joined(places["feed_shift"], size)
        feed_out_ref[...] = joined(places["feed_out_bias"], size)
        own_ref[0:1, :] = gain_ref[:, mine]
        own_ref[1:2, :] = shift_ref[:, mine]
        own_ref[2:3, :] = feed_gain_ref[:, mine]
        own_ref[3:8, :] = jnp.zeros((5, own), F32)
        own_out_ref[...] = feed_out_ref[:, mine]
        skip_ref[...] = channels(places["average_skip"])
        for n in range(rate_ref.shape[0]):
            rate = sigmoid(channels(places["average_decay"] + n * size))
            drive = (1.0 - rate) * channels(places["average_input"] + n * size)
            coef = drive * channels(places["average_output"] + n * size)
            rate_ref[n] = jnp.broadcast_to(rate, (CHUNKS, own))
            coef_ref[n] = jnp.broadcast_to(coef, (CHUNKS, own))
        keyed = offset_ref.shape[1]
        step = keyed // shards
        for r in range(2):
            pair_ref[r : r + 1, :] = joined(places["pair_scale"] + r * step, step)
        offset_ref[...] = joined(places["query_shift"], step)
        feed_in_ref[...] = share(
            places["feed_in_bias"], feed_in_ref.shape[1] * sections // shards
        )
        total = bias_ref.shape[1]
        wide = (total - keyed - 2 * own) // 2
        base_all = 2 * width + keyed + wide * sections
        base_buf[...] = joined(places["base_bias"], base_all // shards)
        low = wide + own + keyed
        bias_ref[:, :wide] = share(places["value_bias"], wide * sections // shards)
        bias_ref[:, wide : wide + own] = base_buf[:, mine]
        bias_ref[:, wide + own : low] = base_buf[:, width : width + keyed]
        bias_ref[:, low : low + wide] = pick(
            base_buf, (slice(None),), width + keyed, wide * sections, shards, sections
        )
        start = pl.multiple_of(width + keyed + wide * sections + section * own, LANES)
        bias_ref[:, low + wide :] = base_buf[:, pl.ds(start, own)]


def unpack(everyone, places, sizes, sections):
    shards, layers = everyone.shape[:2]
    width, dims, total, hidden, keyed, base = sizes
    own = width // sections
    one_layer = (
        [shape((1, width), F32)] * 5
        + [shape((8, own), F32)]
        + [shape((dims, CHUNKS, own), F32)] * 2
        + [
            shape((1, total), F32),
            shape((1, hidden), F32),
            shape((2, keyed), F32),
            shape((1, keyed), F32),
            shape((1, own), F32),
            shape((1, own), F32),
        ]
    )
    outs = pl.pallas_call(
        functools.partial(unpack_kernel, layers, shards, sections, places),
        out_shape=tuple(one_layer * layers),
        in_specs=[vmem()],
        out_specs=(vmem(),) * (len(one_layer) * layers),
        scratch_shapes=[pltpu.VMEM((1, base), F32)],
        cost_estimate=lasting(3),
        compiler_params=params(),
    )(everyone)
    names = (
        "gain",
        "shift",
        "feed_gain",
        "feed_shift",
        "feed_out",
        "own",
        "rate",
        "coef",
        "bias",
        "feed_in",
        "pair",
        "offset",
        "skip",
        "own_out",
    )
    count = len(one_layer)
    return [
        types.SimpleNamespace(**dict(zip(names, outs[k * count : (k + 1) * count])))
        for k in range(layers)
    ]


def body(
    tokens,
    lengths,
    cotangent,
    norm_gain,
    norm_shift,
    average_decay,
    average_input,
    average_output,
    average_skip,
    value_weight,
    value_bias,
    base_weight,
    base_bias,
    pair_scale,
    query_shift,
    out_weight,
    feed_gain,
    feed_shift,
    feed_in_weight,
    feed_in_bias,
    feed_out_weight,
    feed_out_bias,
):
    sections = lax.axis_size("section")
    shards = lax.axis_size("dp")
    section = lax.axis_index("section")
    _, count, width = tokens.shape
    layers = norm_gain.shape[0]
    own = width // sections
    wide = value_weight.shape[2]
    keyed = pair_scale.shape[2] * shards
    hidden = feed_in_weight.shape[2]

    share = wide // sections
    total = share + own + keyed + share + own

    def over_dp(array):
        return lax.all_gather(array, "dp", axis=0, tiled=True)

    weights = []
    for layer in range(layers):
        attention = pack(
            pack_attention_kernel,
            layer,
            total + width // 2,
            shards,
            sections,
            value_weight,
            base_weight,
            out_weight,
        )
        feed = pack(
            pack_feed_kernel,
            layer,
            hidden // sections + width,
            shards,
            sections,
            feed_in_weight,
            feed_out_weight,
        )
        weights.append((over_dp(attention), over_dp(feed)))

    smalls = dict(
        norm_gain=norm_gain,
        norm_shift=norm_shift,
        average_decay=average_decay,
        average_input=average_input,
        average_output=average_output,
        average_skip=average_skip,
        feed_gain=feed_gain,
        feed_shift=feed_shift,
        feed_out_bias=feed_out_bias,
        value_bias=value_bias,
        feed_in_bias=feed_in_bias,
        base_bias=base_bias,
        pair_scale=pair_scale,
        query_shift=query_shift,
    )
    packed = jnp.concatenate([a.reshape(layers, -1) for a in smalls.values()], axis=1)
    places = {}
    low = 0
    for name, array in smalls.items():
        places[name] = low
        low += array.size // layers
    dims = average_decay.shape[1]
    small = unpack(
        lax.all_gather(packed, "dp", axis=0),
        places,
        (width, dims, total, hidden // sections, keyed, base_weight.shape[2]),
        sections,
    )

    idents = iter(range(64))
    x0 = x = tokens[0]
    kept = []
    for layer in range(layers):
        attention_w, feed_w = weights[layer]
        p = small[layer]
        normed, mixed_own, pre, own_n, scale = average_forward(
            lengths, x, p.gain, p.shift, p.rate, p.coef, p.skip
        )
        middle, hidden_pre, mixed, update, shared, reset, value, att, gated, probs = attention_forward(
            lengths,
            normed,
            mixed_own,
            attention_w,
            p.bias,
            p.pair,
            p.offset,
            x,
            shards,
            next(idents),
        )
        feed_saved = [None] * 4
        x_next = None
        if layer + 1 < layers:
            x_next, *feed_saved = feed_forward_joined(
                middle, p.feed_gain, p.feed_shift, feed_w, p.feed_in, p.own_out, next(idents)
            )
        feed_pre, feed_n, feed_normed, feed_scale = feed_saved
        kept.append(
            types.SimpleNamespace(
                x=x,
                middle=middle,
                normed=normed,
                mixed=mixed,
                pre=pre,
                own_n=own_n,
                scale=scale,
                update=update,
                saved=(shared, reset, value, att, probs),
                gated=gated,
                hidden=hidden_pre,
                feed_pre=feed_pre,
                feed_n=feed_n,
                feed_normed=feed_normed,
                feed_scale=feed_scale,
            )
        )
        x = x_next

    def scattered(grad):
        return lax.psum_scatter(grad, "dp", scatter_dimension=0, tiled=True)

    given = cotangent[0]
    feed_grads = [None] * layers
    attention_grads = [None] * layers
    channel_sums = [None] * layers
    gathered = [None] * layers
    for layer in reversed(range(layers)):
        attention_w, feed_w = weights[layer]
        k, p = kept[layer], small[layer]
        gout, gupdate, resid, feed_grad, *last = feed_backward(
            given, k, p, feed_w, shards, next(idents)
        )
        if last:
            block_out = last[0]
        feed_grads[layer] = scattered(feed_grad)
        gmixed, gnormed, attention_grad = attention_backward(
            lengths,
            gout,
            gupdate,
            k,
            attention_w,
            p.pair,
            p.offset,
            shards,
            next(idents),
            () if layer else (attention_grads[1],),
        )
        attention_grads[layer] = scattered(attention_grad)
        z, zstats, channel_sums[layer], gathered[layer] = average_backward(
            lengths,
            gmixed,
            gnormed,
            k,
            resid,
            p.own,
            p.rate,
            p.coef,
            p.skip,
            feed_grads[1] if layer else attention_grads[1],
            next(idents),
        )
        if layer:
            given = (z, zstats, k.x)

    attention_one, feed_one = gathered
    input_grad, feed_zero = final_exchange(
        z, zstats, x0, [feed_grads[0]], sections, next(idents)
    )
    channels, attention_zero = gather_sums(
        jnp.concatenate(channel_sums, axis=0),
        attention_grads[0],
        sections,
        shards,
        own * shards // width,
        next(idents),
    )
    shard = lax.axis_index("dp")
    size = width // shards
    rows = channels.shape[0]
    channels = lax.dynamic_slice_in_dim(channels, shard * size % own, size, axis=1)
    channels = channels.reshape(layers, rows // layers, size)
    g_feed_in, g_feed_out, feed_smalls = assemble(
        feed_outputs,
        (feed_zero, feed_one),
        ((size, hidden), (hidden // shards, width)),
        shards,
    )
    g_value, g_base, g_out, smalls_out = assemble(
        attention_outputs,
        (attention_zero, attention_one),
        ((size, wide), (size, base_weight.shape[2]), (wide // shards, width)),
        shards,
    )

    def of_shard(array):
        part = array.shape[-1] // shards
        return lax.dynamic_slice_in_dim(array, shard * part, part, axis=array.ndim - 1)

    def woven(array):
        split = array.reshape(layers, sections, shards, -1)
        return split.transpose(0, 2, 1, 3).reshape(layers, -1)

    of_states, of_slopes, sums = channels[:, :dims], channels[:, dims : 2 * dims], channels[:, 2 * dims :]
    rate = jax.nn.sigmoid(average_decay)
    gdrive = average_output * of_states
    drive = (1.0 - rate) * average_input
    grate = drive * average_output * of_slopes - average_input * gdrive
    g_gain, g_shift, g_skip = sums[:, 0], sums[:, 1], sums[:, 2]
    g_decay, g_input, g_output = grate * rate * (1.0 - rate), (1.0 - rate) * gdrive, drive * of_states

    edge = share + own
    bias_rows = total // LANES
    bias = smalls_out[:, :, :bias_rows].reshape(layers, sections, total)
    pairs = of_shard(jnp.sum(smalls_out[:, :, bias_rows : bias_rows + 3], axis=1))
    g_pair, g_query = pairs[:, :2], pairs[:, 2]
    g_value_bias = of_shard(woven(bias[..., :share]))
    g_base_bias = of_shard(
        jnp.concatenate(
            (
                bias[..., share:edge].reshape(layers, -1),
                jnp.sum(bias[..., edge : edge + keyed], axis=1),
                woven(bias[..., edge + keyed : edge + keyed + share]),
                bias[..., edge + keyed + share :].reshape(layers, -1),
            ),
            axis=1,
        )
    )
    g_feed_gain = jnp.sum(feed_smalls[:, :, 0, :size], axis=1)
    g_feed_shift = jnp.sum(feed_smalls[:, :, 1, :size], axis=1)
    g_feed_out_bias = feed_smalls[:, 0, 2, :size]
    g_feed_in_bias = feed_smalls[:, :, 3, :size].reshape(layers, -1)
    return (
        block_out[None],
        input_grad[None],
        g_gain,
        g_shift,
        g_decay,
        g_input,
        g_output,
        g_skip,
        g_value,
        g_value_bias,
        g_base,
        g_base_bias,
        g_pair,
        g_query,
        g_out,
        g_feed_gain,
        g_feed_shift,
        g_feed_in,
        g_feed_in_bias,
        g_feed_out,
        g_feed_out_bias,
    )


def solution(mesh):
    row, row2 = P(None, "dp"), P(None, "dp", None)
    deep = P(None, None, "dp")
    in_specs = (
        P("dp", None, None),
        P("dp"),
        P("dp", None, None),
        row,
        row,
        deep,
        deep,
        deep,
        row,
        row2,
        row,
        row2,
        row,
        deep,
        row,
        row2,
        row,
        row,
        row2,
        row,
        row2,
        row,
    )
    out_specs = (
        P("dp", "section", None),
        P("dp", "section", None),
        row,
        row,
        deep,
        deep,
        deep,
        row,
        row2,
        row,
        row2,
        row,
        deep,
        row,
        row2,
        row,
        row,
        row2,
        row,
        row2,
        row,
    )
    return jax.shard_map(body, mesh=mesh, in_specs=in_specs, out_specs=out_specs, check_vma=False)
```

```python
import functools
import types

import jax
import jax.numpy as jnp
from jax import lax
from jax.experimental import pallas as pl
from jax.experimental.pallas import tpu as pltpu
from jax.sharding import PartitionSpec as P

F32 = jnp.float32
BF16 = jnp.bfloat16
MESH = pl.DeviceIdType.MESH
ATT = 128
LANES = 128
CHUNKS = 8
ROWS = 256
STRIP = 64
TILE = 128
LOCAL = "local"
UNROLL = 16
SMALL = 16
SMEM, VMEM, RAW, FETCH, BLOCKS, LATE, OWN_PART, STORE = range(8)
EPS = 1e-05
NEGATIVE = -1000000000.0
VMEM_BYTES = 56 * 1024 * 1024


def vmem():
    return pl.BlockSpec(memory_space=pltpu.VMEM)


def smem():
    return pl.BlockSpec(memory_space=pltpu.SMEM)


def hbm():
    return pl.BlockSpec(memory_space=pl.ANY)


def shape(dims, kind):
    return jax.ShapeDtypeStruct(dims, kind)


def sigmoid(v):
    return 0.5 * jnp.tanh(0.5 * v) + 0.5


def silu(v):
    return v * sigmoid(v)


def silu_slope(v):
    s = sigmoid(v)
    return s * (1.0 + v * (1.0 - s))


def dot(left, right, left_dim=1, right_dim=0):
    return lax.dot_general(
        left, right, (((left_dim,), (right_dim,)), ((), ())), preferred_element_type=F32
    )


def normalise(x):
    centred = x - jnp.mean(x, axis=-1, keepdims=True)
    spread = jnp.mean(centred * centred, axis=-1, keepdims=True)
    scale = lax.rsqrt(spread + EPS)
    return centred * scale, scale


def row_valid(start, rows, length):
    place = start + lax.broadcasted_iota(jnp.int32, (rows, 1), 0)
    return (place < length).astype(F32)


def lasting(microseconds):
    return pl.CostEstimate(
        flops=int(microseconds * 1.0e9),
        bytes_accessed=int(microseconds * 3.0e6),
        transcendentals=0,
    )


def params(**more):
    return pltpu.CompilerParams(vmem_limit_bytes=VMEM_BYTES, **more)


def power(base, exponent):
    result = None
    square = base
    while exponent:
        if exponent % 2:
            result = square if result is None else result * square
        exponent //= 2
        if exponent:
            square = square * square
    return result


def shifted(array, span, reverse=False):
    row = lax.broadcasted_iota(jnp.int32, array.shape, 1)
    if reverse:
        return jnp.where(row < CHUNKS - span, pltpu.roll(array, CHUNKS - span, 1), 0.0)
    return jnp.where(row >= span, pltpu.roll(array, span, 1), 0.0)


def entering(last, rate, steps, reverse=False):
    weight = power(rate, steps)
    span = 1
    while span < CHUNKS:
        last = last + weight * shifted(last, span, reverse)
        weight = weight * weight
        span *= 2
    return shifted(last, 1, reverse)


def entering_pair(last, slope, rate, steps):
    weight = power(rate, steps)
    tilt = float(steps) * power(rate, steps - 1)
    span = 1
    while span < CHUNKS:
        moved = shifted(last, span)
        slope = slope + weight * shifted(slope, span) + tilt * moved
        last = last + weight * moved
        tilt = 2.0 * weight * tilt
        weight = weight * weight
        span *= 2
    return shifted(last, 1), shifted(slope, 1)


def average_forward_kernel(
    length_ref,
    x_ref,
    gain_ref,
    shift_ref,
    rate_ref,
    coef_ref,
    skip_ref,
    normed_ref,
    mixed_ref,
    pre_ref,
    own_ref,
    scale_ref,
    rows_buf,
    m_buf,
    y_buf,
):
    length = length_ref[0]
    count, width = x_ref.shape
    own = mixed_ref.shape[1]
    dims = rate_ref.shape[0]
    steps = count // CHUNKS
    pitch = steps + 1
    mine = pl.ds(pl.multiple_of(lax.axis_index("section") * own, LANES), own)

    def norm_strip(i, carry):
        start = pl.multiple_of(i * STRIP, STRIP)
        here = pl.ds(start, STRIP)
        n, scale = normalise(x_ref[here, :].astype(F32))
        rows_buf[...] = n
        normed_ref[here, :] = (n * gain_ref[...] + shift_ref[...]).astype(BF16)
        part = rows_buf[:, mine]
        own_ref[here, :] = part
        scale_ref[here, :] = jnp.broadcast_to(scale, (STRIP, LANES))
        masked = (part * gain_ref[:, mine] + shift_ref[:, mine]) * row_valid(start, STRIP, length)
        for group in range(own // LANES):
            m_buf[group, pl.ds(start + start // steps, STRIP), :] = masked[:, group * LANES : (group + 1) * LANES]
        return carry

    lax.fori_loop(0, count // STRIP, norm_strip, 0)

    for group in range(own // LANES):
        lanes = slice(group * LANES, (group + 1) * LANES)
        rates = rate_ref[:, :, lanes]
        coefs = coef_ref[:, :, lanes]
        m_part, y_part = m_buf.at[group], y_buf.at[group]

        def finals(t, states):
            return rates * states + m_part[pl.ds(t, CHUNKS, stride=pitch), :]

        ends = lax.fori_loop(0, steps, finals, jnp.zeros_like(rates), unroll=UNROLL)

        def outputs(t, states):
            states = rates * states + m_part[pl.ds(t, CHUNKS, stride=pitch), :]
            y_part[pl.ds(t, CHUNKS, stride=pitch), :] = jnp.sum(coefs * states, axis=0)
            return states

        lax.fori_loop(0, steps, outputs, entering(ends, rates, steps), unroll=UNROLL)

    def mix_strip(i, carry):
        start = pl.multiple_of(i * STRIP, STRIP)
        here = pl.ds(start, STRIP)
        there = pl.ds(start + start // steps, STRIP)
        for group in range(own // LANES):
            lanes = slice(group * LANES, (group + 1) * LANES)
            pre = y_buf[group, there, :] + skip_ref[:, lanes] * m_buf[group, there, :]
            pre_ref[here, lanes] = pre.astype(BF16)
            mixed_ref[here, lanes] = silu(pre).astype(BF16)
        return carry

    lax.fori_loop(0, count // STRIP, mix_strip, 0)


def average_forward(length, x, gain, shift, rate, coef, skip):
    count, width = x.shape
    own = skip.shape[1]
    groups = own // LANES
    return pl.pallas_call(
        average_forward_kernel,
        out_shape=(
            shape((count, width), BF16),
            shape((count, own), BF16),
            shape((count, own), BF16),
            shape((count, own), F32),
            shape((count, LANES), F32),
        ),
        in_specs=[smem()] + [vmem()] * 6,
        out_specs=(vmem(),) * 5,
        scratch_shapes=[
            pltpu.VMEM((STRIP, width), F32),
            pltpu.VMEM((groups, count + CHUNKS, LANES), F32),
            pltpu.VMEM((groups, count + CHUNKS, LANES), F32),
        ],
        cost_estimate=lasting(13),
        compiler_params=params(),
    )(length, x, gain, shift, rate, coef, skip)


def average_backward_work(beside, r):
    length = r.length[0]
    count, own = r.z.shape
    dims = r.rate.shape[0]
    steps = count // CHUNKS
    pitch = steps + 1
    groups = own // LANES
    part_size = dims // 2
    gain_ref, shift_ref = r.norm.at[0:1, :], r.norm.at[1:2, :]
    if beside:
        peers = plane()
        sems, piece = (r.send, r.recv), block_piece(r.whole)
        r.whole[peers[0]] = r.block[...]
        greet(peers[1], peers[2])
        begun = [gather_begin(r.whole, piece, peers, sems, half) for half in range(2)]

    def load_strip(i, carry):
        start = pl.multiple_of(i * STRIP, STRIP)
        here = pl.ds(start, STRIP)
        valid = row_valid(start, STRIP, length)
        there = pl.ds(start + start // steps, STRIP)
        for group in range(groups):
            lanes = slice(group * LANES, (group + 1) * LANES)
            r.m_buf[group, there, :] = (
                r.own_n[here, lanes] * gain_ref[:, lanes] + shift_ref[:, lanes]
            ) * valid
            slope = silu_slope(r.pre[here, lanes].astype(F32))
            r.g_buf[group, there, :] = r.gmixed[here, lanes] * slope
        return carry

    lax.fori_loop(0, count // STRIP, load_strip, 0)

    passed = None
    for group in range(groups):
        lanes = slice(group * LANES, (group + 1) * LANES)
        rates = r.rate[:, :, lanes]
        coefs = r.coef[:, :, lanes]
        m_part, g_part, r_part = r.m_buf.at[group], r.g_buf.at[group], r.r_buf.at[group]
        blank = jnp.zeros_like(rates)

        def back_finals(t, carry):
            states, slopes = carry
            g = g_part[pl.ds(steps - 1 - t, CHUNKS, stride=pitch), :]
            return rates * states + g, rates * slopes + states

        ends, end_slopes = lax.fori_loop(0, steps, back_finals, (blank, blank), unroll=UNROLL)
        starts = entering(ends, rates, steps, reverse=True)

        for half in range(2):
            first = half * part_size
            some = r.rate[first : first + part_size, :, lanes]
            empty = jnp.zeros_like(some)

            def sweep(t, carry):
                states, slopes, of_states, of_slopes = carry
                x = m_part[pl.ds(t, CHUNKS, stride=pitch), :]
                g = g_part[pl.ds(t, CHUNKS, stride=pitch), :]
                slopes = some * slopes + states
                states = some * states + x
                return states, slopes, of_states + g * states, of_slopes + g * slopes

            states, slopes, of_states, of_slopes = lax.fori_loop(
                0, steps, sweep, (empty,) * 4, unroll=UNROLL
            )
            back, back_slope = ends[first : first + part_size], end_slopes[first : first + part_size]
            state, slope = entering_pair(states, slopes, some, steps)
            of_states = of_states + state * (some * back)
            of_slopes = of_slopes + slope * (some * back) + state * (back + some * back_slope)
            r.sums[first : first + part_size, lanes] = jnp.sum(of_states, axis=1)
            r.sums[dims + first : dims + first + part_size, lanes] = jnp.sum(of_slopes, axis=1)

        def back_outputs(t, states):
            here = pl.ds(steps - 1 - t, CHUNKS, stride=pitch)
            states = rates * states + g_part[here, :]
            r_part[here, :] = jnp.sum(coefs * states, axis=0)
            return states

        lax.fori_loop(0, steps, back_outputs, starts, unroll=UNROLL)
        if beside and passed is None:
            passed = gather_forward(r.whole, piece, peers, sems, *begun)

    ones = jnp.ones((CHUNKS, own), BF16)
    first = lax.broadcasted_iota(jnp.int32, (CHUNKS, LANES), 0) == 0

    def finish(i, carry):
        start = pl.multiple_of(i * LANES, LANES)
        here = pl.ds(start, LANES)
        valid = row_valid(start, LANES, length)
        there = pl.ds(start + start // steps, LANES)
        of_gain, of_shift, of_skip = carry
        smoothed = jnp.concatenate([r.r_buf[k, there, :] for k in range(groups)], axis=1)
        gpre = jnp.concatenate([r.g_buf[k, there, :] for k in range(groups)], axis=1)
        masked = jnp.concatenate([r.m_buf[k, there, :] for k in range(groups)], axis=1)
        n = r.own_n[here, :]
        gmasked = r.skip[...] * gpre + smoothed
        gnormed = gmasked * valid + r.gvalue[here, :]
        e = gnormed * gain_ref[...]
        z = r.scale[here, 0:1] * e + r.resid[here, :]
        r.z[here, :] = z.astype(BF16)
        mean_row = dot(ones, e.astype(BF16), 1, 1)
        slope_row = dot(ones, (e * n).astype(BF16), 1, 1)
        r.stats[:, here] = jnp.where(first, mean_row, slope_row)
        return (
            of_gain + jnp.sum(gnormed * n, axis=0, keepdims=True),
            of_shift + jnp.sum(gnormed, axis=0, keepdims=True),
            of_skip + jnp.sum(gpre * masked, axis=0, keepdims=True),
        )

    blank_row = jnp.zeros((1, own), F32)
    of_gain, of_shift, of_skip = lax.fori_loop(
        0, count // LANES, finish, (blank_row, blank_row, blank_row)
    )
    last = 2 * dims
    r.sums[last : last + 1, :] = of_gain
    r.sums[last + 1 : last + 2, :] = of_shift
    r.sums[last + 2 : last + 3, :] = of_skip
    r.sums[last + 3 : last + 8, :] = jnp.zeros((5, own), F32)
    if beside:
        gather_finish(r.whole, piece, peers, sems, *begun, passed)


def average_backward(
    length, gmixed, gvalue, k, resid, norm, rate, coef, skip, block, ident, after=()
):
    count, own = gmixed.shape
    dims = rate.shape[0]
    buffer = pltpu.VMEM((own // LANES, count + CHUNKS, LANES), F32)
    sems = pltpu.SemaphoreType.DMA((6,))
    given = dict(
        gmixed=gmixed,
        gvalue=gvalue,
        pre=k.pre,
        own_n=k.own_n,
        scale=k.scale,
        resid=resid,
        norm=norm,
        rate=rate,
        coef=coef,
        skip=skip,
    )
    beside = block is not None
    outs, held = {}, {}
    if beside:
        given.update(block=block)
        outs.update(whole=(shape((4,) + block.shape, BF16), VMEM))
        held.update(send=sems, recv=sems)
    return transfer(
        functools.partial(average_backward_work, beside),
        dict(length=(length, SMEM), **{name: (a, VMEM) for name, a in given.items()}),
        dict(
            z=(shape((count, own), BF16), VMEM),
            stats=(shape((CHUNKS, count), F32), VMEM),
            sums=(shape((2 * dims + 8, own), F32), VMEM),
            **outs,
        ),
        dict(m_buf=buffer, g_buf=buffer, r_buf=buffer, **held),
        ident,
        17,
        after,
    )


def unfold(packed, in_w, out_w, shards, sems):
    wide, width = out_w.shape
    few = wide // shards
    low = in_w.shape[1]
    copies = [pltpu.make_async_copy(packed.at[:, pl.ds(0, low)], in_w, sems.at[0])]
    for shard in range(shards):
        for half in range(2):
            start = shard * (width // shards) + half * few
            columns = pl.ds(half * (width // 2), width // 2)
            copies.append(
                pltpu.make_async_copy(
                    packed.at[pl.ds(start, few), pl.ds(low, width // 2)],
                    out_w.at[pl.ds(shard * few, few), columns],
                    sems.at[len(copies)],
                )
            )
    return copies


def attention_forward_block(
    length,
    start,
    normed_ref,
    mixed_ref,
    in_ref,
    bias_ref,
    pair_ref,
    offset_ref,
    part_ref,
    update_ref,
    shared_ref,
    reset_ref,
    cand_ref,
    value_ref,
    att_ref,
    gated_ref,
    probs_ref,
    out_w_ref,
):
    rows = normed_ref.shape[0]
    wide = value_ref.shape[1]
    own = update_ref.shape[1]
    keyed = shared_ref.shape[1]
    value = dot(normed_ref[...], in_ref[:, :wide]) + bias_ref[:, :wide]
    value_ref[...] = value.astype(BF16)
    values = silu(value).astype(BF16)
    low = wide
    update = dot(mixed_ref[...], in_ref[:, low : low + own]) + bias_ref[:, low : low + own]
    update_ref[...] = update.astype(BF16)
    low += own
    shared = dot(mixed_ref[...], in_ref[:, low : low + keyed]) + bias_ref[:, low : low + keyed]
    shared_ref[...] = shared.astype(BF16)
    low += keyed
    reset = dot(mixed_ref[...], in_ref[:, low : low + wide]) + bias_ref[:, low : low + wide]
    reset_ref[...] = reset.astype(BF16)
    low += wide
    cand_ref[...] = (
        dot(mixed_ref[...], in_ref[:, low : low + own]) + bias_ref[:, low : low + own]
    ).astype(BF16)
    shared = silu(shared)
    reset = silu(reset)
    queries = (shared * pair_ref[0:1, :] + offset_ref[...]).astype(BF16)
    keys = (shared * pair_ref[1:2, :]).astype(BF16)
    for block in range(rows // ATT):
        here = slice(block * ATT, (block + 1) * ATT)
        begin = start + block * ATT
        scores = dot(queries[here], keys[here], 1, 1) * keyed**-0.5
        key_place = begin + lax.broadcasted_iota(jnp.int32, (ATT, ATT), 1)
        scores = jnp.where(key_place < length, scores, NEGATIVE)
        raised = jnp.exp(scores - jnp.max(scores, axis=-1, keepdims=True))
        probs = (raised / jnp.sum(raised, axis=-1, keepdims=True)).astype(BF16)
        probs_ref[here, :] = probs
        attended = dot(probs, values[here]) * row_valid(begin, ATT, length)
        att_ref[here, :] = attended.astype(BF16)
        gated_ref[here, :] = (attended * reset[here]).astype(BF16)
    part_ref[...] = dot(gated_ref[...], out_w_ref[...]).astype(BF16)


def attention_backward_block(
    length,
    start,
    mine,
    gout_ref,
    gupdate_ref,
    shared_ref,
    reset_ref,
    value_ref,
    att_ref,
    probs_ref,
    in_ref,
    pair_ref,
    offset_ref,
    gmixed_ref,
    gnormed_ref,
    gbase_ref,
    gvalue_ref,
    bias_ref,
    pair_sum_ref,
    out_w_ref,
):
    rows = gout_ref.shape[0]
    total = bias_ref.shape[1]
    wide = value_ref.shape[1]
    own = gupdate_ref.shape[1]
    keyed = shared_ref.shape[1]
    valid = row_valid(start, rows, length)
    ggated = dot(gout_ref[...], out_w_ref[...], 1, 1)
    reset = reset_ref[...].astype(F32)
    gattended = (ggated * silu(reset) * valid).astype(BF16)
    greset = ggated * att_ref[...].astype(F32) * silu_slope(reset)
    value = value_ref[...].astype(F32)
    values = silu(value).astype(BF16)
    shared_pre = shared_ref[...].astype(F32)
    shared = silu(shared_pre)
    scale_q, scale_k = pair_ref[0:1, :], pair_ref[1:2, :]
    queries = (shared * scale_q + offset_ref[...]).astype(BF16)
    keys = (shared * scale_k).astype(BF16)
    gq_parts, gk_parts, gv_parts = [], [], []
    for block in range(rows // ATT):
        here = slice(block * ATT, (block + 1) * ATT)
        probs = probs_ref[here, :]
        gprobs = dot(gattended[here], values[here], 1, 1)
        gv_parts.append(dot(probs, gattended[here], 0, 0))
        probs = probs.astype(F32)
        gscores = probs * (gprobs - jnp.sum(probs * gprobs, axis=-1, keepdims=True))
        key_place = start + block * ATT + lax.broadcasted_iota(jnp.int32, (ATT, ATT), 1)
        gscores = jnp.where(key_place < length, gscores, 0.0)
        gscores = (gscores * keyed**-0.5).astype(BF16)
        gq_parts.append(dot(gscores, keys[here]))
        gk_parts.append(dot(gscores, queries[here], 0, 0))
    gqueries = jnp.concatenate(gq_parts, axis=0)
    gkeys = jnp.concatenate(gk_parts, axis=0)
    gvalue = jnp.concatenate(gv_parts, axis=0) * silu_slope(value)
    gshared = (gqueries * scale_q + gkeys * scale_k) * silu_slope(shared_pre)
    pair_sum_ref[0:1, :] += jnp.sum(gqueries * shared, axis=0, keepdims=True)
    pair_sum_ref[1:2, :] += jnp.sum(gkeys * shared, axis=0, keepdims=True)
    pair_sum_ref[2:3, :] += jnp.sum(gqueries, axis=0, keepdims=True)
    gupdate = gupdate_ref[...]
    gcand = gout_ref[:, mine]
    low = 0
    for piece in (gvalue, gupdate, gshared, greset, gcand):
        size = piece.shape[1]
        bias_ref[0:1, low : low + size] += jnp.sum(piece.astype(F32), axis=0, keepdims=True)
        if low:
            gbase_ref[:, low - wide : low - wide + size] = piece.astype(BF16)
        else:
            gvalue_ref[...] = piece.astype(BF16)
        low += size
    gmixed_ref[...] = dot(gbase_ref[...], in_ref[:, wide:total], 1, 1).astype(BF16)
    gnormed_ref[...] = dot(gvalue_ref[...], in_ref[:, :wide], 1, 1).astype(BF16)


def feed_forward_kernel(
    x_ref, gain_ref, shift_ref, w_ref, bias_ref, part_ref, pre_ref, n_ref, normed_ref, scale_ref
):
    hidden = pre_ref.shape[1]
    n, scale = normalise(x_ref[...].astype(F32))
    n_ref[...] = n.astype(BF16)
    scale_ref[...] = jnp.broadcast_to(scale, scale_ref.shape)
    normed_ref[...] = (n * gain_ref[...] + shift_ref[...]).astype(BF16)
    pre = dot(normed_ref[...], w_ref[:, :hidden]) + bias_ref[...]
    pre_ref[...] = pre.astype(BF16)
    part_ref[...] = dot(silu(pre).astype(BF16), w_ref[:, hidden:]).astype(BF16)


def feed_backward_block(
    g_ref, pre_ref, n_ref, gain_ref, w_ref, part_ref, stats_ref, gpre_ref, act_ref, sums_ref, bias_ref, lanes
):
    hidden = pre_ref.shape[1]
    width = n_ref.shape[1]
    g = g_ref[...]
    pre = pre_ref[...].astype(F32)
    s = sigmoid(pre)
    act_ref[...] = (pre * s).astype(BF16)
    gpre = dot(g, w_ref[:, hidden:], 1, 1) * (s * (1.0 + pre * (1.0 - s)))
    bias_ref[0:1, :] += jnp.sum(gpre, axis=0, keepdims=True)
    gpre_ref[...] = gpre.astype(BF16)
    part = dot(gpre_ref[...], w_ref[:, :hidden], 1, 1)
    part_ref[...] = part.astype(BF16)
    n = n_ref[...].astype(F32)
    sums_ref[0:1, :] += jnp.sum(part * n, axis=0, keepdims=True)
    sums_ref[1:2, :] += jnp.sum(part, axis=0, keepdims=True)
    sums_ref[2:3, :] += jnp.sum(g.astype(F32), axis=0, keepdims=True)
    e = part * gain_ref[...]
    ones = jnp.ones((CHUNKS, width), BF16)
    mean_row = dot(ones, e.astype(BF16), 1, 1)
    slope_row = dot(ones, (e * n).astype(BF16), 1, 1)
    first = lax.broadcasted_iota(jnp.int32, mean_row.shape, 0) == 0
    stats_ref[:, lanes] = jnp.where(first, mean_row, slope_row)


def plane():
    me = lax.axis_index("section")
    across = me + 1 - 2 * (me % 2)
    along = me + 2 - 4 * (me // 2)
    return me, across, along, across + along - me


def greet(*others):
    barrier = pltpu.get_barrier_semaphore()
    for other in others:
        pl.semaphore_signal(barrier, inc=1, device_id={"section": other}, device_id_type=MESH)
    pl.semaphore_wait(barrier, len(others))


def link(source, target, sems, index, other):
    send, recv = sems
    return pltpu.make_async_remote_copy(
        src_ref=source,
        dst_ref=target,
        send_sem=send.at[index],
        recv_sem=recv.at[index],
        device_id={"section": other},
        device_id_type=MESH,
    )


def strips(count, work):
    def one(i, carry):
        work(pl.multiple_of(i * STRIP, STRIP))
        return carry

    lax.fori_loop(0, count // STRIP, one, 0)


def widen(block):
    rows, columns = block.shape
    if columns < LANES:
        block = jnp.concatenate((block, jnp.zeros((rows, LANES - columns), F32)), axis=1)
    return block.astype(BF16)


def grad_tiles(left, right, store, begin, end):
    def one(i, carry):
        rows = pl.ds(pl.multiple_of(i * TILE, TILE), TILE)
        store(rows, dot(left[:, rows], right[...], 0, 0).astype(BF16))
        return carry

    lax.fori_loop(begin, end, one, 0)


def gather_begin(out, piece, peers, sems, half):
    me, across, along, far = peers
    here = out.at[piece(me, half)]
    order = ((along, 0), (across, 1)) if half == 0 else ((across, 1), (along, 0))
    started = {}
    for other, way in order:
        copy = link(here, here, sems, 2 * half + way, other)
        copy.start()
        started[way] = copy
    return started


def gather_forward(out, piece, peers, sems, zero, one):
    me, across, along, far = peers
    zero[0].wait_recv()
    passing = out.at[piece(along, 0)]
    first = link(passing, passing, sems, 4, across)
    first.start()
    one[1].wait_recv()
    passing = out.at[piece(across, 1)]
    second = link(passing, passing, sems, 5, along)
    second.start()
    return first, second


def gather_finish(out, piece, peers, sems, zero, one, passed=None):
    first, second = passed or gather_forward(out, piece, peers, sems, zero, one)
    zero[1].wait_recv()
    one[0].wait_recv()
    first.wait_recv()
    second.wait_recv()
    for copy in (zero[0], zero[1], one[0], one[1], first, second):
        copy.wait_send()


def copy_sems(count):
    return [pltpu.SemaphoreType.DMA((count,)), pltpu.SemaphoreType.DMA((count,))]


def comm_params(ident):
    return params(collective_id=ident, has_side_effects=True)


def own_slice(source, target, sem, own):
    start = pl.multiple_of(lax.axis_index("section") * own, LANES)
    return pltpu.make_async_copy(source.at[:, pl.ds(start, own)], target, sem)


def stats_total(stats, got, stage, peers, sems, index):
    me, across, along, far = peers
    first = link(stats, got.at[0], sems, index, across)
    first.start()
    first.wait_recv()
    stage[...] = stats[...] + got[0]
    second = link(stage, got.at[1], sems, index + 1, along)
    second.start()
    second.wait_recv()
    first.wait_send()
    second.wait_send()
    return stage[...] + got[1]


def transfer(work, ins, outs, scratch, ident, microseconds, after=(), first=None, rows=ROWS):
    order = [n for kind in (FETCH, BLOCKS, LATE, OWN_PART) for n in ins if ins[n][1] == kind]
    stored = [n for n, (_, how) in outs.items() if how == STORE]
    buffers, places, low = {}, {}, 0
    for name in order + stored:
        if name in stored:
            buffers[name] = pltpu.VMEM(outs[name][0].shape, outs[name][0].dtype)
        else:
            array, how = ins[name]
            columns = array.shape[1] // (4 if how == OWN_PART else 1)
            buffers[name] = pltpu.VMEM((array.shape[0], columns), array.dtype)
        places[name] = low
        low += ins[name][0].shape[0] // rows if name in ins and ins[name][1] == BLOCKS else 1
    by_blocks = [n for n in order if ins[n][1] == BLOCKS]

    def kernel(*refs):
        refs = refs[len(after) :]
        names = list(ins) + list(outs)
        given = dict(zip(names, refs))
        refs = refs[len(names) :]
        own_names = list(buffers) + [LOCAL] + list(scratch)
        held = dict(zip(own_names, refs))
        r = types.SimpleNamespace(**{**given, **held})
        local = held[LOCAL]

        def copy(name):
            sem = local.at[places[name]]
            if name in stored:
                return pltpu.make_async_copy(held[name], given[name], sem)
            if ins[name][1] == OWN_PART:
                return own_slice(given[name], held[name], sem, held[name].shape[1])
            return pltpu.make_async_copy(given[name], held[name], sem)

        def block_copy(name, block):
            here = rows_of(block, rows)
            source, target = given[name].at[here, :], held[name].at[here, :]
            return pltpu.make_async_copy(source, target, local.at[places[name] + block])

        def start(*kinds):
            for name in order:
                if ins[name][1] in kinds:
                    copy(name).start()

        def wait_block(block):
            for name in by_blocks:
                block_copy(name, block).wait()

        start(FETCH)
        if first:
            first(r)
        if by_blocks:
            for block in range(ins[by_blocks[0]][0].shape[0] // rows):
                for name in by_blocks:
                    block_copy(name, block).start()
        start(LATE, OWN_PART)
        r.wait = lambda *which: [copy(n).wait() for n in which]
        r.store = lambda *which: [copy(n).start() for n in which]
        r.wait_block = wait_block
        work(r)
        for name in stored:
            copy(name).wait()

    spec = {SMEM: smem, VMEM: vmem}
    return pl.pallas_call(
        kernel,
        out_shape=tuple(o for o, _ in outs.values()),
        in_specs=[hbm()] * len(after) + [spec.get(how, hbm)() for _, how in ins.values()],
        out_specs=tuple(spec.get(how, hbm)() for _, how in outs.values()),
        scratch_shapes=list(buffers.values())
        + [pltpu.SemaphoreType.DMA((max(low, 1),))]
        + list(scratch.values()),
        cost_estimate=lasting(microseconds),
        compiler_params=params() if ident is None else comm_params(ident),
    )(*after, *[a for a, _ in ins.values()])


def rows_of(block, rows=ROWS):
    return pl.ds(pl.multiple_of(block * rows, rows), rows)


def owned(block, owner, half, own, rows):
    start = pl.multiple_of(block * rows + half * (rows // 2), rows // 2)
    return pl.ds(start, rows // 2), pl.ds(pl.multiple_of(owner * own, LANES), own)


def sum_scratch(name, count, own, rows=ROWS):
    buffer = pltpu.VMEM((2, count // 2, own), BF16)
    sems = pltpu.SemaphoreType.DMA((6 * (count // rows),))
    return {
        name + "_early": buffer,
        name + "_direct": buffer,
        name + "_late": buffer,
        name + "_stage": buffer,
        name + "_send": sems,
        name + "_recv": sems,
    }


def block_sum(r, name, part, peers, own, piece=None, place=None, rows=ROWS):
    if piece is None:
        piece = functools.partial(owned, own=own, rows=rows)
        place = functools.partial(rows_of, rows=rows // 2)
    me, across, along, far = peers
    early, direct, late, stage, send, recv = (
        getattr(r, name + end) for end in ("_early", "_direct", "_late", "_stage", "_send", "_recv")
    )
    sems = (send, recv)
    ways = ((across, along), (along, across))

    def early_copy(block, half):
        source = part.at[piece(block, far, half)]
        target = early.at[half, place(block)]
        return link(source, target, sems, block * 6 + half, ways[half][0])

    def direct_copy(block, half):
        first = ways[half][0]
        source = part.at[piece(block, first, half)]
        target = direct.at[half, place(block)]
        return link(source, target, sems, block * 6 + 2 + half, first)

    def late_copy(block, half):
        source = stage.at[half, place(block)]
        target = late.at[half, place(block)]
        return link(source, target, sems, block * 6 + 4 + half, ways[half][1])

    def begin(block):
        for half in range(2):
            early_copy(block, half).start()
        for half in range(2):
            direct_copy(block, half).start()

    def forward(block):
        for half in range(2):
            early_copy(block, half).wait_recv()
            here = place(block)
            passed = part[piece(block, ways[half][1], half)].astype(F32)
            stage[half, here, :] = (passed + early[half, here, :].astype(F32)).astype(BF16)
            late_copy(block, half).start()

    def arrived(block, half):
        direct_copy(block, half).wait_recv()
        late_copy(block, half).wait_recv()

    def total(block, half, start):
        row, column = piece(block, me, half)
        here = pl.ds(place(block).start + start, STRIP)
        mine = part[pl.ds(row.start + start, STRIP), column].astype(F32)
        return mine + direct[half, here, :].astype(F32) + late[half, here, :].astype(F32)

    def end(block):
        for half in range(2):
            early_copy(block, half).wait_send()
            direct_copy(block, half).wait_send()
            late_copy(block, half).wait_send()

    return types.SimpleNamespace(begin=begin, forward=forward, arrived=arrived, total=total, end=end)


def gather_sems(count):
    return pltpu.SemaphoreType.DMA((6 * (count // ROWS),))


def block_gather(out, peers, own, sems):
    me, across, along, far = peers

    def copy(block, owner, half, index, other):
        place = out.at[owned(block, owner, half, own, ROWS)]
        return link(place, place, sems, block * 6 + index, other)

    def own_copy(block, half, way):
        return copy(block, me, half, 2 * half + way, (along, across)[way])

    def pass_copy(block, half):
        return copy(block, (along, across)[half], half, 4 + half, (across, along)[half])

    def begin(block):
        for half, way in ((0, 0), (1, 1), (1, 0), (0, 1)):
            own_copy(block, half, way).start()

    def forward(block):
        for half in range(2):
            own_copy(block, half, half).wait_recv()
            pass_copy(block, half).start()

    def arrive(block):
        own_copy(block, 0, 1).wait_recv()
        own_copy(block, 1, 0).wait_recv()
        for half in range(2):
            pass_copy(block, half).wait_recv()

    def sent(block):
        for half in range(2):
            pass_copy(block, half).wait_send()
            for way in range(2):
                own_copy(block, half, way).wait_send()

    return types.SimpleNamespace(begin=begin, forward=forward, arrive=arrive, sent=sent)


def pipeline(count, compute, sums, finish, gather, extra=None, between=None, before=None, rows=ROWS):
    blocks = count // rows
    if before:
        before.begin(0)
        before.begin(1)
        before.forward(0)

    def tick(i, carry):
        if before:

            @pl.when(i < blocks - 2)
            def _():
                before.begin(i + 2)

            @pl.when(i < blocks - 1)
            def _():
                before.forward(i + 1)

            @pl.when(i < blocks)
            def _():
                before.arrive(i)

        @pl.when(i < blocks)
        def _():
            compute(i)
            for one in sums:
                one.begin(i)

        if between:
            between(i)

        @pl.when((i >= 1) & (i <= blocks))
        def _():
            for one in sums:
                one.forward(i - 1)

        @pl.when((i >= 2) & (i <= blocks + 1))
        def _():
            finish(i - 2)
            if gather:
                gather.begin(i - 2)

        if gather:

            @pl.when(i >= 3)
            def _():
                gather.forward(i - 3)

        if extra:
            extra(i)
        return carry

    lax.fori_loop(0, blocks + (3 if gather else 2), tick, 0)

    def close(i, carry):
        for one in sums:
            one.end(i)
        if gather:
            gather.arrive(i)
            gather.sent(i)
        if before:
            before.sent(i)
        return carry

    lax.fori_loop(0, blocks, close, 0)


def finish_strips(one, block, work, rows=ROWS):
    for half in range(2):
        one.arrived(block, half)

        def strip(start):
            row = pl.multiple_of(block * rows + half * (rows // 2), rows // 2) + start
            work(pl.ds(row, STRIP), one.total(block, half, start))

        strips(rows // 2, strip)


def views(refs, block, rows=ROWS):
    return [ref.at[rows_of(block, rows), :] for ref in refs]


def attention_forward(length, normed, mixed, packed, bias, pair, offset, x, shards, ident):
    count, width = normed.shape
    apart = mixed.shape[1] == width
    own = width // 4
    wide = width // 2
    keyed = pair.shape[1]
    low = packed.shape[1] - width // 2

    def weights(r):
        return unfold(r.packed, r.in_w, r.out_w, shards, r.fold)

    def first(r):
        for copy in weights(r):
            copy.start()

    def work(r):
        peers = plane()
        mine = pl.ds(pl.multiple_of(peers[0] * own, LANES), own)
        real = r.length[0]
        mixing = None
        if not apart:
            r.mixed[:, mine] = r.mixed_own[...]
        greet(peers[1], peers[2])
        if not apart:
            mixing = block_gather(r.mixed, peers, own, (r.mixed_send, r.mixed_recv))
        total = block_sum(r, "sum", r.part, peers, own)
        gather = block_gather(r.out, peers, own, (r.gather_send, r.gather_recv))
        saved = (r.update, r.shared, r.reset, r.cand, r.value, r.att, r.gated, r.probs)

        def compute(block):
            @pl.when(block == 0)
            def _():
                for copy in weights(r):
                    copy.wait()

            r.wait_block(block)
            attention_forward_block(
                real,
                block * ROWS,
                *views((r.normed, r.mixed), block),
                r.in_w,
                r.bias,
                r.pair,
                r.offset,
                *views((r.part,) + saved, block),
                r.out_w,
            )

        def finish(block):
            def strip(here, summed):
                pre = r.cand[here, :].astype(F32) + summed
                r.hidden[here, :] = pre.astype(BF16)
                old = r.x[here, :].astype(F32)
                made = old + sigmoid(r.update[here, :].astype(F32)) * (silu(pre) - old)
                r.out[here, mine] = made.astype(BF16)

            finish_strips(total, block, strip)

        def extra(i):
            @pl.when(i == 0)
            def _():
                r.wait("x")

            @pl.when(i == count // ROWS)
            def _():
                if not apart:
                    r.store("mixed")
                r.store("update", "shared", "reset", "value", "att", "gated", "probs")

        pipeline(count, compute, (total,), finish, gather, extra, before=mixing)

    rows = lambda columns: (shape((count, columns), BF16), STORE)
    return transfer(
        work,
        dict(
            length=(length, SMEM),
            packed=(packed, RAW),
            normed=(normed, BLOCKS),
            **(dict(mixed=(mixed, BLOCKS)) if apart else dict(mixed_own=(mixed, VMEM))),
            x=(x, OWN_PART),
            bias=(bias, VMEM),
            pair=(pair, VMEM),
            offset=(offset, VMEM),
        ),
        dict(
            out=(shape((count, width), BF16), VMEM),
            hidden=(shape((count, own), BF16), VMEM),
            **({} if apart else dict(mixed=rows(width))),
            update=rows(own),
            shared=rows(keyed),
            reset=rows(wide),
            value=rows(wide),
            att=rows(wide),
            gated=rows(wide),
            probs=rows(ATT),
        ),
        dict(
            part=pltpu.VMEM((count, width), BF16),
            cand=pltpu.VMEM((count, own), BF16),
            in_w=pltpu.VMEM((width, low), BF16),
            out_w=pltpu.VMEM((wide, width), BF16),
            fold=pltpu.SemaphoreType.DMA((2 * shards + 1,)),
            mixed_send=gather_sems(count),
            mixed_recv=gather_sems(count),
            **sum_scratch("sum", count, own),
            gather_send=gather_sems(count),
            gather_recv=gather_sems(count),
        ),
        ident,
        54,
        first=first,
    )


def gather_kernel(waits, *refs):
    own_ref, out_ref, send, recv = refs[waits:]
    count, own = own_ref.shape
    peers = plane()
    mine = pl.ds(pl.multiple_of(peers[0] * own, LANES), own)
    out_ref[:, mine] = own_ref[...]
    greet(peers[1], peers[2])
    whole = block_gather(out_ref, peers, own, (send, recv))
    blocks = count // ROWS
    for block in range(blocks):
        whole.begin(block)
        if block:
            whole.forward(block - 1)
    whole.forward(blocks - 1)
    for block in range(blocks):
        whole.arrive(block)
        whole.sent(block)


def gather_columns(own, ident, after=()):
    count, width = own.shape
    return pl.pallas_call(
        functools.partial(gather_kernel, len(after)),
        out_shape=shape((count, width * 4), BF16),
        in_specs=[hbm()] * len(after) + [vmem()],
        out_specs=vmem(),
        scratch_shapes=[gather_sems(count), gather_sems(count)],
        cost_estimate=lasting(20),
        compiler_params=comm_params(ident),
    )(*after, own)


def feed_forward_joined(x, gain, shift, weights, bias, own_out, ident):
    count, width = x.shape
    hidden = bias.shape[1]
    own = width // 4

    def work(r):
        peers = plane()
        mine = pl.ds(pl.multiple_of(peers[0] * own, LANES), own)
        greet(peers[1], peers[2])
        r.wait("weights")
        total = block_sum(r, "sum", r.part, peers, own)
        gather = block_gather(r.out, peers, own, (r.gather_send, r.gather_recv))

        def compute(block):
            r.wait_block(block)
            x_rows, *outs = views((r.x, r.part, r.pre, r.n, r.normed, r.scale), block)
            feed_forward_kernel(x_rows, r.gain, r.shift, r.weights, r.bias, *outs)

        def finish(block):
            def strip(here, summed):
                made = r.x[here, mine].astype(F32) + summed + r.own_out[...]
                r.out[here, mine] = made.astype(BF16)

            finish_strips(total, block, strip)

        def extra(i):
            @pl.when(i == count // ROWS)
            def _():
                r.store("pre", "n", "normed", "scale")

        pipeline(count, compute, (total,), finish, gather, extra)

    rows = lambda columns, kind=BF16: (shape((count, columns), kind), STORE)
    return transfer(
        work,
        dict(
            x=(x, BLOCKS),
            weights=(weights, FETCH),
            gain=(gain, VMEM),
            shift=(shift, VMEM),
            bias=(bias, VMEM),
            own_out=(own_out, VMEM),
        ),
        dict(
            out=(shape((count, width), BF16), VMEM),
            pre=rows(hidden),
            n=rows(width),
            normed=rows(width),
            scale=rows(LANES, F32),
        ),
        dict(
            part=pltpu.VMEM((count, width), BF16),
            **sum_scratch("sum", count, own),
            gather_send=gather_sems(count),
            gather_recv=gather_sems(count),
        ),
        ident,
        40,
    )


def feed_backward(given, k, p, weights, shards, ident, after=()):
    corrected = isinstance(given, tuple)
    both_ways = k.feed_pre is None
    count, width = k.middle.shape
    own = width // 4
    hidden = p.feed_in.shape[1]
    norms, gain = p.own, p.feed_gain
    blocks = count // ROWS

    def work(r):
        peers = plane()
        me, across, along, far = peers
        mine = pl.ds(pl.multiple_of(me * own, LANES), own)
        if corrected:
            r.z[:, mine] = r.z_own[...]
        greet(across, along)
        before = None
        if corrected:
            before = block_gather(r.z, peers, own, (r.z_send, r.z_recv))
        r.sums[...] = jnp.zeros_like(r.sums)
        r.bias[...] = jnp.zeros_like(r.bias)
        total = block_sum(r, "sum", r.part, peers, own)
        gather = block_gather(r.out, peers, own, (r.gather_send, r.gather_recv))

        def quarter(block, owner, half):
            size = count // 4
            return (
                pl.ds(pl.multiple_of(owner * size, size), size),
                pl.ds(half * (width // 2), width // 2),
            )

        if both_ways:
            last = block_sum(
                r, "last", r.made, peers, own, quarter, lambda block: pl.ds(0, count // 4)
            )

        def last_rows():
            for half in range(2):
                last.arrived(0, half)
                lanes = slice(half * (width // 2), (half + 1) * (width // 2))

                def strip(start):
                    here = pl.ds(start, STRIP)
                    row = pl.ds(pl.multiple_of(me * (count // 4), STRIP) + start, STRIP)
                    made = r.middle[row, lanes].astype(F32) + last.total(0, half, start)
                    r.block_out[here, lanes] = (made + r.out_bias[:, lanes]).astype(BF16)

                strips(count // 4, strip)

        def stats_copy(block, step):
            lanes = rows_of(block)
            source = (r.stats, r.stats_stage)[step].at[:, lanes]
            sems = (r.stats_send, r.stats_recv)
            other = (across, along)[step]
            return link(source, r.stats_got.at[step, :, lanes], sems, 2 * block + step, other)

        def compute(block):
            here = rows_of(block)

            @pl.when(block == 0)
            def _():
                r.wait("weights")
                if corrected:
                    sems = (r.means_send, r.means_recv)
                    r.means[...] = stats_total(
                        r.z_stats, r.means_got, r.means_stage, peers, sems, 0
                    )

            r.wait_block(block)
            if corrected:
                xn, xscale = normalise(r.x_full[here, :].astype(F32))
                means = r.means[:, here].T * (1.0 / width)
                z = r.z[here, :].astype(F32)
                g = z - xscale * (means[:, 0:1] + xn * means[:, 1:2])
                r.g[here, :] = g.astype(BF16)
            if both_ways:
                x_rows, *made = views((r.middle, r.made, r.pre, r.n, r.normed, r.scale), block)
                feed_forward_kernel(x_rows, r.gain, r.shift, r.weights, r.in_bias, *made)
            g_rows, pre_rows, n_rows = views((r.g, r.pre, r.n), block)
            part, gpre, act = views((r.part, r.gpre, r.act), block)
            feed_backward_block(
                g_rows,
                pre_rows,
                n_rows,
                r.gain,
                r.weights,
                part,
                r.stats,
                gpre,
                act,
                r.sums,
                r.bias,
                here,
            )
            stats_copy(block, 0).start()

        def finish(block):
            here = rows_of(block)
            stats_copy(block, 1).wait_recv()
            every = r.stats_stage[:, here] + r.stats_got[1, :, here]
            r.columns[here, :] = every.T * (1.0 / width)

            def strip(here, summed):
                e = summed * r.norms[2:3, :]
                n_own = r.n[here, mine].astype(F32)
                inner = e - r.columns[here, 0:1] - n_own * r.columns[here, 1:2]
                g = r.g[here, mine].astype(F32) + r.scale[here, 0:1] * inner
                g = g.astype(BF16).astype(F32)
                u = sigmoid(r.update[here, :].astype(F32))
                pre = r.hidden[here, :].astype(F32)
                s = sigmoid(pre)
                x = r.x[here, :].astype(F32)
                r.gupdate[here, :] = (g * (pre * s - x) * (u * (1.0 - u))).astype(BF16)
                r.resid[here, :] = g * (1.0 - u)
                r.out[here, mine] = (g * u * (s * (1.0 + pre * (1.0 - s)))).astype(BF16)

            finish_strips(total, block, strip)

        def small_grads():
            r.grad[:, hidden + width :] = jnp.zeros((width, LANES), BF16)
            size = width // shards
            for shard in range(shards):
                lanes = slice(shard * size, (shard + 1) * size)
                block = jnp.concatenate(
                    (r.sums[0:3, lanes], r.bias[0:1, lanes], jnp.zeros((SMALL - 4, size), F32)),
                    axis=0,
                )
                r.grad[shard * size : shard * size + SMALL, hidden + width :] = widen(block)

        def in_grad(rows, value):
            r.grad[rows, :hidden] = value

        def out_grad(rows, value):
            r.grad[rows, hidden : hidden + width] = value

        def extra(i):
            @pl.when((i >= 1) & (i <= blocks))
            def _():
                here = rows_of(i - 1)
                stats_copy(i - 1, 0).wait_recv()
                r.stats_stage[:, here] = r.stats[:, here] + r.stats_got[0, :, here]
                stats_copy(i - 1, 1).start()

            @pl.when(i == 0)
            def _():
                r.wait("update", "hidden", "x")
                if not both_ways:
                    r.wait("scale", "normed")

            if both_ways:

                @pl.when(i == blocks - 1)
                def _():
                    last.begin(0)

                @pl.when(i == blocks)
                def _():
                    last.forward(0)

                @pl.when(i == blocks + 2)
                def _():
                    last_rows()
                    last.end(0)

            @pl.when(i == blocks + 1)
            def _():
                r.store("gupdate", "resid")

        def between(i):
            @pl.when(i == blocks)
            def _():
                grad_tiles(r.normed, r.gpre, in_grad, 0, width // TILE)
                small_grads()
                grad_tiles(r.act, r.g, out_grad, 0, hidden // TILE)
                r.store("grad")

        pipeline(count, compute, (total,), finish, gather, extra, between, before)

        def close(i, carry):
            stats_copy(i, 0).wait_send()
            stats_copy(i, 1).wait_send()
            return carry

        lax.fori_loop(0, blocks, close, 0)

    if corrected:
        z_own, z_stats, x_full = given
        first = dict(z_own=(z_own, VMEM), x_full=(x_full, BLOCKS), z_stats=(z_stats, VMEM))
        both = pltpu.SemaphoreType.DMA((2,))
        extra_scratch = dict(
            g=pltpu.VMEM((count, width), BF16),
            z=pltpu.VMEM((count, width), BF16),
            z_send=gather_sems(count),
            z_recv=gather_sems(count),
            means=pltpu.VMEM((CHUNKS, count), F32),
            means_stage=pltpu.VMEM((CHUNKS, count), F32),
            means_got=pltpu.VMEM((2, CHUNKS, count), F32),
            means_send=both,
            means_recv=both,
        )
    else:
        first = dict(g=(given, BLOCKS))
        extra_scratch = {}
    extra_outs = {}
    if both_ways:
        saved = {}
        first.update(
            middle=(k.middle, BLOCKS),
            shift=(p.feed_shift, VMEM),
            in_bias=(p.feed_in, VMEM),
            out_bias=(p.feed_out, VMEM),
        )
        extra_outs.update(block_out=(shape((count // 4, width), BF16), VMEM))
        rows = pltpu.VMEM((count, width), BF16)
        slot = pltpu.VMEM((2, count // 4, width // 2), BF16)
        ends = pltpu.SemaphoreType.DMA((6,))
        extra_scratch.update(
            made=rows,
            pre=pltpu.VMEM((count, hidden), BF16),
            n=rows,
            normed=rows,
            scale=pltpu.VMEM((count, LANES), F32),
            last_early=slot,
            last_direct=slot,
            last_late=slot,
            last_stage=slot,
            last_send=ends,
            last_recv=ends,
        )
    else:
        saved = dict(
            pre=(k.feed_pre, BLOCKS),
            n=(k.feed_n, BLOCKS),
            scale=(k.feed_scale, LATE),
            normed=(k.feed_normed, LATE),
        )
    sems = pltpu.SemaphoreType.DMA((2 * blocks,))
    return transfer(
        work,
        dict(
            weights=(weights, FETCH),
            **first,
            **saved,
            update=(k.update, LATE),
            hidden=(k.hidden, LATE),
            x=(k.x, OWN_PART),
            gain=(gain, VMEM),
            norms=(norms, VMEM),
        ),
        dict(
            out=(shape((count, width), BF16), VMEM),
            gupdate=(shape((count, own), BF16), STORE),
            resid=(shape((count, own), F32), STORE),
            grad=(shape((width, hidden + width + LANES), BF16), STORE),
            **extra_outs,
        ),
        dict(
            part=pltpu.VMEM((count, width), BF16),
            gpre=pltpu.VMEM((count, hidden), BF16),
            act=pltpu.VMEM((count, hidden), BF16),
            sums=pltpu.VMEM((8, width), F32),
            bias=pltpu.VMEM((8, hidden), F32),
            stats=pltpu.VMEM((CHUNKS, count), F32),
            stats_stage=pltpu.VMEM((CHUNKS, count), F32),
            stats_got=pltpu.VMEM((2, CHUNKS, count), F32),
            columns=pltpu.VMEM((count, CHUNKS), F32),
            stats_send=sems,
            stats_recv=sems,
            **extra_scratch,
            **sum_scratch("sum", count, own),
            gather_send=gather_sems(count),
            gather_recv=gather_sems(count),
        ),
        ident,
        46,
        after,
    )


def attention_backward(length, gout, gupdate, k, packed, pair, offset, shards, ident, after=()):
    shared, reset, value, att, probs = k.saved
    count, width = gout.shape
    own = width // 4
    wide = width // 2
    keyed = pair.shape[1]
    total = packed.shape[1] - width // 2
    rows = 2 * ROWS
    blocks = count // rows
    few = wide // shards
    block_rows = width // shards

    def weights(r):
        return unfold(r.packed, r.in_w, r.out_w, shards, r.fold)

    def first(r):
        for copy in weights(r):
            copy.start()

    def work(r):
        peers = plane()
        mine = pl.ds(pl.multiple_of(peers[0] * own, LANES), own)
        real = r.length[0]
        greet(peers[1], peers[2])
        r.bias[...] = jnp.zeros_like(r.bias)
        r.pairs[...] = jnp.zeros_like(r.pairs)
        one = block_sum(r, "one", r.gmixed_part, peers, own, rows=rows)
        two = block_sum(r, "two", r.gvalue_part, peers, own, rows=rows)

        def compute(block):
            @pl.when(block == 0)
            def _():
                for copy in weights(r):
                    copy.wait()

            r.wait_block(block)
            attention_backward_block(
                real,
                block * rows,
                mine,
                *views((r.gout, r.gupdate, r.shared, r.reset, r.value, r.att, r.probs), block, rows),
                r.in_w,
                r.pair,
                r.offset,
                *views((r.gmixed_part, r.gvalue_part, r.gbase, r.gvalue), block, rows),
                r.bias,
                r.pairs,
                r.out_w,
            )

        def finish(block):
            def keep(out):
                def strip(here, summed):
                    out[here, :] = summed

                return strip

            finish_strips(one, block, keep(r.gmixed), rows)
            finish_strips(two, block, keep(r.gnormed), rows)

        def value_grad(rows, value):
            r.grad[rows, :wide] = value

        def base_grad(rows, value):
            r.grad[rows, wide:total] = value

        def out_grad(rows, value):
            for i in range(TILE // few):
                start = (rows.start // few + i) * block_rows
                for half in range(2):
                    here = pl.ds(pl.multiple_of(start + half * few, few), few)
                    r.grad[here, total : total + width // 2] = value[
                        i * few : (i + 1) * few, half * (width // 2) : (half + 1) * (width // 2)
                    ]

        def small_grads():
            last = total + width // 2
            r.grad[:, last:] = jnp.zeros((width, LANES), BF16)
            pieces = [r.bias[0:1, i * LANES : (i + 1) * LANES] for i in range(total // LANES)]
            block = jnp.concatenate(pieces + [r.pairs[0:3, :]], axis=0).astype(BF16)
            for shard in range(shards):
                r.grad[shard * block_rows : shard * block_rows + SMALL, last:] = block

        def extra(i):
            @pl.when(i == 0)
            def _():
                r.wait("normed", "mixed", "gated")

        def between(i):
            @pl.when(i == blocks)
            def _():
                small_grads()
                grad_tiles(r.mixed, r.gbase, base_grad, 0, width // TILE)
                grad_tiles(r.normed, r.gvalue, value_grad, 0, width // TILE)
                grad_tiles(r.gated, r.gout, out_grad, 0, wide // TILE)
                r.store("grad")

        pipeline(count, compute, (one, two), finish, None, extra, between, rows=rows)

    return transfer(
        work,
        dict(
            length=(length, SMEM),
            packed=(packed, RAW),
            gout=(gout, BLOCKS),
            gupdate=(gupdate, BLOCKS),
            shared=(shared, BLOCKS),
            reset=(reset, BLOCKS),
            value=(value, BLOCKS),
            att=(att, BLOCKS),
            probs=(probs, BLOCKS),
            normed=(k.normed, LATE),
            mixed=(k.mixed, LATE),
            gated=(k.gated, LATE),
            pair=(pair, VMEM),
            offset=(offset, VMEM),
        ),
        dict(
            gmixed=(shape((count, own), F32), VMEM),
            gnormed=(shape((count, own), F32), VMEM),
            grad=(shape((width, total + width // 2 + LANES), BF16), STORE),
        ),
        dict(
            gmixed_part=pltpu.VMEM((count, width), BF16),
            gvalue_part=pltpu.VMEM((count, width), BF16),
            gbase=pltpu.VMEM((count, total - wide), BF16),
            gvalue=pltpu.VMEM((count, wide), BF16),
            bias=pltpu.VMEM((8, total), F32),
            pairs=pltpu.VMEM((8, keyed), F32),
            in_w=pltpu.VMEM((width, total), BF16),
            out_w=pltpu.VMEM((wide, width), BF16),
            fold=pltpu.SemaphoreType.DMA((2 * shards + 1,)),
            **sum_scratch("one", count, own, rows),
            **sum_scratch("two", count, own, rows),
        ),
        ident,
        40,
        after,
        first,
        rows,
    )


def block_piece(whole):
    def piece(owner, half):
        size = whole.shape[1] // 2
        return owner, pl.ds(half * size, size), slice(None)

    return piece


def final_kernel(number, z_ref, stats_ref, x_ref, *refs):
    blocks, refs = refs[:number], refs[number:]
    out_ref, refs = refs[0], refs[1:]
    gathered, refs = refs[:number], refs[number:]
    land, x_own, got, stats_stage, total_buf, local_sem, send, recv = refs[:8]
    block_sems = [refs[8 + 2 * i : 10 + 2 * i] for i in range(number)]
    count, own = z_ref.shape
    quarter, width = out_ref.shape
    peers = plane()
    me = peers[0]

    def rows(owner):
        return pl.ds(pl.multiple_of(owner * quarter, quarter), quarter)

    mine = pl.ds(pl.multiple_of(me * own, LANES), own)
    fetch = pltpu.make_async_copy(x_ref.at[rows(me), :], x_own, local_sem)
    fetch.start()
    land[:, mine] = z_ref[rows(me), :]
    for block, whole in zip(blocks, gathered):
        whole[me] = block[...]
    greet(*peers[1:])
    sems = (send, recv)
    copies = []
    for index, other in enumerate(peers[1:]):
        copies.append(link(z_ref.at[rows(other), :], land.at[:, mine], sems, 2 + index, other))
        copies[-1].start()
    total_buf[...] = stats_total(stats_ref, got, stats_stage, peers, sems, 0)
    begun = [
        [gather_begin(whole, block_piece(whole), peers, k, half) for half in range(2)]
        for whole, k in zip(gathered, block_sems)
    ]
    part = total_buf[:, pl.ds(pl.multiple_of(me * quarter, LANES), quarter)]
    means = part.T * (1.0 / width)
    fetch.wait()
    for copy in copies:
        copy.wait_recv()
    n, scale = normalise(x_own[...].astype(F32))
    g = land[...].astype(F32) - scale * (means[:, 0:1] + n * means[:, 1:2])
    out_ref[...] = g.astype(BF16)
    passed = [
        gather_forward(whole, block_piece(whole), peers, k, zero, one)
        for whole, k, (zero, one) in zip(gathered, block_sems, begun)
    ]
    for whole, k, (zero, one), two in zip(gathered, block_sems, begun, passed):
        gather_finish(whole, block_piece(whole), peers, k, zero, one, two)
    for copy in copies:
        copy.wait_send()


def final_exchange(z, stats, x, blocks, sections, ident):
    count, own = z.shape
    width = x.shape[1]
    quarter = count // 4
    number = len(blocks)
    return pl.pallas_call(
        functools.partial(final_kernel, number),
        out_shape=(shape((quarter, width), BF16),)
        + tuple(shape((sections,) + a.shape, BF16) for a in blocks),
        in_specs=[vmem(), vmem(), hbm()] + [vmem()] * number,
        out_specs=(vmem(),) * (1 + number),
        scratch_shapes=[
            pltpu.VMEM((quarter, width), BF16),
            pltpu.VMEM((quarter, width), BF16),
            pltpu.VMEM((2,) + stats.shape, F32),
            pltpu.VMEM(stats.shape, F32),
            pltpu.VMEM(stats.shape, F32),
            pltpu.SemaphoreType.DMA,
        ]
        + copy_sems(5)
        + copy_sems(6) * number,
        cost_estimate=lasting(10 + 20 * number),
        compiler_params=comm_params(ident),
    )(z, stats, x, *blocks)


def sums_kernel(shards, holders, sums_ref, block_ref, channels_ref, whole_ref, *refs):
    sums_land, send_s, recv_s, send_c, recv_c, send, recv = refs
    peers = plane()
    me = peers[0]
    slot = lax.axis_index("dp")
    holding = slot // holders == me
    whole_ref[me] = block_ref[...]
    barrier = pltpu.get_barrier_semaphore()
    for other in peers[1:]:
        pl.semaphore_signal(barrier, inc=1, device_id={"section": other}, device_id_type=MESH)
    for step in range(1, shards):
        other = (slot + step) % shards
        pl.semaphore_signal(barrier, inc=1, device_id={"dp": other}, device_id_type=MESH)
    pl.semaphore_wait(barrier, shards + 2)

    def sums_copy(target, index, place):
        return pltpu.make_async_remote_copy(
            src_ref=sums_ref,
            dst_ref=sums_land.at[place],
            send_sem=send_s.at[index],
            recv_sem=recv_s.at[place],
            device_id={"dp": target},
            device_id_type=MESH,
        )

    def sums_out(index):
        target = me * holders + index
        place = jnp.maximum((slot - target + shards) % shards - 1, 0)
        return target, sums_copy(target, index, place)

    for index in range(holders):
        target, copy = sums_out(index)

        @pl.when(target != slot)
        def _():
            copy.start()

    piece = block_piece(whole_ref)
    zero, one = (gather_begin(whole_ref, piece, peers, (send, recv), half) for half in range(2))
    passed = gather_forward(whole_ref, piece, peers, (send, recv), zero, one)

    def channels_copy(other, index):
        return link(channels_ref, channels_ref, (send_c, recv_c), index, other)

    @pl.when(holding)
    def _():
        summed = sums_ref[...]
        for step in range(1, shards):
            sums_copy((slot + step) % shards, 0, step - 1).wait_recv()
            summed = summed + sums_land[step - 1]
        channels_ref[...] = summed
        for index, other in enumerate(peers[1:]):
            channels_copy(other, index).start()

    gather_finish(whole_ref, piece, peers, (send, recv), zero, one, passed)

    for index, other in enumerate(peers[1:]):

        @pl.when(slot // holders == other)
        def _():
            channels_copy(other, index).wait_recv()

    @pl.when(holding)
    def _():
        for index, other in enumerate(peers[1:]):
            channels_copy(other, index).wait_send()

    for index in range(holders):
        target, copy = sums_out(index)

        @pl.when(target != slot)
        def _():
            copy.wait_send()


def gather_sums(sums, block, sections, shards, holders, ident):
    return pl.pallas_call(
        functools.partial(sums_kernel, shards, holders),
        out_shape=(shape(sums.shape, F32), shape((sections,) + block.shape, BF16)),
        in_specs=[vmem()] * 2,
        out_specs=(vmem(),) * 2,
        scratch_shapes=[pltpu.VMEM((shards - 1,) + sums.shape, F32)]
        + copy_sems(max(shards - 1, holders))
        + copy_sems(3)
        + copy_sems(6),
        cost_estimate=lasting(25),
        compiler_params=comm_params(ident),
    )(sums, block)


def woven_parts(part, here, low, size, shards):
    step = size // shards
    return jnp.concatenate(
        [
            part[k, here, low + d * step : low + (d + 1) * step].astype(F32)
            for d in range(shards)
            for k in range(part.shape[0])
        ],
        axis=1,
    )


def joined_parts(part, here, low, size):
    return jnp.concatenate(
        [part[k, here, low : low + size].astype(F32) for k in range(part.shape[0])], axis=1
    )


def by_strips(rows, work):
    def strip(i, carry):
        work(pl.ds(pl.multiple_of(i * SMALL, SMALL), SMALL))
        return carry

    lax.fori_loop(0, rows // SMALL, strip, 0)


def attention_outputs(shards, layer, part, extras, outs):
    value_ref, base_ref, out_ref, value_bias_ref, base_bias_ref, pair_ref, query_ref = outs[:7]
    norm_outs, average_outs = outs[7:10], outs[10:]
    sections = part.shape[0]
    width = out_ref.shape[2]
    wide = value_ref.shape[2] // sections
    own = width // sections
    keyed = base_ref.shape[2] - 2 * width - wide * sections
    edge = wide + own
    total = edge + keyed + wide + own
    few = wide // shards

    def strip(here):
        value_ref[0, here, :] = woven_parts(part, here, 0, wide, shards)
        base_ref[0, here, :width] = joined_parts(part, here, wide, own)
        shared = part[0, here, edge : edge + keyed].astype(F32)
        for k in range(1, sections):
            shared += part[k, here, edge : edge + keyed].astype(F32)
        low = width
        base_ref[0, here, low : low + keyed] = shared
        low += keyed
        base_ref[0, here, low : low + wide * sections] = woven_parts(
            part, here, edge + keyed, wide, shards
        )
        low += wide * sections
        base_ref[0, here, low:] = joined_parts(part, here, edge + keyed + wide, own)

    by_strips(value_ref.shape[1], strip)
    for k in range(sections):
        for half in range(2):
            columns = slice(half * (width // 2), (half + 1) * (width // 2))
            out_ref[0, k * few : (k + 1) * few, columns] = part[
                k, half * few : (half + 1) * few, total : total + width // 2
            ].astype(F32)
    slot = lax.axis_index("dp")
    row = slice(layer, layer + 1)
    blocks = [part[k, :SMALL, total + width // 2 :].astype(F32) for k in range(sections)]
    lines = [
        jnp.concatenate([b[i : i + 1] for i in range(total // LANES)], axis=1) for b in blocks
    ]
    summed = sum(blocks[1:], blocks[0])

    def mine(line):
        size = line.shape[1] // shards
        return chosen([line[:, d * size : (d + 1) * size] for d in range(shards)], slot)

    value_bias_ref[row, :] = jnp.concatenate([mine(line[:, :wide]) for line in lines], axis=1)
    low = edge + keyed
    base_line = jnp.concatenate(
        [line[:, wide:edge] for line in lines]
        + [sum((line[:, edge:low] for line in lines[1:]), lines[0][:, edge:low])]
        + [
            line[:, low + d * few : low + (d + 1) * few]
            for d in range(shards)
            for line in lines
        ]
        + [line[:, low + wide :] for line in lines],
        axis=1,
    )
    base_bias_ref[row, :] = mine(base_line)
    first = total // LANES
    for k in range(2):
        pair_ref[layer, k : k + 1, :] = mine(summed[first + k : first + k + 1])
    query_ref[row, :] = mine(summed[first + 2 : first + 3])

    channels_ref, decay_ref, input_ref, output_ref = extras
    dims, size = decay_ref.shape[1:]
    holders = own // size
    low = layer * (2 * dims + 8)

    def channels(start, count):
        here = slice(low + start, low + start + count)
        pieces = [channels_ref[here, k * size : (k + 1) * size] for k in range(holders)]
        return chosen(pieces, slot % holders)

    sums = channels(2 * dims, 8)
    for k, ref in enumerate(norm_outs):
        ref[row, :] = sums[k : k + 1]
    of_states, of_slopes = channels(0, dims), channels(dims, dims)
    rate = sigmoid(decay_ref[layer])
    drive = (1.0 - rate) * input_ref[layer]
    gdrive = output_ref[layer] * of_states
    grate = drive * output_ref[layer] * of_slopes - input_ref[layer] * gdrive
    average_outs[0][layer] = grate * rate * (1.0 - rate)
    average_outs[1][layer] = (1.0 - rate) * gdrive
    average_outs[2][layer] = drive * of_states


def feed_outputs(shards, layer, feed, extras, outs):
    in_ref, out_ref, gain_ref, shift_ref, out_bias_ref, in_bias_ref = outs
    sections, rows = feed.shape[:2]
    width = out_ref.shape[2]
    hidden = in_ref.shape[2] // sections

    def strip(here):
        in_ref[0, here, :] = woven_parts(feed, here, 0, hidden, shards)

    by_strips(rows, strip)
    for k in range(sections):
        out_ref[0, k * rows : (k + 1) * rows, :] = feed[k, :, hidden : hidden + width].astype(F32)
    size = width // shards
    row = slice(layer, layer + 1)
    blocks = [feed[k, :SMALL, hidden + width :].astype(F32)[:, :size] for k in range(sections)]
    summed = sum(blocks[1:], blocks[0])
    gain_ref[row, :] = summed[0:1]
    shift_ref[row, :] = summed[1:2]
    out_bias_ref[row, :] = blocks[0][2:3]
    in_bias_ref[row, :] = jnp.concatenate([b[3:4] for b in blocks], axis=1)


def assemble_kernel(work, shards, layers, more, *refs):
    extras, outs = refs[layers : layers + more], refs[layers + more :]
    for layer in range(layers):

        @pl.when(pl.program_id(0) == layer)
        def _():
            work(shards, layer, refs[layer], extras, outs)


def assemble(work, gathered, extras, dims, small_dims, shards):
    layers = len(gathered)

    def whole(dims):
        return pl.BlockSpec(dims, lambda i, n=len(dims): (0,) * n)

    return pl.pallas_call(
        functools.partial(assemble_kernel, work, shards, layers, len(extras)),
        grid=(layers,),
        out_shape=tuple(shape((layers,) + d, F32) for d in dims + small_dims),
        in_specs=[whole(a.shape) for a in gathered + extras],
        out_specs=tuple(
            pl.BlockSpec((1,) + d, lambda i, n=len(d): (i,) + (0,) * n) for d in dims
        )
        + tuple(whole((layers,) + d) for d in small_dims),
        cost_estimate=lasting(6),
        compiler_params=params(),
    )(*gathered, *extras)


def chosen(pieces, section=None):
    if section is None:
        section = lax.axis_index("section")
    result = pieces[0]
    for k in range(1, len(pieces)):
        result = jnp.where(section == k, pieces[k], result)
    return result


def pick(ref, index, low, size, shards, sections):
    step = size // (shards * sections)
    parts = []
    for shard in range(shards):
        start = low + shard * sections * step
        parts.append(
            chosen([ref[index + (slice(start + k * step, start + (k + 1) * step),)] for k in range(sections)])
        )
    return jnp.concatenate(parts, axis=-1)


def pack_attention_kernel(shards, sections, value_ref, base_ref, out_ref, packed_ref):
    rows, wide_all = value_ref.shape[1:]
    few_all, width = out_ref.shape[1:]
    wide, own, few = wide_all // sections, width // sections, few_all // sections
    keyed = base_ref.shape[2] - 2 * width - wide_all
    section = lax.axis_index("section")
    low = wide + own + keyed

    def strip(i, carry):
        here = pl.ds(pl.multiple_of(i * SMALL, SMALL), SMALL)

        def base(start, size):
            return base_ref[0, here, pl.ds(pl.multiple_of(start, LANES), size)]

        packed_ref[here, :wide] = pick(value_ref, (0, here), 0, wide_all, shards, sections)
        packed_ref[here, wide : wide + own] = base(section * own, own)
        packed_ref[here, wide + own : low] = base(width, keyed)
        packed_ref[here, low : low + wide] = pick(
            base_ref, (0, here), width + keyed, wide_all, shards, sections
        )
        packed_ref[here, low + wide : low + wide + own] = base(
            width + keyed + wide_all + section * own, own
        )
        return carry

    lax.fori_loop(0, rows // SMALL, strip, 0)
    low += wide + own
    mine = pl.ds(pl.multiple_of(section * few, few), few)
    for half in range(2):
        packed_ref[half * few : (half + 1) * few, low:] = out_ref[
            0, mine, half * (width // 2) : (half + 1) * (width // 2)
        ]


def pack_feed_kernel(shards, sections, in_ref, out_ref, packed_ref):
    rows, hidden_all = in_ref.shape[1:]
    hidden = hidden_all // sections
    size = out_ref.shape[1] // sections

    def strip(i, carry):
        here = pl.ds(pl.multiple_of(i * SMALL, SMALL), SMALL)
        packed_ref[here, :hidden] = pick(in_ref, (0, here), 0, hidden_all, shards, sections)
        return carry

    lax.fori_loop(0, rows // SMALL, strip, 0)
    start = pl.multiple_of(lax.axis_index("section") * size, size)
    packed_ref[:, hidden:] = out_ref[0, pl.ds(start, size), :]


def pack(work, layer, columns, shards, sections, arrays, after=()):
    rows = arrays[0].shape[1]

    def kernel(*refs):
        work(shards, sections, *refs[len(after) :])

    return pl.pallas_call(
        kernel,
        grid=(1,),
        out_shape=shape((rows, columns), BF16),
        in_specs=[hbm()] * len(after)
        + [pl.BlockSpec((1,) + a.shape[1:], lambda i: (layer, 0, 0)) for a in arrays],
        out_specs=pl.BlockSpec((rows, columns), lambda i: (0, 0)),
        cost_estimate=lasting(3),
        compiler_params=params(),
    )(*after, *arrays)


def unpack_kernel(layers, shards, sections, places, everyone_ref, *refs):
    base_buf = refs[-1]
    section = lax.axis_index("section")
    outs = 14
    for layer in range(layers):
        (
            gain_ref,
            shift_ref,
            feed_gain_ref,
            feed_shift_ref,
            feed_out_ref,
            own_ref,
            rate_ref,
            coef_ref,
            bias_ref,
            feed_in_ref,
            pair_ref,
            offset_ref,
            skip_ref,
            own_out_ref,
        ) = refs[layer * outs : (layer + 1) * outs]
        width = gain_ref.shape[1]
        own = width // sections
        mine = pl.ds(pl.multiple_of(section * own, LANES), own)
        row = slice(layer, layer + 1)

        def joined(low, size):
            return jnp.concatenate(
                [everyone_ref[d, row, low : low + size] for d in range(shards)], axis=1
            )

        def share(low, size):
            step = size // sections
            return jnp.concatenate(
                [
                    chosen(
                        [
                            everyone_ref[d, row, low + k * step : low + (k + 1) * step]
                            for k in range(sections)
                        ]
                    )
                    for d in range(shards)
                ],
                axis=1,
            )

        def channels(low):
            size = width // shards
            count = own // size
            return jnp.concatenate(
                [everyone_ref[section * count + d, row, low : low + size] for d in range(count)],
                axis=1,
            )

        size = width // shards
        gain_ref[...] = joined(places["norm_gain"], size)
        shift_ref[...] = joined(places["norm_shift"], size)
        feed_gain_ref[...] = joined(places["feed_gain"], size)
        feed_shift_ref[...] = joined(places["feed_shift"], size)
        feed_out_ref[...] = joined(places["feed_out_bias"], size)
        own_ref[0:1, :] = gain_ref[:, mine]
        own_ref[1:2, :] = shift_ref[:, mine]
        own_ref[2:3, :] = feed_gain_ref[:, mine]
        own_ref[3:8, :] = jnp.zeros((5, own), F32)
        own_out_ref[...] = feed_out_ref[:, mine]
        skip_ref[...] = channels(places["average_skip"])
        for n in range(rate_ref.shape[0]):
            rate = sigmoid(channels(places["average_decay"] + n * size))
            drive = (1.0 - rate) * channels(places["average_input"] + n * size)
            coef = drive * channels(places["average_output"] + n * size)
            rate_ref[n] = jnp.broadcast_to(rate, (CHUNKS, own))
            coef_ref[n] = jnp.broadcast_to(coef, (CHUNKS, own))
        keyed = offset_ref.shape[1]
        step = keyed // shards
        for r in range(2):
            pair_ref[r : r + 1, :] = joined(places["pair_scale"] + r * step, step)
        offset_ref[...] = joined(places["query_shift"], step)
        feed_in_ref[...] = share(
            places["feed_in_bias"], feed_in_ref.shape[1] * sections // shards
        )
        total = bias_ref.shape[1]
        wide = (total - keyed - 2 * own) // 2
        base_all = 2 * width + keyed + wide * sections
        base_buf[...] = joined(places["base_bias"], base_all // shards)
        low = wide + own + keyed
        bias_ref[:, :wide] = share(places["value_bias"], wide * sections // shards)
        bias_ref[:, wide : wide + own] = base_buf[:, mine]
        bias_ref[:, wide + own : low] = base_buf[:, width : width + keyed]
        bias_ref[:, low : low + wide] = pick(
            base_buf, (slice(None),), width + keyed, wide * sections, shards, sections
        )
        start = pl.multiple_of(width + keyed + wide * sections + section * own, LANES)
        bias_ref[:, low + wide :] = base_buf[:, pl.ds(start, own)]


def unpack(everyone, places, sizes, sections):
    shards, layers = everyone.shape[:2]
    width, dims, total, hidden, keyed, base = sizes
    own = width // sections
    one_layer = (
        [shape((1, width), F32)] * 5
        + [shape((8, own), F32)]
        + [shape((dims, CHUNKS, own), F32)] * 2
        + [
            shape((1, total), F32),
            shape((1, hidden), F32),
            shape((2, keyed), F32),
            shape((1, keyed), F32),
            shape((1, own), F32),
            shape((1, own), F32),
        ]
    )
    outs = pl.pallas_call(
        functools.partial(unpack_kernel, layers, shards, sections, places),
        out_shape=tuple(one_layer * layers),
        in_specs=[vmem()],
        out_specs=(vmem(),) * (len(one_layer) * layers),
        scratch_shapes=[pltpu.VMEM((1, base), F32)],
        cost_estimate=lasting(3),
        compiler_params=params(),
    )(everyone)
    names = (
        "gain",
        "shift",
        "feed_gain",
        "feed_shift",
        "feed_out",
        "own",
        "rate",
        "coef",
        "bias",
        "feed_in",
        "pair",
        "offset",
        "skip",
        "own_out",
    )
    count = len(one_layer)
    return [
        types.SimpleNamespace(**dict(zip(names, outs[k * count : (k + 1) * count])))
        for k in range(layers)
    ]


def body(
    tokens,
    lengths,
    cotangent,
    norm_gain,
    norm_shift,
    average_decay,
    average_input,
    average_output,
    average_skip,
    value_weight,
    value_bias,
    base_weight,
    base_bias,
    pair_scale,
    query_shift,
    out_weight,
    feed_gain,
    feed_shift,
    feed_in_weight,
    feed_in_bias,
    feed_out_weight,
    feed_out_bias,
):
    sections = lax.axis_size("section")
    shards = lax.axis_size("dp")
    section = lax.axis_index("section")
    _, count, width = tokens.shape
    layers = norm_gain.shape[0]
    own = width // sections
    wide = value_weight.shape[2]
    keyed = pair_scale.shape[2] * shards
    hidden = feed_in_weight.shape[2]

    share = wide // sections
    total = share + own + keyed + share + own

    def over_dp(array):
        return lax.all_gather(array, "dp", axis=0, tiled=True)

    def attention_weights(layer, after=()):
        arrays = (value_weight, base_weight, out_weight)
        columns = total + width // 2
        return pack(pack_attention_kernel, layer, columns, shards, sections, arrays, after)

    def feed_weights(layer, after=()):
        arrays = (feed_in_weight, feed_out_weight)
        columns = hidden // sections + width
        return pack(pack_feed_kernel, layer, columns, shards, sections, arrays, after)

    weights = [[None, None] for _ in range(layers)]
    weights[0][0] = over_dp(attention_weights(0))

    smalls = dict(
        norm_gain=norm_gain,
        norm_shift=norm_shift,
        average_decay=average_decay,
        average_input=average_input,
        average_output=average_output,
        average_skip=average_skip,
        feed_gain=feed_gain,
        feed_shift=feed_shift,
        feed_out_bias=feed_out_bias,
        value_bias=value_bias,
        feed_in_bias=feed_in_bias,
        base_bias=base_bias,
        pair_scale=pair_scale,
        query_shift=query_shift,
    )
    packed = jnp.concatenate([a.reshape(layers, -1) for a in smalls.values()], axis=1)
    places = {}
    low = 0
    for name, array in smalls.items():
        places[name] = low
        low += array.size // layers
    dims = average_decay.shape[1]
    small = unpack(
        lax.all_gather(packed, "dp", axis=0),
        places,
        (width, dims, total, hidden // sections, keyed, base_weight.shape[2]),
        sections,
    )

    idents = iter(range(64))
    x0 = x = tokens[0]
    kept = []
    for layer in range(layers):
        p = small[layer]
        normed, mixed_own, pre, own_n, scale = average_forward(
            lengths, x, p.gain, p.shift, p.rate, p.coef, p.skip
        )
        if not layer:
            packed_feed = feed_weights(0, (mixed_own,))
            weights[0][1] = over_dp(packed_feed)
            mixed = mixed_own = gather_columns(mixed_own, next(idents), (packed_feed,))
        middle, hidden_pre, *mixed_out, update, shared, reset, value, att, gated, probs = attention_forward(
            lengths,
            normed,
            mixed_own,
            weights[layer][0],
            p.bias,
            p.pair,
            p.offset,
            x,
            shards,
            next(idents),
        )
        if layer:
            (mixed,) = mixed_out
        if layer + 1 < layers:
            weights[layer + 1] = [
                over_dp(attention_weights(layer + 1, (hidden_pre,))),
                over_dp(feed_weights(layer + 1, (hidden_pre,))),
            ]
        attention_w, feed_w = weights[layer]
        feed_saved = [None] * 4
        x_next = None
        if layer + 1 < layers:
            x_next, *feed_saved = feed_forward_joined(
                middle, p.feed_gain, p.feed_shift, feed_w, p.feed_in, p.own_out, next(idents)
            )
        feed_pre, feed_n, feed_normed, feed_scale = feed_saved
        kept.append(
            types.SimpleNamespace(
                x=x,
                middle=middle,
                normed=normed,
                mixed=mixed,
                pre=pre,
                own_n=own_n,
                scale=scale,
                update=update,
                saved=(shared, reset, value, att, probs),
                gated=gated,
                hidden=hidden_pre,
                feed_pre=feed_pre,
                feed_n=feed_n,
                feed_normed=feed_normed,
                feed_scale=feed_scale,
            )
        )
        x = x_next

    def scattered(grad):
        return lax.psum_scatter(grad, "dp", scatter_dimension=0, tiled=True)

    given = cotangent[0]
    feed_grads = [None] * layers
    attention_grads = [None] * layers
    channel_sums = [None] * layers
    for layer in reversed(range(layers)):
        attention_w, feed_w = weights[layer]
        k, p = kept[layer], small[layer]
        gout, gupdate, resid, feed_grad, *last = feed_backward(
            given, k, p, feed_w, shards, next(idents), () if layer else (feed_grads[1],)
        )
        if last:
            block_out = last[0]
        feed_grads[layer] = scattered(feed_grad)
        gmixed, gnormed, attention_grad = attention_backward(
            lengths,
            gout,
            gupdate,
            k,
            attention_w,
            p.pair,
            p.offset,
            shards,
            next(idents),
            () if layer else (attention_grads[1],),
        )
        attention_grads[layer] = scattered(attention_grad)
        z, zstats, channel_sums[layer], *attention_one = average_backward(
            lengths,
            gmixed,
            gnormed,
            k,
            resid,
            p.own,
            p.rate,
            p.coef,
            p.skip,
            None if layer else attention_grads[1],
            None if layer else next(idents),
        )
        if layer:
            given = (z, zstats, k.x)

    (attention_one,) = attention_one
    input_grad, feed_one, feed_zero = final_exchange(
        z, zstats, x0, [feed_grads[1], feed_grads[0]], sections, next(idents)
    )
    channels, attention_zero = gather_sums(
        jnp.concatenate(channel_sums, axis=0),
        attention_grads[0],
        sections,
        shards,
        own * shards // width,
        next(idents),
    )
    size = width // shards
    dims = average_decay.shape[1]
    g_feed_in, g_feed_out, g_feed_gain, g_feed_shift, g_feed_out_bias, g_feed_in_bias = assemble(
        feed_outputs,
        (feed_zero, feed_one),
        (),
        ((size, hidden), (hidden // shards, width)),
        ((size,), (size,), (size,), (hidden // shards,)),
        shards,
    )
    base = base_weight.shape[2]
    g_value, g_base, g_out, g_value_bias, g_base_bias, g_pair, g_query, *rest = assemble(
        attention_outputs,
        (attention_zero, attention_one),
        (channels, average_decay, average_input, average_output),
        ((size, wide), (size, base), (wide // shards, width)),
        ((wide // shards,), (base // shards,), (2, keyed // shards), (keyed // shards,))
        + ((size,),) * 3
        + ((dims, size),) * 3,
        shards,
    )
    g_gain, g_shift, g_skip, g_decay, g_input, g_output = rest
    return (
        block_out[None],
        input_grad[None],
        g_gain,
        g_shift,
        g_decay,
        g_input,
        g_output,
        g_skip,
        g_value,
        g_value_bias,
        g_base,
        g_base_bias,
        g_pair,
        g_query,
        g_out,
        g_feed_gain,
        g_feed_shift,
        g_feed_in,
        g_feed_in_bias,
        g_feed_out,
        g_feed_out_bias,
    )


def solution(mesh):
    row, row2 = P(None, "dp"), P(None, "dp", None)
    deep = P(None, None, "dp")
    in_specs = (
        P("dp", None, None),
        P("dp"),
        P("dp", None, None),
        row,
        row,
        deep,
        deep,
        deep,
        row,
        row2,
        row,
        row2,
        row,
        deep,
        row,
        row2,
        row,
        row,
        row2,
        row,
        row2,
        row,
    )
    out_specs = (
        P("dp", "section", None),
        P("dp", "section", None),
        row,
        row,
        deep,
        deep,
        deep,
        row,
        row2,
        row,
        row2,
        row,
        deep,
        row,
        row2,
        row,
        row,
        row2,
        row,
        row2,
        row,
    )
    return jax.shard_map(body, mesh=mesh, in_specs=in_specs, out_specs=out_specs, check_vma=False)
```

```python
import functools
import types

import jax
import jax.numpy as jnp
from jax import lax
from jax.experimental import pallas as pl
from jax.experimental.pallas import tpu as pltpu
from jax.sharding import PartitionSpec as P

F32 = jnp.float32
BF16 = jnp.bfloat16
MESH = pl.DeviceIdType.MESH
ATT = 128
LANES = 128
CHUNKS = 8
ROWS = 256
STRIP = 64
TILE = 128
LOCAL = "local"
UNROLL = 16
SMALL = 16
SMEM, VMEM, RAW, FETCH, BLOCKS, LATE, OWN_PART, STORE = range(8)
EPS = 1e-05
NEGATIVE = -1000000000.0
VMEM_BYTES = 56 * 1024 * 1024


def vmem():
    return pl.BlockSpec(memory_space=pltpu.VMEM)


def smem():
    return pl.BlockSpec(memory_space=pltpu.SMEM)


def hbm():
    return pl.BlockSpec(memory_space=pl.ANY)


def shape(dims, kind):
    return jax.ShapeDtypeStruct(dims, kind)


def sigmoid(v):
    return 0.5 * jnp.tanh(0.5 * v) + 0.5


def silu(v):
    return v * sigmoid(v)


def silu_slope(v):
    s = sigmoid(v)
    return s * (1.0 + v * (1.0 - s))


def dot(left, right, left_dim=1, right_dim=0):
    return lax.dot_general(
        left, right, (((left_dim,), (right_dim,)), ((), ())), preferred_element_type=F32
    )


def normalise(x):
    centred = x - jnp.mean(x, axis=-1, keepdims=True)
    spread = jnp.mean(centred * centred, axis=-1, keepdims=True)
    scale = lax.rsqrt(spread + EPS)
    return centred * scale, scale


def row_valid(start, rows, length):
    place = start + lax.broadcasted_iota(jnp.int32, (rows, 1), 0)
    return (place < length).astype(F32)


def lasting(microseconds):
    return pl.CostEstimate(
        flops=int(microseconds * 1.0e9),
        bytes_accessed=int(microseconds * 3.0e6),
        transcendentals=0,
    )


def params(**more):
    return pltpu.CompilerParams(vmem_limit_bytes=VMEM_BYTES, **more)


def power(base, exponent):
    result = None
    square = base
    while exponent:
        if exponent % 2:
            result = square if result is None else result * square
        exponent //= 2
        if exponent:
            square = square * square
    return result


def shifted(array, span, reverse=False):
    row = lax.broadcasted_iota(jnp.int32, array.shape, 1)
    if reverse:
        return jnp.where(row < CHUNKS - span, pltpu.roll(array, CHUNKS - span, 1), 0.0)
    return jnp.where(row >= span, pltpu.roll(array, span, 1), 0.0)


def entering(last, rate, steps, reverse=False):
    weight = power(rate, steps)
    span = 1
    while span < CHUNKS:
        last = last + weight * shifted(last, span, reverse)
        weight = weight * weight
        span *= 2
    return shifted(last, 1, reverse)


def entering_pair(last, slope, rate, steps):
    weight = power(rate, steps)
    tilt = float(steps) * power(rate, steps - 1)
    span = 1
    while span < CHUNKS:
        moved = shifted(last, span)
        slope = slope + weight * shifted(slope, span) + tilt * moved
        last = last + weight * moved
        tilt = 2.0 * weight * tilt
        weight = weight * weight
        span *= 2
    return shifted(last, 1), shifted(slope, 1)


def average_forward_kernel(
    length_ref,
    x_ref,
    gain_ref,
    shift_ref,
    rate_ref,
    coef_ref,
    skip_ref,
    normed_ref,
    mixed_ref,
    pre_ref,
    own_ref,
    scale_ref,
    rows_buf,
    m_buf,
    y_buf,
):
    length = length_ref[0]
    count, width = x_ref.shape
    own = mixed_ref.shape[1]
    dims = rate_ref.shape[0]
    steps = count // CHUNKS
    pitch = steps + 1
    mine = pl.ds(pl.multiple_of(lax.axis_index("section") * own, LANES), own)

    def norm_strip(i, carry):
        start = pl.multiple_of(i * STRIP, STRIP)
        here = pl.ds(start, STRIP)
        n, scale = normalise(x_ref[here, :].astype(F32))
        rows_buf[...] = n
        normed_ref[here, :] = (n * gain_ref[...] + shift_ref[...]).astype(BF16)
        part = rows_buf[:, mine]
        own_ref[here, :] = part
        scale_ref[here, :] = jnp.broadcast_to(scale, (STRIP, LANES))
        masked = (part * gain_ref[:, mine] + shift_ref[:, mine]) * row_valid(start, STRIP, length)
        for group in range(own // LANES):
            m_buf[group, pl.ds(start + start // steps, STRIP), :] = masked[:, group * LANES : (group + 1) * LANES]
        return carry

    lax.fori_loop(0, count // STRIP, norm_strip, 0)

    for group in range(own // LANES):
        lanes = slice(group * LANES, (group + 1) * LANES)
        rates = rate_ref[:, :, lanes]
        coefs = coef_ref[:, :, lanes]
        m_part, y_part = m_buf.at[group], y_buf.at[group]

        def finals(t, states):
            return rates * states + m_part[pl.ds(t, CHUNKS, stride=pitch), :]

        ends = lax.fori_loop(0, steps, finals, jnp.zeros_like(rates), unroll=UNROLL)

        def outputs(t, states):
            states = rates * states + m_part[pl.ds(t, CHUNKS, stride=pitch), :]
            y_part[pl.ds(t, CHUNKS, stride=pitch), :] = jnp.sum(coefs * states, axis=0)
            return states

        lax.fori_loop(0, steps, outputs, entering(ends, rates, steps), unroll=UNROLL)

    def mix_strip(i, carry):
        start = pl.multiple_of(i * STRIP, STRIP)
        here = pl.ds(start, STRIP)
        there = pl.ds(start + start // steps, STRIP)
        for group in range(own // LANES):
            lanes = slice(group * LANES, (group + 1) * LANES)
            pre = y_buf[group, there, :] + skip_ref[:, lanes] * m_buf[group, there, :]
            pre_ref[here, lanes] = pre.astype(BF16)
            mixed_ref[here, lanes] = silu(pre).astype(BF16)
        return carry

    lax.fori_loop(0, count // STRIP, mix_strip, 0)


def average_forward(length, x, gain, shift, rate, coef, skip):
    count, width = x.shape
    own = skip.shape[1]
    groups = own // LANES
    return pl.pallas_call(
        average_forward_kernel,
        out_shape=(
            shape((count, width), BF16),
            shape((count, own), BF16),
            shape((count, own), BF16),
            shape((count, own), F32),
            shape((count, LANES), F32),
        ),
        in_specs=[smem()] + [vmem()] * 6,
        out_specs=(vmem(),) * 5,
        scratch_shapes=[
            pltpu.VMEM((STRIP, width), F32),
            pltpu.VMEM((groups, count + CHUNKS, LANES), F32),
            pltpu.VMEM((groups, count + CHUNKS, LANES), F32),
        ],
        cost_estimate=lasting(13),
        compiler_params=params(),
    )(length, x, gain, shift, rate, coef, skip)


def average_backward_work(beside, r):
    length = r.length[0]
    count, own = r.z.shape
    dims = r.rate.shape[0]
    steps = count // CHUNKS
    pitch = steps + 1
    groups = own // LANES
    gain_ref, shift_ref = r.norm.at[0:1, :], r.norm.at[1:2, :]
    if beside:
        peers = plane()
        sems, piece = (r.send, r.recv), block_piece(r.whole)
        r.whole[peers[0]] = r.block[...]
        greet(peers[1], peers[2])
        begun = [gather_begin(r.whole, piece, peers, sems, half) for half in range(2)]

    def load_strip(i, carry):
        start = pl.multiple_of(i * STRIP, STRIP)
        here = pl.ds(start, STRIP)
        valid = row_valid(start, STRIP, length)
        there = pl.ds(start + start // steps, STRIP)
        for group in range(groups):
            lanes = slice(group * LANES, (group + 1) * LANES)
            r.m_buf[group, there, :] = (
                r.own_n[here, lanes] * gain_ref[:, lanes] + shift_ref[:, lanes]
            ) * valid
            slope = silu_slope(r.pre[here, lanes].astype(F32))
            r.g_buf[group, there, :] = r.gmixed[here, lanes] * slope
        return carry

    lax.fori_loop(0, count // STRIP, load_strip, 0)
    r.store("m_buf", "g_buf")

    passed = None
    for group in range(groups):
        lanes = slice(group * LANES, (group + 1) * LANES)
        rates = r.rate[:, :, lanes]
        coefs = r.coef[:, :, lanes]
        m_part, g_part, r_part = r.m_buf.at[group], r.g_buf.at[group], r.r_buf.at[group]
        blank = jnp.zeros_like(rates)

        def back_finals(t, carry):
            states, slopes = carry
            g = g_part[pl.ds(steps - 1 - t, CHUNKS, stride=pitch), :]
            return rates * states + g, rates * slopes + states

        ends, end_slopes = lax.fori_loop(0, steps, back_finals, (blank, blank), unroll=UNROLL)
        starts = entering(ends, rates, steps, reverse=True)

        r.back[0, :, :, lanes] = ends
        r.back[1, :, :, lanes] = end_slopes

        def back_outputs(t, states):
            here = pl.ds(steps - 1 - t, CHUNKS, stride=pitch)
            states = rates * states + g_part[here, :]
            r_part[here, :] = jnp.sum(coefs * states, axis=0)
            return states

        lax.fori_loop(0, steps, back_outputs, starts, unroll=UNROLL)
        if beside and passed is None:
            passed = gather_forward(r.whole, piece, peers, sems, *begun)

    ones = jnp.ones((CHUNKS, own), BF16)
    first = lax.broadcasted_iota(jnp.int32, (CHUNKS, LANES), 0) == 0

    def finish(i, carry):
        start = pl.multiple_of(i * LANES, LANES)
        here = pl.ds(start, LANES)
        valid = row_valid(start, LANES, length)
        there = pl.ds(start + start // steps, LANES)
        of_gain, of_shift, of_skip = carry
        smoothed = jnp.concatenate([r.r_buf[k, there, :] for k in range(groups)], axis=1)
        gpre = jnp.concatenate([r.g_buf[k, there, :] for k in range(groups)], axis=1)
        masked = jnp.concatenate([r.m_buf[k, there, :] for k in range(groups)], axis=1)
        n = r.own_n[here, :]
        gmasked = r.skip[...] * gpre + smoothed
        gnormed = gmasked * valid + r.gvalue[here, :]
        e = gnormed * gain_ref[...]
        z = r.scale[here, 0:1] * e + r.resid[here, :]
        r.z[here, :] = z.astype(BF16)
        mean_row = dot(ones, e.astype(BF16), 1, 1)
        slope_row = dot(ones, (e * n).astype(BF16), 1, 1)
        r.stats[:, here] = jnp.where(first, mean_row, slope_row)
        return (
            of_gain + jnp.sum(gnormed * n, axis=0, keepdims=True),
            of_shift + jnp.sum(gnormed, axis=0, keepdims=True),
            of_skip + jnp.sum(gpre * masked, axis=0, keepdims=True),
        )

    blank_row = jnp.zeros((1, own), F32)
    of_gain, of_shift, of_skip = lax.fori_loop(
        0, count // LANES, finish, (blank_row, blank_row, blank_row)
    )
    r.sums[0:1, :] = of_gain
    r.sums[1:2, :] = of_shift
    r.sums[2:3, :] = of_skip
    r.sums[3:8, :] = jnp.zeros((5, own), F32)
    if beside:
        gather_finish(r.whole, piece, peers, sems, *begun, passed)


def average_sums(m_ref, g_ref, rate_ref, back_ref, sums_ref, low):
    dims, _, own = rate_ref.shape
    pitch = m_ref.shape[1] // CHUNKS
    steps = pitch - 1
    part_size = dims // 2
    for group in range(own // LANES):
        lanes = slice(group * LANES, (group + 1) * LANES)
        m_part, g_part = m_ref.at[group], g_ref.at[group]
        for half in range(2):
            some = slice(half * part_size, (half + 1) * part_size)
            rates = rate_ref[some, :, lanes]
            empty = jnp.zeros_like(rates)

            def sweep(t, carry):
                states, slopes, of_states, of_slopes = carry
                x = m_part[pl.ds(t, CHUNKS, stride=pitch), :]
                g = g_part[pl.ds(t, CHUNKS, stride=pitch), :]
                slopes = rates * slopes + states
                states = rates * states + x
                return states, slopes, of_states + g * states, of_slopes + g * slopes

            states, slopes, of_states, of_slopes = lax.fori_loop(
                0, steps, sweep, (empty,) * 4, unroll=UNROLL
            )
            back, back_slope = back_ref[0, some, :, lanes], back_ref[1, some, :, lanes]
            state, slope = entering_pair(states, slopes, rates, steps)
            of_states = of_states + state * (rates * back)
            of_slopes = of_slopes + slope * (rates * back) + state * (back + rates * back_slope)
            first = low + half * part_size
            sums_ref[first : first + part_size, lanes] = jnp.sum(of_states, axis=1)
            first += dims
            sums_ref[first : first + part_size, lanes] = jnp.sum(of_slopes, axis=1)


def average_backward(
    length, gmixed, gvalue, k, resid, norm, rate, coef, skip, block, ident, after=()
):
    count, own = gmixed.shape
    dims = rate.shape[0]
    held_dims = (own // LANES, count + CHUNKS, LANES)
    sems = pltpu.SemaphoreType.DMA((6,))
    given = dict(
        gmixed=gmixed,
        gvalue=gvalue,
        pre=k.pre,
        own_n=k.own_n,
        scale=k.scale,
        resid=resid,
        norm=norm,
        rate=rate,
        coef=coef,
        skip=skip,
    )
    beside = block is not None
    outs, held = {}, {}
    if beside:
        given.update(block=block)
        outs.update(whole=(shape((4,) + block.shape, BF16), VMEM))
        held.update(send=sems, recv=sems)
    return transfer(
        functools.partial(average_backward_work, beside),
        dict(length=(length, SMEM), **{name: (a, VMEM) for name, a in given.items()}),
        dict(
            z=(shape((count, own), BF16), VMEM),
            stats=(shape((CHUNKS, count), F32), VMEM),
            sums=(shape((8, own), F32), VMEM),
            m_buf=(shape(held_dims, F32), STORE),
            g_buf=(shape(held_dims, F32), STORE),
            back=(shape((2, dims, CHUNKS, own), F32), VMEM),
            **outs,
        ),
        dict(r_buf=pltpu.VMEM(held_dims, F32), **held),
        ident,
        17,
        after,
    )


def unfold(packed, in_w, out_w, shards, sems):
    wide, width = out_w.shape
    few = wide // shards
    low = in_w.shape[1]
    copies = [pltpu.make_async_copy(packed.at[:, pl.ds(0, low)], in_w, sems.at[0])]
    for shard in range(shards):
        for half in range(2):
            start = shard * (width // shards) + half * few
            columns = pl.ds(half * (width // 2), width // 2)
            copies.append(
                pltpu.make_async_copy(
                    packed.at[pl.ds(start, few), pl.ds(low, width // 2)],
                    out_w.at[pl.ds(shard * few, few), columns],
                    sems.at[len(copies)],
                )
            )
    return copies


def attention_forward_block(
    length,
    start,
    normed_ref,
    mixed_ref,
    in_ref,
    bias_ref,
    pair_ref,
    offset_ref,
    part_ref,
    update_ref,
    shared_ref,
    reset_ref,
    cand_ref,
    value_ref,
    att_ref,
    gated_ref,
    probs_ref,
    out_w_ref,
):
    rows = normed_ref.shape[0]
    wide = value_ref.shape[1]
    own = update_ref.shape[1]
    keyed = shared_ref.shape[1]
    value = dot(normed_ref[...], in_ref[:, :wide]) + bias_ref[:, :wide]
    value_ref[...] = value.astype(BF16)
    values = silu(value).astype(BF16)
    low = wide
    update = dot(mixed_ref[...], in_ref[:, low : low + own]) + bias_ref[:, low : low + own]
    update_ref[...] = update.astype(BF16)
    low += own
    shared = dot(mixed_ref[...], in_ref[:, low : low + keyed]) + bias_ref[:, low : low + keyed]
    shared_ref[...] = shared.astype(BF16)
    low += keyed
    reset = dot(mixed_ref[...], in_ref[:, low : low + wide]) + bias_ref[:, low : low + wide]
    reset_ref[...] = reset.astype(BF16)
    low += wide
    cand_ref[...] = (
        dot(mixed_ref[...], in_ref[:, low : low + own]) + bias_ref[:, low : low + own]
    ).astype(BF16)
    shared = silu(shared)
    reset = silu(reset)
    queries = (shared * pair_ref[0:1, :] + offset_ref[...]).astype(BF16)
    keys = (shared * pair_ref[1:2, :]).astype(BF16)
    for block in range(rows // ATT):
        here = slice(block * ATT, (block + 1) * ATT)
        begin = start + block * ATT
        scores = dot(queries[here], keys[here], 1, 1) * keyed**-0.5
        key_place = begin + lax.broadcasted_iota(jnp.int32, (ATT, ATT), 1)
        scores = jnp.where(key_place < length, scores, NEGATIVE)
        raised = jnp.exp(scores - jnp.max(scores, axis=-1, keepdims=True))
        probs = (raised / jnp.sum(raised, axis=-1, keepdims=True)).astype(BF16)
        probs_ref[here, :] = probs
        attended = dot(probs, values[here]) * row_valid(begin, ATT, length)
        att_ref[here, :] = attended.astype(BF16)
        gated_ref[here, :] = (attended * reset[here]).astype(BF16)
    part_ref[...] = dot(gated_ref[...], out_w_ref[...]).astype(BF16)


def attention_backward_block(
    length,
    start,
    mine,
    gout_ref,
    gupdate_ref,
    shared_ref,
    reset_ref,
    value_ref,
    att_ref,
    probs_ref,
    in_ref,
    pair_ref,
    offset_ref,
    gmixed_ref,
    gnormed_ref,
    gbase_ref,
    gvalue_ref,
    bias_ref,
    pair_sum_ref,
    out_w_ref,
):
    rows = gout_ref.shape[0]
    total = bias_ref.shape[1]
    wide = value_ref.shape[1]
    own = gupdate_ref.shape[1]
    keyed = shared_ref.shape[1]
    valid = row_valid(start, rows, length)
    ggated = dot(gout_ref[...], out_w_ref[...], 1, 1)
    reset = reset_ref[...].astype(F32)
    gattended = (ggated * silu(reset) * valid).astype(BF16)
    greset = ggated * att_ref[...].astype(F32) * silu_slope(reset)
    value = value_ref[...].astype(F32)
    values = silu(value).astype(BF16)
    shared_pre = shared_ref[...].astype(F32)
    shared = silu(shared_pre)
    scale_q, scale_k = pair_ref[0:1, :], pair_ref[1:2, :]
    queries = (shared * scale_q + offset_ref[...]).astype(BF16)
    keys = (shared * scale_k).astype(BF16)
    gq_parts, gk_parts, gv_parts = [], [], []
    for block in range(rows // ATT):
        here = slice(block * ATT, (block + 1) * ATT)
        probs = probs_ref[here, :]
        gprobs = dot(gattended[here], values[here], 1, 1)
        gv_parts.append(dot(probs, gattended[here], 0, 0))
        probs = probs.astype(F32)
        gscores = probs * (gprobs - jnp.sum(probs * gprobs, axis=-1, keepdims=True))
        key_place = start + block * ATT + lax.broadcasted_iota(jnp.int32, (ATT, ATT), 1)
        gscores = jnp.where(key_place < length, gscores, 0.0)
        gscores = (gscores * keyed**-0.5).astype(BF16)
        gq_parts.append(dot(gscores, keys[here]))
        gk_parts.append(dot(gscores, queries[here], 0, 0))
    gqueries = jnp.concatenate(gq_parts, axis=0)
    gkeys = jnp.concatenate(gk_parts, axis=0)
    gvalue = jnp.concatenate(gv_parts, axis=0) * silu_slope(value)
    gshared = (gqueries * scale_q + gkeys * scale_k) * silu_slope(shared_pre)
    pair_sum_ref[0:1, :] += jnp.sum(gqueries * shared, axis=0, keepdims=True)
    pair_sum_ref[1:2, :] += jnp.sum(gkeys * shared, axis=0, keepdims=True)
    pair_sum_ref[2:3, :] += jnp.sum(gqueries, axis=0, keepdims=True)
    gupdate = gupdate_ref[...]
    gcand = gout_ref[:, mine]
    low = 0
    for piece in (gvalue, gupdate, gshared, greset, gcand):
        size = piece.shape[1]
        bias_ref[0:1, low : low + size] += jnp.sum(piece.astype(F32), axis=0, keepdims=True)
        if low:
            gbase_ref[:, low - wide : low - wide + size] = piece.astype(BF16)
        else:
            gvalue_ref[...] = piece.astype(BF16)
        low += size
    gmixed_ref[...] = dot(gbase_ref[...], in_ref[:, wide:total], 1, 1).astype(BF16)
    gnormed_ref[...] = dot(gvalue_ref[...], in_ref[:, :wide], 1, 1).astype(BF16)


def feed_forward_kernel(
    x_ref, gain_ref, shift_ref, w_ref, bias_ref, part_ref, pre_ref, n_ref, normed_ref, scale_ref
):
    hidden = pre_ref.shape[1]
    n, scale = normalise(x_ref[...].astype(F32))
    n_ref[...] = n.astype(BF16)
    scale_ref[...] = jnp.broadcast_to(scale, scale_ref.shape)
    normed_ref[...] = (n * gain_ref[...] + shift_ref[...]).astype(BF16)
    pre = dot(normed_ref[...], w_ref[:, :hidden]) + bias_ref[...]
    pre_ref[...] = pre.astype(BF16)
    part_ref[...] = dot(silu(pre).astype(BF16), w_ref[:, hidden:]).astype(BF16)


def feed_backward_block(
    g_ref, pre_ref, n_ref, gain_ref, w_ref, part_ref, stats_ref, gpre_ref, act_ref, sums_ref, bias_ref, lanes
):
    hidden = pre_ref.shape[1]
    width = n_ref.shape[1]
    g = g_ref[...]
    pre = pre_ref[...].astype(F32)
    s = sigmoid(pre)
    act_ref[...] = (pre * s).astype(BF16)
    gpre = dot(g, w_ref[:, hidden:], 1, 1) * (s * (1.0 + pre * (1.0 - s)))
    bias_ref[0:1, :] += jnp.sum(gpre, axis=0, keepdims=True)
    gpre_ref[...] = gpre.astype(BF16)
    part = dot(gpre_ref[...], w_ref[:, :hidden], 1, 1)
    part_ref[...] = part.astype(BF16)
    n = n_ref[...].astype(F32)
    sums_ref[0:1, :] += jnp.sum(part * n, axis=0, keepdims=True)
    sums_ref[1:2, :] += jnp.sum(part, axis=0, keepdims=True)
    sums_ref[2:3, :] += jnp.sum(g.astype(F32), axis=0, keepdims=True)
    e = part * gain_ref[...]
    ones = jnp.ones((CHUNKS, width), BF16)
    mean_row = dot(ones, e.astype(BF16), 1, 1)
    slope_row = dot(ones, (e * n).astype(BF16), 1, 1)
    first = lax.broadcasted_iota(jnp.int32, mean_row.shape, 0) == 0
    stats_ref[:, lanes] = jnp.where(first, mean_row, slope_row)


def plane():
    me = lax.axis_index("section")
    across = me + 1 - 2 * (me % 2)
    along = me + 2 - 4 * (me // 2)
    return me, across, along, across + along - me


def greet(*others):
    barrier = pltpu.get_barrier_semaphore()
    for other in others:
        pl.semaphore_signal(barrier, inc=1, device_id={"section": other}, device_id_type=MESH)
    pl.semaphore_wait(barrier, len(others))


def link(source, target, sems, index, other):
    send, recv = sems
    return pltpu.make_async_remote_copy(
        src_ref=source,
        dst_ref=target,
        send_sem=send.at[index],
        recv_sem=recv.at[index],
        device_id={"section": other},
        device_id_type=MESH,
    )


def strips(count, work):
    def one(i, carry):
        work(pl.multiple_of(i * STRIP, STRIP))
        return carry

    lax.fori_loop(0, count // STRIP, one, 0)


def widen(block):
    rows, columns = block.shape
    if columns < LANES:
        block = jnp.concatenate((block, jnp.zeros((rows, LANES - columns), F32)), axis=1)
    return block.astype(BF16)


def grad_tiles(left, right, store, begin, end):
    def one(i, carry):
        rows = pl.ds(pl.multiple_of(i * TILE, TILE), TILE)
        store(rows, dot(left[:, rows], right[...], 0, 0).astype(BF16))
        return carry

    lax.fori_loop(begin, end, one, 0)


def gather_begin(out, piece, peers, sems, half):
    me, across, along, far = peers
    here = out.at[piece(me, half)]
    order = ((along, 0), (across, 1)) if half == 0 else ((across, 1), (along, 0))
    started = {}
    for other, way in order:
        copy = link(here, here, sems, 2 * half + way, other)
        copy.start()
        started[way] = copy
    return started


def gather_forward(out, piece, peers, sems, zero, one):
    me, across, along, far = peers
    zero[0].wait_recv()
    passing = out.at[piece(along, 0)]
    first = link(passing, passing, sems, 4, across)
    first.start()
    one[1].wait_recv()
    passing = out.at[piece(across, 1)]
    second = link(passing, passing, sems, 5, along)
    second.start()
    return first, second


def gather_finish(out, piece, peers, sems, zero, one, passed=None):
    first, second = passed or gather_forward(out, piece, peers, sems, zero, one)
    zero[1].wait_recv()
    one[0].wait_recv()
    first.wait_recv()
    second.wait_recv()
    for copy in (zero[0], zero[1], one[0], one[1], first, second):
        copy.wait_send()


def copy_sems(count):
    return [pltpu.SemaphoreType.DMA((count,)), pltpu.SemaphoreType.DMA((count,))]


def comm_params(ident):
    return params(collective_id=ident, has_side_effects=True)


def own_slice(source, target, sem, own):
    start = pl.multiple_of(lax.axis_index("section") * own, LANES)
    return pltpu.make_async_copy(source.at[:, pl.ds(start, own)], target, sem)


def stats_total(stats, got, stage, peers, sems, index):
    me, across, along, far = peers
    first = link(stats, got.at[0], sems, index, across)
    first.start()
    first.wait_recv()
    stage[...] = stats[...] + got[0]
    second = link(stage, got.at[1], sems, index + 1, along)
    second.start()
    second.wait_recv()
    first.wait_send()
    second.wait_send()
    return stage[...] + got[1]


def transfer(work, ins, outs, scratch, ident, microseconds, after=(), first=None, rows=ROWS):
    order = [n for kind in (FETCH, BLOCKS, LATE, OWN_PART) for n in ins if ins[n][1] == kind]
    stored = [n for n, (_, how) in outs.items() if how == STORE]
    buffers, places, low = {}, {}, 0
    for name in order + stored:
        if name in stored:
            buffers[name] = pltpu.VMEM(outs[name][0].shape, outs[name][0].dtype)
        else:
            array, how = ins[name]
            columns = array.shape[1] // (4 if how == OWN_PART else 1)
            buffers[name] = pltpu.VMEM((array.shape[0], columns), array.dtype)
        places[name] = low
        low += ins[name][0].shape[0] // rows if name in ins and ins[name][1] == BLOCKS else 1
    by_blocks = [n for n in order if ins[n][1] == BLOCKS]

    def kernel(*refs):
        refs = refs[len(after) :]
        names = list(ins) + list(outs)
        given = dict(zip(names, refs))
        refs = refs[len(names) :]
        own_names = list(buffers) + [LOCAL] + list(scratch)
        held = dict(zip(own_names, refs))
        r = types.SimpleNamespace(**{**given, **held})
        local = held[LOCAL]

        def copy(name):
            sem = local.at[places[name]]
            if name in stored:
                return pltpu.make_async_copy(held[name], given[name], sem)
            if ins[name][1] == OWN_PART:
                return own_slice(given[name], held[name], sem, held[name].shape[1])
            return pltpu.make_async_copy(given[name], held[name], sem)

        def block_copy(name, block):
            here = rows_of(block, rows)
            source, target = given[name].at[here, :], held[name].at[here, :]
            return pltpu.make_async_copy(source, target, local.at[places[name] + block])

        def start(*kinds):
            for name in order:
                if ins[name][1] in kinds:
                    copy(name).start()

        def wait_block(block):
            for name in by_blocks:
                block_copy(name, block).wait()

        start(FETCH)
        if first:
            first(r)
        if by_blocks:
            for block in range(ins[by_blocks[0]][0].shape[0] // rows):
                for name in by_blocks:
                    block_copy(name, block).start()
        start(LATE, OWN_PART)
        r.wait = lambda *which: [copy(n).wait() for n in which]
        r.store = lambda *which: [copy(n).start() for n in which]
        r.wait_block = wait_block
        work(r)
        for name in stored:
            copy(name).wait()

    spec = {SMEM: smem, VMEM: vmem}
    return pl.pallas_call(
        kernel,
        out_shape=tuple(o for o, _ in outs.values()),
        in_specs=[hbm()] * len(after) + [spec.get(how, hbm)() for _, how in ins.values()],
        out_specs=tuple(spec.get(how, hbm)() for _, how in outs.values()),
        scratch_shapes=list(buffers.values())
        + [pltpu.SemaphoreType.DMA((max(low, 1),))]
        + list(scratch.values()),
        cost_estimate=lasting(microseconds),
        compiler_params=params() if ident is None else comm_params(ident),
    )(*after, *[a for a, _ in ins.values()])


def rows_of(block, rows=ROWS):
    return pl.ds(pl.multiple_of(block * rows, rows), rows)


def owned(block, owner, half, own, rows):
    start = pl.multiple_of(block * rows + half * (rows // 2), rows // 2)
    return pl.ds(start, rows // 2), pl.ds(pl.multiple_of(owner * own, LANES), own)


def sum_scratch(name, count, own, rows=ROWS):
    buffer = pltpu.VMEM((2, count // 2, own), BF16)
    sems = pltpu.SemaphoreType.DMA((6 * (count // rows),))
    return {
        name + "_early": buffer,
        name + "_direct": buffer,
        name + "_late": buffer,
        name + "_stage": buffer,
        name + "_send": sems,
        name + "_recv": sems,
    }


def block_sum(r, name, part, peers, own, piece=None, place=None, rows=ROWS):
    if piece is None:
        piece = functools.partial(owned, own=own, rows=rows)
        place = functools.partial(rows_of, rows=rows // 2)
    me, across, along, far = peers
    early, direct, late, stage, send, recv = (
        getattr(r, name + end) for end in ("_early", "_direct", "_late", "_stage", "_send", "_recv")
    )
    sems = (send, recv)
    ways = ((across, along), (along, across))

    def early_copy(block, half):
        source = part.at[piece(block, far, half)]
        target = early.at[half, place(block)]
        return link(source, target, sems, block * 6 + half, ways[half][0])

    def direct_copy(block, half):
        first = ways[half][0]
        source = part.at[piece(block, first, half)]
        target = direct.at[half, place(block)]
        return link(source, target, sems, block * 6 + 2 + half, first)

    def late_copy(block, half):
        source = stage.at[half, place(block)]
        target = late.at[half, place(block)]
        return link(source, target, sems, block * 6 + 4 + half, ways[half][1])

    def begin(block):
        for half in range(2):
            early_copy(block, half).start()
        for half in range(2):
            direct_copy(block, half).start()

    def forward(block):
        for half in range(2):
            early_copy(block, half).wait_recv()
            here = place(block)
            passed = part[piece(block, ways[half][1], half)].astype(F32)
            stage[half, here, :] = (passed + early[half, here, :].astype(F32)).astype(BF16)
            late_copy(block, half).start()

    def arrived(block, half):
        direct_copy(block, half).wait_recv()
        late_copy(block, half).wait_recv()

    def total(block, half, start):
        row, column = piece(block, me, half)
        here = pl.ds(place(block).start + start, STRIP)
        mine = part[pl.ds(row.start + start, STRIP), column].astype(F32)
        return mine + direct[half, here, :].astype(F32) + late[half, here, :].astype(F32)

    def end(block):
        for half in range(2):
            early_copy(block, half).wait_send()
            direct_copy(block, half).wait_send()
            late_copy(block, half).wait_send()

    return types.SimpleNamespace(begin=begin, forward=forward, arrived=arrived, total=total, end=end)


def gather_sems(count):
    return pltpu.SemaphoreType.DMA((6 * (count // ROWS),))


def block_gather(out, peers, own, sems):
    me, across, along, far = peers

    def copy(block, owner, half, index, other):
        place = out.at[owned(block, owner, half, own, ROWS)]
        return link(place, place, sems, block * 6 + index, other)

    def own_copy(block, half, way):
        return copy(block, me, half, 2 * half + way, (along, across)[way])

    def pass_copy(block, half):
        return copy(block, (along, across)[half], half, 4 + half, (across, along)[half])

    def begin(block):
        for half, way in ((0, 0), (1, 1), (1, 0), (0, 1)):
            own_copy(block, half, way).start()

    def forward(block):
        for half in range(2):
            own_copy(block, half, half).wait_recv()
            pass_copy(block, half).start()

    def arrive(block):
        own_copy(block, 0, 1).wait_recv()
        own_copy(block, 1, 0).wait_recv()
        for half in range(2):
            pass_copy(block, half).wait_recv()

    def sent(block):
        for half in range(2):
            pass_copy(block, half).wait_send()
            for way in range(2):
                own_copy(block, half, way).wait_send()

    return types.SimpleNamespace(begin=begin, forward=forward, arrive=arrive, sent=sent)


def pipeline(count, compute, sums, finish, gather, extra=None, between=None, before=None, rows=ROWS):
    blocks = count // rows
    if before:
        before.begin(0)
        before.begin(1)
        before.forward(0)

    def tick(i, carry):
        if before:

            @pl.when(i < blocks - 2)
            def _():
                before.begin(i + 2)

            @pl.when(i < blocks - 1)
            def _():
                before.forward(i + 1)

            @pl.when(i < blocks)
            def _():
                before.arrive(i)

        @pl.when(i < blocks)
        def _():
            compute(i)
            for one in sums:
                one.begin(i)

        if between:
            between(i)

        @pl.when((i >= 1) & (i <= blocks))
        def _():
            for one in sums:
                one.forward(i - 1)

        @pl.when((i >= 2) & (i <= blocks + 1))
        def _():
            finish(i - 2)
            if gather:
                gather.begin(i - 2)

        if gather:

            @pl.when(i >= 3)
            def _():
                gather.forward(i - 3)

        if extra:
            extra(i)
        return carry

    lax.fori_loop(0, blocks + (3 if gather else 2), tick, 0)

    def close(i, carry):
        for one in sums:
            one.end(i)
        if gather:
            gather.arrive(i)
            gather.sent(i)
        if before:
            before.sent(i)
        return carry

    lax.fori_loop(0, blocks, close, 0)


def finish_strips(one, block, work, rows=ROWS):
    for half in range(2):
        one.arrived(block, half)

        def strip(start):
            row = pl.multiple_of(block * rows + half * (rows // 2), rows // 2) + start
            work(pl.ds(row, STRIP), one.total(block, half, start))

        strips(rows // 2, strip)


def views(refs, block, rows=ROWS):
    return [ref.at[rows_of(block, rows), :] for ref in refs]


def attention_forward(length, normed, mixed, packed, bias, pair, offset, x, shards, ident):
    count, width = normed.shape
    apart = mixed.shape[1] == width
    own = width // 4
    wide = width // 2
    keyed = pair.shape[1]
    low = packed.shape[1] - width // 2

    def weights(r):
        return unfold(r.packed, r.in_w, r.out_w, shards, r.fold)

    def first(r):
        for copy in weights(r):
            copy.start()

    def work(r):
        peers = plane()
        mine = pl.ds(pl.multiple_of(peers[0] * own, LANES), own)
        real = r.length[0]
        mixing = None
        if not apart:
            r.mixed[:, mine] = r.mixed_own[...]
        greet(peers[1], peers[2])
        if not apart:
            mixing = block_gather(r.mixed, peers, own, (r.mixed_send, r.mixed_recv))
        total = block_sum(r, "sum", r.part, peers, own)
        gather = block_gather(r.out, peers, own, (r.gather_send, r.gather_recv))
        saved = (r.update, r.shared, r.reset, r.cand, r.value, r.att, r.gated, r.probs)

        def compute(block):
            @pl.when(block == 0)
            def _():
                for copy in weights(r):
                    copy.wait()

            r.wait_block(block)
            attention_forward_block(
                real,
                block * ROWS,
                *views((r.normed, r.mixed), block),
                r.in_w,
                r.bias,
                r.pair,
                r.offset,
                *views((r.part,) + saved, block),
                r.out_w,
            )

        def finish(block):
            def strip(here, summed):
                pre = r.cand[here, :].astype(F32) + summed
                r.hidden[here, :] = pre.astype(BF16)
                old = r.x[here, :].astype(F32)
                made = old + sigmoid(r.update[here, :].astype(F32)) * (silu(pre) - old)
                r.out[here, mine] = made.astype(BF16)

            finish_strips(total, block, strip)

        def extra(i):
            @pl.when(i == 0)
            def _():
                r.wait("x")

            @pl.when(i == count // ROWS)
            def _():
                if not apart:
                    r.store("mixed")
                r.store("update", "shared", "reset", "value", "att", "gated", "probs")

        pipeline(count, compute, (total,), finish, gather, extra, before=mixing)

    rows = lambda columns: (shape((count, columns), BF16), STORE)
    return transfer(
        work,
        dict(
            length=(length, SMEM),
            packed=(packed, RAW),
            normed=(normed, BLOCKS),
            **(dict(mixed=(mixed, BLOCKS)) if apart else dict(mixed_own=(mixed, VMEM))),
            x=(x, OWN_PART),
            bias=(bias, VMEM),
            pair=(pair, VMEM),
            offset=(offset, VMEM),
        ),
        dict(
            out=(shape((count, width), BF16), VMEM),
            hidden=(shape((count, own), BF16), VMEM),
            **({} if apart else dict(mixed=rows(width))),
            update=rows(own),
            shared=rows(keyed),
            reset=rows(wide),
            value=rows(wide),
            att=rows(wide),
            gated=rows(wide),
            probs=rows(ATT),
        ),
        dict(
            part=pltpu.VMEM((count, width), BF16),
            cand=pltpu.VMEM((count, own), BF16),
            in_w=pltpu.VMEM((width, low), BF16),
            out_w=pltpu.VMEM((wide, width), BF16),
            fold=pltpu.SemaphoreType.DMA((2 * shards + 1,)),
            mixed_send=gather_sems(count),
            mixed_recv=gather_sems(count),
            **sum_scratch("sum", count, own),
            gather_send=gather_sems(count),
            gather_recv=gather_sems(count),
        ),
        ident,
        54,
        first=first,
    )


def gather_kernel(waits, *refs):
    own_ref, out_ref, send, recv = refs[waits:]
    count, own = own_ref.shape
    peers = plane()
    mine = pl.ds(pl.multiple_of(peers[0] * own, LANES), own)
    out_ref[:, mine] = own_ref[...]
    greet(peers[1], peers[2])
    whole = block_gather(out_ref, peers, own, (send, recv))
    blocks = count // ROWS
    for block in range(blocks):
        whole.begin(block)
        if block:
            whole.forward(block - 1)
    whole.forward(blocks - 1)
    for block in range(blocks):
        whole.arrive(block)
        whole.sent(block)


def gather_columns(own, ident, after=()):
    count, width = own.shape
    return pl.pallas_call(
        functools.partial(gather_kernel, len(after)),
        out_shape=shape((count, width * 4), BF16),
        in_specs=[hbm()] * len(after) + [vmem()],
        out_specs=vmem(),
        scratch_shapes=[gather_sems(count), gather_sems(count)],
        cost_estimate=lasting(20),
        compiler_params=comm_params(ident),
    )(*after, own)


def feed_forward_joined(x, gain, shift, weights, bias, own_out, ident):
    count, width = x.shape
    hidden = bias.shape[1]
    own = width // 4

    def work(r):
        peers = plane()
        mine = pl.ds(pl.multiple_of(peers[0] * own, LANES), own)
        greet(peers[1], peers[2])
        r.wait("weights")
        total = block_sum(r, "sum", r.part, peers, own)
        gather = block_gather(r.out, peers, own, (r.gather_send, r.gather_recv))

        def compute(block):
            r.wait_block(block)
            x_rows, *outs = views((r.x, r.part, r.pre, r.n, r.normed, r.scale), block)
            feed_forward_kernel(x_rows, r.gain, r.shift, r.weights, r.bias, *outs)

        def finish(block):
            def strip(here, summed):
                made = r.x[here, mine].astype(F32) + summed + r.own_out[...]
                r.out[here, mine] = made.astype(BF16)

            finish_strips(total, block, strip)

        def extra(i):
            @pl.when(i == count // ROWS)
            def _():
                r.store("pre", "n", "normed", "scale")

        pipeline(count, compute, (total,), finish, gather, extra)

    rows = lambda columns, kind=BF16: (shape((count, columns), kind), STORE)
    return transfer(
        work,
        dict(
            x=(x, BLOCKS),
            weights=(weights, FETCH),
            gain=(gain, VMEM),
            shift=(shift, VMEM),
            bias=(bias, VMEM),
            own_out=(own_out, VMEM),
        ),
        dict(
            out=(shape((count, width), BF16), VMEM),
            pre=rows(hidden),
            n=rows(width),
            normed=rows(width),
            scale=rows(LANES, F32),
        ),
        dict(
            part=pltpu.VMEM((count, width), BF16),
            **sum_scratch("sum", count, own),
            gather_send=gather_sems(count),
            gather_recv=gather_sems(count),
        ),
        ident,
        40,
    )


def feed_backward(given, k, p, weights, shards, ident, after=()):
    corrected = isinstance(given, tuple)
    both_ways = k.feed_pre is None
    count, width = k.middle.shape
    own = width // 4
    hidden = p.feed_in.shape[1]
    norms, gain = p.own, p.feed_gain
    blocks = count // ROWS

    def work(r):
        peers = plane()
        me, across, along, far = peers
        mine = pl.ds(pl.multiple_of(me * own, LANES), own)
        if corrected:
            r.z[:, mine] = r.z_own[...]
        greet(across, along)
        before = None
        if corrected:
            before = block_gather(r.z, peers, own, (r.z_send, r.z_recv))
        r.sums[...] = jnp.zeros_like(r.sums)
        r.bias[...] = jnp.zeros_like(r.bias)
        total = block_sum(r, "sum", r.part, peers, own)
        gather = block_gather(r.out, peers, own, (r.gather_send, r.gather_recv))

        def quarter(block, owner, half):
            size = count // 4
            return (
                pl.ds(pl.multiple_of(owner * size, size), size),
                pl.ds(half * (width // 2), width // 2),
            )

        if both_ways:
            last = block_sum(
                r, "last", r.made, peers, own, quarter, lambda block: pl.ds(0, count // 4)
            )

        def last_rows():
            for half in range(2):
                last.arrived(0, half)
                lanes = slice(half * (width // 2), (half + 1) * (width // 2))

                def strip(start):
                    here = pl.ds(start, STRIP)
                    row = pl.ds(pl.multiple_of(me * (count // 4), STRIP) + start, STRIP)
                    made = r.middle[row, lanes].astype(F32) + last.total(0, half, start)
                    r.block_out[here, lanes] = (made + r.out_bias[:, lanes]).astype(BF16)

                strips(count // 4, strip)

        def stats_copy(block, step):
            lanes = rows_of(block)
            source = (r.stats, r.stats_stage)[step].at[:, lanes]
            sems = (r.stats_send, r.stats_recv)
            other = (across, along)[step]
            return link(source, r.stats_got.at[step, :, lanes], sems, 2 * block + step, other)

        def compute(block):
            here = rows_of(block)

            @pl.when(block == 0)
            def _():
                r.wait("weights")
                if corrected:
                    sems = (r.means_send, r.means_recv)
                    r.means[...] = stats_total(
                        r.z_stats, r.means_got, r.means_stage, peers, sems, 0
                    )

            r.wait_block(block)
            if corrected:
                xn, xscale = normalise(r.x_full[here, :].astype(F32))
                means = r.means[:, here].T * (1.0 / width)
                z = r.z[here, :].astype(F32)
                g = z - xscale * (means[:, 0:1] + xn * means[:, 1:2])
                r.g[here, :] = g.astype(BF16)
            if both_ways:
                x_rows, *made = views((r.middle, r.made, r.pre, r.n, r.normed, r.scale), block)
                feed_forward_kernel(x_rows, r.gain, r.shift, r.weights, r.in_bias, *made)
            g_rows, pre_rows, n_rows = views((r.g, r.pre, r.n), block)
            part, gpre, act = views((r.part, r.gpre, r.act), block)
            feed_backward_block(
                g_rows,
                pre_rows,
                n_rows,
                r.gain,
                r.weights,
                part,
                r.stats,
                gpre,
                act,
                r.sums,
                r.bias,
                here,
            )
            stats_copy(block, 0).start()

        def finish(block):
            here = rows_of(block)
            stats_copy(block, 1).wait_recv()
            every = r.stats_stage[:, here] + r.stats_got[1, :, here]
            r.columns[here, :] = every.T * (1.0 / width)

            def strip(here, summed):
                e = summed * r.norms[2:3, :]
                n_own = r.n[here, mine].astype(F32)
                inner = e - r.columns[here, 0:1] - n_own * r.columns[here, 1:2]
                g = r.g[here, mine].astype(F32) + r.scale[here, 0:1] * inner
                g = g.astype(BF16).astype(F32)
                u = sigmoid(r.update[here, :].astype(F32))
                pre = r.hidden[here, :].astype(F32)
                s = sigmoid(pre)
                x = r.x[here, :].astype(F32)
                r.gupdate[here, :] = (g * (pre * s - x) * (u * (1.0 - u))).astype(BF16)
                r.resid[here, :] = g * (1.0 - u)
                r.out[here, mine] = (g * u * (s * (1.0 + pre * (1.0 - s)))).astype(BF16)

            finish_strips(total, block, strip)

        def small_grads():
            r.grad[:, hidden + width :] = jnp.zeros((width, LANES), BF16)
            size = width // shards
            for shard in range(shards):
                lanes = slice(shard * size, (shard + 1) * size)
                block = jnp.concatenate(
                    (r.sums[0:3, lanes], r.bias[0:1, lanes], jnp.zeros((SMALL - 4, size), F32)),
                    axis=0,
                )
                r.grad[shard * size : shard * size + SMALL, hidden + width :] = widen(block)

        def in_grad(rows, value):
            r.grad[rows, :hidden] = value

        def out_grad(rows, value):
            r.grad[rows, hidden : hidden + width] = value

        def extra(i):
            @pl.when((i >= 1) & (i <= blocks))
            def _():
                here = rows_of(i - 1)
                stats_copy(i - 1, 0).wait_recv()
                r.stats_stage[:, here] = r.stats[:, here] + r.stats_got[0, :, here]
                stats_copy(i - 1, 1).start()

            @pl.when(i == 0)
            def _():
                r.wait("update", "hidden", "x")
                if not both_ways:
                    r.wait("scale", "normed")

            if both_ways:

                @pl.when(i == blocks - 1)
                def _():
                    last.begin(0)

                @pl.when(i == blocks)
                def _():
                    last.forward(0)

                @pl.when(i == blocks + 2)
                def _():
                    last_rows()
                    last.end(0)

            @pl.when(i == blocks + 1)
            def _():
                r.store("gupdate", "resid")

        def between(i):
            @pl.when(i == blocks)
            def _():
                grad_tiles(r.normed, r.gpre, in_grad, 0, width // TILE)
                small_grads()
                grad_tiles(r.act, r.g, out_grad, 0, hidden // TILE)
                r.store("grad")

        pipeline(count, compute, (total,), finish, gather, extra, between, before)

        def close(i, carry):
            stats_copy(i, 0).wait_send()
            stats_copy(i, 1).wait_send()
            return carry

        lax.fori_loop(0, blocks, close, 0)

    if corrected:
        z_own, z_stats, x_full = given
        first = dict(z_own=(z_own, VMEM), x_full=(x_full, BLOCKS), z_stats=(z_stats, VMEM))
        both = pltpu.SemaphoreType.DMA((2,))
        extra_scratch = dict(
            g=pltpu.VMEM((count, width), BF16),
            z=pltpu.VMEM((count, width), BF16),
            z_send=gather_sems(count),
            z_recv=gather_sems(count),
            means=pltpu.VMEM((CHUNKS, count), F32),
            means_stage=pltpu.VMEM((CHUNKS, count), F32),
            means_got=pltpu.VMEM((2, CHUNKS, count), F32),
            means_send=both,
            means_recv=both,
        )
    else:
        first = dict(g=(given, BLOCKS))
        extra_scratch = {}
    extra_outs = {}
    if both_ways:
        saved = {}
        first.update(
            middle=(k.middle, BLOCKS),
            shift=(p.feed_shift, VMEM),
            in_bias=(p.feed_in, VMEM),
            out_bias=(p.feed_out, VMEM),
        )
        extra_outs.update(block_out=(shape((count // 4, width), BF16), VMEM))
        rows = pltpu.VMEM((count, width), BF16)
        slot = pltpu.VMEM((2, count // 4, width // 2), BF16)
        ends = pltpu.SemaphoreType.DMA((6,))
        extra_scratch.update(
            made=rows,
            pre=pltpu.VMEM((count, hidden), BF16),
            n=rows,
            normed=rows,
            scale=pltpu.VMEM((count, LANES), F32),
            last_early=slot,
            last_direct=slot,
            last_late=slot,
            last_stage=slot,
            last_send=ends,
            last_recv=ends,
        )
    else:
        saved = dict(
            pre=(k.feed_pre, BLOCKS),
            n=(k.feed_n, BLOCKS),
            scale=(k.feed_scale, LATE),
            normed=(k.feed_normed, LATE),
        )
    sems = pltpu.SemaphoreType.DMA((2 * blocks,))
    return transfer(
        work,
        dict(
            weights=(weights, FETCH),
            **first,
            **saved,
            update=(k.update, LATE),
            hidden=(k.hidden, LATE),
            x=(k.x, OWN_PART),
            gain=(gain, VMEM),
            norms=(norms, VMEM),
        ),
        dict(
            out=(shape((count, width), BF16), VMEM),
            gupdate=(shape((count, own), BF16), STORE),
            resid=(shape((count, own), F32), STORE),
            grad=(shape((width, hidden + width + LANES), BF16), STORE),
            **extra_outs,
        ),
        dict(
            part=pltpu.VMEM((count, width), BF16),
            gpre=pltpu.VMEM((count, hidden), BF16),
            act=pltpu.VMEM((count, hidden), BF16),
            sums=pltpu.VMEM((8, width), F32),
            bias=pltpu.VMEM((8, hidden), F32),
            stats=pltpu.VMEM((CHUNKS, count), F32),
            stats_stage=pltpu.VMEM((CHUNKS, count), F32),
            stats_got=pltpu.VMEM((2, CHUNKS, count), F32),
            columns=pltpu.VMEM((count, CHUNKS), F32),
            stats_send=sems,
            stats_recv=sems,
            **extra_scratch,
            **sum_scratch("sum", count, own),
            gather_send=gather_sems(count),
            gather_recv=gather_sems(count),
        ),
        ident,
        46,
        after,
    )


def attention_backward(length, gout, gupdate, k, packed, pair, offset, shards, ident, after=()):
    shared, reset, value, att, probs = k.saved
    count, width = gout.shape
    own = width // 4
    wide = width // 2
    keyed = pair.shape[1]
    total = packed.shape[1] - width // 2
    rows = 2 * ROWS
    blocks = count // rows
    few = wide // shards
    block_rows = width // shards

    def weights(r):
        return unfold(r.packed, r.in_w, r.out_w, shards, r.fold)

    def first(r):
        for copy in weights(r):
            copy.start()

    def work(r):
        peers = plane()
        mine = pl.ds(pl.multiple_of(peers[0] * own, LANES), own)
        real = r.length[0]
        greet(peers[1], peers[2])
        r.bias[...] = jnp.zeros_like(r.bias)
        r.pairs[...] = jnp.zeros_like(r.pairs)
        one = block_sum(r, "one", r.gmixed_part, peers, own, rows=rows)
        two = block_sum(r, "two", r.gvalue_part, peers, own, rows=rows)

        def compute(block):
            @pl.when(block == 0)
            def _():
                for copy in weights(r):
                    copy.wait()

            r.wait_block(block)
            attention_backward_block(
                real,
                block * rows,
                mine,
                *views((r.gout, r.gupdate, r.shared, r.reset, r.value, r.att, r.probs), block, rows),
                r.in_w,
                r.pair,
                r.offset,
                *views((r.gmixed_part, r.gvalue_part, r.gbase, r.gvalue), block, rows),
                r.bias,
                r.pairs,
                r.out_w,
            )

        def finish(block):
            def keep(out):
                def strip(here, summed):
                    out[here, :] = summed

                return strip

            finish_strips(one, block, keep(r.gmixed), rows)
            finish_strips(two, block, keep(r.gnormed), rows)

        def value_grad(rows, value):
            r.grad[rows, :wide] = value

        def base_grad(rows, value):
            r.grad[rows, wide:total] = value

        def out_grad(rows, value):
            for i in range(TILE // few):
                start = (rows.start // few + i) * block_rows
                for half in range(2):
                    here = pl.ds(pl.multiple_of(start + half * few, few), few)
                    r.grad[here, total : total + width // 2] = value[
                        i * few : (i + 1) * few, half * (width // 2) : (half + 1) * (width // 2)
                    ]

        def small_grads():
            last = total + width // 2
            r.grad[:, last:] = jnp.zeros((width, LANES), BF16)
            pieces = [r.bias[0:1, i * LANES : (i + 1) * LANES] for i in range(total // LANES)]
            block = jnp.concatenate(pieces + [r.pairs[0:3, :]], axis=0).astype(BF16)
            for shard in range(shards):
                r.grad[shard * block_rows : shard * block_rows + SMALL, last:] = block

        def extra(i):
            @pl.when(i == 0)
            def _():
                r.wait("normed", "mixed", "gated")

        def between(i):
            @pl.when(i == blocks)
            def _():
                small_grads()
                grad_tiles(r.mixed, r.gbase, base_grad, 0, width // TILE)
                grad_tiles(r.normed, r.gvalue, value_grad, 0, width // TILE)
                grad_tiles(r.gated, r.gout, out_grad, 0, wide // TILE)
                r.store("grad")

        pipeline(count, compute, (one, two), finish, None, extra, between, rows=rows)

    return transfer(
        work,
        dict(
            length=(length, SMEM),
            packed=(packed, RAW),
            gout=(gout, BLOCKS),
            gupdate=(gupdate, BLOCKS),
            shared=(shared, BLOCKS),
            reset=(reset, BLOCKS),
            value=(value, BLOCKS),
            att=(att, BLOCKS),
            probs=(probs, BLOCKS),
            normed=(k.normed, LATE),
            mixed=(k.mixed, LATE),
            gated=(k.gated, LATE),
            pair=(pair, VMEM),
            offset=(offset, VMEM),
        ),
        dict(
            gmixed=(shape((count, own), F32), VMEM),
            gnormed=(shape((count, own), F32), VMEM),
            grad=(shape((width, total + width // 2 + LANES), BF16), STORE),
        ),
        dict(
            gmixed_part=pltpu.VMEM((count, width), BF16),
            gvalue_part=pltpu.VMEM((count, width), BF16),
            gbase=pltpu.VMEM((count, total - wide), BF16),
            gvalue=pltpu.VMEM((count, wide), BF16),
            bias=pltpu.VMEM((8, total), F32),
            pairs=pltpu.VMEM((8, keyed), F32),
            in_w=pltpu.VMEM((width, total), BF16),
            out_w=pltpu.VMEM((wide, width), BF16),
            fold=pltpu.SemaphoreType.DMA((2 * shards + 1,)),
            **sum_scratch("one", count, own, rows),
            **sum_scratch("two", count, own, rows),
        ),
        ident,
        40,
        after,
        first,
        rows,
    )


def block_piece(whole):
    def piece(owner, half):
        size = whole.shape[1] // 2
        return owner, pl.ds(half * size, size), slice(None)

    return piece


def final_kernel(number, layers, z_ref, stats_ref, x_ref, *refs):
    blocks, refs = refs[:number], refs[number:]
    average_ins, refs = refs[: 5 * layers], refs[5 * layers :]
    (out_ref, sums_ref), refs = refs[:2], refs[2:]
    gathered, refs = refs[:number], refs[number:]
    land, x_own, got, stats_stage, total_buf, local_sem, send, recv = refs[:8]
    m_buf, g_buf, held_sems = refs[8:11]
    block_sems = [refs[11 + 2 * i : 13 + 2 * i] for i in range(number)]
    count, own = z_ref.shape
    quarter, width = out_ref.shape
    peers = plane()
    me = peers[0]

    def rows(owner):
        return pl.ds(pl.multiple_of(owner * quarter, quarter), quarter)

    mine = pl.ds(pl.multiple_of(me * own, LANES), own)
    fetch = pltpu.make_async_copy(x_ref.at[rows(me), :], x_own, local_sem)
    fetch.start()
    held = []
    for layer in range(layers):
        for k, buffer in enumerate((m_buf, g_buf)):
            source = average_ins[5 * layer + k]
            sem = held_sems.at[2 * layer + k]
            held.append(pltpu.make_async_copy(source, buffer.at[layer], sem))
            held[-1].start()

    def sums_of(layer):
        rate, back, rest = average_ins[5 * layer + 2 : 5 * layer + 5]
        dims = rate.shape[0]
        low = layer * (2 * dims + 8)
        held[2 * layer].wait()
        held[2 * layer + 1].wait()
        average_sums(m_buf.at[layer], g_buf.at[layer], rate, back, sums_ref, low)
        sums_ref[low + 2 * dims : low + 2 * dims + 8, :] = rest[...]

    land[:, mine] = z_ref[rows(me), :]
    for block, whole in zip(blocks, gathered):
        whole[me] = block[...]
    greet(*peers[1:])
    sems = (send, recv)
    copies = []
    for index, other in enumerate(peers[1:]):
        copies.append(link(z_ref.at[rows(other), :], land.at[:, mine], sems, 2 + index, other))
        copies[-1].start()
    total_buf[...] = stats_total(stats_ref, got, stats_stage, peers, sems, 0)
    begun = [
        [gather_begin(whole, block_piece(whole), peers, k, half) for half in range(2)]
        for whole, k in zip(gathered, block_sems)
    ]
    part = total_buf[:, pl.ds(pl.multiple_of(me * quarter, LANES), quarter)]
    means = part.T * (1.0 / width)
    fetch.wait()
    for copy in copies:
        copy.wait_recv()
    n, scale = normalise(x_own[...].astype(F32))
    g = land[...].astype(F32) - scale * (means[:, 0:1] + n * means[:, 1:2])
    out_ref[...] = g.astype(BF16)
    for layer in range(1, layers):
        sums_of(layer)
    passed = [
        gather_forward(whole, block_piece(whole), peers, k, zero, one)
        for whole, k, (zero, one) in zip(gathered, block_sems, begun)
    ]
    sums_of(0)
    for whole, k, (zero, one), two in zip(gathered, block_sems, begun, passed):
        gather_finish(whole, block_piece(whole), peers, k, zero, one, two)
    for copy in copies:
        copy.wait_send()


def final_exchange(z, stats, x, blocks, averages, sections, ident):
    layers = len(averages)
    dims, _, own = averages[0][2].shape
    held_dims = (layers,) + averages[0][0].shape
    count, own = z.shape
    width = x.shape[1]
    quarter = count // 4
    number = len(blocks)
    return pl.pallas_call(
        functools.partial(final_kernel, number, layers),
        out_shape=(
            shape((quarter, width), BF16),
            shape((layers * (2 * dims + 8), own), F32),
        )
        + tuple(shape((sections,) + a.shape, BF16) for a in blocks),
        in_specs=[vmem(), vmem(), hbm()]
        + [vmem()] * number
        + [hbm(), hbm(), vmem(), vmem(), vmem()] * layers,
        out_specs=(vmem(),) * (2 + number),
        scratch_shapes=[
            pltpu.VMEM((quarter, width), BF16),
            pltpu.VMEM((quarter, width), BF16),
            pltpu.VMEM((2,) + stats.shape, F32),
            pltpu.VMEM(stats.shape, F32),
            pltpu.VMEM(stats.shape, F32),
            pltpu.SemaphoreType.DMA,
        ]
        + copy_sems(5)
        + [
            pltpu.VMEM(held_dims, F32),
            pltpu.VMEM(held_dims, F32),
            pltpu.SemaphoreType.DMA((2 * layers,)),
        ]
        + copy_sems(6) * number,
        cost_estimate=lasting(10 + 20 * number),
        compiler_params=comm_params(ident),
    )(z, stats, x, *blocks, *[a for one in averages for a in one])


def sums_kernel(shards, holders, sums_ref, block_ref, channels_ref, whole_ref, *refs):
    sums_land, send_s, recv_s, send_c, recv_c, send, recv = refs
    peers = plane()
    me = peers[0]
    slot = lax.axis_index("dp")
    holding = slot // holders == me
    whole_ref[me] = block_ref[...]
    barrier = pltpu.get_barrier_semaphore()
    for other in peers[1:]:
        pl.semaphore_signal(barrier, inc=1, device_id={"section": other}, device_id_type=MESH)
    for step in range(1, shards):
        other = (slot + step) % shards
        pl.semaphore_signal(barrier, inc=1, device_id={"dp": other}, device_id_type=MESH)
    pl.semaphore_wait(barrier, shards + 2)

    def sums_copy(target, index, place):
        return pltpu.make_async_remote_copy(
            src_ref=sums_ref,
            dst_ref=sums_land.at[place],
            send_sem=send_s.at[index],
            recv_sem=recv_s.at[place],
            device_id={"dp": target},
            device_id_type=MESH,
        )

    def sums_out(index):
        target = me * holders + index
        place = jnp.maximum((slot - target + shards) % shards - 1, 0)
        return target, sums_copy(target, index, place)

    for index in range(holders):
        target, copy = sums_out(index)

        @pl.when(target != slot)
        def _():
            copy.start()

    piece = block_piece(whole_ref)
    zero, one = (gather_begin(whole_ref, piece, peers, (send, recv), half) for half in range(2))
    passed = gather_forward(whole_ref, piece, peers, (send, recv), zero, one)

    def channels_copy(other, index):
        return link(channels_ref, channels_ref, (send_c, recv_c), index, other)

    @pl.when(holding)
    def _():
        summed = sums_ref[...]
        for step in range(1, shards):
            sums_copy((slot + step) % shards, 0, step - 1).wait_recv()
            summed = summed + sums_land[step - 1]
        channels_ref[...] = summed
        for index, other in enumerate(peers[1:]):
            channels_copy(other, index).start()

    gather_finish(whole_ref, piece, peers, (send, recv), zero, one, passed)

    for index, other in enumerate(peers[1:]):

        @pl.when(slot // holders == other)
        def _():
            channels_copy(other, index).wait_recv()

    @pl.when(holding)
    def _():
        for index, other in enumerate(peers[1:]):
            channels_copy(other, index).wait_send()

    for index in range(holders):
        target, copy = sums_out(index)

        @pl.when(target != slot)
        def _():
            copy.wait_send()


def gather_sums(sums, block, sections, shards, holders, ident):
    return pl.pallas_call(
        functools.partial(sums_kernel, shards, holders),
        out_shape=(shape(sums.shape, F32), shape((sections,) + block.shape, BF16)),
        in_specs=[vmem()] * 2,
        out_specs=(vmem(),) * 2,
        scratch_shapes=[pltpu.VMEM((shards - 1,) + sums.shape, F32)]
        + copy_sems(max(shards - 1, holders))
        + copy_sems(3)
        + copy_sems(6),
        cost_estimate=lasting(25),
        compiler_params=comm_params(ident),
    )(sums, block)


def woven_parts(part, here, low, size, shards):
    step = size // shards
    return jnp.concatenate(
        [
            part[k, here, low + d * step : low + (d + 1) * step].astype(F32)
            for d in range(shards)
            for k in range(part.shape[0])
        ],
        axis=1,
    )


def joined_parts(part, here, low, size):
    return jnp.concatenate(
        [part[k, here, low : low + size].astype(F32) for k in range(part.shape[0])], axis=1
    )


def by_strips(rows, work):
    def strip(i, carry):
        work(pl.ds(pl.multiple_of(i * SMALL, SMALL), SMALL))
        return carry

    lax.fori_loop(0, rows // SMALL, strip, 0)


def attention_outputs(shards, layer, part, extras, outs):
    value_ref, base_ref, out_ref, value_bias_ref, base_bias_ref, pair_ref, query_ref = outs[:7]
    norm_outs, average_outs = outs[7:10], outs[10:]
    sections = part.shape[0]
    width = out_ref.shape[2]
    wide = value_ref.shape[2] // sections
    own = width // sections
    keyed = base_ref.shape[2] - 2 * width - wide * sections
    edge = wide + own
    total = edge + keyed + wide + own
    few = wide // shards

    def strip(here):
        value_ref[0, here, :] = woven_parts(part, here, 0, wide, shards)
        base_ref[0, here, :width] = joined_parts(part, here, wide, own)
        shared = part[0, here, edge : edge + keyed].astype(F32)
        for k in range(1, sections):
            shared += part[k, here, edge : edge + keyed].astype(F32)
        low = width
        base_ref[0, here, low : low + keyed] = shared
        low += keyed
        base_ref[0, here, low : low + wide * sections] = woven_parts(
            part, here, edge + keyed, wide, shards
        )
        low += wide * sections
        base_ref[0, here, low:] = joined_parts(part, here, edge + keyed + wide, own)

    by_strips(value_ref.shape[1], strip)
    for k in range(sections):
        for half in range(2):
            columns = slice(half * (width // 2), (half + 1) * (width // 2))
            out_ref[0, k * few : (k + 1) * few, columns] = part[
                k, half * few : (half + 1) * few, total : total + width // 2
            ].astype(F32)
    slot = lax.axis_index("dp")
    row = slice(layer, layer + 1)
    blocks = [part[k, :SMALL, total + width // 2 :].astype(F32) for k in range(sections)]
    lines = [
        jnp.concatenate([b[i : i + 1] for i in range(total // LANES)], axis=1) for b in blocks
    ]
    summed = sum(blocks[1:], blocks[0])

    def mine(line):
        size = line.shape[1] // shards
        return chosen([line[:, d * size : (d + 1) * size] for d in range(shards)], slot)

    value_bias_ref[row, :] = jnp.concatenate([mine(line[:, :wide]) for line in lines], axis=1)
    low = edge + keyed
    base_line = jnp.concatenate(
        [line[:, wide:edge] for line in lines]
        + [sum((line[:, edge:low] for line in lines[1:]), lines[0][:, edge:low])]
        + [
            line[:, low + d * few : low + (d + 1) * few]
            for d in range(shards)
            for line in lines
        ]
        + [line[:, low + wide :] for line in lines],
        axis=1,
    )
    base_bias_ref[row, :] = mine(base_line)
    first = total // LANES
    for k in range(2):
        pair_ref[layer, k : k + 1, :] = mine(summed[first + k : first + k + 1])
    query_ref[row, :] = mine(summed[first + 2 : first + 3])

    channels_ref, decay_ref, input_ref, output_ref = extras
    dims, size = decay_ref.shape[1:]
    holders = own // size
    low = layer * (2 * dims + 8)

    def channels(start, count):
        here = slice(low + start, low + start + count)
        pieces = [channels_ref[here, k * size : (k + 1) * size] for k in range(holders)]
        return chosen(pieces, slot % holders)

    sums = channels(2 * dims, 8)
    for k, ref in enumerate(norm_outs):
        ref[row, :] = sums[k : k + 1]
    of_states, of_slopes = channels(0, dims), channels(dims, dims)
    rate = sigmoid(decay_ref[layer])
    drive = (1.0 - rate) * input_ref[layer]
    gdrive = output_ref[layer] * of_states
    grate = drive * output_ref[layer] * of_slopes - input_ref[layer] * gdrive
    average_outs[0][layer] = grate * rate * (1.0 - rate)
    average_outs[1][layer] = (1.0 - rate) * gdrive
    average_outs[2][layer] = drive * of_states


def feed_outputs(shards, layer, feed, extras, outs):
    in_ref, out_ref, gain_ref, shift_ref, out_bias_ref, in_bias_ref = outs
    sections, rows = feed.shape[:2]
    width = out_ref.shape[2]
    hidden = in_ref.shape[2] // sections

    def strip(here):
        in_ref[0, here, :] = woven_parts(feed, here, 0, hidden, shards)

    by_strips(rows, strip)
    for k in range(sections):
        out_ref[0, k * rows : (k + 1) * rows, :] = feed[k, :, hidden : hidden + width].astype(F32)
    size = width // shards
    row = slice(layer, layer + 1)
    blocks = [feed[k, :SMALL, hidden + width :].astype(F32)[:, :size] for k in range(sections)]
    summed = sum(blocks[1:], blocks[0])
    gain_ref[row, :] = summed[0:1]
    shift_ref[row, :] = summed[1:2]
    out_bias_ref[row, :] = blocks[0][2:3]
    in_bias_ref[row, :] = jnp.concatenate([b[3:4] for b in blocks], axis=1)


def assemble_kernel(work, shards, layers, more, *refs):
    extras, outs = refs[layers : layers + more], refs[layers + more :]
    for layer in range(layers):

        @pl.when(pl.program_id(0) == layer)
        def _():
            work(shards, layer, refs[layer], extras, outs)


def assemble(work, gathered, extras, dims, small_dims, shards):
    layers = len(gathered)

    def whole(dims):
        return pl.BlockSpec(dims, lambda i, n=len(dims): (0,) * n)

    return pl.pallas_call(
        functools.partial(assemble_kernel, work, shards, layers, len(extras)),
        grid=(layers,),
        out_shape=tuple(shape((layers,) + d, F32) for d in dims + small_dims),
        in_specs=[whole(a.shape) for a in gathered + extras],
        out_specs=tuple(
            pl.BlockSpec((1,) + d, lambda i, n=len(d): (i,) + (0,) * n) for d in dims
        )
        + tuple(whole((layers,) + d) for d in small_dims),
        cost_estimate=lasting(6),
        compiler_params=params(),
    )(*gathered, *extras)


def chosen(pieces, section=None):
    if section is None:
        section = lax.axis_index("section")
    result = pieces[0]
    for k in range(1, len(pieces)):
        result = jnp.where(section == k, pieces[k], result)
    return result


def pick(ref, index, low, size, shards, sections):
    step = size // (shards * sections)
    parts = []
    section = lax.axis_index("section")
    for shard in range(shards):
        start = low + shard * sections * step
        if 2 * step == LANES and start % LANES == 0:
            pair = pl.ds(pl.multiple_of(start + section // 2 * LANES, LANES), LANES)
            both = ref[index + (pair,)]
            parts.append(jnp.where(section % 2 == 0, both[:, :step], both[:, step:]))
            continue
        if step == LANES and start % LANES == 0:
            one = pl.ds(pl.multiple_of(start + section * LANES, LANES), LANES)
            parts.append(ref[index + (one,)])
            continue
        parts.append(
            chosen([ref[index + (slice(start + k * step, start + (k + 1) * step),)] for k in range(sections)])
        )
    return jnp.concatenate(parts, axis=-1)


def pack_attention_kernel(shards, sections, value_ref, base_ref, out_ref, packed_ref):
    rows, wide_all = value_ref.shape[1:]
    few_all, width = out_ref.shape[1:]
    wide, own, few = wide_all // sections, width // sections, few_all // sections
    keyed = base_ref.shape[2] - 2 * width - wide_all
    section = lax.axis_index("section")
    low = wide + own + keyed

    def strip(i, carry):
        here = pl.ds(pl.multiple_of(i * SMALL, SMALL), SMALL)

        def base(start, size):
            return base_ref[0, here, pl.ds(pl.multiple_of(start, LANES), size)]

        packed_ref[here, :wide] = pick(value_ref, (0, here), 0, wide_all, shards, sections)
        packed_ref[here, wide : wide + own] = base(section * own, own)
        packed_ref[here, wide + own : low] = base(width, keyed)
        packed_ref[here, low : low + wide] = pick(
            base_ref, (0, here), width + keyed, wide_all, shards, sections
        )
        packed_ref[here, low + wide : low + wide + own] = base(
            width + keyed + wide_all + section * own, own
        )
        return carry

    lax.fori_loop(0, rows // SMALL, strip, 0)
    low += wide + own
    mine = pl.ds(pl.multiple_of(section * few, few), few)
    for half in range(2):
        packed_ref[half * few : (half + 1) * few, low:] = out_ref[
            0, mine, half * (width // 2) : (half + 1) * (width // 2)
        ]


def pack_feed_kernel(shards, sections, in_ref, out_ref, packed_ref):
    rows, hidden_all = in_ref.shape[1:]
    hidden = hidden_all // sections
    size = out_ref.shape[1] // sections

    def strip(i, carry):
        here = pl.ds(pl.multiple_of(i * SMALL, SMALL), SMALL)
        packed_ref[here, :hidden] = pick(in_ref, (0, here), 0, hidden_all, shards, sections)
        return carry

    lax.fori_loop(0, rows // SMALL, strip, 0)
    start = pl.multiple_of(lax.axis_index("section") * size, size)
    packed_ref[:, hidden:] = out_ref[0, pl.ds(start, size), :]


def pack(work, layer, columns, shards, sections, arrays, after=()):
    rows = arrays[0].shape[1]

    def kernel(*refs):
        work(shards, sections, *refs[len(after) :])

    return pl.pallas_call(
        kernel,
        grid=(1,),
        out_shape=shape((rows, columns), BF16),
        in_specs=[hbm()] * len(after)
        + [pl.BlockSpec((1,) + a.shape[1:], lambda i: (layer, 0, 0)) for a in arrays],
        out_specs=pl.BlockSpec((rows, columns), lambda i: (0, 0)),
        cost_estimate=lasting(3),
        compiler_params=params(),
    )(*after, *arrays)


def unpack_kernel(layers, shards, sections, places, everyone_ref, *refs):
    base_buf = refs[-1]
    section = lax.axis_index("section")
    outs = 14
    for layer in range(layers):
        (
            gain_ref,
            shift_ref,
            feed_gain_ref,
            feed_shift_ref,
            feed_out_ref,
            own_ref,
            rate_ref,
            coef_ref,
            bias_ref,
            feed_in_ref,
            pair_ref,
            offset_ref,
            skip_ref,
            own_out_ref,
        ) = refs[layer * outs : (layer + 1) * outs]
        width = gain_ref.shape[1]
        own = width // sections
        mine = pl.ds(pl.multiple_of(section * own, LANES), own)
        row = slice(layer, layer + 1)

        def joined(low, size):
            return jnp.concatenate(
                [everyone_ref[d, row, low : low + size] for d in range(shards)], axis=1
            )

        def share(low, size):
            step = size // sections
            return jnp.concatenate(
                [
                    chosen(
                        [
                            everyone_ref[d, row, low + k * step : low + (k + 1) * step]
                            for k in range(sections)
                        ]
                    )
                    for d in range(shards)
                ],
                axis=1,
            )

        def channels(low):
            size = width // shards
            count = own // size
            return jnp.concatenate(
                [everyone_ref[section * count + d, row, low : low + size] for d in range(count)],
                axis=1,
            )

        size = width // shards
        gain_ref[...] = joined(places["norm_gain"], size)
        shift_ref[...] = joined(places["norm_shift"], size)
        feed_gain_ref[...] = joined(places["feed_gain"], size)
        feed_shift_ref[...] = joined(places["feed_shift"], size)
        feed_out_ref[...] = joined(places["feed_out_bias"], size)
        own_ref[0:1, :] = gain_ref[:, mine]
        own_ref[1:2, :] = shift_ref[:, mine]
        own_ref[2:3, :] = feed_gain_ref[:, mine]
        own_ref[3:8, :] = jnp.zeros((5, own), F32)
        own_out_ref[...] = feed_out_ref[:, mine]
        skip_ref[...] = channels(places["average_skip"])
        for n in range(rate_ref.shape[0]):
            rate = sigmoid(channels(places["average_decay"] + n * size))
            drive = (1.0 - rate) * channels(places["average_input"] + n * size)
            coef = drive * channels(places["average_output"] + n * size)
            rate_ref[n] = jnp.broadcast_to(rate, (CHUNKS, own))
            coef_ref[n] = jnp.broadcast_to(coef, (CHUNKS, own))
        keyed = offset_ref.shape[1]
        step = keyed // shards
        for r in range(2):
            pair_ref[r : r + 1, :] = joined(places["pair_scale"] + r * step, step)
        offset_ref[...] = joined(places["query_shift"], step)
        feed_in_ref[...] = share(
            places["feed_in_bias"], feed_in_ref.shape[1] * sections // shards
        )
        total = bias_ref.shape[1]
        wide = (total - keyed - 2 * own) // 2
        base_all = 2 * width + keyed + wide * sections
        base_buf[...] = joined(places["base_bias"], base_all // shards)
        low = wide + own + keyed
        bias_ref[:, :wide] = share(places["value_bias"], wide * sections // shards)
        bias_ref[:, wide : wide + own] = base_buf[:, mine]
        bias_ref[:, wide + own : low] = base_buf[:, width : width + keyed]
        bias_ref[:, low : low + wide] = pick(
            base_buf, (slice(None),), width + keyed, wide * sections, shards, sections
        )
        start = pl.multiple_of(width + keyed + wide * sections + section * own, LANES)
        bias_ref[:, low + wide :] = base_buf[:, pl.ds(start, own)]


def unpack(everyone, places, sizes, sections):
    shards, layers = everyone.shape[:2]
    width, dims, total, hidden, keyed, base = sizes
    own = width // sections
    one_layer = (
        [shape((1, width), F32)] * 5
        + [shape((8, own), F32)]
        + [shape((dims, CHUNKS, own), F32)] * 2
        + [
            shape((1, total), F32),
            shape((1, hidden), F32),
            shape((2, keyed), F32),
            shape((1, keyed), F32),
            shape((1, own), F32),
            shape((1, own), F32),
        ]
    )
    outs = pl.pallas_call(
        functools.partial(unpack_kernel, layers, shards, sections, places),
        out_shape=tuple(one_layer * layers),
        in_specs=[vmem()],
        out_specs=(vmem(),) * (len(one_layer) * layers),
        scratch_shapes=[pltpu.VMEM((1, base), F32)],
        cost_estimate=lasting(3),
        compiler_params=params(),
    )(everyone)
    names = (
        "gain",
        "shift",
        "feed_gain",
        "feed_shift",
        "feed_out",
        "own",
        "rate",
        "coef",
        "bias",
        "feed_in",
        "pair",
        "offset",
        "skip",
        "own_out",
    )
    count = len(one_layer)
    return [
        types.SimpleNamespace(**dict(zip(names, outs[k * count : (k + 1) * count])))
        for k in range(layers)
    ]


def body(
    tokens,
    lengths,
    cotangent,
    norm_gain,
    norm_shift,
    average_decay,
    average_input,
    average_output,
    average_skip,
    value_weight,
    value_bias,
    base_weight,
    base_bias,
    pair_scale,
    query_shift,
    out_weight,
    feed_gain,
    feed_shift,
    feed_in_weight,
    feed_in_bias,
    feed_out_weight,
    feed_out_bias,
):
    sections = lax.axis_size("section")
    shards = lax.axis_size("dp")
    section = lax.axis_index("section")
    _, count, width = tokens.shape
    layers = norm_gain.shape[0]
    own = width // sections
    wide = value_weight.shape[2]
    keyed = pair_scale.shape[2] * shards
    hidden = feed_in_weight.shape[2]

    share = wide // sections
    total = share + own + keyed + share + own

    def over_dp(array):
        return lax.all_gather(array, "dp", axis=0, tiled=True)

    def attention_weights(layer, after=()):
        arrays = (value_weight, base_weight, out_weight)
        columns = total + width // 2
        return pack(pack_attention_kernel, layer, columns, shards, sections, arrays, after)

    def feed_weights(layer, after=()):
        arrays = (feed_in_weight, feed_out_weight)
        columns = hidden // sections + width
        return pack(pack_feed_kernel, layer, columns, shards, sections, arrays, after)

    weights = [[None, None] for _ in range(layers)]
    weights[0][0] = over_dp(attention_weights(0))

    smalls = dict(
        norm_gain=norm_gain,
        norm_shift=norm_shift,
        average_decay=average_decay,
        average_input=average_input,
        average_output=average_output,
        average_skip=average_skip,
        feed_gain=feed_gain,
        feed_shift=feed_shift,
        feed_out_bias=feed_out_bias,
        value_bias=value_bias,
        feed_in_bias=feed_in_bias,
        base_bias=base_bias,
        pair_scale=pair_scale,
        query_shift=query_shift,
    )
    packed = jnp.concatenate([a.reshape(layers, -1) for a in smalls.values()], axis=1)
    places = {}
    low = 0
    for name, array in smalls.items():
        places[name] = low
        low += array.size // layers
    dims = average_decay.shape[1]
    small = unpack(
        lax.all_gather(packed, "dp", axis=0),
        places,
        (width, dims, total, hidden // sections, keyed, base_weight.shape[2]),
        sections,
    )

    idents = iter(range(64))
    x0 = x = tokens[0]
    kept = []
    for layer in range(layers):
        p = small[layer]
        normed, mixed_own, pre, own_n, scale = average_forward(
            lengths, x, p.gain, p.shift, p.rate, p.coef, p.skip
        )
        if not layer:
            packed_feed = feed_weights(0, (mixed_own,))
            weights[0][1] = over_dp(packed_feed)
            mixed = mixed_own = gather_columns(mixed_own, next(idents), (packed_feed,))
        middle, hidden_pre, *mixed_out, update, shared, reset, value, att, gated, probs = attention_forward(
            lengths,
            normed,
            mixed_own,
            weights[layer][0],
            p.bias,
            p.pair,
            p.offset,
            x,
            shards,
            next(idents),
        )
        if layer:
            (mixed,) = mixed_out
        if layer + 1 < layers:
            weights[layer + 1] = [
                over_dp(attention_weights(layer + 1, (hidden_pre,))),
                over_dp(feed_weights(layer + 1, (hidden_pre,))),
            ]
        attention_w, feed_w = weights[layer]
        feed_saved = [None] * 4
        x_next = None
        if layer + 1 < layers:
            x_next, *feed_saved = feed_forward_joined(
                middle, p.feed_gain, p.feed_shift, feed_w, p.feed_in, p.own_out, next(idents)
            )
        feed_pre, feed_n, feed_normed, feed_scale = feed_saved
        kept.append(
            types.SimpleNamespace(
                x=x,
                middle=middle,
                normed=normed,
                mixed=mixed,
                pre=pre,
                own_n=own_n,
                scale=scale,
                update=update,
                saved=(shared, reset, value, att, probs),
                gated=gated,
                hidden=hidden_pre,
                feed_pre=feed_pre,
                feed_n=feed_n,
                feed_normed=feed_normed,
                feed_scale=feed_scale,
            )
        )
        x = x_next

    def scattered(grad):
        return lax.psum_scatter(grad, "dp", scatter_dimension=0, tiled=True)

    given = cotangent[0]
    feed_grads = [None] * layers
    attention_grads = [None] * layers
    averages = [None] * layers
    for layer in reversed(range(layers)):
        attention_w, feed_w = weights[layer]
        k, p = kept[layer], small[layer]
        gout, gupdate, resid, feed_grad, *last = feed_backward(
            given, k, p, feed_w, shards, next(idents), () if layer else (feed_grads[1],)
        )
        if last:
            block_out = last[0]
        feed_grads[layer] = scattered(feed_grad)
        gmixed, gnormed, attention_grad = attention_backward(
            lengths,
            gout,
            gupdate,
            k,
            attention_w,
            p.pair,
            p.offset,
            shards,
            next(idents),
            () if layer else (attention_grads[1],),
        )
        attention_grads[layer] = scattered(attention_grad)
        z, zstats, norm_sums, m_buf, g_buf, back, *attention_one = average_backward(
            lengths,
            gmixed,
            gnormed,
            k,
            resid,
            p.own,
            p.rate,
            p.coef,
            p.skip,
            None if layer else attention_grads[1],
            None if layer else next(idents),
        )
        averages[layer] = (m_buf, g_buf, p.rate, back, norm_sums)
        if layer:
            given = (z, zstats, k.x)

    (attention_one,) = attention_one
    input_grad, channel_sums, feed_one, feed_zero = final_exchange(
        z, zstats, x0, [feed_grads[1], feed_grads[0]], averages, sections, next(idents)
    )
    channels, attention_zero = gather_sums(
        channel_sums,
        attention_grads[0],
        sections,
        shards,
        own * shards // width,
        next(idents),
    )
    size = width // shards
    dims = average_decay.shape[1]
    g_feed_in, g_feed_out, g_feed_gain, g_feed_shift, g_feed_out_bias, g_feed_in_bias = assemble(
        feed_outputs,
        (feed_zero, feed_one),
        (),
        ((size, hidden), (hidden // shards, width)),
        ((size,), (size,), (size,), (hidden // shards,)),
        shards,
    )
    base = base_weight.shape[2]
    g_value, g_base, g_out, g_value_bias, g_base_bias, g_pair, g_query, *rest = assemble(
        attention_outputs,
        (attention_zero, attention_one),
        (channels, average_decay, average_input, average_output),
        ((size, wide), (size, base), (wide // shards, width)),
        ((wide // shards,), (base // shards,), (2, keyed // shards), (keyed // shards,))
        + ((size,),) * 3
        + ((dims, size),) * 3,
        shards,
    )
    g_gain, g_shift, g_skip, g_decay, g_input, g_output = rest
    return (
        block_out[None],
        input_grad[None],
        g_gain,
        g_shift,
        g_decay,
        g_input,
        g_output,
        g_skip,
        g_value,
        g_value_bias,
        g_base,
        g_base_bias,
        g_pair,
        g_query,
        g_out,
        g_feed_gain,
        g_feed_shift,
        g_feed_in,
        g_feed_in_bias,
        g_feed_out,
        g_feed_out_bias,
    )


def solution(mesh):
    row, row2 = P(None, "dp"), P(None, "dp", None)
    deep = P(None, None, "dp")
    in_specs = (
        P("dp", None, None),
        P("dp"),
        P("dp", None, None),
        row,
        row,
        deep,
        deep,
        deep,
        row,
        row2,
        row,
        row2,
        row,
        deep,
        row,
        row2,
        row,
        row,
        row2,
        row,
        row2,
        row,
    )
    out_specs = (
        P("dp", "section", None),
        P("dp", "section", None),
        row,
        row,
        deep,
        deep,
        deep,
        row,
        row2,
        row,
        row2,
        row,
        deep,
        row,
        row2,
        row,
        row,
        row2,
        row,
        row2,
        row,
    )
    return jax.shard_map(body, mesh=mesh, in_specs=in_specs, out_specs=out_specs, check_vma=False)
```

```python
import functools
import types

import jax
import jax.numpy as jnp
from jax import lax
from jax.experimental import pallas as pl
from jax.experimental.pallas import tpu as pltpu
from jax.sharding import PartitionSpec as P

F32 = jnp.float32
BF16 = jnp.bfloat16
MESH = pl.DeviceIdType.MESH
ATT = 128
LANES = 128
CHUNKS = 8
ROWS = 256
STRIP = 64
TILE = 128
LOCAL = "local"
UNROLL = 16
SMALL = 16
SMEM, VMEM, RAW, FETCH, BLOCKS, LATE, OWN_PART, STORE, STORE_BLOCKS = range(9)
EPS = 1e-05
NEGATIVE = -1000000000.0
VMEM_BYTES = 56 * 1024 * 1024


def vmem():
    return pl.BlockSpec(memory_space=pltpu.VMEM)


def smem():
    return pl.BlockSpec(memory_space=pltpu.SMEM)


def hbm():
    return pl.BlockSpec(memory_space=pl.ANY)


def shape(dims, kind):
    return jax.ShapeDtypeStruct(dims, kind)


def sigmoid(v):
    return 0.5 * jnp.tanh(0.5 * v) + 0.5


def silu(v):
    return v * sigmoid(v)


def silu_slope(v):
    s = sigmoid(v)
    return s * (1.0 + v * (1.0 - s))


def dot(left, right, left_dim=1, right_dim=0):
    return lax.dot_general(
        left, right, (((left_dim,), (right_dim,)), ((), ())), preferred_element_type=F32
    )


def normalise(x):
    centred = x - jnp.mean(x, axis=-1, keepdims=True)
    spread = jnp.mean(centred * centred, axis=-1, keepdims=True)
    scale = lax.rsqrt(spread + EPS)
    return centred * scale, scale


def row_valid(start, rows, length):
    place = start + lax.broadcasted_iota(jnp.int32, (rows, 1), 0)
    return (place < length).astype(F32)


def lasting(microseconds):
    return pl.CostEstimate(
        flops=int(microseconds * 1.0e9),
        bytes_accessed=int(microseconds * 3.0e6),
        transcendentals=0,
    )


def params(**more):
    return pltpu.CompilerParams(vmem_limit_bytes=VMEM_BYTES, **more)


def power(base, exponent):
    result = None
    square = base
    while exponent:
        if exponent % 2:
            result = square if result is None else result * square
        exponent //= 2
        if exponent:
            square = square * square
    return result


def shifted(array, span, reverse=False):
    row = lax.broadcasted_iota(jnp.int32, array.shape, 1)
    if reverse:
        return jnp.where(row < CHUNKS - span, pltpu.roll(array, CHUNKS - span, 1), 0.0)
    return jnp.where(row >= span, pltpu.roll(array, span, 1), 0.0)


def entering(last, rate, steps, reverse=False):
    weight = power(rate, steps)
    span = 1
    while span < CHUNKS:
        last = last + weight * shifted(last, span, reverse)
        weight = weight * weight
        span *= 2
    return shifted(last, 1, reverse)


def entering_pair(last, slope, rate, steps):
    weight = power(rate, steps)
    tilt = float(steps) * power(rate, steps - 1)
    span = 1
    while span < CHUNKS:
        moved = shifted(last, span)
        slope = slope + weight * shifted(slope, span) + tilt * moved
        last = last + weight * moved
        tilt = 2.0 * weight * tilt
        weight = weight * weight
        span *= 2
    return shifted(last, 1), shifted(slope, 1)


def average_forward_work(r):
    length_ref, x_ref, gain_ref, shift_ref, skip_ref = r.length, r.x, r.gain, r.shift, r.skip
    rate_ref, coef_ref, rows_buf, m_buf, y_buf = r.rate, r.coef, r.rows_buf, r.m_buf, r.y_buf
    normed_ref, mixed_ref, pre_ref, own_ref, scale_ref = r.normed, r.mixed, r.pre, r.own_n, r.scale
    length = length_ref[0]
    count, width = x_ref.shape
    own = mixed_ref.shape[1]
    dims = rate_ref.shape[0]
    steps = count // CHUNKS
    pitch = steps + 1
    mine = pl.ds(pl.multiple_of(lax.axis_index("section") * own, LANES), own)

    def norm_strip(i, carry):
        start = pl.multiple_of(i * STRIP, STRIP)
        here = pl.ds(start, STRIP)
        n, scale = normalise(x_ref[here, :].astype(F32))
        rows_buf[...] = n
        normed_ref[here, :] = (n * gain_ref[...] + shift_ref[...]).astype(BF16)
        part = rows_buf[:, mine]
        own_ref[here, :] = part
        scale_ref[here, :] = jnp.broadcast_to(scale, (STRIP, LANES))
        masked = (part * gain_ref[:, mine] + shift_ref[:, mine]) * row_valid(start, STRIP, length)
        for group in range(own // LANES):
            m_buf[group, pl.ds(start + start // steps, STRIP), :] = masked[:, group * LANES : (group + 1) * LANES]
        return carry

    share = ROWS // STRIP
    for block in range(count // ROWS):
        r.wait_block(block)
        lax.fori_loop(block * share, (block + 1) * share, norm_strip, 0)
    r.store("normed", "own_n", "scale")

    for group in range(own // LANES):
        lanes = slice(group * LANES, (group + 1) * LANES)
        rates = rate_ref[:, :, lanes]
        coefs = coef_ref[:, :, lanes]
        m_part, y_part = m_buf.at[group], y_buf.at[group]

        def finals(t, states):
            return rates * states + m_part[pl.ds(t, CHUNKS, stride=pitch), :]

        ends = lax.fori_loop(0, steps, finals, jnp.zeros_like(rates), unroll=UNROLL)

        def outputs(t, states):
            states = rates * states + m_part[pl.ds(t, CHUNKS, stride=pitch), :]
            y_part[pl.ds(t, CHUNKS, stride=pitch), :] = jnp.sum(coefs * states, axis=0)
            return states

        lax.fori_loop(0, steps, outputs, entering(ends, rates, steps), unroll=UNROLL)

    def mix_strip(i, carry):
        start = pl.multiple_of(i * STRIP, STRIP)
        here = pl.ds(start, STRIP)
        there = pl.ds(start + start // steps, STRIP)
        for group in range(own // LANES):
            lanes = slice(group * LANES, (group + 1) * LANES)
            pre = y_buf[group, there, :] + skip_ref[:, lanes] * m_buf[group, there, :]
            pre_ref[here, lanes] = pre.astype(BF16)
            mixed_ref[here, lanes] = silu(pre).astype(BF16)
        return carry

    lax.fori_loop(0, count // STRIP, mix_strip, 0)


def average_forward(length, x, gain, shift, rate, coef, skip):
    count, width = x.shape
    own = skip.shape[1]
    buffer = pltpu.VMEM((own // LANES, count + CHUNKS, LANES), F32)
    small = dict(gain=gain, shift=shift, rate=rate, coef=coef, skip=skip)
    return transfer(
        average_forward_work,
        dict(
            length=(length, SMEM),
            x=(x, BLOCKS),
            **{name: (a, VMEM) for name, a in small.items()},
        ),
        dict(
            normed=(shape((count, width), BF16), STORE),
            mixed=(shape((count, own), BF16), VMEM),
            pre=(shape((count, own), BF16), VMEM),
            own_n=(shape((count, own), F32), STORE),
            scale=(shape((count, LANES), F32), STORE),
        ),
        dict(rows_buf=pltpu.VMEM((STRIP, width), F32), m_buf=buffer, y_buf=buffer),
        None,
        12,
    )


def average_backward_work(beside, r):
    length = r.length[0]
    count, own = r.z.shape
    dims = r.rate.shape[0]
    steps = count // CHUNKS
    pitch = steps + 1
    groups = own // LANES
    gain_ref, shift_ref = r.norm.at[0:1, :], r.norm.at[1:2, :]
    if beside:
        peers = plane()
        sems, piece = (r.send, r.recv), block_piece(r.whole)
        r.wait("block")
        r.whole[peers[0]] = r.block[...]
        greet(peers[1], peers[2])
        begun = [gather_begin(r.whole, piece, peers, sems, half) for half in range(2)]

    r.wait("own_n", "pre", "gmixed", "gvalue", "scale", "resid")

    def load_strip(i, carry):
        start = pl.multiple_of(i * STRIP, STRIP)
        here = pl.ds(start, STRIP)
        valid = row_valid(start, STRIP, length)
        there = pl.ds(start + start // steps, STRIP)
        for group in range(groups):
            lanes = slice(group * LANES, (group + 1) * LANES)
            r.m_buf[group, there, :] = (
                r.own_n[here, lanes] * gain_ref[:, lanes] + shift_ref[:, lanes]
            ) * valid
            slope = silu_slope(r.pre[here, lanes].astype(F32))
            r.g_buf[group, there, :] = r.gmixed[here, lanes] * slope
        return carry

    lax.fori_loop(0, count // STRIP, load_strip, 0)
    r.store("m_buf", "g_buf")

    passed = None
    for group in range(groups):
        lanes = slice(group * LANES, (group + 1) * LANES)
        rates = r.rate[:, :, lanes]
        coefs = r.coef[:, :, lanes]
        m_part, g_part, r_part = r.m_buf.at[group], r.g_buf.at[group], r.r_buf.at[group]
        blank = jnp.zeros_like(rates)

        def back_finals(t, carry):
            states, slopes = carry
            g = g_part[pl.ds(steps - 1 - t, CHUNKS, stride=pitch), :]
            return rates * states + g, rates * slopes + states

        ends, end_slopes = lax.fori_loop(0, steps, back_finals, (blank, blank), unroll=UNROLL)
        starts = entering(ends, rates, steps, reverse=True)

        r.back[0, :, :, lanes] = ends
        r.back[1, :, :, lanes] = end_slopes

        def back_outputs(t, states):
            here = pl.ds(steps - 1 - t, CHUNKS, stride=pitch)
            states = rates * states + g_part[here, :]
            r_part[here, :] = jnp.sum(coefs * states, axis=0)
            return states

        lax.fori_loop(0, steps, back_outputs, starts, unroll=UNROLL)
        if beside and passed is None:
            passed = gather_forward(r.whole, piece, peers, sems, *begun)

    ones = jnp.ones((CHUNKS, own), BF16)
    first = lax.broadcasted_iota(jnp.int32, (CHUNKS, LANES), 0) == 0

    def finish(i, carry):
        start = pl.multiple_of(i * LANES, LANES)
        here = pl.ds(start, LANES)
        valid = row_valid(start, LANES, length)
        there = pl.ds(start + start // steps, LANES)
        of_gain, of_shift, of_skip = carry
        smoothed = jnp.concatenate([r.r_buf[k, there, :] for k in range(groups)], axis=1)
        gpre = jnp.concatenate([r.g_buf[k, there, :] for k in range(groups)], axis=1)
        masked = jnp.concatenate([r.m_buf[k, there, :] for k in range(groups)], axis=1)
        n = r.own_n[here, :]
        gmasked = r.skip[...] * gpre + smoothed
        gnormed = gmasked * valid + r.gvalue[here, :]
        e = gnormed * gain_ref[...]
        z = r.scale[here, 0:1] * e + r.resid[here, :]
        r.z[here, :] = z.astype(BF16)
        mean_row = dot(ones, e.astype(BF16), 1, 1)
        slope_row = dot(ones, (e * n).astype(BF16), 1, 1)
        r.stats[:, here] = jnp.where(first, mean_row, slope_row)
        return (
            of_gain + jnp.sum(gnormed * n, axis=0, keepdims=True),
            of_shift + jnp.sum(gnormed, axis=0, keepdims=True),
            of_skip + jnp.sum(gpre * masked, axis=0, keepdims=True),
        )

    blank_row = jnp.zeros((1, own), F32)
    of_gain, of_shift, of_skip = lax.fori_loop(
        0, count // LANES, finish, (blank_row, blank_row, blank_row)
    )
    r.sums[0:1, :] = of_gain
    r.sums[1:2, :] = of_shift
    r.sums[2:3, :] = of_skip
    r.sums[3:8, :] = jnp.zeros((5, own), F32)
    if beside:
        gather_finish(r.whole, piece, peers, sems, *begun, passed)


def average_sums(m_ref, g_ref, rate_ref, back_ref, sums_ref, low):
    dims, _, own = rate_ref.shape
    pitch = m_ref.shape[1] // CHUNKS
    steps = pitch - 1
    part_size = dims // 2
    for group in range(own // LANES):
        lanes = slice(group * LANES, (group + 1) * LANES)
        m_part, g_part = m_ref.at[group], g_ref.at[group]
        for half in range(2):
            some = slice(half * part_size, (half + 1) * part_size)
            rates = rate_ref[some, :, lanes]
            empty = jnp.zeros_like(rates)

            def sweep(t, carry):
                states, slopes, of_states, of_slopes = carry
                x = m_part[pl.ds(t, CHUNKS, stride=pitch), :]
                g = g_part[pl.ds(t, CHUNKS, stride=pitch), :]
                slopes = rates * slopes + states
                states = rates * states + x
                return states, slopes, of_states + g * states, of_slopes + g * slopes

            states, slopes, of_states, of_slopes = lax.fori_loop(
                0, steps, sweep, (empty,) * 4, unroll=UNROLL
            )
            back, back_slope = back_ref[0, some, :, lanes], back_ref[1, some, :, lanes]
            state, slope = entering_pair(states, slopes, rates, steps)
            of_states = of_states + state * (rates * back)
            of_slopes = of_slopes + slope * (rates * back) + state * (back + rates * back_slope)
            first = low + half * part_size
            sums_ref[first : first + part_size, lanes] = jnp.sum(of_states, axis=1)
            first += dims
            sums_ref[first : first + part_size, lanes] = jnp.sum(of_slopes, axis=1)


def average_backward(
    length, gmixed, gvalue, k, resid, norm, rate, coef, skip, block, ident, after=()
):
    count, own = gmixed.shape
    dims = rate.shape[0]
    held_dims = (own // LANES, count + CHUNKS, LANES)
    sems = pltpu.SemaphoreType.DMA((6,))
    given = dict(
        own_n=k.own_n,
        pre=k.pre,
        gmixed=gmixed,
        gvalue=gvalue,
        scale=k.scale,
        resid=resid,
    )
    small = dict(norm=norm, rate=rate, coef=coef, skip=skip)
    beside = block is not None
    outs, held = {}, {}
    if beside:
        given = dict(block=block, **given)
        outs.update(whole=(shape((4,) + block.shape, BF16), VMEM))
        held.update(send=sems, recv=sems)
    return transfer(
        functools.partial(average_backward_work, beside),
        dict(
            length=(length, SMEM),
            **{name: (a, FETCH) for name, a in given.items()},
            **{name: (a, VMEM) for name, a in small.items()},
        ),
        dict(
            z=(shape((count, own), BF16), VMEM),
            stats=(shape((CHUNKS, count), F32), VMEM),
            sums=(shape((8, own), F32), VMEM),
            m_buf=(shape(held_dims, F32), STORE),
            g_buf=(shape(held_dims, F32), STORE),
            back=(shape((2, dims, CHUNKS, own), F32), VMEM),
            **outs,
        ),
        dict(r_buf=pltpu.VMEM(held_dims, F32), **held),
        ident,
        17,
        after,
    )


def unfold(packed, in_w, out_w, shards, sems):
    wide, width = out_w.shape
    few = wide // shards
    low = in_w.shape[1]
    copies = [pltpu.make_async_copy(packed.at[:, pl.ds(0, low)], in_w, sems.at[0])]
    for shard in range(shards):
        for half in range(2):
            start = shard * (width // shards) + half * few
            columns = pl.ds(half * (width // 2), width // 2)
            copies.append(
                pltpu.make_async_copy(
                    packed.at[pl.ds(start, few), pl.ds(low, width // 2)],
                    out_w.at[pl.ds(shard * few, few), columns],
                    sems.at[len(copies)],
                )
            )
    return copies


def attention_forward_block(
    length,
    start,
    normed_ref,
    mixed_ref,
    in_ref,
    bias_ref,
    pair_ref,
    offset_ref,
    part_ref,
    update_ref,
    shared_ref,
    reset_ref,
    cand_ref,
    value_ref,
    att_ref,
    gated_ref,
    probs_ref,
    out_w_ref,
):
    rows = normed_ref.shape[0]
    wide = value_ref.shape[1]
    own = update_ref.shape[1]
    keyed = shared_ref.shape[1]
    value = dot(normed_ref[...], in_ref[:, :wide]) + bias_ref[:, :wide]
    value_ref[...] = value.astype(BF16)
    values = silu(value).astype(BF16)
    low = wide
    update = dot(mixed_ref[...], in_ref[:, low : low + own]) + bias_ref[:, low : low + own]
    update_ref[...] = update.astype(BF16)
    low += own
    shared = dot(mixed_ref[...], in_ref[:, low : low + keyed]) + bias_ref[:, low : low + keyed]
    shared_ref[...] = shared.astype(BF16)
    low += keyed
    reset = dot(mixed_ref[...], in_ref[:, low : low + wide]) + bias_ref[:, low : low + wide]
    reset_ref[...] = reset.astype(BF16)
    low += wide
    cand_ref[...] = (
        dot(mixed_ref[...], in_ref[:, low : low + own]) + bias_ref[:, low : low + own]
    ).astype(BF16)
    shared = silu(shared)
    reset = silu(reset)
    queries = (shared * pair_ref[0:1, :] + offset_ref[...]).astype(BF16)
    keys = (shared * pair_ref[1:2, :]).astype(BF16)
    for block in range(rows // ATT):
        here = slice(block * ATT, (block + 1) * ATT)
        begin = start + block * ATT
        scores = dot(queries[here], keys[here], 1, 1) * keyed**-0.5
        key_place = begin + lax.broadcasted_iota(jnp.int32, (ATT, ATT), 1)
        scores = jnp.where(key_place < length, scores, NEGATIVE)
        raised = jnp.exp(scores - jnp.max(scores, axis=-1, keepdims=True))
        probs = (raised / jnp.sum(raised, axis=-1, keepdims=True)).astype(BF16)
        probs_ref[here, :] = probs
        attended = dot(probs, values[here]) * row_valid(begin, ATT, length)
        att_ref[here, :] = attended.astype(BF16)
        gated_ref[here, :] = (attended * reset[here]).astype(BF16)
    part_ref[...] = dot(gated_ref[...], out_w_ref[...]).astype(BF16)


def attention_backward_block(
    length,
    start,
    mine,
    gout_ref,
    gupdate_ref,
    shared_ref,
    reset_ref,
    value_ref,
    att_ref,
    probs_ref,
    in_ref,
    pair_ref,
    offset_ref,
    gmixed_ref,
    gnormed_ref,
    gbase_ref,
    gvalue_ref,
    bias_ref,
    pair_sum_ref,
    out_w_ref,
):
    rows = gout_ref.shape[0]
    total = bias_ref.shape[1]
    wide = value_ref.shape[1]
    own = gupdate_ref.shape[1]
    keyed = shared_ref.shape[1]
    valid = row_valid(start, rows, length)
    ggated = dot(gout_ref[...], out_w_ref[...], 1, 1)
    reset = reset_ref[...].astype(F32)
    gattended = (ggated * silu(reset) * valid).astype(BF16)
    greset = ggated * att_ref[...].astype(F32) * silu_slope(reset)
    value = value_ref[...].astype(F32)
    values = silu(value).astype(BF16)
    shared_pre = shared_ref[...].astype(F32)
    shared = silu(shared_pre)
    scale_q, scale_k = pair_ref[0:1, :], pair_ref[1:2, :]
    queries = (shared * scale_q + offset_ref[...]).astype(BF16)
    keys = (shared * scale_k).astype(BF16)
    gq_parts, gk_parts, gv_parts = [], [], []
    for block in range(rows // ATT):
        here = slice(block * ATT, (block + 1) * ATT)
        probs = probs_ref[here, :]
        gprobs = dot(gattended[here], values[here], 1, 1)
        gv_parts.append(dot(probs, gattended[here], 0, 0))
        probs = probs.astype(F32)
        gscores = probs * (gprobs - jnp.sum(probs * gprobs, axis=-1, keepdims=True))
        key_place = start + block * ATT + lax.broadcasted_iota(jnp.int32, (ATT, ATT), 1)
        gscores = jnp.where(key_place < length, gscores, 0.0)
        gscores = (gscores * keyed**-0.5).astype(BF16)
        gq_parts.append(dot(gscores, keys[here]))
        gk_parts.append(dot(gscores, queries[here], 0, 0))
    gqueries = jnp.concatenate(gq_parts, axis=0)
    gkeys = jnp.concatenate(gk_parts, axis=0)
    gvalue = jnp.concatenate(gv_parts, axis=0) * silu_slope(value)
    gshared = (gqueries * scale_q + gkeys * scale_k) * silu_slope(shared_pre)
    pair_sum_ref[0:1, :] += jnp.sum(gqueries * shared, axis=0, keepdims=True)
    pair_sum_ref[1:2, :] += jnp.sum(gkeys * shared, axis=0, keepdims=True)
    pair_sum_ref[2:3, :] += jnp.sum(gqueries, axis=0, keepdims=True)
    gupdate = gupdate_ref[...]
    gcand = gout_ref[:, mine]
    low = 0
    for piece in (gvalue, gupdate, gshared, greset, gcand):
        size = piece.shape[1]
        bias_ref[0:1, low : low + size] += jnp.sum(piece.astype(F32), axis=0, keepdims=True)
        if low:
            gbase_ref[:, low - wide : low - wide + size] = piece.astype(BF16)
        else:
            gvalue_ref[...] = piece.astype(BF16)
        low += size
    gmixed_ref[...] = dot(gbase_ref[...], in_ref[:, wide:total], 1, 1).astype(BF16)
    gnormed_ref[...] = dot(gvalue_ref[...], in_ref[:, :wide], 1, 1).astype(BF16)


def feed_forward_kernel(
    x_ref, gain_ref, shift_ref, w_ref, bias_ref, part_ref, pre_ref, n_ref, normed_ref, scale_ref
):
    hidden = pre_ref.shape[1]
    n, scale = normalise(x_ref[...].astype(F32))
    n_ref[...] = n.astype(BF16)
    scale_ref[...] = jnp.broadcast_to(scale, scale_ref.shape)
    normed_ref[...] = (n * gain_ref[...] + shift_ref[...]).astype(BF16)
    pre = dot(normed_ref[...], w_ref[:, :hidden]) + bias_ref[...]
    pre_ref[...] = pre.astype(BF16)
    part_ref[...] = dot(silu(pre).astype(BF16), w_ref[:, hidden:]).astype(BF16)


def feed_backward_block(
    g_ref, pre_ref, n_ref, gain_ref, w_ref, part_ref, stats_ref, gpre_ref, act_ref, sums_ref, bias_ref, lanes
):
    hidden = pre_ref.shape[1]
    width = n_ref.shape[1]
    g = g_ref[...]
    pre = pre_ref[...].astype(F32)
    s = sigmoid(pre)
    act_ref[...] = (pre * s).astype(BF16)
    gpre = dot(g, w_ref[:, hidden:], 1, 1) * (s * (1.0 + pre * (1.0 - s)))
    bias_ref[0:1, :] += jnp.sum(gpre, axis=0, keepdims=True)
    gpre_ref[...] = gpre.astype(BF16)
    part = dot(gpre_ref[...], w_ref[:, :hidden], 1, 1)
    part_ref[...] = part.astype(BF16)
    n = n_ref[...].astype(F32)
    sums_ref[0:1, :] += jnp.sum(part * n, axis=0, keepdims=True)
    sums_ref[1:2, :] += jnp.sum(part, axis=0, keepdims=True)
    sums_ref[2:3, :] += jnp.sum(g.astype(F32), axis=0, keepdims=True)
    e = part * gain_ref[...]
    ones = jnp.ones((CHUNKS, width), BF16)
    mean_row = dot(ones, e.astype(BF16), 1, 1)
    slope_row = dot(ones, (e * n).astype(BF16), 1, 1)
    first = lax.broadcasted_iota(jnp.int32, mean_row.shape, 0) == 0
    stats_ref[:, lanes] = jnp.where(first, mean_row, slope_row)


def plane():
    me = lax.axis_index("section")
    across = me + 1 - 2 * (me % 2)
    along = me + 2 - 4 * (me // 2)
    return me, across, along, across + along - me


def greet(*others):
    barrier = pltpu.get_barrier_semaphore()
    for other in others:
        pl.semaphore_signal(barrier, inc=1, device_id={"section": other}, device_id_type=MESH)
    pl.semaphore_wait(barrier, len(others))


def link(source, target, sems, index, other):
    send, recv = sems
    return pltpu.make_async_remote_copy(
        src_ref=source,
        dst_ref=target,
        send_sem=send.at[index],
        recv_sem=recv.at[index],
        device_id={"section": other},
        device_id_type=MESH,
    )


def strips(count, work):
    def one(i, carry):
        work(pl.multiple_of(i * STRIP, STRIP))
        return carry

    lax.fori_loop(0, count // STRIP, one, 0)


def widen(block):
    rows, columns = block.shape
    if columns < LANES:
        block = jnp.concatenate((block, jnp.zeros((rows, LANES - columns), F32)), axis=1)
    return block.astype(BF16)


def grad_tiles(left, right, store, begin, end):
    def one(i, carry):
        rows = pl.ds(pl.multiple_of(i * TILE, TILE), TILE)
        store(rows, dot(left[:, rows], right[...], 0, 0).astype(BF16))
        return carry

    lax.fori_loop(begin, end, one, 0)


def gather_begin(out, piece, peers, sems, half):
    me, across, along, far = peers
    here = out.at[piece(me, half)]
    order = ((along, 0), (across, 1)) if half == 0 else ((across, 1), (along, 0))
    started = {}
    for other, way in order:
        copy = link(here, here, sems, 2 * half + way, other)
        copy.start()
        started[way] = copy
    return started


def gather_forward(out, piece, peers, sems, zero, one):
    me, across, along, far = peers
    zero[0].wait_recv()
    passing = out.at[piece(along, 0)]
    first = link(passing, passing, sems, 4, across)
    first.start()
    one[1].wait_recv()
    passing = out.at[piece(across, 1)]
    second = link(passing, passing, sems, 5, along)
    second.start()
    return first, second


def gather_finish(out, piece, peers, sems, zero, one, passed=None):
    first, second = passed or gather_forward(out, piece, peers, sems, zero, one)
    zero[1].wait_recv()
    one[0].wait_recv()
    first.wait_recv()
    second.wait_recv()
    for copy in (zero[0], zero[1], one[0], one[1], first, second):
        copy.wait_send()


def copy_sems(count):
    return [pltpu.SemaphoreType.DMA((count,)), pltpu.SemaphoreType.DMA((count,))]


def comm_params(ident):
    return params(collective_id=ident, has_side_effects=True)


def own_slice(source, target, sem, own):
    start = pl.multiple_of(lax.axis_index("section") * own, LANES)
    return pltpu.make_async_copy(source.at[:, pl.ds(start, own)], target, sem)


def stats_total(stats, got, stage, peers, sems, index):
    me, across, along, far = peers
    first = link(stats, got.at[0], sems, index, across)
    first.start()
    first.wait_recv()
    stage[...] = stats[...] + got[0]
    second = link(stage, got.at[1], sems, index + 1, along)
    second.start()
    second.wait_recv()
    first.wait_send()
    second.wait_send()
    return stage[...] + got[1]


def transfer(work, ins, outs, scratch, ident, microseconds, after=(), first=None, rows=ROWS):
    order = [n for kind in (FETCH, BLOCKS, LATE, OWN_PART) for n in ins if ins[n][1] == kind]
    stored = [n for n, (_, how) in outs.items() if how in (STORE, STORE_BLOCKS)]
    buffers, places, low = {}, {}, 0
    for name in order + stored:
        if name in stored:
            buffers[name] = pltpu.VMEM(outs[name][0].shape, outs[name][0].dtype)
        else:
            array, how = ins[name]
            columns = array.shape[1] // (4 if how == OWN_PART else 1)
            buffers[name] = pltpu.VMEM((array.shape[0], columns), array.dtype)
        places[name] = low
        array, how = ins[name] if name in ins else outs[name]
        low += array.shape[0] // rows if how in (BLOCKS, STORE_BLOCKS) else 1
    by_blocks = [n for n in order if ins[n][1] == BLOCKS]

    def kernel(*refs):
        refs = refs[len(after) :]
        names = list(ins) + list(outs)
        given = dict(zip(names, refs))
        refs = refs[len(names) :]
        own_names = list(buffers) + [LOCAL] + list(scratch)
        held = dict(zip(own_names, refs))
        r = types.SimpleNamespace(**{**given, **held})
        local = held[LOCAL]

        def copy(name):
            sem = local.at[places[name]]
            if name in stored:
                return pltpu.make_async_copy(held[name], given[name], sem)
            if ins[name][1] == OWN_PART:
                return own_slice(given[name], held[name], sem, held[name].shape[1])
            return pltpu.make_async_copy(given[name], held[name], sem)

        def block_copy(name, block):
            here = rows_of(block, rows)
            source, target = given[name].at[here, :], held[name].at[here, :]
            return pltpu.make_async_copy(source, target, local.at[places[name] + block])

        def store_block(name, block):
            here = rows_of(block, rows)
            source, target = held[name].at[here, :], given[name].at[here, :]
            return pltpu.make_async_copy(source, target, local.at[places[name] + block])

        def start(*kinds):
            for name in order:
                if ins[name][1] in kinds:
                    copy(name).start()

        def wait_block(block):
            for name in by_blocks:
                block_copy(name, block).wait()

        start(FETCH)
        if first:
            first(r)
        if by_blocks:
            for block in range(ins[by_blocks[0]][0].shape[0] // rows):
                for name in by_blocks:
                    block_copy(name, block).start()
        start(LATE, OWN_PART)
        r.wait = lambda *which: [copy(n).wait() for n in which]
        r.store = lambda *which: [copy(n).start() for n in which]
        r.wait_block = wait_block
        r.store_block = lambda name, block: store_block(name, block).start()
        work(r)
        for name in stored:
            if outs[name][1] == STORE:
                copy(name).wait()
                continue
            for block in range(outs[name][0].shape[0] // rows):
                store_block(name, block).wait()

    spec = {SMEM: smem, VMEM: vmem}
    return pl.pallas_call(
        kernel,
        out_shape=tuple(o for o, _ in outs.values()),
        in_specs=[hbm()] * len(after) + [spec.get(how, hbm)() for _, how in ins.values()],
        out_specs=tuple(spec.get(how, hbm)() for _, how in outs.values()),
        scratch_shapes=list(buffers.values())
        + [pltpu.SemaphoreType.DMA((max(low, 1),))]
        + list(scratch.values()),
        cost_estimate=lasting(microseconds),
        compiler_params=params() if ident is None else comm_params(ident),
    )(*after, *[a for a, _ in ins.values()])


def rows_of(block, rows=ROWS):
    return pl.ds(pl.multiple_of(block * rows, rows), rows)


def owned(block, owner, half, own, rows):
    start = pl.multiple_of(block * rows + half * (rows // 2), rows // 2)
    return pl.ds(start, rows // 2), pl.ds(pl.multiple_of(owner * own, LANES), own)


def sum_scratch(name, count, own, rows=ROWS):
    buffer = pltpu.VMEM((2, count // 2, own), BF16)
    sems = pltpu.SemaphoreType.DMA((6 * (count // rows),))
    return {
        name + "_early": buffer,
        name + "_direct": buffer,
        name + "_late": buffer,
        name + "_stage": buffer,
        name + "_send": sems,
        name + "_recv": sems,
    }


def block_sum(r, name, part, peers, own, piece=None, place=None, rows=ROWS):
    if piece is None:
        piece = functools.partial(owned, own=own, rows=rows)
        place = functools.partial(rows_of, rows=rows // 2)
    me, across, along, far = peers
    early, direct, late, stage, send, recv = (
        getattr(r, name + end) for end in ("_early", "_direct", "_late", "_stage", "_send", "_recv")
    )
    sems = (send, recv)
    ways = ((across, along), (along, across))

    def early_copy(block, half):
        source = part.at[piece(block, far, half)]
        target = early.at[half, place(block)]
        return link(source, target, sems, block * 6 + half, ways[half][0])

    def direct_copy(block, half):
        first = ways[half][0]
        source = part.at[piece(block, first, half)]
        target = direct.at[half, place(block)]
        return link(source, target, sems, block * 6 + 2 + half, first)

    def late_copy(block, half):
        source = stage.at[half, place(block)]
        target = late.at[half, place(block)]
        return link(source, target, sems, block * 6 + 4 + half, ways[half][1])

    def begin(block):
        for half in range(2):
            early_copy(block, half).start()
        for half in range(2):
            direct_copy(block, half).start()

    def forward(block):
        for half in range(2):
            early_copy(block, half).wait_recv()
            here = place(block)
            passed = part[piece(block, ways[half][1], half)].astype(F32)
            stage[half, here, :] = (passed + early[half, here, :].astype(F32)).astype(BF16)
            late_copy(block, half).start()

    def arrived(block, half):
        direct_copy(block, half).wait_recv()
        late_copy(block, half).wait_recv()

    def total(block, half, start):
        row, column = piece(block, me, half)
        here = pl.ds(place(block).start + start, STRIP)
        mine = part[pl.ds(row.start + start, STRIP), column].astype(F32)
        return mine + direct[half, here, :].astype(F32) + late[half, here, :].astype(F32)

    def end(block):
        for half in range(2):
            early_copy(block, half).wait_send()
            direct_copy(block, half).wait_send()
            late_copy(block, half).wait_send()

    return types.SimpleNamespace(begin=begin, forward=forward, arrived=arrived, total=total, end=end)


def gather_sems(count):
    return pltpu.SemaphoreType.DMA((6 * (count // ROWS),))


def block_gather(out, peers, own, sems, rows=ROWS):
    me, across, along, far = peers

    def copy(block, owner, half, index, other):
        place = out.at[owned(block, owner, half, own, rows)]
        return link(place, place, sems, block * 6 + index, other)

    def own_copy(block, half, way):
        return copy(block, me, half, 2 * half + way, (along, across)[way])

    def pass_copy(block, half):
        return copy(block, (along, across)[half], half, 4 + half, (across, along)[half])

    def begin(block):
        for half, way in ((0, 0), (1, 1), (1, 0), (0, 1)):
            own_copy(block, half, way).start()

    def forward(block):
        for half in range(2):
            own_copy(block, half, half).wait_recv()
            pass_copy(block, half).start()

    def arrive(block):
        own_copy(block, 0, 1).wait_recv()
        own_copy(block, 1, 0).wait_recv()
        for half in range(2):
            pass_copy(block, half).wait_recv()

    def sent(block):
        for half in range(2):
            pass_copy(block, half).wait_send()
            for way in range(2):
                own_copy(block, half, way).wait_send()

    return types.SimpleNamespace(begin=begin, forward=forward, arrive=arrive, sent=sent)


def pipeline(count, compute, sums, finish, gather, extra=None, between=None, before=None, rows=ROWS, arrived=None):
    blocks = count // rows
    if before:
        before.begin(0)
        before.begin(1)
        before.forward(0)

    def tick(i, carry):
        if before:

            @pl.when(i < blocks - 2)
            def _():
                before.begin(i + 2)

            @pl.when(i < blocks - 1)
            def _():
                before.forward(i + 1)

            @pl.when(i < blocks)
            def _():
                before.arrive(i)

        @pl.when(i < blocks)
        def _():
            compute(i)
            for one in sums:
                one.begin(i)

        if between:
            between(i)

        @pl.when((i >= 1) & (i <= blocks))
        def _():
            for one in sums:
                one.forward(i - 1)

        @pl.when((i >= 2) & (i <= blocks + 1))
        def _():
            finish(i - 2)
            if gather:
                gather.begin(i - 2)

        if gather:

            @pl.when(i >= 3)
            def _():
                gather.forward(i - 3)

        if extra:
            extra(i)
        return carry

    lax.fori_loop(0, blocks + (3 if gather else 2), tick, 0)

    def close(i, carry):
        for one in sums:
            one.end(i)
        if gather:
            gather.arrive(i)
            if arrived:
                arrived(i)
            gather.sent(i)
        if before:
            before.sent(i)
        return carry

    lax.fori_loop(0, blocks, close, 0)


def finish_strips(one, block, work, rows=ROWS):
    for half in range(2):
        one.arrived(block, half)

        def strip(start):
            row = pl.multiple_of(block * rows + half * (rows // 2), rows // 2) + start
            work(pl.ds(row, STRIP), one.total(block, half, start))

        strips(rows // 2, strip)


def views(refs, block, rows=ROWS):
    return [ref.at[rows_of(block, rows), :] for ref in refs]


def attention_forward(length, normed, mixed, packed, bias, pair, offset, x, shards, ident):
    count, width = normed.shape
    apart = mixed.shape[1] == width
    own = width // 4
    wide = width // 2
    keyed = pair.shape[1]
    low = packed.shape[1] - width // 2

    def weights(r):
        return unfold(r.packed, r.in_w, r.out_w, shards, r.fold)

    def first(r):
        for copy in weights(r):
            copy.start()

    def work(r):
        peers = plane()
        mine = pl.ds(pl.multiple_of(peers[0] * own, LANES), own)
        real = r.length[0]
        mixing = None
        if not apart:
            r.mixed[:, mine] = r.mixed_own[...]
        greet(peers[1], peers[2])
        if not apart:
            mixing = block_gather(r.mixed, peers, own, (r.mixed_send, r.mixed_recv))
        total = block_sum(r, "sum", r.part, peers, own)
        gather = block_gather(r.out, peers, own, (r.gather_send, r.gather_recv))
        saved = (r.update, r.shared, r.reset, r.cand, r.value, r.att, r.gated, r.probs)

        def compute(block):
            @pl.when(block == 0)
            def _():
                for copy in weights(r):
                    copy.wait()

            r.wait_block(block)
            attention_forward_block(
                real,
                block * ROWS,
                *views((r.normed, r.mixed), block),
                r.in_w,
                r.bias,
                r.pair,
                r.offset,
                *views((r.part,) + saved, block),
                r.out_w,
            )

        def finish(block):
            def strip(here, summed):
                pre = r.cand[here, :].astype(F32) + summed
                r.hidden[here, :] = pre.astype(BF16)
                old = r.x[here, :].astype(F32)
                made = old + sigmoid(r.update[here, :].astype(F32)) * (silu(pre) - old)
                r.out[here, mine] = made.astype(BF16)

            finish_strips(total, block, strip)

        def extra(i):
            @pl.when(i == 0)
            def _():
                r.wait("x")

            @pl.when(i == count // ROWS)
            def _():
                if not apart:
                    r.store("mixed")
                r.store("update", "shared", "reset", "value", "att", "gated", "probs")

        pipeline(
            count,
            compute,
            (total,),
            finish,
            gather,
            extra,
            before=mixing,
            arrived=lambda block: r.store_block("out", block),
        )

    rows = lambda columns: (shape((count, columns), BF16), STORE)
    return transfer(
        work,
        dict(
            length=(length, SMEM),
            packed=(packed, RAW),
            normed=(normed, BLOCKS),
            **(dict(mixed=(mixed, BLOCKS)) if apart else dict(mixed_own=(mixed, VMEM))),
            x=(x, OWN_PART),
            bias=(bias, VMEM),
            pair=(pair, VMEM),
            offset=(offset, VMEM),
        ),
        dict(
            out=(shape((count, width), BF16), STORE_BLOCKS),
            hidden=(shape((count, own), BF16), VMEM),
            **({} if apart else dict(mixed=rows(width))),
            update=rows(own),
            shared=rows(keyed),
            reset=rows(wide),
            value=rows(wide),
            att=rows(wide),
            gated=rows(wide),
            probs=rows(ATT),
        ),
        dict(
            part=pltpu.VMEM((count, width), BF16),
            cand=pltpu.VMEM((count, own), BF16),
            in_w=pltpu.VMEM((width, low), BF16),
            out_w=pltpu.VMEM((wide, width), BF16),
            fold=pltpu.SemaphoreType.DMA((2 * shards + 1,)),
            mixed_send=gather_sems(count),
            mixed_recv=gather_sems(count),
            **sum_scratch("sum", count, own),
            gather_send=gather_sems(count),
            gather_recv=gather_sems(count),
        ),
        ident,
        54,
        first=first,
    )


def gather_kernel(waits, *refs):
    own_ref, out_ref, send, recv = refs[waits:]
    count, own = own_ref.shape
    peers = plane()
    mine = pl.ds(pl.multiple_of(peers[0] * own, LANES), own)
    out_ref[:, mine] = own_ref[...]
    greet(peers[1], peers[2])
    whole = block_gather(out_ref, peers, own, (send, recv))
    blocks = count // ROWS
    for block in range(blocks):
        whole.begin(block)
        if block:
            whole.forward(block - 1)
    whole.forward(blocks - 1)
    for block in range(blocks):
        whole.arrive(block)
        whole.sent(block)


def gather_columns(own, ident, after=()):
    count, width = own.shape
    return pl.pallas_call(
        functools.partial(gather_kernel, len(after)),
        out_shape=shape((count, width * 4), BF16),
        in_specs=[hbm()] * len(after) + [vmem()],
        out_specs=vmem(),
        scratch_shapes=[gather_sems(count), gather_sems(count)],
        cost_estimate=lasting(20),
        compiler_params=comm_params(ident),
    )(*after, own)


def feed_forward_joined(x, gain, shift, weights, bias, own_out, ident):
    count, width = x.shape
    hidden = bias.shape[1]
    own = width // 4

    def work(r):
        peers = plane()
        mine = pl.ds(pl.multiple_of(peers[0] * own, LANES), own)
        greet(peers[1], peers[2])
        r.wait("weights")
        total = block_sum(r, "sum", r.part, peers, own)
        gather = block_gather(r.out, peers, own, (r.gather_send, r.gather_recv))

        def compute(block):
            r.wait_block(block)
            x_rows, *outs = views((r.x, r.part, r.pre, r.n, r.normed, r.scale), block)
            feed_forward_kernel(x_rows, r.gain, r.shift, r.weights, r.bias, *outs)

        def finish(block):
            def strip(here, summed):
                made = r.x[here, mine].astype(F32) + summed + r.own_out[...]
                r.out[here, mine] = made.astype(BF16)

            finish_strips(total, block, strip)

        def extra(i):
            @pl.when(i == count // ROWS)
            def _():
                r.store("pre", "n", "normed", "scale")

        pipeline(
            count,
            compute,
            (total,),
            finish,
            gather,
            extra,
            arrived=lambda block: r.store_block("out", block),
        )

    rows = lambda columns, kind=BF16: (shape((count, columns), kind), STORE)
    return transfer(
        work,
        dict(
            x=(x, BLOCKS),
            weights=(weights, FETCH),
            gain=(gain, VMEM),
            shift=(shift, VMEM),
            bias=(bias, VMEM),
            own_out=(own_out, VMEM),
        ),
        dict(
            out=(shape((count, width), BF16), STORE_BLOCKS),
            pre=rows(hidden),
            n=rows(width),
            normed=rows(width),
            scale=rows(LANES, F32),
        ),
        dict(
            part=pltpu.VMEM((count, width), BF16),
            **sum_scratch("sum", count, own),
            gather_send=gather_sems(count),
            gather_recv=gather_sems(count),
        ),
        ident,
        40,
    )


def feed_backward(given, k, p, weights, shards, ident, after=()):
    corrected = isinstance(given, tuple)
    both_ways = k.feed_pre is None
    count, width = k.middle.shape
    own = width // 4
    hidden = p.feed_in.shape[1]
    norms, gain = p.own, p.feed_gain
    rows = ROWS
    blocks = count // rows

    def work(r):
        peers = plane()
        me, across, along, far = peers
        mine = pl.ds(pl.multiple_of(me * own, LANES), own)
        if corrected:
            r.z[:, mine] = r.z_own[...]
        greet(across, along)
        before = None
        if corrected:
            before = block_gather(r.z, peers, own, (r.z_send, r.z_recv), rows)
        r.sums[...] = jnp.zeros_like(r.sums)
        r.bias[...] = jnp.zeros_like(r.bias)
        total = block_sum(r, "sum", r.part, peers, own, rows=rows)
        gather = block_gather(r.out, peers, own, (r.gather_send, r.gather_recv), rows)

        def quarter(block, owner, half):
            size = count // 4
            return (
                pl.ds(pl.multiple_of(owner * size, size), size),
                pl.ds(half * (width // 2), width // 2),
            )

        if both_ways:
            last = block_sum(
                r, "last", r.made, peers, own, quarter, lambda block: pl.ds(0, count // 4)
            )

        def last_rows():
            for half in range(2):
                last.arrived(0, half)
                lanes = slice(half * (width // 2), (half + 1) * (width // 2))

                def strip(start):
                    here = pl.ds(start, STRIP)
                    row = pl.ds(pl.multiple_of(me * (count // 4), STRIP) + start, STRIP)
                    made = r.middle[row, lanes].astype(F32) + last.total(0, half, start)
                    r.block_out[here, lanes] = (made + r.out_bias[:, lanes]).astype(BF16)

                strips(count // 4, strip)

        def stats_copy(block, step):
            lanes = rows_of(block, rows)
            source = (r.stats, r.stats_stage)[step].at[:, lanes]
            sems = (r.stats_send, r.stats_recv)
            other = (across, along)[step]
            return link(source, r.stats_got.at[step, :, lanes], sems, 2 * block + step, other)

        def mean_copy(step):
            source = (r.z_stats, r.means_stage)[step]
            other = (across, along)[step]
            return link(source, r.means_got.at[step], (r.means_send, r.means_recv), step, other)

        if corrected:
            mean_copy(0).start()

        def compute(block):
            here = rows_of(block, rows)

            @pl.when(block == 0)
            def _():
                r.wait("weights")
                if corrected:
                    mean_copy(0).wait_recv()
                    r.means_stage[...] = r.z_stats[...] + r.means_got[0]
                    mean_copy(1).start()
                    mean_copy(1).wait_recv()
                    r.means[...] = r.means_stage[...] + r.means_got[1]

            r.wait_block(block)
            if corrected:
                xn, xscale = normalise(r.x_full[here, :].astype(F32))
                means = r.means[:, here].T * (1.0 / width)
                z = r.z[here, :].astype(F32)
                g = z - xscale * (means[:, 0:1] + xn * means[:, 1:2])
                r.g[here, :] = g.astype(BF16)
            if both_ways:
                x_rows, *made = views((r.middle, r.made, r.pre, r.n, r.normed, r.scale), block, rows)
                feed_forward_kernel(x_rows, r.gain, r.shift, r.weights, r.in_bias, *made)
            g_rows, pre_rows, n_rows = views((r.g, r.pre, r.n), block, rows)
            part, gpre, act = views((r.part, r.gpre, r.act), block, rows)
            feed_backward_block(
                g_rows,
                pre_rows,
                n_rows,
                r.gain,
                r.weights,
                part,
                r.stats,
                gpre,
                act,
                r.sums,
                r.bias,
                here,
            )
            stats_copy(block, 0).start()

        def finish(block):
            here = rows_of(block, rows)
            stats_copy(block, 1).wait_recv()
            every = r.stats_stage[:, here] + r.stats_got[1, :, here]
            r.columns[here, :] = every.T * (1.0 / width)

            def strip(here, summed):
                e = summed * r.norms[2:3, :]
                n_own = r.n[here, mine].astype(F32)
                inner = e - r.columns[here, 0:1] - n_own * r.columns[here, 1:2]
                g = r.g[here, mine].astype(F32) + r.scale[here, 0:1] * inner
                g = g.astype(BF16).astype(F32)
                u = sigmoid(r.update[here, :].astype(F32))
                pre = r.hidden[here, :].astype(F32)
                s = sigmoid(pre)
                x = r.x[here, :].astype(F32)
                r.gupdate[here, :] = (g * (pre * s - x) * (u * (1.0 - u))).astype(BF16)
                r.resid[here, :] = g * (1.0 - u)
                r.out[here, mine] = (g * u * (s * (1.0 + pre * (1.0 - s)))).astype(BF16)

            finish_strips(total, block, strip, rows)

        def small_grads():
            r.grad[:, hidden + width :] = jnp.zeros((width, LANES), BF16)
            size = width // shards
            for shard in range(shards):
                lanes = slice(shard * size, (shard + 1) * size)
                block = jnp.concatenate(
                    (r.sums[0:3, lanes], r.bias[0:1, lanes], jnp.zeros((SMALL - 4, size), F32)),
                    axis=0,
                )
                r.grad[shard * size : shard * size + SMALL, hidden + width :] = widen(block)

        def in_grad(rows, value):
            r.grad[rows, :hidden] = value

        def out_grad(rows, value):
            r.grad[rows, hidden : hidden + width] = value

        def extra(i):
            @pl.when((i >= 1) & (i <= blocks))
            def _():
                here = rows_of(i - 1, rows)
                stats_copy(i - 1, 0).wait_recv()
                r.stats_stage[:, here] = r.stats[:, here] + r.stats_got[0, :, here]
                stats_copy(i - 1, 1).start()

            @pl.when(i == 0)
            def _():
                r.wait("update", "hidden", "x")
                if not both_ways:
                    r.wait("scale", "normed")

            if both_ways:

                @pl.when(i == blocks - 1)
                def _():
                    last.begin(0)

                @pl.when(i == blocks)
                def _():
                    last.forward(0)

                @pl.when(i == blocks + 2)
                def _():
                    last_rows()
                    last.end(0)

            @pl.when(i == blocks + 1)
            def _():
                r.store("gupdate", "resid")

        def between(i):
            @pl.when(i == blocks)
            def _():
                grad_tiles(r.normed, r.gpre, in_grad, 0, width // TILE)
                small_grads()
                grad_tiles(r.act, r.g, out_grad, 0, hidden // TILE)
                r.store("grad")

        pipeline(
            count,
            compute,
            (total,),
            finish,
            gather,
            extra,
            between,
            before,
            rows,
            arrived=lambda block: r.store_block("out", block),
        )

        def close(i, carry):
            stats_copy(i, 0).wait_send()
            stats_copy(i, 1).wait_send()
            return carry

        lax.fori_loop(0, blocks, close, 0)
        if corrected:
            mean_copy(0).wait_send()
            mean_copy(1).wait_send()

    if corrected:
        z_own, z_stats, x_full = given
        first = dict(z_own=(z_own, VMEM), x_full=(x_full, BLOCKS), z_stats=(z_stats, VMEM))
        both = pltpu.SemaphoreType.DMA((2,))
        extra_scratch = dict(
            g=pltpu.VMEM((count, width), BF16),
            z=pltpu.VMEM((count, width), BF16),
            z_send=gather_sems(count),
            z_recv=gather_sems(count),
            means=pltpu.VMEM((CHUNKS, count), F32),
            means_stage=pltpu.VMEM((CHUNKS, count), F32),
            means_got=pltpu.VMEM((2, CHUNKS, count), F32),
            means_send=both,
            means_recv=both,
        )
    else:
        first = dict(g=(given, BLOCKS))
        extra_scratch = {}
    extra_outs = {}
    if both_ways:
        saved = {}
        first.update(
            middle=(k.middle, BLOCKS),
            shift=(p.feed_shift, VMEM),
            in_bias=(p.feed_in, VMEM),
            out_bias=(p.feed_out, VMEM),
        )
        extra_outs.update(block_out=(shape((count // 4, width), BF16), VMEM))
        buffer = pltpu.VMEM((count, width), BF16)
        slot = pltpu.VMEM((2, count // 4, width // 2), BF16)
        ends = pltpu.SemaphoreType.DMA((6,))
        extra_scratch.update(
            made=buffer,
            pre=pltpu.VMEM((count, hidden), BF16),
            n=buffer,
            normed=buffer,
            scale=pltpu.VMEM((count, LANES), F32),
            last_early=slot,
            last_direct=slot,
            last_late=slot,
            last_stage=slot,
            last_send=ends,
            last_recv=ends,
        )
    else:
        saved = dict(
            pre=(k.feed_pre, BLOCKS),
            n=(k.feed_n, BLOCKS),
            scale=(k.feed_scale, LATE),
            normed=(k.feed_normed, LATE),
        )
    sems = pltpu.SemaphoreType.DMA((2 * blocks,))
    return transfer(
        work,
        dict(
            weights=(weights, FETCH),
            **first,
            **saved,
            update=(k.update, LATE),
            hidden=(k.hidden, LATE),
            x=(k.x, OWN_PART),
            gain=(gain, VMEM),
            norms=(norms, VMEM),
        ),
        dict(
            out=(shape((count, width), BF16), STORE_BLOCKS),
            gupdate=(shape((count, own), BF16), STORE),
            resid=(shape((count, own), F32), STORE),
            grad=(shape((width, hidden + width + LANES), BF16), STORE),
            **extra_outs,
        ),
        dict(
            part=pltpu.VMEM((count, width), BF16),
            gpre=pltpu.VMEM((count, hidden), BF16),
            act=pltpu.VMEM((count, hidden), BF16),
            sums=pltpu.VMEM((8, width), F32),
            bias=pltpu.VMEM((8, hidden), F32),
            stats=pltpu.VMEM((CHUNKS, count), F32),
            stats_stage=pltpu.VMEM((CHUNKS, count), F32),
            stats_got=pltpu.VMEM((2, CHUNKS, count), F32),
            columns=pltpu.VMEM((count, CHUNKS), F32),
            stats_send=sems,
            stats_recv=sems,
            **extra_scratch,
            **sum_scratch("sum", count, own, rows),
            gather_send=gather_sems(count),
            gather_recv=gather_sems(count),
        ),
        ident,
        46,
        after,
        rows=rows,
    )


def attention_backward(length, gout, gupdate, k, packed, pair, offset, shards, ident, after=()):
    shared, reset, value, att, probs = k.saved
    count, width = gout.shape
    own = width // 4
    wide = width // 2
    keyed = pair.shape[1]
    total = packed.shape[1] - width // 2
    rows = 2 * ROWS
    blocks = count // rows
    few = wide // shards
    block_rows = width // shards

    def weights(r):
        return unfold(r.packed, r.in_w, r.out_w, shards, r.fold)

    def first(r):
        for copy in weights(r):
            copy.start()

    def work(r):
        peers = plane()
        mine = pl.ds(pl.multiple_of(peers[0] * own, LANES), own)
        real = r.length[0]
        greet(peers[1], peers[2])
        r.bias[...] = jnp.zeros_like(r.bias)
        r.pairs[...] = jnp.zeros_like(r.pairs)
        one = block_sum(r, "one", r.gmixed_part, peers, own, rows=rows)
        two = block_sum(r, "two", r.gvalue_part, peers, own, rows=rows)

        def compute(block):
            @pl.when(block == 0)
            def _():
                for copy in weights(r):
                    copy.wait()

            r.wait_block(block)
            attention_backward_block(
                real,
                block * rows,
                mine,
                *views((r.gout, r.gupdate, r.shared, r.reset, r.value, r.att, r.probs), block, rows),
                r.in_w,
                r.pair,
                r.offset,
                *views((r.gmixed_part, r.gvalue_part, r.gbase, r.gvalue), block, rows),
                r.bias,
                r.pairs,
                r.out_w,
            )

        def finish(block):
            def keep(out):
                def strip(here, summed):
                    out[here, :] = summed

                return strip

            finish_strips(one, block, keep(r.gmixed), rows)
            finish_strips(two, block, keep(r.gnormed), rows)

        def value_grad(rows, value):
            r.grad[rows, :wide] = value

        def base_grad(rows, value):
            r.grad[rows, wide:total] = value

        def out_grad(rows, value):
            for i in range(TILE // few):
                start = (rows.start // few + i) * block_rows
                for half in range(2):
                    here = pl.ds(pl.multiple_of(start + half * few, few), few)
                    r.grad[here, total : total + width // 2] = value[
                        i * few : (i + 1) * few, half * (width // 2) : (half + 1) * (width // 2)
                    ]

        def small_grads():
            last = total + width // 2
            r.grad[:, last:] = jnp.zeros((width, LANES), BF16)
            pieces = [r.bias[0:1, i * LANES : (i + 1) * LANES] for i in range(total // LANES)]
            block = jnp.concatenate(pieces + [r.pairs[0:3, :]], axis=0).astype(BF16)
            for shard in range(shards):
                r.grad[shard * block_rows : shard * block_rows + SMALL, last:] = block

        def extra(i):
            @pl.when(i == 0)
            def _():
                r.wait("normed", "mixed", "gated")

        def between(i):
            @pl.when(i == blocks)
            def _():
                small_grads()
                grad_tiles(r.mixed, r.gbase, base_grad, 0, width // TILE)
                grad_tiles(r.normed, r.gvalue, value_grad, 0, width // TILE)
                grad_tiles(r.gated, r.gout, out_grad, 0, wide // TILE)
                r.store("grad")

        pipeline(count, compute, (one, two), finish, None, extra, between, rows=rows)

    return transfer(
        work,
        dict(
            length=(length, SMEM),
            packed=(packed, RAW),
            gout=(gout, BLOCKS),
            gupdate=(gupdate, BLOCKS),
            shared=(shared, BLOCKS),
            reset=(reset, BLOCKS),
            value=(value, BLOCKS),
            att=(att, BLOCKS),
            probs=(probs, BLOCKS),
            normed=(k.normed, LATE),
            mixed=(k.mixed, LATE),
            gated=(k.gated, LATE),
            pair=(pair, VMEM),
            offset=(offset, VMEM),
        ),
        dict(
            gmixed=(shape((count, own), F32), VMEM),
            gnormed=(shape((count, own), F32), VMEM),
            grad=(shape((width, total + width // 2 + LANES), BF16), STORE),
        ),
        dict(
            gmixed_part=pltpu.VMEM((count, width), BF16),
            gvalue_part=pltpu.VMEM((count, width), BF16),
            gbase=pltpu.VMEM((count, total - wide), BF16),
            gvalue=pltpu.VMEM((count, wide), BF16),
            bias=pltpu.VMEM((8, total), F32),
            pairs=pltpu.VMEM((8, keyed), F32),
            in_w=pltpu.VMEM((width, total), BF16),
            out_w=pltpu.VMEM((wide, width), BF16),
            fold=pltpu.SemaphoreType.DMA((2 * shards + 1,)),
            **sum_scratch("one", count, own, rows),
            **sum_scratch("two", count, own, rows),
        ),
        ident,
        40,
        after,
        first,
        rows,
    )


def block_piece(whole):
    def piece(owner, half):
        size = whole.shape[1] // 2
        return owner, pl.ds(half * size, size), slice(None)

    return piece


def final_kernel(number, layers, z_ref, stats_ref, x_ref, *refs):
    blocks, refs = refs[:number], refs[number:]
    average_ins, refs = refs[: 5 * layers], refs[5 * layers :]
    (out_ref, sums_ref), refs = refs[:2], refs[2:]
    gathered, refs = refs[:number], refs[number:]
    land, x_own, got, stats_stage, total_buf, local_sem, send, recv = refs[:8]
    m_buf, g_buf, held_sems = refs[8:11]
    block_sems = [refs[11 + 2 * i : 13 + 2 * i] for i in range(number)]
    count, own = z_ref.shape
    quarter, width = out_ref.shape
    peers = plane()
    me = peers[0]

    def rows(owner):
        return pl.ds(pl.multiple_of(owner * quarter, quarter), quarter)

    mine = pl.ds(pl.multiple_of(me * own, LANES), own)
    fetch = pltpu.make_async_copy(x_ref.at[rows(me), :], x_own, local_sem)
    fetch.start()
    held = []
    for layer in range(layers):
        for k, buffer in enumerate((m_buf, g_buf)):
            source = average_ins[5 * layer + k]
            sem = held_sems.at[2 * layer + k]
            held.append(pltpu.make_async_copy(source, buffer.at[layer], sem))
            held[-1].start()

    def sums_of(layer):
        rate, back, rest = average_ins[5 * layer + 2 : 5 * layer + 5]
        dims = rate.shape[0]
        low = layer * (2 * dims + 8)
        held[2 * layer].wait()
        held[2 * layer + 1].wait()
        average_sums(m_buf.at[layer], g_buf.at[layer], rate, back, sums_ref, low)
        sums_ref[low + 2 * dims : low + 2 * dims + 8, :] = rest[...]

    land[:, mine] = z_ref[rows(me), :]
    for block, whole in zip(blocks, gathered):
        whole[me] = block[...]
    greet(*peers[1:])
    sems = (send, recv)
    copies = []
    for index, other in enumerate(peers[1:]):
        copies.append(link(z_ref.at[rows(other), :], land.at[:, mine], sems, 2 + index, other))
        copies[-1].start()
    total_buf[...] = stats_total(stats_ref, got, stats_stage, peers, sems, 0)
    begun = [
        [gather_begin(whole, block_piece(whole), peers, k, half) for half in range(2)]
        for whole, k in zip(gathered, block_sems)
    ]
    part = total_buf[:, pl.ds(pl.multiple_of(me * quarter, LANES), quarter)]
    means = part.T * (1.0 / width)
    fetch.wait()
    for copy in copies:
        copy.wait_recv()
    n, scale = normalise(x_own[...].astype(F32))
    g = land[...].astype(F32) - scale * (means[:, 0:1] + n * means[:, 1:2])
    out_ref[...] = g.astype(BF16)
    for layer in range(1, layers):
        sums_of(layer)
    passed = [
        gather_forward(whole, block_piece(whole), peers, k, zero, one)
        for whole, k, (zero, one) in zip(gathered, block_sems, begun)
    ]
    sums_of(0)
    for whole, k, (zero, one), two in zip(gathered, block_sems, begun, passed):
        gather_finish(whole, block_piece(whole), peers, k, zero, one, two)
    for copy in copies:
        copy.wait_send()


def final_exchange(z, stats, x, blocks, averages, sections, ident):
    layers = len(averages)
    dims, _, own = averages[0][2].shape
    held_dims = (layers,) + averages[0][0].shape
    count, own = z.shape
    width = x.shape[1]
    quarter = count // 4
    number = len(blocks)
    return pl.pallas_call(
        functools.partial(final_kernel, number, layers),
        out_shape=(
            shape((quarter, width), BF16),
            shape((layers * (2 * dims + 8), own), F32),
        )
        + tuple(shape((sections,) + a.shape, BF16) for a in blocks),
        in_specs=[vmem(), vmem(), hbm()]
        + [vmem()] * number
        + [hbm(), hbm(), vmem(), vmem(), vmem()] * layers,
        out_specs=(vmem(),) * (2 + number),
        scratch_shapes=[
            pltpu.VMEM((quarter, width), BF16),
            pltpu.VMEM((quarter, width), BF16),
            pltpu.VMEM((2,) + stats.shape, F32),
            pltpu.VMEM(stats.shape, F32),
            pltpu.VMEM(stats.shape, F32),
            pltpu.SemaphoreType.DMA,
        ]
        + copy_sems(5)
        + [
            pltpu.VMEM(held_dims, F32),
            pltpu.VMEM(held_dims, F32),
            pltpu.SemaphoreType.DMA((2 * layers,)),
        ]
        + copy_sems(6) * number,
        cost_estimate=lasting(10 + 20 * number),
        compiler_params=comm_params(ident),
    )(z, stats, x, *blocks, *[a for one in averages for a in one])


def sums_kernel(shards, holders, sums_ref, block_ref, channels_ref, whole_ref, *refs):
    sums_land, send_s, recv_s, send_c, recv_c, send, recv = refs
    peers = plane()
    me = peers[0]
    slot = lax.axis_index("dp")
    holding = slot // holders == me
    whole_ref[me] = block_ref[...]
    barrier = pltpu.get_barrier_semaphore()
    for other in peers[1:]:
        pl.semaphore_signal(barrier, inc=1, device_id={"section": other}, device_id_type=MESH)
    for step in range(1, shards):
        other = (slot + step) % shards
        pl.semaphore_signal(barrier, inc=1, device_id={"dp": other}, device_id_type=MESH)
    pl.semaphore_wait(barrier, shards + 2)

    def sums_copy(target, index, place):
        return pltpu.make_async_remote_copy(
            src_ref=sums_ref,
            dst_ref=sums_land.at[place],
            send_sem=send_s.at[index],
            recv_sem=recv_s.at[place],
            device_id={"dp": target},
            device_id_type=MESH,
        )

    def sums_out(index):
        target = me * holders + index
        place = jnp.maximum((slot - target + shards) % shards - 1, 0)
        return target, sums_copy(target, index, place)

    for index in range(holders):
        target, copy = sums_out(index)

        @pl.when(target != slot)
        def _():
            copy.start()

    piece = block_piece(whole_ref)
    zero, one = (gather_begin(whole_ref, piece, peers, (send, recv), half) for half in range(2))
    passed = gather_forward(whole_ref, piece, peers, (send, recv), zero, one)

    def channels_copy(other, index):
        return link(channels_ref, channels_ref, (send_c, recv_c), index, other)

    @pl.when(holding)
    def _():
        summed = sums_ref[...]
        for step in range(1, shards):
            sums_copy((slot + step) % shards, 0, step - 1).wait_recv()
            summed = summed + sums_land[step - 1]
        channels_ref[...] = summed
        for index, other in enumerate(peers[1:]):
            channels_copy(other, index).start()

    gather_finish(whole_ref, piece, peers, (send, recv), zero, one, passed)

    for index, other in enumerate(peers[1:]):

        @pl.when(slot // holders == other)
        def _():
            channels_copy(other, index).wait_recv()

    @pl.when(holding)
    def _():
        for index, other in enumerate(peers[1:]):
            channels_copy(other, index).wait_send()

    for index in range(holders):
        target, copy = sums_out(index)

        @pl.when(target != slot)
        def _():
            copy.wait_send()


def gather_sums(sums, block, sections, shards, holders, ident):
    return pl.pallas_call(
        functools.partial(sums_kernel, shards, holders),
        out_shape=(shape(sums.shape, F32), shape((sections,) + block.shape, BF16)),
        in_specs=[vmem()] * 2,
        out_specs=(vmem(),) * 2,
        scratch_shapes=[pltpu.VMEM((shards - 1,) + sums.shape, F32)]
        + copy_sems(max(shards - 1, holders))
        + copy_sems(3)
        + copy_sems(6),
        cost_estimate=lasting(25),
        compiler_params=comm_params(ident),
    )(sums, block)


def woven_parts(part, here, low, size, shards):
    step = size // shards
    return jnp.concatenate(
        [
            part[k, here, low + d * step : low + (d + 1) * step].astype(F32)
            for d in range(shards)
            for k in range(part.shape[0])
        ],
        axis=1,
    )


def joined_parts(part, here, low, size):
    return jnp.concatenate(
        [part[k, here, low : low + size].astype(F32) for k in range(part.shape[0])], axis=1
    )


def by_strips(rows, work):
    def strip(i, carry):
        work(pl.ds(pl.multiple_of(i * SMALL, SMALL), SMALL))
        return carry

    lax.fori_loop(0, rows // SMALL, strip, 0)


def attention_outputs(shards, layer, part, extras, outs):
    value_ref, base_ref, out_ref, value_bias_ref, base_bias_ref, pair_ref, query_ref = outs[:7]
    norm_outs, average_outs = outs[7:10], outs[10:]
    sections = part.shape[0]
    width = out_ref.shape[2]
    wide = value_ref.shape[2] // sections
    own = width // sections
    keyed = base_ref.shape[2] - 2 * width - wide * sections
    edge = wide + own
    total = edge + keyed + wide + own
    few = wide // shards

    def strip(here):
        value_ref[0, here, :] = woven_parts(part, here, 0, wide, shards)
        base_ref[0, here, :width] = joined_parts(part, here, wide, own)
        shared = part[0, here, edge : edge + keyed].astype(F32)
        for k in range(1, sections):
            shared += part[k, here, edge : edge + keyed].astype(F32)
        low = width
        base_ref[0, here, low : low + keyed] = shared
        low += keyed
        base_ref[0, here, low : low + wide * sections] = woven_parts(
            part, here, edge + keyed, wide, shards
        )
        low += wide * sections
        base_ref[0, here, low:] = joined_parts(part, here, edge + keyed + wide, own)

    by_strips(value_ref.shape[1], strip)
    for k in range(sections):
        for half in range(2):
            columns = slice(half * (width // 2), (half + 1) * (width // 2))
            out_ref[0, k * few : (k + 1) * few, columns] = part[
                k, half * few : (half + 1) * few, total : total + width // 2
            ].astype(F32)
    slot = lax.axis_index("dp")
    row = slice(layer, layer + 1)
    blocks = [part[k, :SMALL, total + width // 2 :].astype(F32) for k in range(sections)]
    lines = [
        jnp.concatenate([b[i : i + 1] for i in range(total // LANES)], axis=1) for b in blocks
    ]
    summed = sum(blocks[1:], blocks[0])

    def mine(line):
        size = line.shape[1] // shards
        return chosen([line[:, d * size : (d + 1) * size] for d in range(shards)], slot)

    value_bias_ref[row, :] = jnp.concatenate([mine(line[:, :wide]) for line in lines], axis=1)
    low = edge + keyed
    base_line = jnp.concatenate(
        [line[:, wide:edge] for line in lines]
        + [sum((line[:, edge:low] for line in lines[1:]), lines[0][:, edge:low])]
        + [
            line[:, low + d * few : low + (d + 1) * few]
            for d in range(shards)
            for line in lines
        ]
        + [line[:, low + wide :] for line in lines],
        axis=1,
    )
    base_bias_ref[row, :] = mine(base_line)
    first = total // LANES
    for k in range(2):
        pair_ref[layer, k : k + 1, :] = mine(summed[first + k : first + k + 1])
    query_ref[row, :] = mine(summed[first + 2 : first + 3])

    channels_ref, decay_ref, input_ref, output_ref = extras
    dims, size = decay_ref.shape[1:]
    holders = own // size
    low = layer * (2 * dims + 8)

    def channels(start, count):
        here = slice(low + start, low + start + count)
        pieces = [channels_ref[here, k * size : (k + 1) * size] for k in range(holders)]
        return chosen(pieces, slot % holders)

    sums = channels(2 * dims, 8)
    for k, ref in enumerate(norm_outs):
        ref[row, :] = sums[k : k + 1]
    of_states, of_slopes = channels(0, dims), channels(dims, dims)
    rate = sigmoid(decay_ref[layer])
    drive = (1.0 - rate) * input_ref[layer]
    gdrive = output_ref[layer] * of_states
    grate = drive * output_ref[layer] * of_slopes - input_ref[layer] * gdrive
    average_outs[0][layer] = grate * rate * (1.0 - rate)
    average_outs[1][layer] = (1.0 - rate) * gdrive
    average_outs[2][layer] = drive * of_states


def feed_outputs(shards, layer, feed, extras, outs):
    in_ref, out_ref, gain_ref, shift_ref, out_bias_ref, in_bias_ref = outs
    sections, rows = feed.shape[:2]
    width = out_ref.shape[2]
    hidden = in_ref.shape[2] // sections

    def strip(here):
        in_ref[0, here, :] = woven_parts(feed, here, 0, hidden, shards)

    by_strips(rows, strip)
    for k in range(sections):
        out_ref[0, k * rows : (k + 1) * rows, :] = feed[k, :, hidden : hidden + width].astype(F32)
    size = width // shards
    row = slice(layer, layer + 1)
    blocks = [feed[k, :SMALL, hidden + width :].astype(F32)[:, :size] for k in range(sections)]
    summed = sum(blocks[1:], blocks[0])
    gain_ref[row, :] = summed[0:1]
    shift_ref[row, :] = summed[1:2]
    out_bias_ref[row, :] = blocks[0][2:3]
    in_bias_ref[row, :] = jnp.concatenate([b[3:4] for b in blocks], axis=1)


def assemble_kernel(work, shards, layers, more, *refs):
    extras, outs = refs[layers : layers + more], refs[layers + more :]
    for layer in range(layers):

        @pl.when(pl.program_id(0) == layer)
        def _():
            work(shards, layer, refs[layer], extras, outs)


def assemble(work, gathered, extras, dims, small_dims, shards):
    layers = len(gathered)

    def whole(dims):
        return pl.BlockSpec(dims, lambda i, n=len(dims): (0,) * n)

    return pl.pallas_call(
        functools.partial(assemble_kernel, work, shards, layers, len(extras)),
        grid=(layers,),
        out_shape=tuple(shape((layers,) + d, F32) for d in dims + small_dims),
        in_specs=[whole(a.shape) for a in gathered + extras],
        out_specs=tuple(
            pl.BlockSpec((1,) + d, lambda i, n=len(d): (i,) + (0,) * n) for d in dims
        )
        + tuple(whole((layers,) + d) for d in small_dims),
        cost_estimate=lasting(6),
        compiler_params=params(),
    )(*gathered, *extras)


def chosen(pieces, section=None):
    if section is None:
        section = lax.axis_index("section")
    result = pieces[0]
    for k in range(1, len(pieces)):
        result = jnp.where(section == k, pieces[k], result)
    return result


def pick(ref, index, low, size, shards, sections):
    step = size // (shards * sections)
    parts = []
    section = lax.axis_index("section")
    for shard in range(shards):
        start = low + shard * sections * step
        if 2 * step == LANES and start % LANES == 0:
            pair = pl.ds(pl.multiple_of(start + section // 2 * LANES, LANES), LANES)
            both = ref[index + (pair,)]
            parts.append(jnp.where(section % 2 == 0, both[:, :step], both[:, step:]))
            continue
        if step == LANES and start % LANES == 0:
            one = pl.ds(pl.multiple_of(start + section * LANES, LANES), LANES)
            parts.append(ref[index + (one,)])
            continue
        parts.append(
            chosen([ref[index + (slice(start + k * step, start + (k + 1) * step),)] for k in range(sections)])
        )
    return jnp.concatenate(parts, axis=-1)


def pack_attention_kernel(shards, sections, value_ref, base_ref, out_ref, packed_ref):
    rows, wide_all = value_ref.shape[1:]
    few_all, width = out_ref.shape[1:]
    wide, own, few = wide_all // sections, width // sections, few_all // sections
    keyed = base_ref.shape[2] - 2 * width - wide_all
    section = lax.axis_index("section")
    low = wide + own + keyed

    def strip(i, carry):
        here = pl.ds(pl.multiple_of(i * SMALL, SMALL), SMALL)

        def base(start, size):
            return base_ref[0, here, pl.ds(pl.multiple_of(start, LANES), size)]

        packed_ref[here, :wide] = pick(value_ref, (0, here), 0, wide_all, shards, sections)
        packed_ref[here, wide : wide + own] = base(section * own, own)
        packed_ref[here, wide + own : low] = base(width, keyed)
        packed_ref[here, low : low + wide] = pick(
            base_ref, (0, here), width + keyed, wide_all, shards, sections
        )
        packed_ref[here, low + wide : low + wide + own] = base(
            width + keyed + wide_all + section * own, own
        )
        return carry

    lax.fori_loop(0, rows // SMALL, strip, 0)
    low += wide + own
    mine = pl.ds(pl.multiple_of(section * few, few), few)
    for half in range(2):
        packed_ref[half * few : (half + 1) * few, low:] = out_ref[
            0, mine, half * (width // 2) : (half + 1) * (width // 2)
        ]


def pack_feed_kernel(shards, sections, in_ref, out_ref, packed_ref):
    rows, hidden_all = in_ref.shape[1:]
    hidden = hidden_all // sections
    size = out_ref.shape[1] // sections

    def strip(i, carry):
        here = pl.ds(pl.multiple_of(i * SMALL, SMALL), SMALL)
        packed_ref[here, :hidden] = pick(in_ref, (0, here), 0, hidden_all, shards, sections)
        return carry

    lax.fori_loop(0, rows // SMALL, strip, 0)
    start = pl.multiple_of(lax.axis_index("section") * size, size)
    packed_ref[:, hidden:] = out_ref[0, pl.ds(start, size), :]


def pack(work, layer, columns, shards, sections, arrays, after=()):
    rows = arrays[0].shape[1]

    def kernel(*refs):
        work(shards, sections, *refs[len(after) :])

    return pl.pallas_call(
        kernel,
        grid=(1,),
        out_shape=shape((rows, columns), BF16),
        in_specs=[hbm()] * len(after)
        + [pl.BlockSpec((1,) + a.shape[1:], lambda i: (layer, 0, 0)) for a in arrays],
        out_specs=pl.BlockSpec((rows, columns), lambda i: (0, 0)),
        cost_estimate=lasting(3),
        compiler_params=params(),
    )(*after, *arrays)


def unpack_kernel(layers, shards, sections, places, everyone_ref, *refs):
    base_buf = refs[-1]
    section = lax.axis_index("section")
    outs = 14
    for layer in range(layers):
        (
            gain_ref,
            shift_ref,
            feed_gain_ref,
            feed_shift_ref,
            feed_out_ref,
            own_ref,
            rate_ref,
            coef_ref,
            bias_ref,
            feed_in_ref,
            pair_ref,
            offset_ref,
            skip_ref,
            own_out_ref,
        ) = refs[layer * outs : (layer + 1) * outs]
        width = gain_ref.shape[1]
        own = width // sections
        mine = pl.ds(pl.multiple_of(section * own, LANES), own)
        row = slice(layer, layer + 1)

        def joined(low, size):
            return jnp.concatenate(
                [everyone_ref[d, row, low : low + size] for d in range(shards)], axis=1
            )

        def share(low, size):
            step = size // sections
            return jnp.concatenate(
                [
                    chosen(
                        [
                            everyone_ref[d, row, low + k * step : low + (k + 1) * step]
                            for k in range(sections)
                        ]
                    )
                    for d in range(shards)
                ],
                axis=1,
            )

        def channels(low):
            size = width // shards
            count = own // size
            return jnp.concatenate(
                [everyone_ref[section * count + d, row, low : low + size] for d in range(count)],
                axis=1,
            )

        size = width // shards
        gain_ref[...] = joined(places["norm_gain"], size)
        shift_ref[...] = joined(places["norm_shift"], size)
        feed_gain_ref[...] = joined(places["feed_gain"], size)
        feed_shift_ref[...] = joined(places["feed_shift"], size)
        feed_out_ref[...] = joined(places["feed_out_bias"], size)
        own_ref[0:1, :] = gain_ref[:, mine]
        own_ref[1:2, :] = shift_ref[:, mine]
        own_ref[2:3, :] = feed_gain_ref[:, mine]
        own_ref[3:8, :] = jnp.zeros((5, own), F32)
        own_out_ref[...] = feed_out_ref[:, mine]
        skip_ref[...] = channels(places["average_skip"])
        for n in range(rate_ref.shape[0]):
            rate = sigmoid(channels(places["average_decay"] + n * size))
            drive = (1.0 - rate) * channels(places["average_input"] + n * size)
            coef = drive * channels(places["average_output"] + n * size)
            rate_ref[n] = jnp.broadcast_to(rate, (CHUNKS, own))
            coef_ref[n] = jnp.broadcast_to(coef, (CHUNKS, own))
        keyed = offset_ref.shape[1]
        step = keyed // shards
        for r in range(2):
            pair_ref[r : r + 1, :] = joined(places["pair_scale"] + r * step, step)
        offset_ref[...] = joined(places["query_shift"], step)
        feed_in_ref[...] = share(
            places["feed_in_bias"], feed_in_ref.shape[1] * sections // shards
        )
        total = bias_ref.shape[1]
        wide = (total - keyed - 2 * own) // 2
        base_all = 2 * width + keyed + wide * sections
        base_buf[...] = joined(places["base_bias"], base_all // shards)
        low = wide + own + keyed
        bias_ref[:, :wide] = share(places["value_bias"], wide * sections // shards)
        bias_ref[:, wide : wide + own] = base_buf[:, mine]
        bias_ref[:, wide + own : low] = base_buf[:, width : width + keyed]
        bias_ref[:, low : low + wide] = pick(
            base_buf, (slice(None),), width + keyed, wide * sections, shards, sections
        )
        start = pl.multiple_of(width + keyed + wide * sections + section * own, LANES)
        bias_ref[:, low + wide :] = base_buf[:, pl.ds(start, own)]


def unpack(everyone, places, sizes, sections):
    shards, layers = everyone.shape[:2]
    width, dims, total, hidden, keyed, base = sizes
    own = width // sections
    one_layer = (
        [shape((1, width), F32)] * 5
        + [shape((8, own), F32)]
        + [shape((dims, CHUNKS, own), F32)] * 2
        + [
            shape((1, total), F32),
            shape((1, hidden), F32),
            shape((2, keyed), F32),
            shape((1, keyed), F32),
            shape((1, own), F32),
            shape((1, own), F32),
        ]
    )
    outs = pl.pallas_call(
        functools.partial(unpack_kernel, layers, shards, sections, places),
        out_shape=tuple(one_layer * layers),
        in_specs=[vmem()],
        out_specs=(vmem(),) * (len(one_layer) * layers),
        scratch_shapes=[pltpu.VMEM((1, base), F32)],
        cost_estimate=lasting(3),
        compiler_params=params(),
    )(everyone)
    names = (
        "gain",
        "shift",
        "feed_gain",
        "feed_shift",
        "feed_out",
        "own",
        "rate",
        "coef",
        "bias",
        "feed_in",
        "pair",
        "offset",
        "skip",
        "own_out",
    )
    count = len(one_layer)
    return [
        types.SimpleNamespace(**dict(zip(names, outs[k * count : (k + 1) * count])))
        for k in range(layers)
    ]


def body(
    tokens,
    lengths,
    cotangent,
    norm_gain,
    norm_shift,
    average_decay,
    average_input,
    average_output,
    average_skip,
    value_weight,
    value_bias,
    base_weight,
    base_bias,
    pair_scale,
    query_shift,
    out_weight,
    feed_gain,
    feed_shift,
    feed_in_weight,
    feed_in_bias,
    feed_out_weight,
    feed_out_bias,
):
    sections = lax.axis_size("section")
    shards = lax.axis_size("dp")
    section = lax.axis_index("section")
    _, count, width = tokens.shape
    layers = norm_gain.shape[0]
    own = width // sections
    wide = value_weight.shape[2]
    keyed = pair_scale.shape[2] * shards
    hidden = feed_in_weight.shape[2]

    share = wide // sections
    total = share + own + keyed + share + own

    def over_dp(array):
        return lax.all_gather(array, "dp", axis=0, tiled=True)

    def attention_weights(layer, after=()):
        arrays = (value_weight, base_weight, out_weight)
        columns = total + width // 2
        return pack(pack_attention_kernel, layer, columns, shards, sections, arrays, after)

    def feed_weights(layer, after=()):
        arrays = (feed_in_weight, feed_out_weight)
        columns = hidden // sections + width
        return pack(pack_feed_kernel, layer, columns, shards, sections, arrays, after)

    weights = [[None, None] for _ in range(layers)]
    weights[0][0] = over_dp(attention_weights(0))

    smalls = dict(
        norm_gain=norm_gain,
        norm_shift=norm_shift,
        average_decay=average_decay,
        average_input=average_input,
        average_output=average_output,
        average_skip=average_skip,
        feed_gain=feed_gain,
        feed_shift=feed_shift,
        feed_out_bias=feed_out_bias,
        value_bias=value_bias,
        feed_in_bias=feed_in_bias,
        base_bias=base_bias,
        pair_scale=pair_scale,
        query_shift=query_shift,
    )
    packed = jnp.concatenate([a.reshape(layers, -1) for a in smalls.values()], axis=1)
    places = {}
    low = 0
    for name, array in smalls.items():
        places[name] = low
        low += array.size // layers
    dims = average_decay.shape[1]
    small = unpack(
        lax.all_gather(packed, "dp", axis=0),
        places,
        (width, dims, total, hidden // sections, keyed, base_weight.shape[2]),
        sections,
    )

    idents = iter(range(64))
    x0 = x = tokens[0]
    kept = []
    for layer in range(layers):
        p = small[layer]
        normed, mixed_own, pre, own_n, scale = average_forward(
            lengths, x, p.gain, p.shift, p.rate, p.coef, p.skip
        )
        if not layer:
            packed_feed = feed_weights(0, (mixed_own,))
            weights[0][1] = over_dp(packed_feed)
            mixed = mixed_own = gather_columns(mixed_own, next(idents), (packed_feed,))
        middle, hidden_pre, *mixed_out, update, shared, reset, value, att, gated, probs = attention_forward(
            lengths,
            normed,
            mixed_own,
            weights[layer][0],
            p.bias,
            p.pair,
            p.offset,
            x,
            shards,
            next(idents),
        )
        if layer:
            (mixed,) = mixed_out
        if layer + 1 < layers:
            weights[layer + 1] = [
                over_dp(attention_weights(layer + 1, (hidden_pre,))),
                over_dp(feed_weights(layer + 1, (hidden_pre,))),
            ]
        attention_w, feed_w = weights[layer]
        feed_saved = [None] * 4
        x_next = None
        if layer + 1 < layers:
            x_next, *feed_saved = feed_forward_joined(
                middle, p.feed_gain, p.feed_shift, feed_w, p.feed_in, p.own_out, next(idents)
            )
        feed_pre, feed_n, feed_normed, feed_scale = feed_saved
        kept.append(
            types.SimpleNamespace(
                x=x,
                middle=middle,
                normed=normed,
                mixed=mixed,
                pre=pre,
                own_n=own_n,
                scale=scale,
                update=update,
                saved=(shared, reset, value, att, probs),
                gated=gated,
                hidden=hidden_pre,
                feed_pre=feed_pre,
                feed_n=feed_n,
                feed_normed=feed_normed,
                feed_scale=feed_scale,
            )
        )
        x = x_next

    def scattered(grad):
        return lax.psum_scatter(grad, "dp", scatter_dimension=0, tiled=True)

    given = cotangent[0]
    feed_grads = [None] * layers
    attention_grads = [None] * layers
    averages = [None] * layers
    for layer in reversed(range(layers)):
        attention_w, feed_w = weights[layer]
        k, p = kept[layer], small[layer]
        gout, gupdate, resid, feed_grad, *last = feed_backward(
            given, k, p, feed_w, shards, next(idents), () if layer else (feed_grads[1],)
        )
        if last:
            block_out = last[0]
        feed_grads[layer] = scattered(feed_grad)
        gmixed, gnormed, attention_grad = attention_backward(
            lengths,
            gout,
            gupdate,
            k,
            attention_w,
            p.pair,
            p.offset,
            shards,
            next(idents),
            () if layer else (attention_grads[1],),
        )
        attention_grads[layer] = scattered(attention_grad)
        z, zstats, norm_sums, m_buf, g_buf, back, *attention_one = average_backward(
            lengths,
            gmixed,
            gnormed,
            k,
            resid,
            p.own,
            p.rate,
            p.coef,
            p.skip,
            None if layer else attention_grads[1],
            None if layer else next(idents),
        )
        averages[layer] = (m_buf, g_buf, p.rate, back, norm_sums)
        if layer:
            given = (z, zstats, k.x)

    (attention_one,) = attention_one
    input_grad, channel_sums, feed_one, feed_zero = final_exchange(
        z, zstats, x0, [feed_grads[1], feed_grads[0]], averages, sections, next(idents)
    )
    channels, attention_zero = gather_sums(
        channel_sums,
        attention_grads[0],
        sections,
        shards,
        own * shards // width,
        next(idents),
    )
    size = width // shards
    dims = average_decay.shape[1]
    g_feed_in, g_feed_out, g_feed_gain, g_feed_shift, g_feed_out_bias, g_feed_in_bias = assemble(
        feed_outputs,
        (feed_zero, feed_one),
        (),
        ((size, hidden), (hidden // shards, width)),
        ((size,), (size,), (size,), (hidden // shards,)),
        shards,
    )
    base = base_weight.shape[2]
    g_value, g_base, g_out, g_value_bias, g_base_bias, g_pair, g_query, *rest = assemble(
        attention_outputs,
        (attention_zero, attention_one),
        (channels, average_decay, average_input, average_output),
        ((size, wide), (size, base), (wide // shards, width)),
        ((wide // shards,), (base // shards,), (2, keyed // shards), (keyed // shards,))
        + ((size,),) * 3
        + ((dims, size),) * 3,
        shards,
    )
    g_gain, g_shift, g_skip, g_decay, g_input, g_output = rest
    return (
        block_out[None],
        input_grad[None],
        g_gain,
        g_shift,
        g_decay,
        g_input,
        g_output,
        g_skip,
        g_value,
        g_value_bias,
        g_base,
        g_base_bias,
        g_pair,
        g_query,
        g_out,
        g_feed_gain,
        g_feed_shift,
        g_feed_in,
        g_feed_in_bias,
        g_feed_out,
        g_feed_out_bias,
    )


def solution(mesh):
    row, row2 = P(None, "dp"), P(None, "dp", None)
    deep = P(None, None, "dp")
    in_specs = (
        P("dp", None, None),
        P("dp"),
        P("dp", None, None),
        row,
        row,
        deep,
        deep,
        deep,
        row,
        row2,
        row,
        row2,
        row,
        deep,
        row,
        row2,
        row,
        row,
        row2,
        row,
        row2,
        row,
    )
    out_specs = (
        P("dp", "section", None),
        P("dp", "section", None),
        row,
        row,
        deep,
        deep,
        deep,
        row,
        row2,
        row,
        row2,
        row,
        deep,
        row,
        row2,
        row,
        row,
        row2,
        row,
        row2,
        row,
    )
    return jax.shard_map(body, mesh=mesh, in_specs=in_specs, out_specs=out_specs, check_vma=False)
```
